32 devices in a mesh: dp: 4 (over y, x), expert: 8 (over z, core).
Axes of the slice: x: 2, y: 2, z: 4, core: 2. Of those that a mesh axis runs over, the one named last changes fastest.
Arguments:
- tokens: bfloat16 [32, 197, 768], P(('dp', 'expert')), may hold values from -6 to 6
- cotangent: bfloat16 [32, 197, 768], P(('dp', 'expert')), may hold values from -6 to 6
- expert_picks: int32 [6304, 2], P(('dp', 'expert')), may hold values from 0 to 7, all different within a row
- priority: int32 [32, 197], P(('dp', 'expert')), may hold values from 0 to 196, each once within a row
- dense_master: float32 [9449472], P(('dp', 'expert')), may hold values from -2 to 2
- dense_momentum: float32 [9449472], P(('dp', 'expert')), may hold values from -1.25 to 1.25
- dense_variance: float32 [9449472], P(('dp', 'expert')), may hold values from 0.005 to 0.08
- expert_master: float32 [8, 4718592], P('expert', 'dp'), may hold values from -6 to 6
- expert_momentum: float32 [8, 4718592], P('expert', 'dp'), may hold values from -0.1875 to 0.1875
- expert_variance: float32 [8, 4718592], P('expert', 'dp'), may hold values from 5e-05 to 0.0008
Outputs:
- block_output: float32 [32, 197, 768], P(('dp', 'expert'))
- input_grad: float32 [32, 197, 768], P(('dp', 'expert'))
- dense_grad: float32 [9449472], P(('dp', 'expert'))
- expert_grad: float32 [8, 4718592], P('expert', 'dp')
- dense_update: float32 [9449472], P(('dp', 'expert'))
- momentum_dense: float32 [9449472], P(('dp', 'expert'))
- variance_dense: float32 [9449472], P(('dp', 'expert'))
- expert_update: float32 [8, 4718592], P('expert', 'dp')
- momentum_expert: float32 [8, 4718592], P('expert', 'dp')
- variance_expert: float32 [8, 4718592], P('expert', 'dp')
- gain_grads: float32 [4, 768], replicated
The draws below stay inside these ranges and needn't reach their ends.
Inputs may be any that keep to these rules, and one draw needn't show every extreme that they name: `expert_picks`: each row names two different experts. `priority`: each row is a permutation of the ranks of one group's tokens.
All inputs are finite; a program needn't handle non-finite values.
Results may differ from the reference program's by a relative error of at most 0.02.
Values may be sent and summed in bfloat16 or wider, within the bound.
No kernel may reach another device: no remote copies, remote signals or barrier semaphores. Data moves between devices by JAX's collectives and lax.ppermute only.
A program may use at most 320 MiB of HBM per device.

```python
import math
import jax
import jax.numpy as jnp
from jax import lax

D = 768
HEADS = 12
HEAD_DIM = 64
FF = 3072
SEQ = 197
IMG_DEV = 1
EXPERTS = 8
BLOCKS = 32
IMAGES = 32
TOK_DEV = 197
TOKENS = 6304
CAPACITY = 49
DENSE_RAW = 9446400
DENSE_PARAMS = 9449472
EXPERT_PARAMS = 4718592
PARAM_COUNT = 47198208


def draw_dense_master(key, part):
    key = jax.random.fold_in(key, 11)
    layouts = [(D * D, D ** (-0.5))] * 3 + [(D * D, 4.0 * D ** (-0.5))]
    layouts = layouts * 2 + [(D * FF, 4.0 * D ** (-0.5)), (FF * D, 0.5 * FF ** (-0.5)), (D * EXPERTS, 0.7 * D ** (-0.5)), (4 * D, 0.1)]
    tail = DENSE_PARAMS - DENSE_RAW
    if tail > 0:
        layouts = layouts + [(tail, 0.1)]
    factors = jnp.concatenate([jnp.full((length,), factor, jnp.float32) for length, factor in layouts])
    offsets = jnp.concatenate([jnp.zeros((DENSE_RAW - 4 * D,), jnp.float32), jnp.ones((4 * D,), jnp.float32), jnp.zeros((tail,), jnp.float32)])
    sample = jax.random.truncated_normal(key, -4.0, 4.0, (DENSE_PARAMS,), jnp.float32)
    return sample * factors + offsets


def draw_expert_master(key, part):
    key = jax.random.fold_in(key, 23)
    sample = jax.random.truncated_normal(key, -4.0, 4.0, (EXPERTS, 2 * D * FF), jnp.float32)
    column = jnp.arange(2 * D * FF)
    factors = jnp.where(column < D * FF, D ** (-0.5), 12.0 * FF ** (-0.5)).astype(jnp.float32)
    return sample * factors[None, :]


def shard_levels(rng, dims, shards, least, top_value):
    level = 1.0
    for axis_at, parts in shards:
        draws = jax.random.uniform(jax.random.fold_in(jax.random.fold_in(rng, 6), axis_at), (parts,), jnp.float32, least / len(shards), top_value / len(shards))
        level = level * jnp.repeat(jnp.exp(draws), dims[axis_at] // parts).reshape((-1,) + (1,) * (len(dims) - 1 - axis_at))
    return level


def choose_distinct(key, rows, amount, top, lift):
    order = jax.random.permutation(jax.random.fold_in(key, 1), amount)
    favour = order
    for power in range(3):
        favour = favour * favour // amount
    favour = favour * lift // amount
    lots = jax.random.randint(jax.random.fold_in(key, 2), (rows, amount), 0, 4096) + favour
    holders = jax.random.permutation(jax.random.fold_in(key, 3), rows)[jnp.arange(amount) % rows]
    lots = jnp.where(jnp.arange(rows)[:, None] == holders[None, :], 1 << 14, lots)
    score = lots * amount + jnp.arange(amount)
    return lax.top_k(score.astype(jnp.int32), top)[1].astype(jnp.int32)


def scatter_about(rng, dims, deviation, most, cuts=(), held_as=jnp.bfloat16):
    values = jax.random.normal(rng, dims, jnp.float32) * deviation
    if len(cuts) > 0:
        values = shard_levels(rng, dims, cuts, -0.22, 0.18) * values
    return jnp.clip(values, min=-most, max=most).astype(held_as)


def setup_inputs(seed: int = 0) -> dict:
    keys = jax.random.split(jax.random.key(seed), 11)
    return {
        "tokens": scatter_about(keys[0], (IMAGES, SEQ, D), 1.0, 6.0, ((0, 32),)),
        "cotangent": scatter_about(keys[1], (IMAGES, SEQ, D), 1.0, 6.0, ((0, 32),)),
        "expert_picks": choose_distinct(keys[2], TOKENS, EXPERTS, 2, 2048),
        "priority": jax.vmap(lambda own: jax.random.permutation(own, TOK_DEV))(jax.random.split(keys[3], BLOCKS)).reshape((BLOCKS, TOK_DEV)).astype(jnp.int32),
        "dense_master": draw_dense_master(jax.random.fold_in(keys[10], 71), 0),
        "dense_momentum": scatter_about(keys[5], (DENSE_PARAMS,), 0.2, 1.25, ((0, 32),), jnp.float32),
        "dense_variance": jnp.clip(jnp.exp(math.log(0.08) - 2.7725887 * jax.random.uniform(keys[6], (DENSE_PARAMS,), jnp.float32) ** shard_levels(keys[6], (DENSE_PARAMS,), ((0, 32),), -0.2, 0.2)), 0.005, 0.08),
        "expert_master": draw_expert_master(jax.random.fold_in(keys[10], 71), 0),
        "expert_momentum": scatter_about(keys[8], (EXPERTS, EXPERT_PARAMS), 0.03, 0.1875, ((0, 8), (1, 4)), jnp.float32),
        "expert_variance": jnp.clip(jnp.exp(math.log(0.0008) - 2.7725887 * jax.random.uniform(keys[9], (EXPERTS, EXPERT_PARAMS), jnp.float32) ** shard_levels(keys[9], (EXPERTS, EXPERT_PARAMS), ((0, 8), (1, 4)), -0.2, 0.2)), 4.999999873689376e-05, 0.0008),
    }


@jax.custom_vjp
def low(v):
    return lax.optimization_barrier(v.astype(jnp.bfloat16)).astype(jnp.float32)

@jax.custom_vjp
def low_back(v):
    return v

def low_keep(v):
    return (low(v), None)

def low_pass(kept, grad):
    return (grad,)

def back_keep(v):
    return (v, None)

def back_low(kept, grad):
    return (low(grad),)
low.defvjp(low_keep, low_pass)
low_back.defvjp(back_keep, back_low)
eps_norm = 1e-06
beta_first = 0.9
beta_second = 0.999
adam_eps = 1e-08
adam_step = 10.0
highest = lax.Precision.HIGHEST

def product(left, right):
    return jnp.dot(left, right, precision=highest, preferred_element_type=jnp.float32)

def layer_norm(hidden, gain):
    center = hidden - lax.optimization_barrier(jnp.mean(hidden, axis=-1, keepdims=True))
    spread = lax.optimization_barrier(jnp.mean(center * center, axis=-1, keepdims=True))
    return center * lax.rsqrt(spread + eps_norm) * gain

def unpack(flat_params, experts):
    layouts = [(D, D)] * 8 + [(D, FF), (FF, D), (D, experts)] + [(D,)] * 4
    pieces = []
    offset = 0
    for layout in layouts:
        length = math.prod(layout)
        pieces.append(flat_params[offset:offset + length].reshape(layout))
        offset += length
    return pieces

def slot_places(picks, ranks, experts):
    token_count = ranks.shape[0]
    order_keys = jnp.stack([ranks, ranks + token_count], axis=1)
    expert_by_key = jnp.zeros((2 * token_count,), jnp.int32).at[order_keys.reshape(-1)].set(picks.reshape(-1))
    one_hot = (expert_by_key[:, None] == jnp.arange(experts, dtype=jnp.int32)[None, :]).astype(jnp.int32)
    earlier = jnp.cumsum(one_hot, axis=0) - one_hot
    place_by_key = lax.optimization_barrier(jnp.sum(earlier * one_hot, axis=1))
    return place_by_key[order_keys]

def routing_slots(expert_picks, priority):
    picks_grouped = expert_picks.reshape(BLOCKS, TOK_DEV, 2)
    places = jax.vmap(lambda picks, ranks: slot_places(picks, ranks, EXPERTS))(picks_grouped, priority)
    admitted = places < CAPACITY
    group_index = jnp.arange(BLOCKS, dtype=jnp.int32)[:, None, None]
    pair_slots = jnp.where(admitted, picks_grouped * (BLOCKS * CAPACITY) + group_index * CAPACITY + places, EXPERTS * BLOCKS * CAPACITY)
    return pair_slots.reshape(TOKENS, 2).astype(jnp.int32)

def attend(normed, weights):
    w_query, w_key, w_value, w_out = weights
    images = normed.shape[0]
    head_split = (images, SEQ, HEADS, HEAD_DIM)
    queries = low_back(low(jnp.einsum('gsd,de->gse', normed, w_query, precision=highest))).reshape(head_split)
    key_rows = low_back(low(jnp.einsum('gsd,de->gse', normed, w_key, precision=highest))).reshape(head_split)
    value_rows = low_back(low(jnp.einsum('gsd,de->gse', normed, w_value, precision=highest))).reshape(head_split)
    scores = low_back(jnp.einsum('gqhc,gkhc->ghqk', queries, key_rows, precision=highest) * HEAD_DIM ** (-0.5))
    soft_weights = jax.nn.softmax(scores, axis=-1)
    mixed = jnp.einsum('ghqk,gkhc->gqhc', low(soft_weights), value_rows, precision=highest)
    mixed = low_back(low(mixed.reshape(images, SEQ, D)))
    return low_back(jnp.einsum('gsd,de->gse', mixed, w_out, precision=highest))

def dense_mlp(row_block, w_first, w_second):
    pre_act = low_back(product(low(row_block), w_first))
    activated = low(jax.nn.gelu(pre_act, approximate=False))
    return low_back(product(activated, w_second))

def expert_mlp(row_block, w_first, w_second):
    pre_act = low_back(product(row_block, w_first))
    activated = low(jax.nn.gelu(pre_act, approximate=False))
    return low_back(low(product(activated, w_second)))

def mixture(normed, w_router, expert_first, expert_second, expert_picks, pair_slots, slot_token):
    rows_low = low(normed)
    logits = low_back(product(rows_low, w_router))
    soft_weights = jax.nn.softmax(logits, axis=-1)
    gate_values = jnp.take_along_axis(soft_weights, expert_picks, axis=1)
    total_slots = EXPERTS * BLOCKS * CAPACITY
    padded = jnp.concatenate([rows_low, jnp.zeros((1, D), jnp.float32)], axis=0)
    dispatched = low_back(padded[slot_token]).reshape(EXPERTS, BLOCKS * CAPACITY, D)
    returned = lax.map(jax.checkpoint(lambda triple: expert_mlp(triple[0], triple[1], triple[2])), (dispatched, expert_first, expert_second))
    returned = jnp.concatenate([returned.reshape(total_slots, D), jnp.zeros((1, D), jnp.float32)], axis=0)
    pair_out = returned[pair_slots]
    return lax.optimization_barrier(jnp.sum(gate_values[:, :, None] * pair_out, axis=1))

def forward(inputs, dense_params, expert_params, expert_picks, pair_slots, slot_token):
    pieces = unpack(low(dense_params), EXPERTS)
    expert_low = low(expert_params)
    expert_first = expert_low[:, :D * FF].reshape(EXPERTS, D, FF)
    expert_second = expert_low[:, D * FF:].reshape(EXPERTS, FF, D)
    hidden = inputs
    for layer_index in range(2):
        attn_weights = tuple(pieces[4 * layer_index:4 * layer_index + 4])
        normed = low(layer_norm(hidden, pieces[11 + 2 * layer_index]))
        grouped = normed.reshape(BLOCKS, IMG_DEV, SEQ, D)
        branch = lax.map(jax.checkpoint(lambda group_rows: attend(group_rows, attn_weights)), grouped)
        hidden = hidden + branch.reshape(IMAGES, SEQ, D)
        normed = layer_norm(hidden, pieces[12 + 2 * layer_index])
        if layer_index == 0:
            branch = lax.map(jax.checkpoint(lambda row_block: dense_mlp(row_block, pieces[8], pieces[9])), normed.reshape(BLOCKS, TOK_DEV, D))
        else:
            branch = mixture(normed.reshape(TOKENS, D), pieces[10], expert_first, expert_second, expert_picks, pair_slots, slot_token)
        hidden = hidden + branch.reshape(IMAGES, SEQ, D)
    return hidden

def adam_update(momentum, variance, gradient, clip_factor):
    clipped = gradient * clip_factor
    momentum_new = beta_first * momentum + (1.0 - beta_first) * clipped
    variance_new = beta_second * variance + (1.0 - beta_second) * clipped * clipped
    first_hat = momentum_new / (1.0 - beta_first ** adam_step)
    second_hat = variance_new / (1.0 - beta_second ** adam_step)
    return (-first_hat / (jnp.sqrt(second_hat) + adam_eps), momentum_new, variance_new)

def reference(tokens, cotangent, expert_picks, priority, dense_master, dense_momentum, dense_variance, expert_master, expert_momentum, expert_variance):
    pair_slots = routing_slots(expert_picks, priority)
    total_slots = EXPERTS * BLOCKS * CAPACITY
    pair_token = jnp.arange(2 * TOKENS, dtype=jnp.int32) // 2
    slot_token = jnp.full((total_slots + 1,), TOKENS, jnp.int32).at[pair_slots.reshape(-1)].set(pair_token)
    slot_token = slot_token[:total_slots]

    def run(inputs, dense_params, expert_params):
        return forward(inputs, dense_params, expert_params, expert_picks, pair_slots, slot_token)
    output, pullback = jax.vjp(run, tokens.astype(jnp.float32), dense_master, expert_master)
    input_grad, dense_grad, expert_grad = pullback(cotangent.astype(jnp.float32))
    gain_offset = 8 * D * D + 2 * D * FF + D * EXPERTS
    gain_grads = dense_grad[gain_offset:gain_offset + 4 * D].reshape(4, D)
    square_sum = jnp.sum(dense_grad * dense_grad) + jnp.sum(expert_grad * expert_grad)
    clip_factor = jnp.minimum(1.0, jnp.sqrt(PARAM_COUNT / (square_sum + 1e-06)))
    dense_update, momentum_dense, variance_dense = adam_update(dense_momentum, dense_variance, dense_grad, clip_factor)
    expert_update, momentum_expert, variance_expert = adam_update(expert_momentum, expert_variance, expert_grad, clip_factor)
    return (output, input_grad, dense_grad, expert_grad, dense_update, momentum_dense, variance_dense, expert_update, momentum_expert, variance_expert, gain_grads)
```

```python
import functools
import math

import jax
import jax.numpy as jnp
from jax import lax
from jax.experimental import pallas as pl
from jax.experimental.pallas import tpu as pltpu
from jax.sharding import PartitionSpec as P

HEADS = 12
HEAD_DIM = 64
LANES = 128

f32 = jnp.float32
bf16 = jnp.bfloat16

eps_norm = 1e-06
beta_first = 0.9
beta_second = 0.999
adam_eps = 1e-08
adam_step = 10.0

VMEM = pl.BlockSpec(memory_space=pltpu.VMEM)
SMEM = pl.BlockSpec(memory_space=pltpu.SMEM)


def params(mib=56):
    return pltpu.CompilerParams(vmem_limit_bytes=mib << 20)


def cost(flops, nbytes, trans=0):
    return pl.CostEstimate(flops=int(flops), bytes_accessed=int(nbytes), transcendentals=int(trans))


def dot(a, b):
    return lax.dot_general(a, b, (((1,), (0,)), ((), ())), preferred_element_type=f32)


def dot_nt(a, b):
    return lax.dot_general(a, b, (((1,), (1,)), ((), ())), preferred_element_type=f32)


def dot_tn(a, b):
    return lax.dot_general(a, b, (((0,), (0,)), ((), ())), preferred_element_type=f32)


def norm_rows(hidden):
    center = hidden - jnp.mean(hidden, axis=-1, keepdims=True)
    inverse = lax.rsqrt(jnp.mean(center * center, axis=-1, keepdims=True) + eps_norm)
    return center * inverse, inverse


def norm_back(upstream, normed, inverse, gain):
    scaled = upstream * gain
    gain_grad = jnp.sum(upstream * normed, axis=0, keepdims=True)
    centered = (
        scaled
        - jnp.mean(scaled, axis=-1, keepdims=True)
        - normed * jnp.mean(scaled * normed, axis=-1, keepdims=True)
    )
    return inverse * centered, gain_grad


def normal_cdf(v):
    return 0.5 * (1.0 + lax.erf(v * 0.7071067811865476))


def density(v):
    return jnp.exp(-0.5 * v * v) * 0.3989422804014327


def to_rows(read, write, first_q, rows, wide, tiles):
    if wide:
        quarter = rows // 4
        for q in range(4):
            for j in range(tiles):
                write(q * quarter, quarter, j, read(first_q + tiles * q + j, quarter, 4 * tiles))
    else:
        for j in range(tiles):
            write(0, rows, j, read(first_q + j, rows, tiles))


def pack_dense_kernel(dims, k_ref, tail_ref, own_ref, out_ref, buf):
    rows, tail_rows, tail, own, step, tiles, chunks, wide_ok = dims
    buf[0:tail] = tail_ref[...]
    buf[tail : tail + own] = own_ref[...]
    buf[tail + own :] = jnp.zeros((buf.shape[0] - tail - own, LANES), f32)
    k = k_ref[0]
    start = tail - step * k

    def read(first, count, stride):
        return buf[pl.ds(first, count, stride=stride), :]

    def write(first, count, j, value):
        out_ref[first : first + count, LANES * j : LANES * (j + 1)] = value.astype(bf16)

    wide = (k >= chunks // 2) & (k < 3 * chunks // 4) & wide_ok

    @pl.when(wide)
    def _():
        to_rows(read, write, start, rows, True, tiles)

    @pl.when(jnp.logical_not(wide))
    def _():
        to_rows(read, write, start, rows, False, tiles)

    for j in range(tiles):
        write(rows, tail_rows, j, read(own + j, tail_rows, tiles))


def pack_expert_kernel(dims, wide_ref, own_ref, out_ref):
    rows, tiles = dims

    def read(first, count, stride):
        return own_ref[pl.ds(first, count, stride=stride), :]

    def write(first, count, j, value):
        out_ref[first : first + count, LANES * j : LANES * (j + 1)] = value.astype(bf16)

    wide = wide_ref[0] > 0

    @pl.when(wide)
    def _():
        to_rows(read, write, 0, rows, True, tiles)

    @pl.when(jnp.logical_not(wide))
    def _():
        to_rows(read, write, 0, rows, False, tiles)


def unpack_kernel(dims, wide_ref, rows_ref, out_ref, square_ref):
    rows, tiles = dims
    wide = wide_ref[0] > 0

    def store(is_wide):
        total = jnp.zeros((1, LANES), f32)
        quarter = rows // 4
        for q in range(4):
            for j in range(tiles):
                piece = rows_ref[q * quarter : (q + 1) * quarter, LANES * j : LANES * (j + 1)].astype(f32)
                if is_wide:
                    out_ref[pl.ds(tiles * q + j, quarter, stride=4 * tiles), :] = piece
                else:
                    out_ref[pl.ds(tiles * quarter * q + j, quarter, stride=tiles), :] = piece
                total = total + jnp.sum(piece * piece, axis=0, keepdims=True)
        square_ref[...] = total

    @pl.when(wide)
    def _():
        store(True)

    @pl.when(jnp.logical_not(wide))
    def _():
        store(False)


def shift_kernel(dims, k_ref, flat_ref, head_ref, out_ref, square_ref, buf):
    step, own = dims
    count = flat_ref.shape[0]
    buf[0:count] = flat_ref[...]
    buf[count : count + head_ref.shape[0]] = head_ref[...]
    value = buf[pl.ds(step * k_ref[0], own), :]
    out_ref[...] = value
    square_ref[...] = jnp.sum(value * value, axis=0, keepdims=True)


def adam_kernel(clip_ref, grad_ref, momentum_ref, variance_ref, update_ref, momentum_out, variance_out):
    clipped = grad_ref[...] * clip_ref[0]
    momentum_new = beta_first * momentum_ref[...] + (1.0 - beta_first) * clipped
    variance_new = beta_second * variance_ref[...] + (1.0 - beta_second) * clipped * clipped
    first_hat = momentum_new / (1.0 - beta_first**adam_step)
    second_hat = variance_new / (1.0 - beta_second**adam_step)
    update_ref[...] = -first_hat / (jnp.sqrt(second_hat) + adam_eps)
    momentum_out[...] = momentum_new
    variance_out[...] = variance_new


def adam(clip, grad, momentum, variance, block):
    count = grad.shape[0]
    spec = pl.BlockSpec((block, LANES), lambda i: (i, 0))
    shape = jax.ShapeDtypeStruct(grad.shape, f32)
    return pl.pallas_call(
        adam_kernel,
        grid=(pl.cdiv(count, block),),
        in_specs=[SMEM, spec, spec, spec],
        out_specs=[spec] * 3,
        out_shape=[shape] * 3,
        compiler_params=params(),
        cost_estimate=cost(20 * grad.size, 24 * grad.size, 2 * grad.size),
        name="adam",
    )(clip, grad, momentum, variance)


def route_kernel(experts, capacity, stride, prio_row, prio_col, picks, picks_t, cols_ref, rows_ref):
    seq = picks.shape[0]
    before = (prio_row[...] < prio_col[...]).astype(f32).astype(bf16)
    lane = lax.broadcasted_iota(jnp.int32, (seq, experts), 1)
    sub = lax.broadcasted_iota(jnp.int32, (experts, seq), 0)
    hot = [(picks[:, j : j + 1] == lane).astype(f32) for j in range(2)]
    hot_t = [(picks_t[j : j + 1, :] == sub).astype(f32) for j in range(2)]
    first = jnp.sum(hot[0], axis=0, keepdims=True)
    first_t = jnp.sum(hot_t[0], axis=1, keepdims=True)
    for j in range(2):
        earlier = dot(before, hot[j].astype(bf16)) + (first if j else 0.0)
        earlier_t = dot_nt(hot_t[j].astype(bf16), before) + (first_t if j else 0.0)
        place = jnp.sum(earlier * hot[j], axis=1, keepdims=True).astype(jnp.int32)
        place_t = jnp.sum(earlier_t * hot_t[j], axis=0, keepdims=True).astype(jnp.int32)
        cols_ref[:, j : j + 1] = jnp.where(
            place < capacity, picks[:, j : j + 1] * stride + place, -1
        )
        rows_ref[j : j + 1, :] = jnp.where(
            place_t < capacity, picks_t[j : j + 1, :] * stride + place_t, -1
        )


def head_masks():
    lane = lax.broadcasted_iota(jnp.int32, (1, 2 * HEAD_DIM), 1)
    first = (lane < HEAD_DIM).astype(f32)
    return first.astype(bf16), (1.0 - first).astype(bf16)


def soft_scores(queries, key_rows, key_ok):
    scores = dot_nt(queries, key_rows) * HEAD_DIM ** (-0.5)
    scores = jnp.where(key_ok, scores, -1e30)
    top = jnp.max(scores, axis=-1, keepdims=True)
    raised = jnp.exp(scores - top)
    return raised * (1.0 / jnp.sum(raised, axis=-1, keepdims=True))


def matrix(w_ref, index):
    per = w_ref.shape[0] // 4
    width = w_ref.shape[2]
    rows = width // per
    return w_ref[index * per : (index + 1) * per, 0:rows, :].reshape(width, width)


def quarter_in(w_ref, q):
    width = w_ref.shape[2]
    rows = width // w_ref.shape[0]
    return w_ref[:, q * rows : (q + 1) * rows, :].reshape(width, width)


def attn_fwd_kernel(seq, stream_ref, gain_ref, w_ref, out_ref, a_ref, q_ref, k_ref, v_ref, o_ref):
    normed, _ = norm_rows(stream_ref[...])
    a_ref[...] = (normed * gain_ref[...]).astype(bf16)
    for index, ref in enumerate((q_ref, k_ref, v_ref)):
        ref[...] = dot(a_ref[...], matrix(w_ref, index)).astype(bf16)
    count = stream_ref.shape[0]
    key_ok = lax.broadcasted_iota(jnp.int32, (count, count), 1) < seq
    masks = head_masks()
    for pair in range(HEADS // 2):
        lanes = slice(2 * HEAD_DIM * pair, 2 * HEAD_DIM * (pair + 1))
        mixed = None
        for mask in masks:
            soft = soft_scores(q_ref[:, lanes] * mask, k_ref[:, lanes], key_ok).astype(bf16)
            part = dot(soft, v_ref[:, lanes] * mask)
            mixed = part if mixed is None else mixed + part
        o_ref[:, lanes] = mixed.astype(bf16)
    out_ref[...] = stream_ref[...] + dot(o_ref[...], matrix(w_ref, 3))


def attn_bwd_kernel(
    seq, grad_ref, stream_ref, gain_ref, w_ref, a_ref, q_ref, k_ref, v_ref, o_ref,
    out_ref, gain_out, dw_ref, do_ref, dq_ref, dk_ref, dv_ref,
):
    width = grad_ref.shape[1]
    branch = grad_ref[...].astype(bf16)

    def put(index, value):
        per = dw_ref.shape[0] // 4
        dw_ref[index * per : (index + 1) * per] = value.astype(bf16).reshape(per, width // per, width)

    do_ref[...] = dot_nt(branch, matrix(w_ref, 3)).astype(bf16)
    put(3, dot_tn(o_ref[...], branch))
    count = grad_ref.shape[0]
    key_ok = lax.broadcasted_iota(jnp.int32, (count, count), 1) < seq
    masks = head_masks()
    scale = HEAD_DIM ** (-0.5)
    for pair in range(HEADS // 2):
        lanes = slice(2 * HEAD_DIM * pair, 2 * HEAD_DIM * (pair + 1))
        dq = dk = dv = None
        for mask in masks:
            q_h = q_ref[:, lanes] * mask
            k_h = k_ref[:, lanes] * mask
            do_h = do_ref[:, lanes] * mask
            soft = soft_scores(q_h, k_ref[:, lanes], key_ok)
            dsoft = dot_nt(do_h, v_ref[:, lanes])
            dv_h = dot_tn(soft.astype(bf16), do_h)
            inner = jnp.sum(dsoft * soft, axis=-1, keepdims=True)
            dscore = (soft * (dsoft - inner)).astype(bf16)
            dq_h = dot(dscore, k_h)
            dk_h = dot_tn(dscore, q_h)
            dq = dq_h if dq is None else dq + dq_h
            dk = dk_h if dk is None else dk + dk_h
            dv = dv_h if dv is None else dv + dv_h
        dq_ref[:, lanes] = (dq * scale).astype(bf16)
        dk_ref[:, lanes] = (dk * scale).astype(bf16)
        dv_ref[:, lanes] = dv.astype(bf16)
    back = None
    for index, ref in enumerate((dq_ref, dk_ref, dv_ref)):
        put(index, dot_tn(a_ref[...], ref[...]))
        part = dot_nt(ref[...], matrix(w_ref, index))
        back = part if back is None else back + part
    normed, inverse = norm_rows(stream_ref[...])
    addend, gain_grad = norm_back(back, normed, inverse, gain_ref[...])
    out_ref[...] = grad_ref[...] + addend
    gain_out[...] = gain_grad


def mlp_fwd_kernel(stream_ref, gain_ref, w1_ref, w2_ref, out_ref, b_ref, u_ref):
    width = stream_ref.shape[1]
    normed, _ = norm_rows(stream_ref[...])
    b_ref[...] = (normed * gain_ref[...]).astype(bf16)
    out_ref[...] = stream_ref[...]
    total = None
    for q in range(4):
        pre = dot(b_ref[...], quarter_in(w1_ref, q))
        u_ref[:, q * width : (q + 1) * width] = pre
        part = dot((pre * normal_cdf(pre)).astype(bf16), matrix(w2_ref, q))
        total = part if total is None else total + part
    out_ref[...] = stream_ref[...] + total


def mlp_bwd_kernel(
    grad_ref, stream_ref, gain_ref, w1_ref, w2_ref, b_ref, u_ref, out_ref, gain_out, dw1_ref, dw2_ref
):
    width = grad_ref.shape[1]
    upper = grad_ref[...].astype(bf16)
    back = None
    for q in range(4):
        pre = u_ref[:, q * width : (q + 1) * width]
        cdf = normal_cdf(pre)
        act = (pre * cdf).astype(bf16)
        per = dw2_ref.shape[0] // 4
        dw2_ref[q * per : (q + 1) * per] = dot_tn(act, upper).astype(bf16).reshape(per, width // per, width)
        dact = dot_nt(upper, matrix(w2_ref, q))
        dpre = (dact * (cdf + pre * density(pre))).astype(bf16)
        groups = dw1_ref.shape[0]
        rows = width // groups
        dw1_ref[:, q * rows : (q + 1) * rows, :] = (
            dot_tn(b_ref[...], dpre).astype(bf16).reshape(groups, rows, width)
        )
        part = dot_nt(dpre, quarter_in(w1_ref, q))
        back = part if back is None else back + part
    normed, inverse = norm_rows(stream_ref[...])
    addend, gain_grad = norm_back(back, normed, inverse, gain_ref[...])
    out_ref[...] = grad_ref[...] + addend
    gain_out[...] = gain_grad


def pick_hots(picks, experts):
    lane = lax.broadcasted_iota(jnp.int32, (picks.shape[0], experts), 1)
    return [(picks[:, j : j + 1] == lane).astype(f32) for j in range(2)]


def softmax_rows(logits):
    raised = jnp.exp(logits - jnp.max(logits, axis=-1, keepdims=True))
    return raised / jnp.sum(raised, axis=-1, keepdims=True)


def dispatch_kernel(
    slots, stream_ref, gain_ref, wr_ref, picks_ref, rows_ref, cot_ref, c_ref, probs_ref, x_ref, dy_ref
):
    count = stream_ref.shape[0]
    experts = wr_ref.shape[1]
    normed, _ = norm_rows(stream_ref[...])
    c_ref[...] = (normed * gain_ref[...]).astype(bf16)
    probs = softmax_rows(dot(c_ref[...], wr_ref[...]))
    probs_ref[...] = probs
    hots = pick_hots(picks_ref, experts)
    sub = lax.broadcasted_iota(jnp.int32, (slots, count), 0)
    chosen = None
    dy = None
    for j in range(2):
        gate = jnp.sum(probs * hots[j], axis=-1, keepdims=True)
        select = (rows_ref[j : j + 1, :] == sub).astype(f32).astype(bf16)
        chosen = select if chosen is None else chosen + select
        part = dot(select, (gate * cot_ref[...]).astype(bf16))
        dy = part if dy is None else dy + part
    x_ref[...] = dot(chosen, c_ref[...]).astype(bf16)
    dy_ref[...] = dy.astype(bf16)


def expert_kernel(x_ref, dy_ref, u1_ref, u2_ref, y_ref, dx_ref, act_ref, dpre_ref, y_sum, dx_sum):
    q = pl.program_id(0)
    width = x_ref.shape[1]
    first = u1_ref[...].reshape(width, width)
    pre = dot(x_ref[...], first)
    cdf = normal_cdf(pre)
    act = (pre * cdf).astype(bf16)
    act_ref[...] = act
    dact = dot_nt(dy_ref[...], u2_ref[...])
    dpre = (dact * (cdf + pre * density(pre))).astype(bf16)
    dpre_ref[...] = dpre
    y_part = dot(act, u2_ref[...])
    dx_part = dot_nt(dpre, first)

    @pl.when(q == 0)
    def _():
        y_sum[...] = y_part
        dx_sum[...] = dx_part

    @pl.when(q > 0)
    def _():
        y_sum[...] += y_part
        dx_sum[...] += dx_part

    @pl.when(q == pl.num_programs(0) - 1)
    def _():
        y_ref[...] = y_sum[...].astype(bf16)
        dx_ref[...] = dx_sum[...].astype(bf16)


def expert_grad_kernel(x_ref, dy_ref, act_ref, dpre_ref, out_ref):
    q = pl.program_id(0)
    groups, _, rows, width = out_ref.shape
    half = groups // 2
    out_ref[0:half, q] = dot_tn(x_ref[...], dpre_ref[...]).astype(bf16).reshape(half, rows, width)
    second = dot_tn(act_ref[...], dy_ref[...]).astype(bf16)
    per = width // rows
    for part in range(per):
        flat = q * per + part
        out_ref[half + flat // 4, flat % 4] = second[part * rows : (part + 1) * rows]


def combine_kernel(
    stream_ref, gain_ref, wr_ref, picks_ref, cols_ref, cot_ref, c_ref, probs_ref, y_ref, dx_ref,
    out_ref, grad_ref, gain_out, router_out,
):
    count = stream_ref.shape[0]
    slots = y_ref.shape[0]
    experts = wr_ref.shape[1]
    probs = probs_ref[...]
    hots = pick_hots(picks_ref, experts)
    lane = lax.broadcasted_iota(jnp.int32, (count, slots), 1)
    cot = cot_ref[...]
    total = stream_ref[...]
    chosen = None
    prob_grad = None
    for j in range(2):
        select = (cols_ref[:, j : j + 1] == lane).astype(f32).astype(bf16)
        chosen = select if chosen is None else chosen + select
        pair_out = dot(select, y_ref[...])
        gate = jnp.sum(probs * hots[j], axis=-1, keepdims=True)
        total = total + gate * pair_out
        part = jnp.sum(cot * pair_out, axis=-1, keepdims=True) * hots[j]
        prob_grad = part if prob_grad is None else prob_grad + part
    out_ref[...] = total
    logit_grad = probs * (prob_grad - jnp.sum(prob_grad * probs, axis=-1, keepdims=True))
    logit_grad = logit_grad.astype(bf16)
    router_out[...] = dot_tn(c_ref[...], logit_grad)
    back = dot(chosen, dx_ref[...]) + dot_nt(logit_grad, wr_ref[...])
    normed, inverse = norm_rows(stream_ref[...])
    addend, gain_grad = norm_back(back, normed, inverse, gain_ref[...])
    grad_ref[...] = cot + addend
    gain_out[...] = gain_grad


def all_sum(value, axes):
    for axis in axes:
        size = lax.axis_size(axis)
        hop = 1
        while hop < size:
            value = value + lax.ppermute(value, axis, [(i, i ^ hop) for i in range(size)])
            hop *= 2
    return value


def shape(dims, dtype=f32):
    return jax.ShapeDtypeStruct(dims, dtype)


def on_device(
    tokens,
    cotangent,
    expert_picks,
    priority,
    dense_master,
    dense_momentum,
    dense_variance,
    expert_master,
    expert_momentum,
    expert_variance,
):
    both = ("dp", "expert")
    dp_ranks = lax.axis_size("dp")
    expert_ranks = lax.axis_size("expert")
    devices = dp_ranks * expert_ranks
    local_experts = expert_master.shape[0]
    experts = local_experts * expert_ranks
    images, seq, width = tokens.shape
    assert local_experts == 1 and images == 1
    tiles = width // LANES
    me = lax.axis_index("dp") * expert_ranks + lax.axis_index("expert")
    me_arr = me.reshape(1).astype(jnp.int32)

    own = dense_master.shape[0] // LANES
    expert_flat = expert_master.shape[1] // LANES
    hidden = expert_master.shape[1] * dp_ranks // (2 * width)
    matrix_rows = 8 * width + 2 * hidden
    rows = matrix_rows // devices
    step = own - rows * tiles
    tail = step * devices
    tail_rows = -(-tail // (16 * tiles)) * 16
    wide_ok = rows % 64 == 0
    expert_rows = expert_flat // tiles

    dense_flat = dense_master.reshape(own, LANES)
    forward_ring = [(i, (i + 1) % devices) for i in range(devices)]
    backward_ring = [((i + 1) % devices, i) for i in range(devices)]
    tail_from = lax.ppermute(dense_flat[own - tail :], both, forward_ring)
    buf_rows = -(-(own + max(tail, tail_rows * tiles)) // 8) * 8
    chunk = pl.pallas_call(
        functools.partial(
            pack_dense_kernel, (rows, tail_rows, tail, own, step, tiles, devices, wide_ok)
        ),
        in_specs=[SMEM, VMEM, VMEM],
        out_specs=VMEM,
        out_shape=shape((rows + tail_rows, width), bf16),
        scratch_shapes=[pltpu.VMEM((buf_rows, LANES), f32)],
        compiler_params=params(),
        cost_estimate=cost(0, 6 * dense_master.size),
        name="pack_dense",
    )(me_arr, tail_from, dense_flat)
    gathered = lax.all_gather(chunk, both, axis=0, tiled=True)
    gathered = gathered.reshape(devices, rows + tail_rows, width)

    expert_wide = (lax.axis_index("dp") < dp_ranks // 2).astype(jnp.int32).reshape(1)
    expert_chunk = pl.pallas_call(
        functools.partial(pack_expert_kernel, (expert_rows, tiles)),
        in_specs=[SMEM, VMEM],
        out_specs=VMEM,
        out_shape=shape((expert_rows, width), bf16),
        compiler_params=params(),
        cost_estimate=cost(0, 6 * expert_master.size),
        name="pack_expert",
    )(expert_wide, expert_master.reshape(expert_flat, LANES))
    expert_all = lax.all_gather(expert_chunk, "dp", axis=0, tiled=True)

    capacity = 2 * seq // experts
    stride = -(-capacity // 8) * 8
    slots = experts * stride
    padded = -(-seq // 16) * 16
    cols, rows_slots = pl.pallas_call(
        functools.partial(route_kernel, experts, capacity, stride),
        in_specs=[VMEM] * 4,
        out_specs=[VMEM] * 2,
        out_shape=[shape((seq, 2), jnp.int32), shape((2, seq), jnp.int32)],
        compiler_params=params(),
        cost_estimate=cost(2e6, 1e5),
        name="route",
    )(priority, priority.reshape(seq, 1), expert_picks, expert_picks.T)
    fill = padded - seq
    cols = jnp.pad(cols, ((0, fill), (0, 0)), constant_values=-1)
    rows_slots = jnp.pad(rows_slots, ((0, 0), (0, fill)), constant_values=-1)
    picks = jnp.pad(expert_picks, ((0, fill), (0, 0)))
    stream = jnp.pad(tokens.reshape(seq, width).astype(f32), ((0, fill), (0, 0)))
    cot = jnp.pad(cotangent.reshape(seq, width).astype(f32), ((0, fill), (0, 0)))

    tail_flat = gathered[devices - 1, rows:, :].reshape(-1)
    router = tail_flat[: width * experts].reshape(width, experts)
    gains = tail_flat[width * experts : width * (experts + 4)].reshape(4, width).astype(f32)
    gain = [gains[i : i + 1] for i in range(4)]

    per = devices // 4
    dense_block = (per, rows + tail_rows, width)

    def layer_spec(index):
        return pl.BlockSpec(dense_block, lambda *_: (index, 0, 0), pipeline_mode=pl.Buffered(1))

    if wide_ok:
        first_in, first_spec, first_shape = gathered, layer_spec(2), (per, rows, width)
    else:
        first_in = gathered[2 * per : 3 * per, :rows].reshape(width, 4, width)
        first_in = first_in.transpose(1, 0, 2).reshape(1, 4 * width, width)
        first_spec, first_shape = VMEM, (1, 4 * width, width)

    act_shape = shape((padded, width), bf16)
    stream_shape = shape((padded, width), f32)
    gain_shape = shape((1, width), f32)
    tok_flops = 2 * padded * width * width
    weight_bytes = 2 * width * width

    def call(kernel, ins, in_specs, outs, name, flops, nbytes, trans=0, scratch=()):
        whole = [pl.BlockSpec(a.shape, lambda *_, n=len(a.shape): (0,) * n) for a in outs]
        specs = [
            s if s is not None else pl.BlockSpec(a.shape, lambda *_, n=a.ndim: (0,) * n)
            for a, s in zip(ins, in_specs, strict=True)
        ]
        return pl.pallas_call(
            kernel,
            grid=(1,),
            in_specs=specs,
            out_specs=whole,
            out_shape=outs,
            scratch_shapes=list(scratch),
            compiler_params=params(),
            cost_estimate=cost(flops, nbytes, trans),
            name=name,
        )(*ins)

    def attn_fwd(value, layer, which):
        return call(
            functools.partial(attn_fwd_kernel, seq),
            (value, gain[which], gathered),
            (None, None, layer_spec(layer)),
            [stream_shape] + [act_shape] * 5,
            "attn_fwd",
            5 * tok_flops,
            4 * weight_bytes,
        )

    def attn_bwd(grad, value, kept, layer, which):
        return call(
            functools.partial(attn_bwd_kernel, seq),
            (grad, value, gain[which], gathered, *kept),
            (None, None, None, layer_spec(layer)) + (None,) * 5,
            [stream_shape, gain_shape, shape((per, rows, width), bf16)],
            "attn_bwd",
            11 * tok_flops,
            8 * weight_bytes,
            scratch=[pltpu.VMEM((padded, width), bf16)] * 4,
        )

    stream_one, *kept_one = attn_fwd(stream, 0, 0)
    stream_two, mlp_in, mlp_pre = call(
        mlp_fwd_kernel,
        (stream_one, gain[1], first_in, gathered),
        (None, None, first_spec, layer_spec(3)),
        [stream_shape, act_shape, shape((padded, hidden), f32)],
        "mlp_fwd",
        8 * tok_flops,
        8 * weight_bytes,
    )
    stream_three, *kept_two = attn_fwd(stream_two, 1, 2)
    moe_in, probs, outgoing, outgoing_grad = call(
        functools.partial(dispatch_kernel, slots),
        (stream_three, gain[3], router, picks, rows_slots, cot),
        (None,) * 6,
        [act_shape, shape((padded, experts)), shape((slots, width), bf16), shape((slots, width), bf16)],
        "dispatch",
        3 * 2 * padded * slots * width,
        4e6,
    )

    def exchange(value):
        value = value.reshape(expert_ranks, slots // expert_ranks, width)
        value = lax.all_to_all(value, "expert", split_axis=0, concat_axis=0, tiled=True)
        return value.reshape(slots, width)

    arriving = exchange(outgoing)
    arriving_grad = exchange(outgoing_grad)

    quarter = expert_rows // 4
    half = dp_ranks // 2
    expert_flops = 2 * slots * width * width
    expert_out, input_back, expert_act, pre_grad = pl.pallas_call(
        expert_kernel,
        grid=(4,),
        in_specs=[
            pl.BlockSpec((slots, width), lambda q: (0, 0)),
            pl.BlockSpec((slots, width), lambda q: (0, 0)),
            pl.BlockSpec((half, 1, quarter, width), lambda q: (0, q, 0, 0)),
            pl.BlockSpec((width, width), lambda q: (4 + q, 0)),
        ],
        out_specs=[
            pl.BlockSpec((slots, width), lambda q: (0, 0)),
            pl.BlockSpec((slots, width), lambda q: (0, 0)),
            pl.BlockSpec((slots, width), lambda q: (0, q)),
            pl.BlockSpec((slots, width), lambda q: (0, q)),
        ],
        out_shape=[
            shape((slots, width), bf16),
            shape((slots, width), bf16),
            shape((slots, hidden), bf16),
            shape((slots, hidden), bf16),
        ],
        scratch_shapes=[pltpu.VMEM((slots, width), f32)] * 2,
        compiler_params=params(),
        cost_estimate=cost(16 * expert_flops, 8 * weight_bytes),
        name="expert",
    )(
        arriving,
        arriving_grad,
        expert_all.reshape(dp_ranks, 4, quarter, width),
        expert_all,
    )
    returned = exchange(expert_out)
    returned_grad = exchange(input_back)
    expert_local = pl.pallas_call(
        expert_grad_kernel,
        grid=(4,),
        in_specs=[
            pl.BlockSpec((slots, width), lambda q: (0, 0)),
            pl.BlockSpec((slots, width), lambda q: (0, 0)),
            pl.BlockSpec((slots, width), lambda q: (0, q)),
            pl.BlockSpec((slots, width), lambda q: (0, q)),
        ],
        out_specs=pl.BlockSpec((dp_ranks, 4, quarter, width), lambda q: (0, 0, 0, 0)),
        out_shape=shape((dp_ranks, 4, quarter, width), bf16),
        compiler_params=params(),
        cost_estimate=cost(8 * expert_flops, 8 * weight_bytes),
        name="expert_grad",
    )(arriving, arriving_grad, expert_act, pre_grad)
    expert_sum = lax.psum_scatter(
        expert_local.reshape(dp_ranks * expert_rows, width), "dp", scatter_dimension=0, tiled=True
    )

    output, grad, gain_four, router_grad = call(
        combine_kernel,
        (stream_three, gain[3], router, picks, cols, cot, moe_in, probs, returned, returned_grad),
        (None,) * 10,
        [stream_shape, stream_shape, gain_shape, shape((width, experts))],
        "combine",
        3 * 2 * padded * slots * width,
        6e6,
    )
    grad, gain_three, second_dw = attn_bwd(grad, stream_two, kept_two, 1, 2)
    grad, gain_two, first_dw1, second_dw2 = call(
        mlp_bwd_kernel,
        (grad, stream_one, gain[1], first_in, gathered, mlp_in, mlp_pre),
        (None, None, None, first_spec, layer_spec(3), None, None),
        [stream_shape, gain_shape, shape(first_shape, bf16), shape((per, rows, width), bf16)],
        "mlp_bwd",
        16 * tok_flops,
        16 * weight_bytes,
    )
    grad, gain_one, first_dw = attn_bwd(grad, stream, kept_one, 0, 0)
    if not wide_ok:
        first_dw1 = first_dw1.reshape(4, width, width).transpose(1, 0, 2)
    dense_local = jnp.concatenate(
        [part.reshape(-1, width) for part in (first_dw, second_dw, first_dw1, second_dw2)], axis=0
    )
    dense_sum = lax.psum_scatter(dense_local, both, scatter_dimension=0, tiled=True)

    small = jnp.concatenate(
        [router_grad.reshape(-1)] + [g.reshape(-1) for g in (gain_one, gain_two, gain_three, gain_four)]
    )
    small = jnp.pad(small, (0, tail * LANES - small.shape[0])).reshape(tail, LANES)
    small = all_sum(small, ("expert", "dp"))
    gain_at = width * experts
    gain_grads = small.reshape(-1)[gain_at : gain_at + 4 * width].reshape(4, width)

    dense_wide = (me >= devices // 2) & (me < 3 * devices // 4) & wide_ok
    dense_rows, _ = pl.pallas_call(
        functools.partial(unpack_kernel, (rows, tiles)),
        in_specs=[SMEM, VMEM],
        out_specs=[VMEM, VMEM],
        out_shape=[shape((rows * tiles, LANES)), shape((1, LANES))],
        compiler_params=params(),
        cost_estimate=cost(0, 6 * rows * width),
        name="unpack_dense",
    )(dense_wide.astype(jnp.int32).reshape(1), dense_sum)
    head = lax.ppermute(dense_rows[:tail], both, backward_ring)
    head = jnp.where(me == devices - 1, small, head)
    dense_grad, dense_square = pl.pallas_call(
        functools.partial(shift_kernel, (step, own)),
        in_specs=[SMEM, VMEM, VMEM],
        out_specs=[VMEM, VMEM],
        out_shape=[shape((own, LANES)), shape((1, LANES))],
        scratch_shapes=[pltpu.VMEM((-(-(rows * tiles + tail) // 8) * 8, LANES), f32)],
        compiler_params=params(),
        cost_estimate=cost(0, 8 * rows * width),
        name="shift_dense",
    )(me_arr, dense_rows, head)
    expert_grad, expert_square = pl.pallas_call(
        functools.partial(unpack_kernel, (expert_rows, tiles)),
        in_specs=[SMEM, VMEM],
        out_specs=[VMEM, VMEM],
        out_shape=[shape((expert_flat, LANES)), shape((1, LANES))],
        compiler_params=params(),
        cost_estimate=cost(0, 6 * expert_rows * width),
        name="unpack_expert",
    )(expert_wide, expert_sum)

    square = all_sum(dense_square + expert_square, ("expert", "dp"))
    square_sum = jnp.sum(square)
    param_count = (dense_master.size + expert_master.size) * devices
    clip_factor = jnp.minimum(1.0, jnp.sqrt(param_count / (square_sum + 1e-06))).reshape(1)

    dense_update, momentum_dense, variance_dense = adam(
        clip_factor,
        dense_grad,
        dense_momentum.reshape(own, LANES),
        dense_variance.reshape(own, LANES),
        own,
    )
    expert_update, momentum_expert, variance_expert = adam(
        clip_factor,
        expert_grad,
        expert_momentum.reshape(expert_flat, LANES),
        expert_variance.reshape(expert_flat, LANES),
        expert_flat // 8,
    )
    image = (1, seq, width)
    return (
        output[:seq].reshape(image),
        grad[:seq].reshape(image),
        dense_grad.reshape(dense_master.shape),
        expert_grad.reshape(expert_master.shape),
        dense_update.reshape(dense_master.shape),
        momentum_dense.reshape(dense_master.shape),
        variance_dense.reshape(dense_master.shape),
        expert_update.reshape(expert_master.shape),
        momentum_expert.reshape(expert_master.shape),
        variance_expert.reshape(expert_master.shape),
        gain_grads,
    )


def solution(mesh):
    tokens = P(("dp", "expert"), None, None)
    flat = P(("dp", "expert"))
    pairs = P(("dp", "expert"), None)
    expert = P("expert", "dp")
    return jax.shard_map(
        on_device,
        mesh=mesh,
        in_specs=(tokens, tokens, pairs, pairs, flat, flat, flat, expert, expert, expert),
        out_specs=(tokens, tokens, flat, expert, flat, flat, flat, expert, expert, expert, P()),
        check_vma=False,
    )
```

```python
import functools
import math

import jax
import jax.numpy as jnp
from jax import lax
from jax.experimental import pallas as pl
from jax.experimental.pallas import tpu as pltpu
from jax.sharding import PartitionSpec as P

HEADS = 12
HEAD_DIM = 64
LANES = 128

f32 = jnp.float32
bf16 = jnp.bfloat16

eps_norm = 1e-06
beta_first = 0.9
beta_second = 0.999
adam_eps = 1e-08
adam_step = 10.0

VMEM = pl.BlockSpec(memory_space=pltpu.VMEM)
SMEM = pl.BlockSpec(memory_space=pltpu.SMEM)


def params(mib=56):
    return pltpu.CompilerParams(vmem_limit_bytes=mib << 20)


def cost(flops, nbytes, trans=0):
    return pl.CostEstimate(flops=int(flops), bytes_accessed=int(nbytes), transcendentals=int(trans))


def dot(a, b):
    return lax.dot_general(a, b, (((1,), (0,)), ((), ())), preferred_element_type=f32)


def dot_nt(a, b):
    return lax.dot_general(a, b, (((1,), (1,)), ((), ())), preferred_element_type=f32)


def dot_tn(a, b):
    return lax.dot_general(a, b, (((0,), (0,)), ((), ())), preferred_element_type=f32)


def norm_rows(hidden):
    center = hidden - jnp.mean(hidden, axis=-1, keepdims=True)
    inverse = lax.rsqrt(jnp.mean(center * center, axis=-1, keepdims=True) + eps_norm)
    return center * inverse, inverse


def norm_back(upstream, normed, inverse, gain):
    scaled = upstream * gain
    gain_grad = jnp.sum(upstream * normed, axis=0, keepdims=True)
    centered = (
        scaled
        - jnp.mean(scaled, axis=-1, keepdims=True)
        - normed * jnp.mean(scaled * normed, axis=-1, keepdims=True)
    )
    return inverse * centered, gain_grad


def normal_cdf(v):
    return 0.5 * (1.0 + lax.erf(v * 0.7071067811865476))


def density(v):
    return jnp.exp(-0.5 * v * v) * 0.3989422804014327


def to_rows(read, write, first_q, rows, wide, tiles):
    blocks = 4 if rows % 64 == 0 else 1
    count = rows // blocks
    for b in range(blocks):
        for j in range(tiles):
            if wide:
                write(b * count, count, j, read(first_q + tiles * b + j, count, 4 * tiles))
            else:
                write(b * count, count, j, read(first_q + tiles * count * b + j, count, tiles))


def pack_dense_kernel(dims, k_ref, tail_ref, own_ref, out_ref, buf):
    rows, tail_rows, tail, own, step, tiles, chunks, wide_ok = dims
    buf[0:tail] = tail_ref[...]
    buf[tail : tail + own] = own_ref[...]
    buf[tail + own :] = jnp.zeros((buf.shape[0] - tail - own, LANES), f32)
    k = k_ref[0]
    start = tail - step * k

    def read(first, count, stride):
        return buf[pl.ds(first, count, stride=stride), :]

    def write(first, count, j, value):
        out_ref[first : first + count, LANES * j : LANES * (j + 1)] = value.astype(bf16)

    wide = (k >= chunks // 2) & (k < 3 * chunks // 4) & wide_ok

    if wide_ok:

        @pl.when(wide)
        def _():
            to_rows(read, write, start, rows, True, tiles)

    @pl.when(jnp.logical_not(wide))
    def _():
        to_rows(read, write, start, rows, False, tiles)

    for j in range(tiles):
        write(rows, tail_rows, j, read(own + j, tail_rows, tiles))


def pack_expert_kernel(dims, wide_ref, own_ref, *out_refs):
    rows, tiles = dims
    half = rows // 2

    def read(first, count, stride):
        return own_ref[pl.ds(first, count, stride=stride), :]

    def write(first, count, j, value):
        at = first % half
        out_refs[first // half][at : at + count, LANES * j : LANES * (j + 1)] = value.astype(bf16)

    wide = wide_ref[0] > 0

    @pl.when(wide)
    def _():
        to_rows(read, write, 0, rows, True, tiles)

    @pl.when(jnp.logical_not(wide))
    def _():
        to_rows(read, write, 0, rows, False, tiles)


def unpack_kernel(dims, wide_ref, *refs):
    rows, tiles = dims
    piece_refs, (out_ref, square_ref, rows_ref) = refs[:-3], refs[-3:]
    at = 0
    for ref in piece_refs:
        rows_ref[at : at + ref.shape[0]] = ref[...].astype(f32)
        at += ref.shape[0]
    wide = wide_ref[0] > 0

    def store(is_wide):
        total = jnp.zeros((1, LANES), f32)
        quarter = rows // 4
        for q in range(4):
            for j in range(tiles):
                piece = rows_ref[q * quarter : (q + 1) * quarter, LANES * j : LANES * (j + 1)]
                if is_wide:
                    out_ref[pl.ds(tiles * q + j, quarter, stride=4 * tiles), :] = piece
                else:
                    out_ref[pl.ds(tiles * quarter * q + j, quarter, stride=tiles), :] = piece
                total = total + jnp.sum(piece * piece, axis=0, keepdims=True)
        square_ref[...] = total

    @pl.when(wide)
    def _():
        store(True)

    @pl.when(jnp.logical_not(wide))
    def _():
        store(False)


def shift_kernel(dims, k_ref, flat_ref, head_ref, out_ref, square_ref, buf):
    step, own = dims
    count = flat_ref.shape[0]
    buf[0:count] = flat_ref[...]
    buf[count : count + head_ref.shape[0]] = head_ref[...]
    value = buf[pl.ds(step * k_ref[0], own), :]
    out_ref[...] = value
    square_ref[...] = jnp.sum(value * value, axis=0, keepdims=True)


def adam_kernel(clip_ref, grad_ref, momentum_ref, variance_ref, update_ref, momentum_out, variance_out):
    clipped = grad_ref[...] * clip_ref[0]
    momentum_new = beta_first * momentum_ref[...] + (1.0 - beta_first) * clipped
    variance_new = beta_second * variance_ref[...] + (1.0 - beta_second) * clipped * clipped
    first_hat = momentum_new / (1.0 - beta_first**adam_step)
    second_hat = variance_new / (1.0 - beta_second**adam_step)
    update_ref[...] = -first_hat / (jnp.sqrt(second_hat) + adam_eps)
    momentum_out[...] = momentum_new
    variance_out[...] = variance_new


def adam(clip, grad, momentum, variance, block):
    count = grad.shape[0]
    spec = pl.BlockSpec((block, LANES), lambda i: (i, 0))
    shape = jax.ShapeDtypeStruct(grad.shape, f32)
    return pl.pallas_call(
        adam_kernel,
        grid=(pl.cdiv(count, block),),
        in_specs=[SMEM, spec, spec, spec],
        out_specs=[spec] * 3,
        out_shape=[shape] * 3,
        compiler_params=params(),
        cost_estimate=cost(20 * grad.size, 24 * grad.size, 2 * grad.size),
        name="adam",
    )(clip, grad, momentum, variance)


def route_kernel(experts, capacity, stride, prio_row, prio_col, picks, picks_t, cot, cols_ref, rows_ref, g_ref):
    count = picks.shape[0]
    before = (prio_row[...] < prio_col[...]).astype(f32).astype(bf16)
    lane = lax.broadcasted_iota(jnp.int32, (count, experts), 1)
    sub = lax.broadcasted_iota(jnp.int32, (experts, count), 0)
    hot = [(picks[:, j : j + 1] == lane).astype(f32) for j in range(2)]
    hot_t = [(picks_t[j : j + 1, :] == sub).astype(f32) for j in range(2)]
    first = jnp.sum(hot[0], axis=0, keepdims=True)
    first_t = jnp.sum(hot_t[0], axis=1, keepdims=True)
    for j in range(2):
        earlier = dot(before, hot[j].astype(bf16)) + (first if j else 0.0)
        earlier_t = dot_nt(hot_t[j].astype(bf16), before) + (first_t if j else 0.0)
        place = jnp.sum(earlier * hot[j], axis=1, keepdims=True).astype(jnp.int32)
        place_t = jnp.sum(earlier_t * hot_t[j], axis=0, keepdims=True).astype(jnp.int32)
        cols_ref[:, j : j + 1] = jnp.where(
            place < capacity, picks[:, j : j + 1] * stride + place, -1
        )
        rows_ref[j : j + 1, :] = jnp.where(
            place_t < capacity, picks_t[j : j + 1, :] * stride + place_t, -1
        )
    first, second = slot_selects(rows_ref, g_ref.shape[0])
    g_ref[...] = dot(first + second, cot[...]).astype(bf16)


def slot_selects(rows_ref, slots):
    sub = lax.broadcasted_iota(jnp.int32, (slots, rows_ref.shape[1]), 0)
    return [(rows_ref[j : j + 1, :] == sub).astype(f32).astype(bf16) for j in range(2)]


def token_selects(cols_ref, slots):
    lane = lax.broadcasted_iota(jnp.int32, (cols_ref.shape[0], slots), 1)
    return [(cols_ref[:, j : j + 1] == lane).astype(f32).astype(bf16) for j in range(2)]


def split_lanes(column):
    high = column.astype(bf16).astype(f32)
    rest = column - high
    middle = rest.astype(bf16).astype(f32)
    low = rest - middle
    lane = lax.broadcasted_iota(jnp.int32, (column.shape[0], LANES), 1)
    wide = jnp.where(lane == 0, high, jnp.where(lane == 1, middle, jnp.where(lane == 2, low, 0.0)))
    return wide.astype(bf16)


def head_masks():
    lane = lax.broadcasted_iota(jnp.int32, (1, 2 * HEAD_DIM), 1)
    first = (lane < HEAD_DIM).astype(f32)
    return first.astype(bf16), (1.0 - first).astype(bf16)


def soft_scores(queries, key_rows, key_ok):
    scores = dot_nt(queries, key_rows) * HEAD_DIM ** (-0.5)
    scores = jnp.where(key_ok, scores, -1e30)
    top = jnp.max(scores, axis=-1, keepdims=True)
    raised = jnp.exp(scores - top)
    return raised * (1.0 / jnp.sum(raised, axis=-1, keepdims=True))


def put_chunk(scratch, low, chunk, value, first=0):
    place = chunk ^ low
    scratch[place & 1, place >> 1, first : first + value.shape[0], :] = value


def flush(scratch, keep_ref, send_ref, sems):
    copies = [
        pltpu.make_async_copy(scratch.at[i], ref, sems.at[i]) for i, ref in enumerate((keep_ref, send_ref))
    ]
    for copy in copies:
        copy.start()
    for copy in copies:
        copy.wait()


def matrix(w_ref, index):
    per = w_ref.shape[0] // 4
    width = w_ref.shape[2]
    rows = width // per
    return w_ref[index * per : (index + 1) * per, 0:rows, :].reshape(width, width)


def quarter_in(w_ref, q):
    width = w_ref.shape[2]
    rows = width // w_ref.shape[0]
    return w_ref[:, q * rows : (q + 1) * rows, :].reshape(width, width)


def attn_fwd_kernel(seq, stream_ref, gain_ref, w_ref, out_ref, a_ref, q_ref, k_ref, v_ref, o_ref):
    normed, _ = norm_rows(stream_ref[...])
    a_ref[...] = (normed * gain_ref[...]).astype(bf16)
    for index, ref in enumerate((q_ref, k_ref, v_ref)):
        ref[...] = dot(a_ref[...], matrix(w_ref, index)).astype(bf16)
    count = stream_ref.shape[0]
    key_ok = lax.broadcasted_iota(jnp.int32, (count, count), 1) < seq
    masks = head_masks()
    for pair in range(HEADS // 2):
        lanes = slice(2 * HEAD_DIM * pair, 2 * HEAD_DIM * (pair + 1))
        mixed = None
        for mask in masks:
            soft = soft_scores(q_ref[:, lanes] * mask, k_ref[:, lanes], key_ok).astype(bf16)
            part = dot(soft, v_ref[:, lanes] * mask)
            mixed = part if mixed is None else mixed + part
        o_ref[:, lanes] = mixed.astype(bf16)
    out_ref[...] = stream_ref[...] + dot(o_ref[...], matrix(w_ref, 3))


def attn_bwd_kernel(
    seq, low_ref, grad_ref, stream_ref, gain_ref, w_ref, a_ref, q_ref, k_ref, v_ref, o_ref,
    out_ref, gain_out, keep_ref, send_ref, dw, do_ref, dq_ref, dk_ref, dv_ref, sems,
):
    width = grad_ref.shape[1]
    branch = grad_ref[...].astype(bf16)
    low = low_ref[0]

    def put(index, value):
        rows = dw.shape[2]
        per = width // rows
        for i in range(per):
            put_chunk(dw, low, index * per + i, value[i * rows : (i + 1) * rows].astype(bf16))

    do_ref[...] = dot_nt(branch, matrix(w_ref, 3)).astype(bf16)
    put(3, dot_tn(o_ref[...], branch))
    count = grad_ref.shape[0]
    key_ok = lax.broadcasted_iota(jnp.int32, (count, count), 1) < seq
    masks = head_masks()
    scale = HEAD_DIM ** (-0.5)
    for pair in range(HEADS // 2):
        lanes = slice(2 * HEAD_DIM * pair, 2 * HEAD_DIM * (pair + 1))
        dq = dk = dv = None
        for mask in masks:
            q_h = q_ref[:, lanes] * mask
            k_h = k_ref[:, lanes] * mask
            do_h = do_ref[:, lanes] * mask
            soft = soft_scores(q_h, k_ref[:, lanes], key_ok)
            dsoft = dot_nt(do_h, v_ref[:, lanes])
            dv_h = dot_tn(soft.astype(bf16), do_h)
            inner = jnp.sum(dsoft * soft, axis=-1, keepdims=True)
            dscore = (soft * (dsoft - inner)).astype(bf16)
            dq_h = dot(dscore, k_h)
            dk_h = dot_tn(dscore, q_h)
            dq = dq_h if dq is None else dq + dq_h
            dk = dk_h if dk is None else dk + dk_h
            dv = dv_h if dv is None else dv + dv_h
        dq_ref[:, lanes] = (dq * scale).astype(bf16)
        dk_ref[:, lanes] = (dk * scale).astype(bf16)
        dv_ref[:, lanes] = dv.astype(bf16)
    back = None
    for index, ref in enumerate((dq_ref, dk_ref, dv_ref)):
        put(index, dot_tn(a_ref[...], ref[...]))
        part = dot_nt(ref[...], matrix(w_ref, index))
        back = part if back is None else back + part
    flush(dw, keep_ref, send_ref, sems)
    normed, inverse = norm_rows(stream_ref[...])
    addend, gain_grad = norm_back(back, normed, inverse, gain_ref[...])
    out_ref[...] = grad_ref[...] + addend
    gain_out[...] = gain_grad


def mlp_fwd_kernel(stream_ref, gain_ref, w1_ref, w2_ref, out_ref, b_ref, u_ref):
    width = stream_ref.shape[1]
    normed, _ = norm_rows(stream_ref[...])
    b_ref[...] = (normed * gain_ref[...]).astype(bf16)
    out_ref[...] = stream_ref[...]
    total = None
    for q in range(4):
        pre = dot(b_ref[...], quarter_in(w1_ref, q))
        u_ref[:, q * width : (q + 1) * width] = pre
        part = dot((pre * normal_cdf(pre)).astype(bf16), matrix(w2_ref, q))
        total = part if total is None else total + part
    out_ref[...] = stream_ref[...] + total


def mlp_bwd_kernel(
    by_core, low_ref, grad_ref, stream_ref, gain_ref, w1_ref, w2_ref, b_ref, u_ref,
    out_ref, gain_out, keep2_ref, send2_ref, *refs,
):
    if by_core:
        keep1_ref, send1_ref, dw2, dw1, sems = refs
    else:
        dw1_ref, dw2, sems = refs
    width = grad_ref.shape[1]
    upper = grad_ref[...].astype(bf16)
    low = low_ref[0]
    back = None
    for q in range(4):
        pre = u_ref[:, q * width : (q + 1) * width]
        cdf = normal_cdf(pre)
        act = (pre * cdf).astype(bf16)
        rows = dw2.shape[2]
        per = width // rows
        second = dot_tn(act, upper)
        for i in range(per):
            put_chunk(dw2, low, q * per + i, second[i * rows : (i + 1) * rows].astype(bf16))
        dact = dot_nt(upper, matrix(w2_ref, q))
        dpre = (dact * (cdf + pre * density(pre))).astype(bf16)
        first = dot_tn(b_ref[...], dpre).astype(bf16)
        groups = w1_ref.shape[0]
        rows = width // groups
        for i in range(groups):
            piece = first[i * rows : (i + 1) * rows]
            if by_core:
                put_chunk(dw1, low, i, piece, q * rows)
            else:
                dw1_ref[i, q * rows : (q + 1) * rows, :] = piece
        part = dot_nt(dpre, quarter_in(w1_ref, q))
        back = part if back is None else back + part
    flush(dw2, keep2_ref, send2_ref, sems)
    if by_core:
        flush(dw1, keep1_ref, send1_ref, sems)
    normed, inverse = norm_rows(stream_ref[...])
    addend, gain_grad = norm_back(back, normed, inverse, gain_ref[...])
    out_ref[...] = grad_ref[...] + addend
    gain_out[...] = gain_grad


def pick_hots(picks, experts):
    lane = lax.broadcasted_iota(jnp.int32, (picks.shape[0], experts), 1)
    return [(picks[:, j : j + 1] == lane).astype(f32) for j in range(2)]


def softmax_rows(logits):
    raised = jnp.exp(logits - jnp.max(logits, axis=-1, keepdims=True))
    return raised / jnp.sum(raised, axis=-1, keepdims=True)


def dispatch_kernel(stream_ref, gain_ref, wr_ref, picks_ref, rows_ref, c_ref, probs_ref, x_ref):
    width = stream_ref.shape[1]
    experts = wr_ref.shape[1]
    normed, _ = norm_rows(stream_ref[...])
    c_ref[...] = (normed * gain_ref[...]).astype(bf16)
    probs = softmax_rows(dot(c_ref[...], wr_ref[...]))
    probs_ref[...] = probs
    hots = pick_hots(picks_ref, experts)
    selects = slot_selects(rows_ref, x_ref.shape[0])
    gates = None
    for j in range(2):
        part = dot(selects[j], split_lanes(jnp.sum(probs * hots[j], axis=-1, keepdims=True)))
        gates = part if gates is None else gates + part
    x_ref[:, 0:width] = dot(selects[0] + selects[1], c_ref[...]).astype(bf16)
    x_ref[:, width:] = gates.astype(bf16)


def add_lanes(wide):
    wide = wide.astype(f32)
    return wide[:, 0:1] + wide[:, 1:2] + wide[:, 2:3]


def expert_kernel(dims, dp_ref, x_ref, g_ref, *refs):
    parts, quarter = dims
    weight_refs, refs = refs[: 2 * parts], refs[2 * parts :]
    y_ref, dx_ref, dy_ref, act_ref, dpre_ref, weights, y_sum, dx_sum, sems = refs
    q = pl.program_id(0)
    width = g_ref.shape[1]
    half = parts // 2
    rows = weights.shape[1] // 2
    me = dp_ref[0]

    def copies(side):
        return [
            pltpu.make_async_copy(
                weight_refs[side * parts + r],
                weights.at[r ^ me, side * rows : (side + 1) * rows],
                sems.at[side * parts + r],
            )
            for r in range(parts)
        ]

    @pl.when(q == 0)
    def _():
        for side in range(2):
            for copy in copies(side):
                copy.start()
        dy_ref[...] = (add_lanes(x_ref[:, width:]) * g_ref[...].astype(f32)).astype(bf16)
        for side in range(2):
            for copy in copies(side):
                copy.wait()

    first = weights[0:half, pl.ds(pl.multiple_of(q * quarter, 16), quarter), :].reshape(width, width)
    if 4 * quarter >= width:
        per = 4 * quarter // width
        at = pl.ds(pl.multiple_of(lax.rem(q, per) * width, 16), width)
        second = weights[half + q // per, at, :]
    else:
        per = width // (4 * quarter)
        second = weights[pl.ds(half + q * per, per)].reshape(width, width)
    x = x_ref[:, 0:width]
    pre = dot(x, first)
    cdf = normal_cdf(pre)
    act = (pre * cdf).astype(bf16)
    act_ref[...] = act
    dact = dot_nt(dy_ref[...], second)
    dpre = (dact * (cdf + pre * density(pre))).astype(bf16)
    dpre_ref[...] = dpre
    y_part = dot(act, second)
    dx_part = dot_nt(dpre, first)

    @pl.when(q == 0)
    def _():
        y_sum[...] = y_part
        dx_sum[...] = dx_part

    @pl.when(q > 0)
    def _():
        y_sum[...] += y_part
        dx_sum[...] += dx_part

    @pl.when(q == pl.num_programs(0) - 1)
    def _():
        y = y_sum[...].astype(bf16)
        y_ref[...] = y
        dx_ref[:, 0:width] = dx_sum[...].astype(bf16)
        gate_grad = jnp.sum(g_ref[...].astype(f32) * y.astype(f32), axis=-1, keepdims=True)
        dx_ref[:, width:] = split_lanes(gate_grad)


def expert_grad_kernel(dims, dp_ref, x_ref, dy_ref, act_ref, dpre_ref, *refs):
    parts, quarter = dims
    out_refs, scratch, sems = refs[:4], refs[4], refs[5]
    q = pl.program_id(0)
    me = dp_ref[0]
    width = dy_ref.shape[1]
    half = parts // 2
    rows = scratch.shape[1]
    first = dot_tn(x_ref[:, 0:width], dpre_ref[...]).astype(bf16)
    count = width // half
    for i in range(half):
        at = pl.ds(pl.multiple_of(q * quarter, 16), quarter)
        scratch[i ^ me, at, :] = first[i * count : (i + 1) * count]
    second = dot_tn(act_ref[...], dy_ref[...]).astype(bf16)
    if rows >= width:
        per = rows // width
        at = pl.ds(pl.multiple_of(lax.rem(q, per) * width, 16), width)
        scratch[(half + q // per) ^ me, at, :] = second
    else:
        per = width // rows
        for i in range(per):
            scratch[(half + q * per + i) ^ me] = second[i * rows : (i + 1) * rows]

    @pl.when(q == pl.num_programs(0) - 1)
    def _():
        copies = []
        for side, bit in ((0, 1), (1, parts // 2)):
            lists = [r for r in range(parts) if r & bit], [r for r in range(parts) if not r & bit]
            for which, group in enumerate(lists):
                for i, r in enumerate(group):
                    copies.append(
                        pltpu.make_async_copy(
                            scratch.at[r, side * rows // 2 : (side + 1) * rows // 2],
                            out_refs[2 * side + which].at[i],
                            sems.at[side * parts + r],
                        )
                    )
        for copy in copies:
            copy.start()
        for copy in copies:
            copy.wait()


def combine_kernel(
    stream_ref, gain_ref, wr_ref, picks_ref, cols_ref, cot_ref, c_ref, probs_ref, dx_ref,
    grad_ref, gain_out, router_out,
):
    width = stream_ref.shape[1]
    experts = wr_ref.shape[1]
    probs = probs_ref[...]
    hots = pick_hots(picks_ref, experts)
    selects = token_selects(cols_ref, dx_ref.shape[0])
    prob_grad = None
    for j in range(2):
        part = add_lanes(dot(selects[j], dx_ref[:, width:])) * hots[j]
        prob_grad = part if prob_grad is None else prob_grad + part
    logit_grad = probs * (prob_grad - jnp.sum(prob_grad * probs, axis=-1, keepdims=True))
    logit_grad = logit_grad.astype(bf16)
    router_out[...] = dot_tn(c_ref[...], logit_grad)
    back = dot(selects[0] + selects[1], dx_ref[:, 0:width]) + dot_nt(logit_grad, wr_ref[...])
    normed, inverse = norm_rows(stream_ref[...])
    addend, gain_grad = norm_back(back, normed, inverse, gain_ref[...])
    grad_ref[...] = cot_ref[...].astype(f32) + addend
    gain_out[...] = gain_grad


def output_kernel(stream_ref, picks_ref, cols_ref, probs_ref, y_ref, out_ref):
    seq = out_ref.shape[0]
    probs = probs_ref[...]
    hots = pick_hots(picks_ref, probs.shape[1])
    selects = token_selects(cols_ref, y_ref.shape[0])
    total = stream_ref[...]
    for j in range(2):
        gate = jnp.sum(probs * hots[j], axis=-1, keepdims=True)
        total = total + gate * dot(selects[j], y_ref[...])
    out_ref[...] = total[0:seq]


def swap(value, axes, bit):
    size = 1
    for axis in axes:
        size *= lax.axis_size(axis)
    return lax.ppermute(value, axes, [(i, i ^ (1 << bit)) for i in range(size)])


def all_sum(value, axes, bits):
    for bit in range(bits):
        value = value + swap(value, axes, bit)
    return value


def gather_parts(value, axes, order):
    parts = {0: value}
    for bit in order:
        parts.update({at | (1 << bit): swap(part, axes, bit) for at, part in list(parts.items())})
    return [parts[at] for at in sorted(parts)]


def reduce_low(value, axes, bits):
    for bit in bits:
        pairs = value.reshape((value.shape[0] // 2, 2) + value.shape[1:])
        value = pairs[:, 0] + swap(pairs[:, 1], axes, bit)
    return value[0]


def reduce_high(value, axes, bits):
    for bit in reversed(bits):
        pairs = value.reshape((2, value.shape[0] // 2) + value.shape[1:])
        value = pairs[0] + swap(pairs[1], axes, bit)
    return value[0]


def reduce_layers(layers, axes, bits, me, low_first):
    grid = [[layers[0], layers[1]], [layers[2], layers[3]]]
    if not low_first:
        grid = [list(column) for column in zip(*grid)]
    first, second = (bits[0], bits[1]) if low_first else (bits[1], bits[0])
    own = (me >> first) & 1
    keep = [jnp.where(own == 0, row[0], row[1]) for row in grid]
    send = [jnp.where(own == 0, row[1], row[0]) for row in grid]
    arrived = swap(jnp.stack(send), axes, first)
    sums = [keep[i] + arrived[i] for i in range(2)]
    own = (me >> second) & 1
    return jnp.where(own == 0, sums[0], sums[1]) + swap(jnp.where(own == 0, sums[1], sums[0]), axes, second)


def shape(dims, dtype=f32):
    return jax.ShapeDtypeStruct(dims, dtype)


def on_device(
    tokens,
    cotangent,
    expert_picks,
    priority,
    dense_master,
    dense_momentum,
    dense_variance,
    expert_master,
    expert_momentum,
    expert_variance,
):
    both = ("dp", "expert")
    dp_ranks = lax.axis_size("dp")
    expert_ranks = lax.axis_size("expert")
    devices = dp_ranks * expert_ranks
    local_experts = expert_master.shape[0]
    experts = local_experts * expert_ranks
    images, seq, width = tokens.shape
    assert local_experts == 1 and images == 1
    assert devices & (devices - 1) == 0 and dp_ranks >= 4
    tiles = width // LANES
    dp_me = lax.axis_index("dp").astype(jnp.int32)
    me = dp_me * expert_ranks + lax.axis_index("expert").astype(jnp.int32)
    me_arr = me.reshape(1)
    dp_arr = dp_me.reshape(1)
    dp_bits = dp_ranks.bit_length() - 1
    all_bits = devices.bit_length() - 1

    own = dense_master.shape[0] // LANES
    expert_flat = expert_master.shape[1] // LANES
    hidden = expert_master.shape[1] * dp_ranks // (2 * width)
    matrix_rows = 8 * width + 2 * hidden
    rows = matrix_rows // devices
    step = own - rows * tiles
    tail = step * devices
    tail_rows = -(-tail // (16 * tiles)) * 16
    wide_ok = rows % 64 == 0
    expert_rows = expert_flat // tiles

    dense_flat = dense_master.reshape(own, LANES)
    forward_ring = [(i, (i + 1) % devices) for i in range(devices)]
    backward_ring = [((i + 1) % devices, i) for i in range(devices)]
    tail_from = lax.ppermute(dense_flat[own - tail :], both, forward_ring)
    buf_rows = -(-(own + max(tail, tail_rows * tiles)) // 8) * 8
    chunk = pl.pallas_call(
        functools.partial(
            pack_dense_kernel, (rows, tail_rows, tail, own, step, tiles, devices, wide_ok)
        ),
        in_specs=[SMEM, VMEM, VMEM],
        out_specs=VMEM,
        out_shape=shape((rows + tail_rows, width), bf16),
        scratch_shapes=[pltpu.VMEM((buf_rows, LANES), f32)],
        compiler_params=params(),
        cost_estimate=cost(0, 6 * dense_master.size),
        name="pack_dense",
    )(me_arr, tail_from, dense_flat)
    gathered = lax.all_gather(chunk, both, axis=0, tiled=True)
    gathered = gathered.reshape(devices, rows + tail_rows, width)

    expert_wide = (dp_me < dp_ranks // 2).astype(jnp.int32).reshape(1)
    half_shape = shape((expert_rows // 2, width), bf16)
    halves = pl.pallas_call(
        functools.partial(pack_expert_kernel, (expert_rows, tiles)),
        in_specs=[SMEM, VMEM],
        out_specs=[VMEM, VMEM],
        out_shape=[half_shape, half_shape],
        compiler_params=params(),
        cost_estimate=cost(0, 6 * expert_master.size),
        name="pack_expert",
    )(expert_wide, expert_master.reshape(expert_flat, LANES))
    dp_axis = ("dp",)
    dp_order = list(range(dp_bits))
    expert_parts = gather_parts(halves[0], dp_axis, dp_order)
    expert_parts += gather_parts(halves[1], dp_axis, dp_order[::-1])

    capacity = 2 * seq // experts
    stride = -(-capacity // 8) * 8
    slots = experts * stride
    padded = -(-seq // 16) * 16
    fill = padded - seq
    ranks = jnp.pad(priority, ((0, 0), (0, fill)), constant_values=1 << 20)
    picks = jnp.pad(expert_picks, ((0, fill), (0, 0)), constant_values=-1)
    cot = jnp.pad(cotangent.reshape(seq, width), ((0, fill), (0, 0)))
    stream = jnp.pad(tokens.reshape(seq, width).astype(f32), ((0, fill), (0, 0)))
    cols, rows_slots, outgoing_cot = pl.pallas_call(
        functools.partial(route_kernel, experts, capacity, stride),
        in_specs=[VMEM] * 5,
        out_specs=[VMEM] * 3,
        out_shape=[
            shape((padded, 2), jnp.int32),
            shape((2, padded), jnp.int32),
            shape((slots, width), bf16),
        ],
        compiler_params=params(),
        cost_estimate=cost(2 * padded * slots * width, 1e6),
        name="route",
    )(ranks, ranks.reshape(padded, 1), picks, picks.T, cot)

    def exchange(value):
        dims = value.shape
        value = value.reshape(expert_ranks, slots // expert_ranks, dims[1])
        value = lax.all_to_all(value, "expert", split_axis=0, concat_axis=0, tiled=True)
        return value.reshape(dims)

    arriving_cot = exchange(outgoing_cot)

    tail_flat = gathered[devices - 1, rows:, :].reshape(-1)
    router = tail_flat[: width * experts].reshape(width, experts)
    gains = tail_flat[width * experts : width * (experts + 4)].reshape(4, width).astype(f32)
    gain = [gains[i : i + 1] for i in range(4)]

    per = devices // 4
    dense_block = (per, rows + tail_rows, width)
    low = me & (per - 1)
    low_arr = low.reshape(1)

    def layer_spec(index):
        return pl.BlockSpec(dense_block, lambda *_: (index, 0, 0), pipeline_mode=pl.Buffered(1))

    if wide_ok:
        first_in, first_spec = gathered, layer_spec(2)
    else:
        first_in = gathered[2 * per : 3 * per, :rows].reshape(width, 4, width)
        first_in = first_in.transpose(1, 0, 2).reshape(1, 4 * width, width)
        first_spec = None

    act_shape = shape((padded, width), bf16)
    stream_shape = shape((padded, width), f32)
    gain_shape = shape((1, width), f32)
    tok_flops = 2 * padded * width * width
    weight_bytes = 2 * width * width
    ANY = pl.BlockSpec(memory_space=pl.ANY)

    def call(kernel, ins, in_specs, outs, name, flops, nbytes, out_specs=None, scratch=()):
        out_specs = out_specs or [None] * len(outs)

        def whole(a):
            return pl.BlockSpec(a.shape, lambda *_, n=len(a.shape): (0,) * n)

        return pl.pallas_call(
            kernel,
            grid=(1,),
            in_specs=[s or whole(a) for a, s in zip(ins, in_specs, strict=True)],
            out_specs=[s or whole(a) for a, s in zip(outs, out_specs, strict=True)],
            out_shape=outs,
            scratch_shapes=list(scratch),
            compiler_params=params(),
            cost_estimate=cost(flops, nbytes),
            name=name,
        )(*ins)

    def attn_fwd(value, layer, which):
        return call(
            functools.partial(attn_fwd_kernel, seq),
            (value, gain[which], gathered),
            (None, None, layer_spec(layer)),
            [stream_shape] + [act_shape] * 5,
            "attn_fwd",
            5 * tok_flops,
            4 * weight_bytes,
        )

    core_shape = shape((per // 2, rows, width), bf16)
    by_core = pltpu.VMEM((2, per // 2, rows, width), bf16)
    two_sems = pltpu.SemaphoreType.DMA((2,))

    def attn_bwd(grad, value, kept, layer, which):
        return call(
            functools.partial(attn_bwd_kernel, seq),
            (low_arr, grad, value, gain[which], gathered, *kept),
            (SMEM, None, None, None, layer_spec(layer)) + (None,) * 5,
            [stream_shape, gain_shape, core_shape, core_shape],
            "attn_bwd",
            11 * tok_flops,
            8 * weight_bytes,
            out_specs=[None, None, ANY, ANY],
            scratch=[by_core] + [pltpu.VMEM((padded, width), bf16)] * 4 + [two_sems],
        )

    stream_one, *kept_one = attn_fwd(stream, 0, 0)
    stream_two, mlp_in, mlp_pre = call(
        mlp_fwd_kernel,
        (stream_one, gain[1], first_in, gathered),
        (None, None, first_spec, layer_spec(3)),
        [stream_shape, act_shape, shape((padded, hidden), f32)],
        "mlp_fwd",
        8 * tok_flops,
        8 * weight_bytes,
    )
    stream_three, *kept_two = attn_fwd(stream_two, 1, 2)
    moe_in, probs, outgoing = call(
        dispatch_kernel,
        (stream_three, gain[3], router, picks, rows_slots),
        (None,) * 5,
        [act_shape, shape((padded, experts)), shape((slots, width + LANES), bf16)],
        "dispatch",
        2 * padded * slots * width,
        4e6,
    )
    arriving = exchange(outgoing)

    quarter = expert_rows // 4
    expert_flops = 2 * slots * width * width
    slot_spec = pl.BlockSpec((slots, width), lambda q: (0, 0))
    wide_spec = pl.BlockSpec((slots, width + LANES), lambda q: (0, 0))
    hidden_spec = pl.BlockSpec((slots, width), lambda q: (0, q))
    expert_out, input_back, slot_grad, expert_act, pre_grad = pl.pallas_call(
        functools.partial(expert_kernel, (dp_ranks, quarter)),
        grid=(4,),
        in_specs=[SMEM, wide_spec, slot_spec] + [ANY] * (2 * dp_ranks),
        out_specs=[slot_spec, wide_spec, slot_spec, hidden_spec, hidden_spec],
        out_shape=[
            shape((slots, width), bf16),
            shape((slots, width + LANES), bf16),
            shape((slots, width), bf16),
            shape((slots, hidden), bf16),
            shape((slots, hidden), bf16),
        ],
        scratch_shapes=[
            pltpu.VMEM((dp_ranks, expert_rows, width), bf16),
            pltpu.VMEM((slots, width), f32),
            pltpu.VMEM((slots, width), f32),
            pltpu.SemaphoreType.DMA((2 * dp_ranks,)),
        ],
        compiler_params=params(),
        cost_estimate=cost(16 * expert_flops, 8 * weight_bytes),
        name="expert",
    )(dp_arr, arriving, arriving_cot, *expert_parts)
    returned_grad = exchange(input_back)
    part_shape = shape((dp_ranks // 2, expert_rows // 2, width), bf16)
    expert_parts = pl.pallas_call(
        functools.partial(expert_grad_kernel, (dp_ranks, quarter)),
        grid=(4,),
        in_specs=[SMEM, wide_spec, slot_spec, hidden_spec, hidden_spec],
        out_specs=[ANY] * 4,
        out_shape=[part_shape] * 4,
        scratch_shapes=[
            pltpu.VMEM((dp_ranks, expert_rows, width), bf16),
            pltpu.SemaphoreType.DMA((2 * dp_ranks,)),
        ],
        compiler_params=params(),
        cost_estimate=cost(8 * expert_flops, 8 * weight_bytes),
        name="expert_grad",
    )(dp_arr, arriving, slot_grad, expert_act, pre_grad)
    expert_first = expert_parts[1] + swap(expert_parts[0], dp_axis, 0)
    expert_second = expert_parts[3] + swap(expert_parts[2], dp_axis, dp_bits - 1)
    expert_sums = (
        reduce_low(expert_first, dp_axis, dp_order[1:]),
        reduce_high(expert_second, dp_axis, dp_order[:-1]),
    )

    grad, gain_four, router_grad = call(
        combine_kernel,
        (stream_three, gain[3], router, picks, cols, cot, moe_in, probs, returned_grad),
        (None,) * 9,
        [stream_shape, gain_shape, shape((width, experts))],
        "combine",
        2 * padded * slots * width,
        6e6,
    )
    grad, gain_three, *second_dw = attn_bwd(grad, stream_two, kept_two, 1, 2)
    mlp_out = [core_shape, core_shape]
    mlp_scratch = [by_core]
    if wide_ok:
        mlp_out, mlp_scratch = mlp_out * 2, mlp_scratch * 2
    else:
        mlp_out = mlp_out + [shape((1, 4 * width, width), bf16)]
    grad, gain_two, *mlp_dw = call(
        functools.partial(mlp_bwd_kernel, wide_ok),
        (low_arr, grad, stream_one, gain[1], first_in, gathered, mlp_in, mlp_pre),
        (SMEM, None, None, None, first_spec, layer_spec(3), None, None),
        [stream_shape, gain_shape] + mlp_out,
        "mlp_bwd",
        16 * tok_flops,
        16 * weight_bytes,
        out_specs=[None, None] + [ANY if len(o.shape) == 3 and o.shape == core_shape.shape else None for o in mlp_out],
        scratch=mlp_scratch + [two_sems],
    )
    if not wide_ok:
        wide_grad = mlp_dw[2].reshape(4, width, width).transpose(1, 0, 2).reshape(per, rows, width)
        wide_grad = jnp.take(wide_grad, jnp.arange(per) ^ low, axis=0)
        wide_grad = wide_grad.reshape(per // 2, 2, rows, width)
        mlp_dw = mlp_dw[:2] + [wide_grad[:, 0], wide_grad[:, 1]]
    grad, gain_one, *first_dw = attn_bwd(grad, stream, kept_one, 0, 0)

    per_bits = per.bit_length() - 1
    cut = rows // 32 * 16
    top = (per_bits, per_bits + 1)
    z_bits = list(range(1, per_bits))
    layers = []
    for keep, send in (second_dw, mlp_dw[:2], mlp_dw[2:], first_dw):
        arrived = swap(send, both, 0)
        upper = reduce_low(keep[:, :cut] + arrived[:, :cut], both, z_bits)
        layers.append((upper, keep[:, cut:] + arrived[:, cut:]))
    layers = [layers[i] for i in (3, 0, 2, 1)]
    pieces = []
    for low_first in (True, False):
        at = slice(0, cut // 2) if low_first else slice(cut // 2, cut)
        pieces.append(reduce_layers([u[at] for u, _ in layers], both, top, me, low_first))
    for low_first in (True, False):
        middle = (rows - cut) // 2
        at = slice(0, middle) if low_first else slice(middle, rows - cut)
        part = reduce_layers([v[:, at] for _, v in layers], both, top, me, low_first)
        pieces.append(reduce_low(part, both, z_bits))

    output = call(
        output_kernel,
        (stream_three, picks, cols, probs, exchange(expert_out)),
        (None,) * 5,
        [shape((seq, width))],
        "output",
        4 * padded * slots * width,
        4e6,
    )[0]

    small = jnp.concatenate(
        [router_grad.reshape(-1)] + [g.reshape(-1) for g in (gain_one, gain_two, gain_three, gain_four)]
    )
    small = jnp.pad(small, (0, tail * LANES - small.shape[0])).reshape(tail, LANES)
    small = all_sum(small, both, all_bits)
    gain_at = width * experts
    gain_grads = small.reshape(-1)[gain_at : gain_at + 4 * width].reshape(4, width)

    def unpack(wide, pieces, count, name):
        return pl.pallas_call(
            functools.partial(unpack_kernel, (count, tiles)),
            in_specs=[SMEM] + [VMEM] * len(pieces),
            out_specs=[VMEM, VMEM],
            out_shape=[shape((count * tiles, LANES)), shape((1, LANES))],
            scratch_shapes=[pltpu.VMEM((count, width), f32)],
            compiler_params=params(),
            cost_estimate=cost(0, 6 * count * width),
            name=name,
        )(wide, *pieces)

    expert_grad, expert_square = unpack(expert_wide, expert_sums, expert_rows, "unpack_expert")
    dense_wide = (me >= devices // 2) & (me < 3 * devices // 4) & wide_ok
    dense_rows, _ = unpack(dense_wide.astype(jnp.int32).reshape(1), pieces, rows, "unpack_dense")
    head = lax.ppermute(dense_rows[:tail], both, backward_ring)
    head = jnp.where(me == devices - 1, small, head)
    dense_grad, dense_square = pl.pallas_call(
        functools.partial(shift_kernel, (step, own)),
        in_specs=[SMEM, VMEM, VMEM],
        out_specs=[VMEM, VMEM],
        out_shape=[shape((own, LANES)), shape((1, LANES))],
        scratch_shapes=[pltpu.VMEM((-(-(rows * tiles + tail) // 8) * 8, LANES), f32)],
        compiler_params=params(),
        cost_estimate=cost(0, 8 * rows * width),
        name="shift_dense",
    )(me_arr, dense_rows, head)

    square = all_sum(dense_square + expert_square, both, all_bits)
    square_sum = jnp.sum(square)
    param_count = (dense_master.size + expert_master.size) * devices
    clip_factor = jnp.minimum(1.0, jnp.sqrt(param_count / (square_sum + 1e-06))).reshape(1)

    dense_update, momentum_dense, variance_dense = adam(
        clip_factor,
        dense_grad,
        dense_momentum.reshape(own, LANES),
        dense_variance.reshape(own, LANES),
        own,
    )
    expert_update, momentum_expert, variance_expert = adam(
        clip_factor,
        expert_grad,
        expert_momentum.reshape(expert_flat, LANES),
        expert_variance.reshape(expert_flat, LANES),
        expert_flat // 8,
    )
    image = (1, seq, width)
    return (
        output.reshape(image),
        grad[:seq].reshape(image),
        dense_grad.reshape(dense_master.shape),
        expert_grad.reshape(expert_master.shape),
        dense_update.reshape(dense_master.shape),
        momentum_dense.reshape(dense_master.shape),
        variance_dense.reshape(dense_master.shape),
        expert_update.reshape(expert_master.shape),
        momentum_expert.reshape(expert_master.shape),
        variance_expert.reshape(expert_master.shape),
        gain_grads,
    )


def solution(mesh):
    tokens = P(("dp", "expert"), None, None)
    flat = P(("dp", "expert"))
    pairs = P(("dp", "expert"), None)
    expert = P("expert", "dp")
    return jax.shard_map(
        on_device,
        mesh=mesh,
        in_specs=(tokens, tokens, pairs, pairs, flat, flat, flat, expert, expert, expert),
        out_specs=(tokens, tokens, flat, expert, flat, flat, flat, expert, expert, expert, P()),
        check_vma=False,
    )
```

```python
import functools
import math

import jax
import jax.numpy as jnp
from jax import lax
from jax.experimental import pallas as pl
from jax.experimental.pallas import tpu as pltpu
from jax.sharding import PartitionSpec as P

HEADS = 12
HEAD_DIM = 64
LANES = 128

f32 = jnp.float32
bf16 = jnp.bfloat16

eps_norm = 1e-06
beta_first = 0.9
beta_second = 0.999
adam_eps = 1e-08
adam_step = 10.0

VMEM = pl.BlockSpec(memory_space=pltpu.VMEM)
SMEM = pl.BlockSpec(memory_space=pltpu.SMEM)


def params(mib=56):
    return pltpu.CompilerParams(vmem_limit_bytes=mib << 20)


def cost(*_):
    return pl.CostEstimate(flops=1, bytes_accessed=1, transcendentals=0)


def dot(a, b):
    return lax.dot_general(a, b, (((1,), (0,)), ((), ())), preferred_element_type=f32)


def dot_nt(a, b):
    return lax.dot_general(a, b, (((1,), (1,)), ((), ())), preferred_element_type=f32)


def dot_tn(a, b):
    return lax.dot_general(a, b, (((0,), (0,)), ((), ())), preferred_element_type=f32)


def norm_rows(hidden):
    center = hidden - jnp.mean(hidden, axis=-1, keepdims=True)
    inverse = lax.rsqrt(jnp.mean(center * center, axis=-1, keepdims=True) + eps_norm)
    return center * inverse, inverse


def norm_back(upstream, normed, inverse, gain):
    scaled = upstream * gain
    gain_grad = jnp.sum(upstream * normed, axis=0, keepdims=True)
    centered = (
        scaled
        - jnp.mean(scaled, axis=-1, keepdims=True)
        - normed * jnp.mean(scaled * normed, axis=-1, keepdims=True)
    )
    return inverse * centered, gain_grad


def normal_cdf(v):
    return 0.5 * (1.0 + lax.erf(v * 0.7071067811865476))


def density(v):
    return jnp.exp(-0.5 * v * v) * 0.3989422804014327


def to_rows(read, write, first_q, rows, wide, tiles):
    blocks = 4 if rows % 64 == 0 else 1
    count = rows // blocks
    for b in range(blocks):
        for j in range(tiles):
            if wide:
                write(b * count, count, j, read(first_q + tiles * b + j, count, 4 * tiles))
            else:
                write(b * count, count, j, read(first_q + tiles * count * b + j, count, tiles))


def pack_dense_kernel(dims, k_ref, tail_ref, own_ref, out_ref, buf):
    rows, tail_rows, tail, own, step, tiles, chunks, wide_ok = dims
    buf[0:tail] = tail_ref[...]
    buf[tail : tail + own] = own_ref[...]
    buf[tail + own :] = jnp.zeros((buf.shape[0] - tail - own, LANES), f32)
    k = k_ref[0]
    start = tail - step * k

    def read(first, count, stride):
        return buf[pl.ds(first, count, stride=stride), :]

    def write(first, count, j, value):
        out_ref[first : first + count, LANES * j : LANES * (j + 1)] = value.astype(bf16)

    wide = (k >= chunks // 2) & (k < 3 * chunks // 4) & wide_ok

    if wide_ok:

        @pl.when(wide)
        def _():
            to_rows(read, write, start, rows, True, tiles)

    @pl.when(jnp.logical_not(wide))
    def _():
        to_rows(read, write, start, rows, False, tiles)

    for j in range(tiles):
        write(rows, tail_rows, j, read(own + j, tail_rows, tiles))


def pack_expert_kernel(dims, wide_ref, own_ref, *out_refs):
    rows, tiles = dims
    half = rows // 2

    def read(first, count, stride):
        return own_ref[pl.ds(first, count, stride=stride), :]

    def write(first, count, j, value):
        at = first % half
        out_refs[first // half][at : at + count, LANES * j : LANES * (j + 1)] = value.astype(bf16)

    wide = wide_ref[0] > 0

    @pl.when(wide)
    def _():
        to_rows(read, write, 0, rows, True, tiles)

    @pl.when(jnp.logical_not(wide))
    def _():
        to_rows(read, write, 0, rows, False, tiles)


def add_up(refs):
    return sum(ref[...].astype(f32) for ref in refs)


def unpack_kernel(dims, groups, wide_ref, *refs):
    rows, tiles = dims
    refs, (out_ref, square_ref, rows_ref) = refs[:-3], refs[-3:]
    at = 0
    for count in groups:
        value = add_up(refs[:count])
        refs = refs[count:]
        rows_ref[at : at + value.shape[0]] = value
        at += value.shape[0]
    wide = wide_ref[0] > 0

    def store(is_wide):
        total = jnp.zeros((1, LANES), f32)
        quarter = rows // 4
        for q in range(4):
            for j in range(tiles):
                piece = rows_ref[q * quarter : (q + 1) * quarter, LANES * j : LANES * (j + 1)]
                if is_wide:
                    out_ref[pl.ds(tiles * q + j, quarter, stride=4 * tiles), :] = piece
                else:
                    out_ref[pl.ds(tiles * quarter * q + j, quarter, stride=tiles), :] = piece
                total = total + jnp.sum(piece * piece, axis=0, keepdims=True)
        square_ref[...] = total

    @pl.when(wide)
    def _():
        store(True)

    @pl.when(jnp.logical_not(wide))
    def _():
        store(False)


def stack_rows_kernel(*refs):
    out_ref = refs[-1]
    at = 0
    for ref in refs[:-1]:
        out_ref[at : at + ref.shape[0]] = ref[...]
        at += ref.shape[0]


def shift_kernel(dims, k_ref, flat_ref, head_ref, out_ref, buf):
    step, own = dims
    count = flat_ref.shape[0]
    buf[0:count] = flat_ref[...]
    buf[count : count + head_ref.shape[0]] = head_ref[...]
    out_ref[...] = buf[pl.ds(step * k_ref[0], own), :]


def adam_kernel(clip_ref, grad_ref, momentum_ref, variance_ref, update_ref, momentum_out, variance_out):
    clipped = grad_ref[...] * clip_ref[0]
    momentum_new = beta_first * momentum_ref[...] + (1.0 - beta_first) * clipped
    variance_new = beta_second * variance_ref[...] + (1.0 - beta_second) * clipped * clipped
    first_hat = momentum_new / (1.0 - beta_first**adam_step)
    second_hat = variance_new / (1.0 - beta_second**adam_step)
    update_ref[...] = -first_hat / (jnp.sqrt(second_hat) + adam_eps)
    momentum_out[...] = momentum_new
    variance_out[...] = variance_new


def adam(clip, grad, momentum, variance, block):
    count = grad.shape[0]
    spec = pl.BlockSpec((block, LANES), lambda i: (i, 0))
    shape = jax.ShapeDtypeStruct(grad.shape, f32)
    return pl.pallas_call(
        adam_kernel,
        grid=(pl.cdiv(count, block),),
        in_specs=[SMEM, spec, spec, spec],
        out_specs=[spec] * 3,
        out_shape=[shape] * 3,
        compiler_params=params(),
        cost_estimate=cost(20 * grad.size, 24 * grad.size, 2 * grad.size),
        name="adam",
    )(clip, grad, momentum, variance)


def route_kernel(
    experts, capacity, stride, me_ref, prio_row, prio_col, picks, picks_t, cot,
    cols_ref, near_ref, rows_ref, g_ref,
):
    count = picks.shape[0]
    me = me_ref[0]
    before = (prio_row[...] < prio_col[...]).astype(f32).astype(bf16)
    lane = lax.broadcasted_iota(jnp.int32, (count, experts), 1)
    sub = lax.broadcasted_iota(jnp.int32, (experts, count), 0)
    hot = [(picks[:, j : j + 1] == lane).astype(f32) for j in range(2)]
    hot_t = [(picks_t[j : j + 1, :] == sub).astype(f32) for j in range(2)]
    first = jnp.sum(hot[0], axis=0, keepdims=True)
    first_t = jnp.sum(hot_t[0], axis=1, keepdims=True)
    for j in range(2):
        earlier = dot(before, hot[j].astype(bf16)) + (first if j else 0.0)
        earlier_t = dot_nt(hot_t[j].astype(bf16), before) + (first_t if j else 0.0)
        place = jnp.sum(earlier * hot[j], axis=1, keepdims=True).astype(jnp.int32)
        place_t = jnp.sum(earlier_t * hot_t[j], axis=0, keepdims=True).astype(jnp.int32)
        pick, pick_t = picks[:, j : j + 1], picks_t[j : j + 1, :]
        kept = (place < capacity) & (pick >= 0)
        cols_ref[:, j : j + 1] = jnp.where(kept, pick * stride + place, -1)
        near_ref[:, j : j + 1] = jnp.where(kept, (pick ^ me) * stride + place, -1)
        kept = (place_t < capacity) & (pick_t >= 0)
        rows_ref[j : j + 1, :] = jnp.where(kept, pick_t * stride + place_t, -1)
    first, second = slot_selects(rows_ref, experts * stride)
    g_ref[...] = dot(first + second, cot[...]).astype(bf16)


def slot_selects(rows_ref, slots):
    sub = lax.broadcasted_iota(jnp.int32, (slots, rows_ref.shape[1]), 0)
    return [(rows_ref[j : j + 1, :] == sub).astype(f32).astype(bf16) for j in range(2)]


def token_selects(cols_ref, slots):
    lane = lax.broadcasted_iota(jnp.int32, (cols_ref.shape[0], slots), 1)
    return [(cols_ref[:, j : j + 1] == lane).astype(f32).astype(bf16) for j in range(2)]


def split_lanes(column):
    high = column.astype(bf16).astype(f32)
    rest = column - high
    middle = rest.astype(bf16).astype(f32)
    low = rest - middle
    lane = lax.broadcasted_iota(jnp.int32, (column.shape[0], LANES), 1)
    wide = jnp.where(lane == 0, high, jnp.where(lane == 1, middle, jnp.where(lane == 2, low, 0.0)))
    return wide.astype(bf16)


def head_masks():
    lane = lax.broadcasted_iota(jnp.int32, (1, 2 * HEAD_DIM), 1)
    first = (lane < HEAD_DIM).astype(f32)
    return first.astype(bf16), (1.0 - first).astype(bf16)


def soft_scores(queries, key_rows, key_ok):
    scores = dot_nt(queries, key_rows) * HEAD_DIM ** (-0.5)
    scores = jnp.where(key_ok, scores, -1e30)
    top = jnp.max(scores, axis=-1, keepdims=True)
    raised = jnp.exp(scores - top)
    return raised * (1.0 / jnp.sum(raised, axis=-1, keepdims=True))


def put_chunk(scratch, low, chunk, value, first=0):
    place = chunk ^ low
    scratch[place & 1, place >> 1, first : first + value.shape[0], :] = value


def flush(scratch, keep_ref, send_ref, sems):
    copies = [
        pltpu.make_async_copy(scratch.at[i], ref, sems.at[i]) for i, ref in enumerate((keep_ref, send_ref))
    ]
    for copy in copies:
        copy.start()
    for copy in copies:
        copy.wait()


def matrix(w_ref, index):
    per = w_ref.shape[0] // 4
    width = w_ref.shape[2]
    rows = width // per
    return w_ref[index * per : (index + 1) * per, 0:rows, :].reshape(width, width)


def quarter_in(w_ref, q):
    width = w_ref.shape[2]
    rows = width // w_ref.shape[0]
    return w_ref[:, q * rows : (q + 1) * rows, :].reshape(width, width)


def attn_fwd_kernel(seq, stream_ref, gain_ref, w_ref, out_ref, a_ref, q_ref, k_ref, v_ref, o_ref):
    normed, _ = norm_rows(stream_ref[...])
    a_ref[...] = (normed * gain_ref[...]).astype(bf16)
    for index, ref in enumerate((q_ref, k_ref, v_ref)):
        ref[...] = dot(a_ref[...], matrix(w_ref, index)).astype(bf16)
    count = stream_ref.shape[0]
    key_ok = lax.broadcasted_iota(jnp.int32, (count, count), 1) < seq
    masks = head_masks()
    for pair in range(HEADS // 2):
        lanes = slice(2 * HEAD_DIM * pair, 2 * HEAD_DIM * (pair + 1))
        mixed = None
        for mask in masks:
            soft = soft_scores(q_ref[:, lanes] * mask, k_ref[:, lanes], key_ok).astype(bf16)
            part = dot(soft, v_ref[:, lanes] * mask)
            mixed = part if mixed is None else mixed + part
        o_ref[:, lanes] = mixed.astype(bf16)
    out_ref[...] = stream_ref[...] + dot(o_ref[...], matrix(w_ref, 3))


def attn_bwd_kernel(
    seq, grad_ref, stream_ref, gain_ref, w_ref, q_ref, k_ref, v_ref, out_ref, gain_out, dq_ref, dk_ref, dv_ref, do_ref
):
    do_ref[...] = dot_nt(grad_ref[...].astype(bf16), matrix(w_ref, 3)).astype(bf16)
    count = grad_ref.shape[0]
    key_ok = lax.broadcasted_iota(jnp.int32, (count, count), 1) < seq
    masks = head_masks()
    scale = HEAD_DIM ** (-0.5)
    for pair in range(HEADS // 2):
        lanes = slice(2 * HEAD_DIM * pair, 2 * HEAD_DIM * (pair + 1))
        dq = dk = dv = None
        for mask in masks:
            q_h = q_ref[:, lanes] * mask
            k_h = k_ref[:, lanes] * mask
            do_h = do_ref[:, lanes] * mask
            soft = soft_scores(q_h, k_ref[:, lanes], key_ok)
            dsoft = dot_nt(do_h, v_ref[:, lanes])
            dv_h = dot_tn(soft.astype(bf16), do_h)
            inner = jnp.sum(dsoft * soft, axis=-1, keepdims=True)
            dscore = (soft * (dsoft - inner)).astype(bf16)
            dq_h = dot(dscore, k_h)
            dk_h = dot_tn(dscore, q_h)
            dq = dq_h if dq is None else dq + dq_h
            dk = dk_h if dk is None else dk + dk_h
            dv = dv_h if dv is None else dv + dv_h
        dq_ref[:, lanes] = (dq * scale).astype(bf16)
        dk_ref[:, lanes] = (dk * scale).astype(bf16)
        dv_ref[:, lanes] = dv.astype(bf16)
    back = None
    for index, ref in enumerate((dq_ref, dk_ref, dv_ref)):
        part = dot_nt(ref[...], matrix(w_ref, index))
        back = part if back is None else back + part
    normed, inverse = norm_rows(stream_ref[...])
    addend, gain_grad = norm_back(back, normed, inverse, gain_ref[...])
    out_ref[...] = grad_ref[...] + addend
    gain_out[...] = gain_grad


def attn_weights_kernel(
    low_ref, grad_ref, a_ref, o_ref, dq_ref, dk_ref, dv_ref, keep_ref, send_ref, dw, sems
):
    low = low_ref[0]
    rows = dw.shape[2]
    per = grad_ref.shape[1] // rows
    branch = grad_ref[...].astype(bf16)
    for index in range(4):
        left = o_ref if index == 3 else a_ref
        right = branch if index == 3 else (dq_ref, dk_ref, dv_ref)[index][...]
        value = dot_tn(left[...], right)
        for i in range(per):
            put_chunk(dw, low, index * per + i, value[i * rows : (i + 1) * rows].astype(bf16))
    flush(dw, keep_ref, send_ref, sems)


def mlp_fwd_kernel(stream_ref, gain_ref, w1_ref, w2_ref, out_ref, b_ref, u_ref):
    width = stream_ref.shape[1]
    normed, _ = norm_rows(stream_ref[...])
    b_ref[...] = (normed * gain_ref[...]).astype(bf16)
    out_ref[...] = stream_ref[...]
    total = None
    for q in range(4):
        pre = dot(b_ref[...], quarter_in(w1_ref, q))
        u_ref[:, q * width : (q + 1) * width] = pre
        part = dot((pre * normal_cdf(pre)).astype(bf16), matrix(w2_ref, q))
        total = part if total is None else total + part
    out_ref[...] = stream_ref[...] + total


def mlp_bwd_kernel(
    by_core, low_ref, grad_ref, stream_ref, gain_ref, w1_ref, w2_ref, b_ref, u_ref,
    out_ref, gain_out, keep2_ref, send2_ref, *refs,
):
    if by_core:
        keep1_ref, send1_ref, dw2, dw1, sems = refs
    else:
        dw1_ref, dw2, sems = refs
    width = grad_ref.shape[1]
    upper = grad_ref[...].astype(bf16)
    low = low_ref[0]
    back = None
    for q in range(4):
        pre = u_ref[:, q * width : (q + 1) * width]
        cdf = normal_cdf(pre)
        act = (pre * cdf).astype(bf16)
        rows = dw2.shape[2]
        per = width // rows
        second = dot_tn(act, upper)
        for i in range(per):
            put_chunk(dw2, low, q * per + i, second[i * rows : (i + 1) * rows].astype(bf16))
        dact = dot_nt(upper, matrix(w2_ref, q))
        dpre = (dact * (cdf + pre * density(pre))).astype(bf16)
        first = dot_tn(b_ref[...], dpre).astype(bf16)
        groups = w1_ref.shape[0]
        rows = width // groups
        for i in range(groups):
            piece = first[i * rows : (i + 1) * rows]
            if by_core:
                put_chunk(dw1, low, i, piece, q * rows)
            else:
                dw1_ref[i, q * rows : (q + 1) * rows, :] = piece
        part = dot_nt(dpre, quarter_in(w1_ref, q))
        back = part if back is None else back + part
    flush(dw2, keep2_ref, send2_ref, sems)
    if by_core:
        flush(dw1, keep1_ref, send1_ref, sems)
    normed, inverse = norm_rows(stream_ref[...])
    addend, gain_grad = norm_back(back, normed, inverse, gain_ref[...])
    out_ref[...] = grad_ref[...] + addend
    gain_out[...] = gain_grad


def pick_hots(picks, experts):
    lane = lax.broadcasted_iota(jnp.int32, (picks.shape[0], experts), 1)
    return [(picks[:, j : j + 1] == lane).astype(f32) for j in range(2)]


def softmax_rows(logits):
    raised = jnp.exp(logits - jnp.max(logits, axis=-1, keepdims=True))
    return raised / jnp.sum(raised, axis=-1, keepdims=True)


def dispatch_kernel(stream_ref, gain_ref, wr_ref, picks_ref, rows_ref, c_ref, probs_ref, x_ref):
    width = stream_ref.shape[1]
    experts = wr_ref.shape[1]
    normed, _ = norm_rows(stream_ref[...])
    c_ref[...] = (normed * gain_ref[...]).astype(bf16)
    probs = softmax_rows(dot(c_ref[...], wr_ref[...]))
    probs_ref[...] = probs
    hots = pick_hots(picks_ref, experts)
    selects = slot_selects(rows_ref, x_ref.shape[0])
    gates = None
    for j in range(2):
        part = dot(selects[j], split_lanes(jnp.sum(probs * hots[j], axis=-1, keepdims=True)))
        gates = part if gates is None else gates + part
    x_ref[:, 0:width] = dot(selects[0] + selects[1], c_ref[...]).astype(bf16)
    x_ref[:, width:] = gates.astype(bf16)


def add_lanes(wide):
    wide = wide.astype(f32)
    return wide[:, 0:1] + wide[:, 1:2] + wide[:, 2:3]


def expert_kernel(dims, spans, me_ref, x_ref, g_ref, *refs):
    parts, quarter, blocks = dims
    weight_refs, refs = refs[: len(spans)], refs[len(spans) :]
    y_refs, refs = refs[: blocks // 2], refs[blocks // 2 :]
    dx_ref, dy_ref, act_ref, dpre_ref, weights, y_near, y_sum, dx_sum, sems = refs
    q = pl.program_id(0)
    width = g_ref.shape[1]
    half = parts // 2
    me = me_ref[0]

    @pl.when(q == 0)
    def _():
        copies = [
            pltpu.make_async_copy(ref, weights.at[place ^ me, first : first + ref.shape[0]], sems.at[i])
            for i, ((place, first), ref) in enumerate(zip(spans, weight_refs))
        ]
        for copy in copies:
            copy.start()
        dy_ref[...] = (add_lanes(x_ref[:, width:]) * g_ref[...].astype(f32)).astype(bf16)
        for copy in copies:
            copy.wait()

    first = weights[0:half, pl.ds(pl.multiple_of(q * quarter, 16), quarter), :].reshape(width, width)
    if 4 * quarter >= width:
        per = 4 * quarter // width
        at = pl.ds(pl.multiple_of(lax.rem(q, per) * width, 16), width)
        second = weights[half + q // per, at, :]
    else:
        per = width // (4 * quarter)
        second = weights[pl.ds(half + q * per, per)].reshape(width, width)
    pre = dot(x_ref[:, 0:width], first)
    cdf = normal_cdf(pre)
    act = (pre * cdf).astype(bf16)
    act_ref[...] = act
    dact = dot_nt(dy_ref[...], second)
    dpre = (dact * (cdf + pre * density(pre))).astype(bf16)
    dpre_ref[...] = dpre
    y_part = dot(act, second)
    dx_part = dot_nt(dpre, first)

    @pl.when(q == 0)
    def _():
        y_sum[...] = y_part
        dx_sum[...] = dx_part

    @pl.when(q > 0)
    def _():
        y_sum[...] += y_part
        dx_sum[...] += dx_part

    @pl.when(q == pl.num_programs(0) - 1)
    def _():
        y = y_sum[...].astype(bf16).astype(f32)
        stride = y.shape[0] // blocks
        for block in range(blocks):
            y_near[block ^ me_ref[1]] = y[block * stride : (block + 1) * stride].astype(bf16)
        for pair, ref in enumerate(y_refs):
            ref[...] = y_near[2 * pair : 2 * pair + 2]
        dx_ref[:, 0:width] = dx_sum[...].astype(bf16)
        gate_grad = jnp.sum(g_ref[...].astype(f32) * y, axis=-1, keepdims=True)
        dx_ref[:, width:] = split_lanes(gate_grad)


def expert_grad_kernel(dims, dp_ref, x_ref, dy_ref, act_ref, dpre_ref, *refs):
    parts, quarter = dims
    out_refs, scratch, sems = refs[: 2 * parts], refs[-2], refs[-1]
    q = pl.program_id(0)
    me = dp_ref[0]
    width = dy_ref.shape[1]
    half = parts // 2
    rows = scratch.shape[1]
    first = dot_tn(x_ref[:, 0:width], dpre_ref[...]).astype(bf16)
    count = width // half
    for i in range(half):
        at = pl.ds(pl.multiple_of(q * quarter, 16), quarter)
        scratch[i ^ me, at, :] = first[i * count : (i + 1) * count]
    second = dot_tn(act_ref[...], dy_ref[...]).astype(bf16)
    if rows >= width:
        per = rows // width
        at = pl.ds(pl.multiple_of(lax.rem(q, per) * width, 16), width)
        scratch[(half + q // per) ^ me, at, :] = second
    else:
        per = width // rows
        for i in range(per):
            scratch[(half + q * per + i) ^ me] = second[i * rows : (i + 1) * rows]

    @pl.when(q == pl.num_programs(0) - 1)
    def _():
        copies = []
        for side, bit in ((0, 1), (1, parts // 2)):
            lists = [r for r in range(parts) if r & bit], [r for r in range(parts) if not r & bit]
            for which, group in enumerate(lists):
                for i, r in enumerate(group):
                    copies.append(
                        pltpu.make_async_copy(
                            scratch.at[r, side * rows // 2 : (side + 1) * rows // 2],
                            out_refs[side * parts + which * half + i],
                            sems.at[side * parts + r],
                        )
                    )
        for copy in copies:
            copy.start()
        for copy in copies:
            copy.wait()


def combine_kernel(
    stream_ref, gain_ref, wr_ref, picks_ref, cols_ref, cot_ref, c_ref, probs_ref, dx_ref,
    grad_ref, gain_out, router_out,
):
    width = stream_ref.shape[1]
    experts = wr_ref.shape[1]
    probs = probs_ref[...]
    hots = pick_hots(picks_ref, experts)
    selects = token_selects(cols_ref, dx_ref.shape[0])
    prob_grad = None
    for j in range(2):
        part = add_lanes(dot(selects[j], dx_ref[:, width:])) * hots[j]
        prob_grad = part if prob_grad is None else prob_grad + part
    logit_grad = probs * (prob_grad - jnp.sum(prob_grad * probs, axis=-1, keepdims=True))
    logit_grad = logit_grad.astype(bf16)
    router_out[...] = dot_tn(logit_grad, c_ref[...])
    back = dot(selects[0] + selects[1], dx_ref[:, 0:width]) + dot_nt(logit_grad, wr_ref[...])
    normed, inverse = norm_rows(stream_ref[...])
    addend, gain_grad = norm_back(back, normed, inverse, gain_ref[...])
    grad_ref[...] = cot_ref[...].astype(f32) + addend
    gain_out[...] = gain_grad


def output_kernel(stream_ref, picks_ref, near_ref, probs_ref, *refs):
    y_refs, (other_ref, out_ref, wide) = refs[:-3], refs[-3:]
    stride = other_ref.shape[1]
    for pair, ref in enumerate(y_refs):
        wide[2 * pair * stride : (2 * pair + 1) * stride] = ref[0].astype(f32)
        wide[(2 * pair + 1) * stride : (2 * pair + 2) * stride] = other_ref[pair].astype(f32)
    y = wide[...].astype(bf16)
    seq = out_ref.shape[0]
    probs = probs_ref[...]
    hots = pick_hots(picks_ref, probs.shape[1])
    selects = token_selects(near_ref, y.shape[0])
    total = stream_ref[...]
    for j in range(2):
        gate = jnp.sum(probs * hots[j], axis=-1, keepdims=True)
        total = total + gate * dot(selects[j], y)
    out_ref[...] = total[0:seq]


def add_pair(left, right):
    return (left.astype(f32) + right.astype(f32)).astype(bf16)


def fold_layers_kernel(cut, top_ref, *refs):
    layers, refs = [refs[2 * i : 2 * i + 2] for i in range(4)], refs[8:]
    uppers, (send_x, keep_x, send_y, keep_y, scratch) = refs[:4], refs[4:]
    middle = send_x.shape[2]
    place = pl.program_id(0)
    for layer, (keep, got) in enumerate(layers):
        value = add_pair(keep[0], got[0])
        for j, upper in enumerate(uppers):

            @pl.when(lax.rem(place, 4) == j)
            def _():
                upper[layer, place // 4] = value[:cut]

        scratch[layer ^ top_ref[0]] = value[cut:]
    for i in range(2):
        keep_x[i, 0] = scratch[2 * i, 0:middle]
        send_x[i, 0] = scratch[2 * i + 1, 0:middle]
        keep_y[i, 0] = scratch[i, middle:]
        send_y[i, 0] = scratch[i + 2, middle:]


def fold_plane_kernel(keep_x, got_x, keep_y, got_y, own_a, send_y, own_b, send_x):
    for keep, got, own, send in ((keep_x, got_x, own_a, send_y), (keep_y, got_y, own_b, send_x)):
        own[...] = add_pair(keep[0], got[0])
        send[...] = add_pair(keep[1], got[1])


def fold_rows_kernel(own_a, got_a, own_b, got_b, *outs):
    middle = own_a.shape[1]
    for place in range(own_a.shape[0]):
        out = outs[place % 4].at[place // 4]
        out[0:middle] = add_pair(own_a[place], got_a[place])
        out[middle:] = add_pair(own_b[place], got_b[place])


def fold_uppers_kernel(top_ref, *refs):
    refs, outs, scratch = refs[:-5], refs[-5:-1], refs[-1]
    for layer in range(4):
        scratch[layer ^ top_ref[0]] = sum(ref[layer].astype(f32) for ref in refs).astype(bf16)
    for place, out in enumerate(outs):
        out[...] = scratch[place]


def fold_expert_kernel(highs, *refs):
    count = len(refs) // 6
    ins, outs = refs[: 4 * count], refs[4 * count :]
    for side, high in enumerate(highs):
        half = count // 2
        for i in range(count):
            which, at = (i // half, i % half) if high else (i % 2, i // 2)
            keep, got = ins[2 * side * count + i], ins[(2 * side + 1) * count + i]
            outs[side * count + which * half + at][...] = add_pair(keep[...], got[...])


def swap(value, axes, mask):
    size = 1
    for axis in axes:
        size *= lax.axis_size(axis)
    return lax.ppermute(value, axes, [(i, i ^ mask) for i in range(size)])


def after(value, *others):
    return lax.optimization_barrier((value, others))[0]


def bit_groups(bits):
    return [bits[i : i + 2] for i in range(0, len(bits), 2)]


def all_sum_step(value, axes, bits):
    if len(bits) == 1:
        return value + swap(value, axes, 1 << bits[0])
    low, high = 1 << bits[0], 1 << bits[1]
    near, far, both = swap(value, axes, low), swap(value, axes, high), swap(value, axes, low | high)
    return (value + near) + (far + both)


def reduce_bits(value, axes, bits):
    for bit in bits:
        pairs = value.reshape((value.shape[0] // 2, 2) + value.shape[1:])
        value = pairs[:, 0] + swap(pairs[:, 1], axes, 1 << bit)
    return value[0]


def shape(dims, dtype=f32):
    return jax.ShapeDtypeStruct(dims, dtype)


def on_device(
    tokens,
    cotangent,
    expert_picks,
    priority,
    dense_master,
    dense_momentum,
    dense_variance,
    expert_master,
    expert_momentum,
    expert_variance,
):
    both = ("dp", "expert")
    dp_ranks = lax.axis_size("dp")
    expert_ranks = lax.axis_size("expert")
    devices = dp_ranks * expert_ranks
    local_experts = expert_master.shape[0]
    experts = local_experts * expert_ranks
    images, seq, width = tokens.shape
    assert local_experts == 1 and images == 1
    assert devices & (devices - 1) == 0 and dp_ranks >= 4
    tiles = width // LANES
    dp_me = lax.axis_index("dp").astype(jnp.int32)
    me = dp_me * expert_ranks + lax.axis_index("expert").astype(jnp.int32)
    me_arr = me.reshape(1)
    dp_arr = dp_me.reshape(1)
    dp_bits = dp_ranks.bit_length() - 1
    all_bits = devices.bit_length() - 1

    own = dense_master.shape[0] // LANES
    expert_flat = expert_master.shape[1] // LANES
    hidden = expert_master.shape[1] * dp_ranks // (2 * width)
    matrix_rows = 8 * width + 2 * hidden
    rows = matrix_rows // devices
    step = own - rows * tiles
    tail = step * devices
    tail_rows = -(-tail // (16 * tiles)) * 16
    wide_ok = rows % 64 == 0
    expert_rows = expert_flat // tiles

    dense_flat = dense_master.reshape(own, LANES)
    forward_ring = [(i, (i + 1) % devices) for i in range(devices)]
    backward_ring = [((i + 1) % devices, i) for i in range(devices)]
    tail_from = lax.ppermute(dense_flat[own - tail :], both, forward_ring)
    buf_rows = -(-(own + max(tail, tail_rows * tiles)) // 8) * 8
    chunk = pl.pallas_call(
        functools.partial(
            pack_dense_kernel, (rows, tail_rows, tail, own, step, tiles, devices, wide_ok)
        ),
        in_specs=[SMEM, VMEM, VMEM],
        out_specs=VMEM,
        out_shape=shape((rows + tail_rows, width), bf16),
        scratch_shapes=[pltpu.VMEM((buf_rows, LANES), f32)],
        compiler_params=params(),
        cost_estimate=cost(0, 6 * dense_master.size),
        name="pack_dense",
    )(me_arr, tail_from, dense_flat)
    gathered = lax.all_gather(chunk, both, axis=0, tiled=True)
    gathered = gathered.reshape(devices, rows + tail_rows, width)

    expert_wide = (dp_me < dp_ranks // 2).astype(jnp.int32).reshape(1)
    halves = pl.pallas_call(
        functools.partial(pack_expert_kernel, (expert_rows, tiles)),
        in_specs=[SMEM, VMEM],
        out_specs=[VMEM, VMEM],
        out_shape=[shape((expert_rows // 2, width), bf16)] * 2,
        compiler_params=params(),
        cost_estimate=cost(0, 6 * expert_master.size),
        name="pack_expert",
    )(expert_wide, expert_master.reshape(expert_flat, LANES))
    dp_axis = ("dp",)
    dp_order = list(range(dp_bits))

    def gather_step(parts, bit):
        return {**parts, **{at | (1 << bit): swap(part, dp_axis, 1 << bit) for at, part in parts.items()}}

    half_rows = expert_rows // 2
    orders = (dp_order, dp_order[::-1])
    sides = [gather_step({0: half}, bits[0]) for half, bits in zip(halves, orders)]
    gathered, sides = lax.optimization_barrier((gathered, sides))
    sides = [gather_step(side, bits[1]) for side, bits in zip(sides, orders)]
    for i, bits in enumerate(orders):
        for bit in bits[2:]:
            sides[i] = gather_step(sides[i], bit)
    expert_parts = [side[at] for side in sides for at in sorted(side)]
    expert_spans = [(at, i * half_rows) for i, side in enumerate(sides) for at in sorted(side)]
    soon = [sides[i][1 << bits[1]] for i, bits in enumerate(orders)]

    capacity = 2 * seq // experts
    stride = -(-capacity // 8) * 8
    slots = experts * stride
    padded = -(-seq // 16) * 16
    fill = padded - seq
    ranks = jnp.pad(priority, ((0, 0), (0, fill)), constant_values=1 << 20)
    picks = jnp.pad(expert_picks, ((0, fill), (0, 0)), constant_values=-1)
    cot = jnp.pad(cotangent.reshape(seq, width), ((0, fill), (0, 0)))
    stream = jnp.pad(tokens.reshape(seq, width).astype(f32), ((0, fill), (0, 0)))
    e_me = lax.axis_index("expert").astype(jnp.int32).reshape(1)
    pair_shape = shape((2, stride, width), bf16)
    cols, near_cols, rows_slots, outgoing_cot = pl.pallas_call(
        functools.partial(route_kernel, experts, capacity, stride),
        in_specs=[SMEM] + [VMEM] * 5,
        out_specs=[VMEM] * 4,
        out_shape=[shape((padded, 2), jnp.int32)] * 2
        + [shape((2, padded), jnp.int32), shape((slots, width), bf16)],
        compiler_params=params(),
        cost_estimate=cost(),
        name="route",
    )(e_me, ranks, ranks.reshape(padded, 1), picks, picks.T, cot)

    def exchange(value):
        dims = value.shape
        value = value.reshape(expert_ranks, slots // expert_ranks, dims[1])
        value = lax.all_to_all(value, "expert", split_axis=0, concat_axis=0, tiled=True)
        return value.reshape(dims)

    arriving_cot = exchange(outgoing_cot)

    tail_flat = gathered[devices - 1, rows:, :].reshape(-1)
    router = tail_flat[: width * experts].reshape(width, experts)
    gains = tail_flat[width * experts : width * (experts + 4)].reshape(4, width).astype(f32)
    gain = [gains[i : i + 1] for i in range(4)]

    per = devices // 4
    dense_block = (per, rows + tail_rows, width)
    low = me & (per - 1)
    low_arr = low.reshape(1)

    def layer_spec(index):
        return pl.BlockSpec(dense_block, lambda *_: (index, 0, 0), pipeline_mode=pl.Buffered(1))

    if wide_ok:
        first_in, first_spec = gathered, layer_spec(2)
    else:
        first_in = gathered[2 * per : 3 * per, :rows].reshape(width, 4, width)
        first_in = first_in.transpose(1, 0, 2).reshape(1, 4 * width, width)
        first_spec = None

    act_shape = shape((padded, width), bf16)
    stream_shape = shape((padded, width), f32)
    gain_shape = shape((1, width), f32)
    tok_flops = 2 * padded * width * width
    weight_bytes = 2 * width * width
    ANY = pl.BlockSpec(memory_space=pl.ANY)

    def call(kernel, ins, in_specs, outs, name, flops, nbytes, out_specs=None, scratch=()):
        out_specs = out_specs or [None] * len(outs)

        def whole(a):
            return pl.BlockSpec(a.shape, lambda *_, n=len(a.shape): (0,) * n)

        return pl.pallas_call(
            kernel,
            grid=(1,),
            in_specs=[s or whole(a) for a, s in zip(ins, in_specs, strict=True)],
            out_specs=[s or whole(a) for a, s in zip(outs, out_specs, strict=True)],
            out_shape=outs,
            scratch_shapes=list(scratch),
            compiler_params=params(),
            cost_estimate=cost(flops, nbytes),
            name=name,
        )(*ins)

    def attn_fwd(value, layer, which):
        return call(
            functools.partial(attn_fwd_kernel, seq),
            (value, gain[which], gathered),
            (None, None, layer_spec(layer)),
            [stream_shape] + [act_shape] * 5,
            "attn_fwd",
            5 * tok_flops,
            4 * weight_bytes,
        )

    places = per // 2
    core_shape = shape((places, rows, width), bf16)
    by_core = pltpu.VMEM((2, places, rows, width), bf16)
    sems = pltpu.SemaphoreType.DMA((2,))

    def attn_bwd(grad, value, kept, layer, which):
        return call(
            functools.partial(attn_bwd_kernel, seq),
            (grad, value, gain[which], gathered, *kept[1:4]),
            (None, None, None, layer_spec(layer)) + (None,) * 3,
            [stream_shape, gain_shape] + [act_shape] * 3,
            "attn_bwd",
            0,
            0,
            scratch=[pltpu.VMEM((padded, width), bf16)],
        )

    def attn_weights(grad, kept, found):
        return call(
            attn_weights_kernel,
            (low_arr, grad, kept[0], kept[4], *found),
            (SMEM,) + (None,) * 6,
            [core_shape, core_shape],
            "attn_weights",
            0,
            0,
            out_specs=[ANY] * 2,
            scratch=[by_core, sems],
        )

    stream_one, *kept_one = attn_fwd(stream, 0, 0)
    stream_two, mlp_in, mlp_pre = call(
        mlp_fwd_kernel,
        (stream_one, gain[1], first_in, gathered),
        (None, None, first_spec, layer_spec(3)),
        [stream_shape, act_shape, shape((padded, hidden), f32)],
        "mlp_fwd",
        8 * tok_flops,
        8 * weight_bytes,
    )
    stream_three, *kept_two = attn_fwd(stream_two, 1, 2)
    stream_three = after(stream_three, soon)
    moe_in, probs, outgoing = call(
        dispatch_kernel,
        (stream_three, gain[3], router, picks, rows_slots),
        (None,) * 5,
        [act_shape, shape((padded, experts)), shape((slots, width + LANES), bf16)],
        "dispatch",
        0,
        0,
    )
    arriving = exchange(outgoing)

    quarter = expert_rows // 4
    slot_spec = pl.BlockSpec((slots, width), lambda q: (0, 0))
    wide_spec = pl.BlockSpec((slots, width + LANES), lambda q: (0, 0))
    pair_spec = pl.BlockSpec((2, stride, width), lambda q: (0, 0, 0))
    hidden_spec = pl.BlockSpec((slots, width), lambda q: (0, q))
    pairs = experts // 2
    *expert_out, input_back, slot_grad, expert_act, pre_grad = pl.pallas_call(
        functools.partial(expert_kernel, (dp_ranks, quarter, experts), expert_spans),
        grid=(4,),
        in_specs=[SMEM, wide_spec, slot_spec] + [ANY] * len(expert_parts),
        out_specs=[pair_spec] * pairs + [wide_spec, slot_spec, hidden_spec, hidden_spec],
        out_shape=[pair_shape] * pairs
        + [shape((slots, width + LANES), bf16), shape((slots, width), bf16)]
        + [shape((slots, hidden), bf16)] * 2,
        scratch_shapes=[
            pltpu.VMEM((dp_ranks, expert_rows, width), bf16),
            pltpu.VMEM((experts, stride, width), bf16),
            pltpu.VMEM((slots, width), f32),
            pltpu.VMEM((slots, width), f32),
            pltpu.SemaphoreType.DMA((len(expert_parts),)),
        ],
        compiler_params=params(),
        cost_estimate=cost(),
        name="expert",
    )(jnp.concatenate([dp_arr, e_me]), arriving, arriving_cot, *expert_parts)
    returned_grad = exchange(input_back)
    part_shape = shape((expert_rows // 2, width), bf16)
    expert_first = pl.pallas_call(
        functools.partial(expert_grad_kernel, (dp_ranks, quarter)),
        grid=(4,),
        in_specs=[SMEM, wide_spec, slot_spec, hidden_spec, hidden_spec],
        out_specs=[ANY] * (2 * dp_ranks),
        out_shape=[part_shape] * (2 * dp_ranks),
        scratch_shapes=[
            pltpu.VMEM((dp_ranks, expert_rows, width), bf16),
            pltpu.SemaphoreType.DMA((2 * dp_ranks,)),
        ],
        compiler_params=params(),
        cost_estimate=cost(),
        name="expert_grad",
    )(dp_arr, arriving, slot_grad, expert_act, pre_grad)
    count = dp_ranks // 2
    expert_first = [expert_first[i * count : (i + 1) * count] for i in range(4)]
    returned_grad = after(returned_grad, expert_first)

    per_bits = per.bit_length() - 1
    cut = max(16, rows // 96 * 16)
    middle = (rows - cut) // 2
    top_bits = (per_bits, per_bits + 1)
    top = (me >> per_bits).reshape(1)
    z_bits = list(range(1, per_bits))
    z_masks = [2 * j for j in (1, 2, 3)]
    assert places % 4 == 0

    def over_z(values):
        return [values[0]] + [swap(value, both, mask) for value, mask in zip(values[1:], z_masks)]

    def rest_of_z(values):
        if len(z_bits) == 2:
            return values
        total = sum(value.astype(f32) for value in values).astype(bf16)
        lead = total.ndim - 3
        total = jnp.moveaxis(total, lead, 0)
        return [reduce_bits(total, both, z_bits[2:])]

    grad, gain_four, router_grad = call(
        combine_kernel,
        (stream_three, gain[3], router, picks, cols, cot, moe_in, probs, returned_grad),
        (None,) * 9,
        [stream_shape, gain_shape, shape((experts, width))],
        "combine",
        0,
        0,
    )
    def to_other_core(parts):
        return [parts[0], swap(parts[1], both, 1)]

    expert_got = [
        [swap(value[i], dp_axis, mask) for i in range(dp_ranks // 2)]
        for value, mask in ((expert_first[0], 1), (expert_first[2], dp_ranks // 2))
    ]
    upper = grad
    grad, gain_three, *found = attn_bwd(upper, stream_two, kept_two, 1, 2)
    second_dw = to_other_core(attn_weights(upper, kept_two, found))

    mlp_out = [core_shape, core_shape]
    mlp_out = mlp_out * 2 if wide_ok else mlp_out + [shape((1, 4 * width, width), bf16)]
    grad, gain_two, *mlp_dw = call(
        functools.partial(mlp_bwd_kernel, wide_ok),
        (low_arr, grad, stream_one, gain[1], first_in, gathered, mlp_in, mlp_pre),
        (SMEM, None, None, None, first_spec, layer_spec(3), None, None),
        [stream_shape, gain_shape] + mlp_out,
        "mlp_bwd",
        0,
        0,
        out_specs=[None, None] + ([ANY] * 4 if wide_ok else [ANY] * 2 + [None]),
        scratch=[by_core] * (2 if wide_ok else 1) + [sems],
    )
    if not wide_ok:
        wide_grad = mlp_dw[2].reshape(4, width, width).transpose(1, 0, 2).reshape(per, rows, width)
        wide_grad = jnp.take(wide_grad, jnp.arange(per) ^ low, axis=0)
        wide_grad = wide_grad.reshape(places, 2, rows, width)
        mlp_dw = mlp_dw[:2] + [wide_grad[:, 0], wide_grad[:, 1]]
    mlp_dw = [to_other_core(mlp_dw[i : i + 2]) for i in (0, 2)]

    upper = grad
    grad, gain_one, *found = attn_bwd(upper, stream, kept_one, 0, 0)
    found, expert_got = lax.optimization_barrier((found, expert_got))
    first_dw = to_other_core(attn_weights(upper, kept_one, found))

    small = call(
        stack_rows_kernel,
        (router_grad, gain_one, gain_two, gain_three, gain_four),
        (None,) * 5,
        [shape((experts + 4, width))],
        "stack_rows",
        0,
        0,
    )[0]
    found_small = small
    small = jnp.sum(lax.all_gather(small, both, axis=0, tiled=False), axis=0)

    plane_shape = shape((2, places, middle, width), bf16)
    plane_spec = pl.BlockSpec((2, 1, middle, width), lambda i: (0, i, 0, 0))
    line_shape = shape((places, middle, width), bf16)
    line_spec = pl.BlockSpec((1, middle, width), lambda i: (i, 0, 0))
    upper_shape = shape((4, places // 4, cut, width), bf16)
    part_spec = pl.BlockSpec((1, rows, width), lambda i: (i, 0, 0))
    layers = (first_dw, second_dw, mlp_dw[1], mlp_dw[0])
    *uppers, send_x, keep_x, send_y, keep_y = pl.pallas_call(
        functools.partial(fold_layers_kernel, cut),
        grid=(places,),
        in_specs=[SMEM] + [part_spec] * 8,
        out_specs=[pl.BlockSpec(upper_shape.shape, lambda i: (0, 0, 0, 0))] * 4 + [plane_spec] * 4,
        out_shape=[upper_shape] * 4 + [plane_shape] * 4,
        scratch_shapes=[pltpu.VMEM((4, rows - cut, width), bf16)],
        compiler_params=params(),
        cost_estimate=cost(),
        name="fold_layers",
    )(top, *[part for layer in layers for part in layer])
    masks = [1 << bit for bit in top_bits]
    got_x, got_y = swap(send_x, both, masks[0]), swap(send_y, both, masks[1])
    uppers = over_z(uppers)
    expert_ins = [part for i in (0, 1) for group in (expert_first[2 * i + 1], expert_got[i]) for part in group]
    expert_second = call(
        functools.partial(fold_expert_kernel, (dp_bits == 1, True)),
        expert_ins,
        (None,) * len(expert_ins),
        [part_shape] * (2 * count),
        "fold_expert",
        0,
        0,
    )

    uppers = [value.reshape(4, -1, cut, width) for value in uppers]
    uppers = [value.reshape(4, cut, width) for value in rest_of_z(uppers)]
    uppers, expert_second = lax.optimization_barrier((uppers, expert_second))
    upper_rows = call(
        fold_uppers_kernel,
        (top, *uppers),
        (SMEM,) + (None,) * len(uppers),
        [shape((cut, width), bf16)] * 4,
        "fold_uppers",
        0,
        0,
        scratch=[pltpu.VMEM((4, cut, width), bf16)],
    )
    got_x, got_y, upper_rows = lax.optimization_barrier((got_x, got_y, upper_rows))

    expert_out = after(expert_out, upper_rows)
    expert_out = [expert_out[0]] + [swap(v, ("expert",), 2 * j) for j, v in enumerate(expert_out) if j]
    own_a, send_y, own_b, send_x = pl.pallas_call(
        fold_plane_kernel,
        grid=(places,),
        in_specs=[plane_spec] * 4,
        out_specs=[line_spec] * 4,
        out_shape=[line_shape] * 4,
        compiler_params=params(),
        cost_estimate=cost(),
        name="fold_plane",
    )(keep_x, got_x, keep_y, got_y)
    got_y, got_x = swap(send_y, both, masks[1]), swap(send_x, both, masks[0])
    got_x, got_y, expert_out = lax.optimization_barrier((got_x, got_y, expert_out))
    other_out = swap(jnp.stack([value[1] for value in expert_out]), ("expert",), 1)
    lower_rows = call(
        fold_rows_kernel,
        (own_a, got_y, own_b, got_x),
        (None,) * 4,
        [shape((places // 4, rows - cut, width), bf16)] * 4,
        "fold_rows",
        0,
        0,
    )
    lower_rows, other_out, expert_second, _ = lax.optimization_barrier((lower_rows, other_out, expert_second, found_small))
    lower_rows = over_z(lower_rows)
    half = count // 2
    expert_groups = []
    for side, bits in enumerate(orders):
        keep, send = (expert_second[(2 * side + i) * half : (2 * side + i + 1) * half] for i in range(2))
        got = [swap(part, dp_axis, 1 << bits[1]) for part in send]
        expert_groups.append([list(pair) for pair in zip(keep, got)])
    if dp_bits > 2:
        for side, bits in enumerate(orders):
            value = [sum(pair) for pair in expert_groups[side]]
            for bit in bits[2:]:
                half = len(value) // 2
                keep, send = (value[:half], value[half:]) if side else (value[0::2], value[1::2])
                value = [k + swap(v, dp_axis, 1 << bit) for k, v in zip(keep, send)]
            expert_groups[side] = [value]
    expert_groups = [side[0] for side in expert_groups]
    upper_rows, expert_groups = lax.optimization_barrier((upper_rows, expert_groups))

    output = call(
        output_kernel,
        (stream_three, picks, near_cols, probs, *expert_out, other_out),
        (None,) * (5 + pairs),
        [shape((seq, width))],
        "output",
        0,
        0,
        scratch=[pltpu.VMEM((slots, width), f32)],
    )[0]

    lower_rows, output = lax.optimization_barrier((lower_rows, output))
    lower_rows = rest_of_z(lower_rows)
    upper_rows = [upper_rows[0]] + [
        swap(value, both, masks[0] * j) for j, value in enumerate(upper_rows) if j
    ]
    dense_groups = [upper_rows, [value.reshape(rows - cut, width) for value in lower_rows]]

    gain_grads = small[experts:]
    small_square = jnp.sum(small * small)
    small = jnp.concatenate([small[:experts].T.reshape(-1, LANES), gain_grads.reshape(-1, LANES)])
    small = jnp.pad(small, ((0, tail - small.shape[0]), (0, 0)))

    def unpack(wide, groups, count, name):
        pieces = [piece for group in groups for piece in group]
        return pl.pallas_call(
            functools.partial(unpack_kernel, (count, tiles), [len(group) for group in groups]),
            in_specs=[SMEM] + [VMEM] * len(pieces),
            out_specs=[VMEM, VMEM],
            out_shape=[shape((count * tiles, LANES)), shape((1, LANES))],
            scratch_shapes=[pltpu.VMEM((count, width), f32)],
            compiler_params=params(),
            cost_estimate=cost(0, 6 * count * width),
            name=name,
        )(wide, *pieces)

    expert_grad, expert_square = unpack(expert_wide, expert_groups, expert_rows, "unpack_expert")
    dense_wide = (me >= devices // 2) & (me < 3 * devices // 4) & wide_ok
    dense_rows, dense_square = unpack(dense_wide.astype(jnp.int32).reshape(1), dense_groups, rows, "unpack_dense")
    head = lax.ppermute(dense_rows[:tail], both, backward_ring)
    head = jnp.where(me == devices - 1, small, head)
    dense_grad = pl.pallas_call(
        functools.partial(shift_kernel, (step, own)),
        in_specs=[SMEM, VMEM, VMEM],
        out_specs=VMEM,
        out_shape=shape((own, LANES)),
        scratch_shapes=[pltpu.VMEM((-(-(rows * tiles + tail) // 8) * 8, LANES), f32)],
        compiler_params=params(),
        cost_estimate=cost(0, 8 * rows * width),
        name="shift_dense",
    )(me_arr, dense_rows, head)

    square = dense_square + expert_square
    for bits in bit_groups(list(range(all_bits))):
        square = all_sum_step(square, both, bits)
    square_sum = jnp.sum(square) + small_square
    param_count = (dense_master.size + expert_master.size) * devices
    clip_factor = jnp.minimum(1.0, jnp.sqrt(param_count / (square_sum + 1e-06))).reshape(1)

    dense_update, momentum_dense, variance_dense = adam(
        clip_factor,
        dense_grad,
        dense_momentum.reshape(own, LANES),
        dense_variance.reshape(own, LANES),
        own,
    )
    expert_update, momentum_expert, variance_expert = adam(
        clip_factor,
        expert_grad,
        expert_momentum.reshape(expert_flat, LANES),
        expert_variance.reshape(expert_flat, LANES),
        expert_flat // 8,
    )
    image = (1, seq, width)
    return (
        output.reshape(image),
        grad[:seq].reshape(image),
        dense_grad.reshape(dense_master.shape),
        expert_grad.reshape(expert_master.shape),
        dense_update.reshape(dense_master.shape),
        momentum_dense.reshape(dense_master.shape),
        variance_dense.reshape(dense_master.shape),
        expert_update.reshape(expert_master.shape),
        momentum_expert.reshape(expert_master.shape),
        variance_expert.reshape(expert_master.shape),
        gain_grads,
    )


def solution(mesh):
    tokens = P(("dp", "expert"), None, None)
    flat = P(("dp", "expert"))
    pairs = P(("dp", "expert"), None)
    expert = P("expert", "dp")
    return jax.shard_map(
        on_device,
        mesh=mesh,
        in_specs=(tokens, tokens, pairs, pairs, flat, flat, flat, expert, expert, expert),
        out_specs=(tokens, tokens, flat, expert, flat, flat, flat, expert, expert, expert, P()),
        check_vma=False,
    )
```

```python
import functools
import math

import jax
import jax.numpy as jnp
from jax import lax
from jax.experimental import pallas as pl
from jax.experimental.pallas import tpu as pltpu
from jax.sharding import PartitionSpec as P

HEADS = 12
HEAD_DIM = 64
LANES = 128

f32 = jnp.float32
bf16 = jnp.bfloat16

eps_norm = 1e-06
beta_first = 0.9
beta_second = 0.999
adam_eps = 1e-08
adam_step = 10.0

VMEM = pl.BlockSpec(memory_space=pltpu.VMEM)
SMEM = pl.BlockSpec(memory_space=pltpu.SMEM)


def params(mib=56):
    return pltpu.CompilerParams(vmem_limit_bytes=mib << 20)


def cost(*_):
    return pl.CostEstimate(flops=1, bytes_accessed=1, transcendentals=0)


def dot(a, b):
    return lax.dot_general(a, b, (((1,), (0,)), ((), ())), preferred_element_type=f32)


def dot_nt(a, b):
    return lax.dot_general(a, b, (((1,), (1,)), ((), ())), preferred_element_type=f32)


def dot_tn(a, b):
    return lax.dot_general(a, b, (((0,), (0,)), ((), ())), preferred_element_type=f32)


def norm_rows(hidden):
    center = hidden - jnp.mean(hidden, axis=-1, keepdims=True)
    inverse = lax.rsqrt(jnp.mean(center * center, axis=-1, keepdims=True) + eps_norm)
    return center * inverse, inverse


def norm_back(upstream, normed, inverse, gain):
    scaled = upstream * gain
    gain_grad = jnp.sum(upstream * normed, axis=0, keepdims=True)
    centered = (
        scaled
        - jnp.mean(scaled, axis=-1, keepdims=True)
        - normed * jnp.mean(scaled * normed, axis=-1, keepdims=True)
    )
    return inverse * centered, gain_grad


def normal_cdf(v):
    return 0.5 * (1.0 + lax.erf(v * 0.7071067811865476))


def density(v):
    return jnp.exp(-0.5 * v * v) * 0.3989422804014327


def to_rows(read, write, first_q, rows, wide, tiles):
    blocks = 4 if rows % 64 == 0 else 1
    count = rows // blocks
    for b in range(blocks):
        for j in range(tiles):
            if wide:
                write(b * count, count, j, read(first_q + tiles * b + j, count, 4 * tiles))
            else:
                write(b * count, count, j, read(first_q + tiles * count * b + j, count, tiles))


def pack_dense_kernel(dims, k_ref, tail_ref, own_ref, out_ref, buf):
    rows, tail_rows, tail, own, step, tiles, chunks, wide_ok = dims
    buf[0:tail] = tail_ref[...]
    buf[tail : tail + own] = own_ref[...]
    buf[tail + own :] = jnp.zeros((buf.shape[0] - tail - own, LANES), f32)
    k = k_ref[0]
    start = tail - step * k

    def read(first, count, stride):
        return buf[pl.ds(first, count, stride=stride), :]

    def write(first, count, j, value):
        out_ref[first : first + count, LANES * j : LANES * (j + 1)] = value.astype(bf16)

    wide = (k >= chunks // 2) & (k < 3 * chunks // 4) & wide_ok

    if wide_ok:

        @pl.when(wide)
        def _():
            to_rows(read, write, start, rows, True, tiles)

    @pl.when(jnp.logical_not(wide))
    def _():
        to_rows(read, write, start, rows, False, tiles)

    for j in range(tiles):
        write(rows, tail_rows, j, read(own + j, tail_rows, tiles))


def pack_expert_kernel(dims, wide_ref, own_ref, out_ref):
    rows, tiles = dims

    def read(first, count, stride):
        return own_ref[pl.ds(first, count, stride=stride), :]

    def write(first, count, j, value):
        out_ref[first : first + count, LANES * j : LANES * (j + 1)] = value.astype(bf16)

    wide = wide_ref[0] > 0

    @pl.when(wide)
    def _():
        to_rows(read, write, 0, rows, True, tiles)

    @pl.when(jnp.logical_not(wide))
    def _():
        to_rows(read, write, 0, rows, False, tiles)


def add_up(refs):
    return sum(ref[...].astype(f32) for ref in refs)


def unpack_kernel(dims, groups, wide_ref, *refs):
    rows, tiles = dims
    refs, (out_ref, square_ref, rows_ref) = refs[:-3], refs[-3:]
    at = 0
    for count in groups:
        value = add_up(refs[:count])
        refs = refs[count:]
        rows_ref[at : at + value.shape[0]] = value
        at += value.shape[0]
    wide = wide_ref[0] > 0

    def store(is_wide):
        total = jnp.zeros((1, LANES), f32)
        quarter = rows // 4
        for q in range(4):
            for j in range(tiles):
                piece = rows_ref[q * quarter : (q + 1) * quarter, LANES * j : LANES * (j + 1)]
                if is_wide:
                    out_ref[pl.ds(tiles * q + j, quarter, stride=4 * tiles), :] = piece
                else:
                    out_ref[pl.ds(tiles * quarter * q + j, quarter, stride=tiles), :] = piece
                total = total + jnp.sum(piece * piece, axis=0, keepdims=True)
        square_ref[...] = total

    @pl.when(wide)
    def _():
        store(True)

    @pl.when(jnp.logical_not(wide))
    def _():
        store(False)


def stack_rows_kernel(*refs):
    out_ref = refs[-1]
    at = 0
    for ref in refs[:-1]:
        out_ref[at : at + ref.shape[0]] = ref[...]
        at += ref.shape[0]


def adam_shift_kernel(
    dims, clip_ref, k_ref, flat_ref, head_ref, momentum_ref, variance_ref,
    update_ref, momentum_out, variance_out, grad_ref, buf,
):
    step, own = dims
    count = flat_ref.shape[0]
    buf[0:count] = flat_ref[...]
    buf[count : count + head_ref.shape[0]] = head_ref[...]
    grad_ref[...] = buf[pl.ds(step * k_ref[0], own), :]
    adam_kernel(clip_ref, grad_ref, momentum_ref, variance_ref, update_ref, momentum_out, variance_out)


def adam_kernel(clip_ref, grad_ref, momentum_ref, variance_ref, update_ref, momentum_out, variance_out):
    clipped = grad_ref[...] * clip_ref[0]
    momentum_new = beta_first * momentum_ref[...] + (1.0 - beta_first) * clipped
    variance_new = beta_second * variance_ref[...] + (1.0 - beta_second) * clipped * clipped
    first_hat = momentum_new / (1.0 - beta_first**adam_step)
    second_hat = variance_new / (1.0 - beta_second**adam_step)
    update_ref[...] = -first_hat / (jnp.sqrt(second_hat) + adam_eps)
    momentum_out[...] = momentum_new
    variance_out[...] = variance_new


def adam(clip, grad, momentum, variance, block):
    count = grad.shape[0]
    spec = pl.BlockSpec((block, LANES), lambda i: (i, 0))
    shape = jax.ShapeDtypeStruct(grad.shape, f32)
    return pl.pallas_call(
        adam_kernel,
        grid=(pl.cdiv(count, block),),
        in_specs=[SMEM, spec, spec, spec],
        out_specs=[spec] * 3,
        out_shape=[shape] * 3,
        compiler_params=params(),
        cost_estimate=cost(),
        name="adam",
    )(clip, grad, momentum, variance)


def route_kernel(
    experts, capacity, stride, me_ref, prio_row, prio_col, picks, picks_t, cot,
    cols_ref, near_ref, rows_ref, g_ref,
):
    count = picks.shape[0]
    me = me_ref[0]
    before = (prio_row[...] < prio_col[...]).astype(f32).astype(bf16)
    lane = lax.broadcasted_iota(jnp.int32, (count, experts), 1)
    sub = lax.broadcasted_iota(jnp.int32, (experts, count), 0)
    hot = [(picks[:, j : j + 1] == lane).astype(f32) for j in range(2)]
    hot_t = [(picks_t[j : j + 1, :] == sub).astype(f32) for j in range(2)]
    first = jnp.sum(hot[0], axis=0, keepdims=True)
    first_t = jnp.sum(hot_t[0], axis=1, keepdims=True)
    for j in range(2):
        earlier = dot(before, hot[j].astype(bf16)) + (first if j else 0.0)
        earlier_t = dot_nt(hot_t[j].astype(bf16), before) + (first_t if j else 0.0)
        place = jnp.sum(earlier * hot[j], axis=1, keepdims=True).astype(jnp.int32)
        place_t = jnp.sum(earlier_t * hot_t[j], axis=0, keepdims=True).astype(jnp.int32)
        pick, pick_t = picks[:, j : j + 1], picks_t[j : j + 1, :]
        kept = (place < capacity) & (pick >= 0)
        cols_ref[:, j : j + 1] = jnp.where(kept, pick * stride + place, -1)
        near_ref[:, j : j + 1] = jnp.where(kept, (pick ^ me) * stride + place, -1)
        kept = (place_t < capacity) & (pick_t >= 0)
        rows_ref[j : j + 1, :] = jnp.where(kept, pick_t * stride + place_t, -1)
    first, second = slot_selects(rows_ref, experts * stride)
    g_ref[...] = dot(first + second, cot[...]).astype(bf16)


def slot_selects(rows_ref, slots):
    sub = lax.broadcasted_iota(jnp.int32, (slots, rows_ref.shape[1]), 0)
    return [(rows_ref[j : j + 1, :] == sub).astype(f32).astype(bf16) for j in range(2)]


def token_selects(cols_ref, slots):
    lane = lax.broadcasted_iota(jnp.int32, (cols_ref.shape[0], slots), 1)
    return [(cols_ref[:, j : j + 1] == lane).astype(f32).astype(bf16) for j in range(2)]


def split_lanes(column):
    high = column.astype(bf16).astype(f32)
    rest = column - high
    middle = rest.astype(bf16).astype(f32)
    low = rest - middle
    lane = lax.broadcasted_iota(jnp.int32, (column.shape[0], LANES), 1)
    wide = jnp.where(lane == 0, high, jnp.where(lane == 1, middle, jnp.where(lane == 2, low, 0.0)))
    return wide.astype(bf16)


def head_masks():
    lane = lax.broadcasted_iota(jnp.int32, (1, 2 * HEAD_DIM), 1)
    first = (lane < HEAD_DIM).astype(f32)
    return first.astype(bf16), (1.0 - first).astype(bf16)


def soft_scores(queries, key_rows, key_ok):
    scores = dot_nt(queries, key_rows) * HEAD_DIM ** (-0.5)
    scores = jnp.where(key_ok, scores, -1e30)
    top = jnp.max(scores, axis=-1, keepdims=True)
    raised = jnp.exp(scores - top)
    return raised * (1.0 / jnp.sum(raised, axis=-1, keepdims=True))


def put_chunk(scratch, low, chunk, value, first=0):
    place = chunk ^ low
    scratch[place & 1, place >> 1, first : first + value.shape[0], :] = value


def matrix(w_ref, index):
    per = w_ref.shape[0] // 4
    width = w_ref.shape[2]
    rows = width // per
    return w_ref[index * per : (index + 1) * per, 0:rows, :].reshape(width, width)


def quarter_in(w_ref, q):
    width = w_ref.shape[2]
    rows = width // w_ref.shape[0]
    return w_ref[:, q * rows : (q + 1) * rows, :].reshape(width, width)


def start_all(sources, targets, sems):
    copies = [pltpu.make_async_copy(a, b, sems.at[i]) for i, (a, b) in enumerate(zip(sources, targets))]
    for copy in copies:
        copy.start()
    return copies


def wait_all(copies):
    for copy in copies:
        copy.wait()


def layer_copies(spots, arrays, place_ref, layer, target, sems):
    low, top = place_ref[0], place_ref[1]
    found = []
    for j, (array, before, behind) in enumerate(spots):
        source = arrays[array].at[before + (layer ^ top,) + behind + (pl.ds(0, target.shape[1]),)]
        found.append(pltpu.make_async_copy(source, target.at[j ^ low], sems.at[j ^ low]))
    return found


def attn_fwd(seq, stream_ref, gain, w_ref, out_ref, a_ref, q_ref, k_ref, v_ref, o_ref):
    normed, _ = norm_rows(stream_ref[...])
    a_ref[...] = (normed * gain).astype(bf16)
    for index, ref in enumerate((q_ref, k_ref, v_ref)):
        ref[...] = dot(a_ref[...], matrix(w_ref, index)).astype(bf16)
    count = stream_ref.shape[0]
    key_ok = lax.broadcasted_iota(jnp.int32, (count, count), 1) < seq
    masks = head_masks()
    for pair in range(HEADS // 2):
        lanes = slice(2 * HEAD_DIM * pair, 2 * HEAD_DIM * (pair + 1))
        mixed = None
        for mask in masks:
            soft = soft_scores(q_ref[:, lanes] * mask, k_ref[:, lanes], key_ok).astype(bf16)
            part = dot(soft, v_ref[:, lanes] * mask)
            mixed = part if mixed is None else mixed + part
        o_ref[:, lanes] = mixed.astype(bf16)
    out_ref[...] = stream_ref[...] + dot(o_ref[...], matrix(w_ref, 3))


def attn_bwd_kernel(seq, spots, layer, place_ref, gain_ref, *refs):
    ins, arrays, refs = refs[:5], refs[5 : 5 + len(refs) - 24], refs[len(refs) - 19 :]
    out_ref, gain_out, *outs = refs[:5]
    grad_ref, stream_ref, q_ref, k_ref, v_ref = refs[5:10]
    held_out, dq_ref, dk_ref, dv_ref, do_ref, w_ref, w_sems, in_sems, out_sems = refs[10:]
    copies = layer_copies(spots, arrays, place_ref, layer, w_ref, w_sems)
    for copy in copies:
        copy.start()
    arriving = start_all(ins, (grad_ref, stream_ref, q_ref, k_ref, v_ref), in_sems)
    wait_all(copies)
    wait_all(arriving)
    do_ref[...] = dot_nt(grad_ref[...].astype(bf16), matrix(w_ref, 3)).astype(bf16)
    count = grad_ref.shape[0]
    key_ok = lax.broadcasted_iota(jnp.int32, (count, count), 1) < seq
    masks = head_masks()
    scale = HEAD_DIM ** (-0.5)
    for pair in range(HEADS // 2):
        lanes = slice(2 * HEAD_DIM * pair, 2 * HEAD_DIM * (pair + 1))
        dq = dk = dv = None
        for mask in masks:
            q_h = q_ref[:, lanes] * mask
            k_h = k_ref[:, lanes] * mask
            do_h = do_ref[:, lanes] * mask
            soft = soft_scores(q_h, k_ref[:, lanes], key_ok)
            dsoft = dot_nt(do_h, v_ref[:, lanes])
            dv_h = dot_tn(soft.astype(bf16), do_h)
            inner = jnp.sum(dsoft * soft, axis=-1, keepdims=True)
            dscore = (soft * (dsoft - inner)).astype(bf16)
            dq_h = dot(dscore, k_h)
            dk_h = dot_tn(dscore, q_h)
            dq = dq_h if dq is None else dq + dq_h
            dk = dk_h if dk is None else dk + dk_h
            dv = dv_h if dv is None else dv + dv_h
        dq_ref[:, lanes] = (dq * scale).astype(bf16)
        dk_ref[:, lanes] = (dk * scale).astype(bf16)
        dv_ref[:, lanes] = dv.astype(bf16)
    leaving = start_all((dq_ref, dk_ref, dv_ref), outs, out_sems)
    back = None
    for index, ref in enumerate((dq_ref, dk_ref, dv_ref)):
        part = dot_nt(ref[...], matrix(w_ref, index))
        back = part if back is None else back + part
    normed, inverse = norm_rows(stream_ref[...])
    addend, gain_grad = norm_back(back, normed, inverse, gain_ref[...])
    held_out[...] = grad_ref[...] + addend
    last = pltpu.make_async_copy(held_out, out_ref, out_sems.at[3])
    last.start()
    gain_out[...] = gain_grad
    wait_all(leaving)
    last.wait()


def leave_chunk(scratch, low, chunk, keep_ref, send_ref, sem):
    place = chunk ^ low
    source = scratch.at[place & 1, place >> 1]

    @pl.when((place & 1) == 0)
    def _():
        pltpu.make_async_copy(source, keep_ref.at[place >> 1], sem).start()

    @pl.when((place & 1) == 1)
    def _():
        pltpu.make_async_copy(source, send_ref.at[place >> 1], sem).start()


def wait_chunks(scratch, low, keep_ref, sems):
    for chunk in range(2 * scratch.shape[1]):
        place = chunk ^ low
        pltpu.make_async_copy(scratch.at[place & 1, place >> 1], keep_ref.at[place >> 1], sems.at[chunk]).wait()


def attn_weights_kernel(low_ref, *refs):
    ins, keep_ref, send_ref, refs = refs[:6], refs[6], refs[7], refs[8:]
    (grad_ref, a_ref, o_ref, dq_ref, dk_ref, dv_ref), (dw, in_sems, sems) = refs[:6], refs[6:]
    low = low_ref[0]
    rows = dw.shape[2]
    per = grad_ref.shape[1] // rows
    arriving = start_all(ins, refs[:6], in_sems)
    wait_all(arriving)
    branch = grad_ref[...].astype(bf16)
    for index in range(4):
        left = o_ref if index == 3 else a_ref
        right = branch if index == 3 else (dq_ref, dk_ref, dv_ref)[index][...]
        value = dot_tn(left[...], right)
        for i in range(per):
            put_chunk(dw, low, index * per + i, value[i * rows : (i + 1) * rows].astype(bf16))
            leave_chunk(dw, low, index * per + i, keep_ref, send_ref, sems.at[index * per + i])
    wait_chunks(dw, low, keep_ref, sems)


def mlp_fwd(stream_ref, gain, w1_ref, w2_ref, out_ref, b_ref, u_ref):
    width = stream_ref.shape[1]
    normed, _ = norm_rows(stream_ref[...])
    b_ref[...] = (normed * gain).astype(bf16)
    total = None
    for q in range(4):
        pre = dot(b_ref[...], quarter_in(w1_ref, q))
        u_ref[:, q * width : (q + 1) * width] = pre
        part = dot((pre * normal_cdf(pre)).astype(bf16), matrix(w2_ref, q))
        total = part if total is None else total + part
    out_ref[...] = stream_ref[...] + total


def forward_kernel(seq, spots, dims, by_core, place_ref, stream_ref, picks_ref, rows_ref, *refs):
    rows, experts, count = dims
    arrays, refs = refs[:count], refs[count:]
    if not by_core:
        w1_ref, refs = refs[0], refs[1:]
    outs, refs = refs[:15], refs[15:]
    gains_ref, wr_ref, c_ref, probs_ref, x_ref = refs[:5]
    held, (weights, tails, w_sems, tail_sems, out_sems) = refs[5:20], refs[20:]
    low, top = place_ref[0], place_ref[1]
    per = weights.shape[1]
    copies = {
        layer: layer_copies(spots, arrays, place_ref, layer, weights.at[layer], w_sems.at[layer])
        for layer in (0, 2, 3, 1)
    }
    tail_copies = []
    for j, (array, before, behind) in enumerate(spots):
        source = arrays[array].at[before + (3 ^ top,) + behind + (pl.ds(rows, tails.shape[1]),)]
        tail_copies.append(pltpu.make_async_copy(source, tails.at[j ^ low], tail_sems.at[j]))
    for copy in copies[0] + tail_copies:
        copy.start()
    for copy in copies[0] + tail_copies:
        copy.wait()
    for copy in copies[2] + copies[3] + copies[1]:
        copy.start()
    tail = tails[per - 1].astype(f32)
    gains = [tail[experts + i : experts + i + 1] for i in range(4)]
    gains_ref[...] = tail[experts : experts + 4]
    leaving = []

    def leave(first, last):
        for i in range(first, last):
            leaving.append(pltpu.make_async_copy(held[i], outs[i], out_sems.at[i]))
            leaving[-1].start()

    attn_fwd(seq, stream_ref, gains[0], weights.at[0], *held[0:6])
    leave(0, 6)
    for copy in copies[2] + copies[3]:
        copy.wait()
    mlp_fwd(held[0], gains[1], weights.at[2] if by_core else w1_ref, weights.at[3], *held[6:9])
    leave(6, 9)
    for copy in copies[1]:
        copy.wait()
    attn_fwd(seq, held[6], gains[2], weights.at[1], *held[9:15])
    leave(9, 15)
    wr_ref[...] = router_matrix(tail, stream_ref.shape[1], experts)
    dispatch(held[9], gains[3], wr_ref, picks_ref, rows_ref, c_ref, probs_ref, x_ref)
    for copy in leaving:
        copy.wait()


def mlp_bwd_kernel(by_core, spots, count, place_ref, gain_ref, *refs):
    ins, arrays, refs = refs[:4], refs[4 : 4 + count], refs[4 + count :]
    if by_core:
        out_ref, gain_out, keep2_ref, send2_ref, keep1_ref, send1_ref, *refs = refs
        dw2, dw1, w2_ref, w1_ref, *refs = refs
    else:
        w1_ref, out_ref, gain_out, keep2_ref, send2_ref, dw1_ref, *refs = refs
        dw2, w2_ref, *refs = refs
    grad_ref, stream_ref, b_ref, u_ref, held_out, w_sems, in_sems, out_sems, last_sem = refs
    low = place_ref[0]
    arriving = start_all(ins, (grad_ref, stream_ref, b_ref, u_ref), in_sems)
    copies = layer_copies(spots, arrays, place_ref, 3, w2_ref, w_sems.at[0])
    if by_core:
        copies += layer_copies(spots, arrays, place_ref, 2, w1_ref, w_sems.at[1])
    for copy in copies:
        copy.start()
    wait_all(arriving)
    width = grad_ref.shape[1]
    upper = grad_ref[...].astype(bf16)
    back = None
    groups = w1_ref.shape[0]
    for q in range(4):
        pre = u_ref[:, q * width : (q + 1) * width]
        cdf = normal_cdf(pre)
        act = (pre * cdf).astype(bf16)
        rows = dw2.shape[2]
        per = width // rows
        second = dot_tn(act, upper)
        for i in range(per):
            put_chunk(dw2, low, q * per + i, second[i * rows : (i + 1) * rows].astype(bf16))
            leave_chunk(dw2, low, q * per + i, keep2_ref, send2_ref, out_sems.at[0, q * per + i])
        if q == 0:
            wait_all(copies)
        dact = dot_nt(upper, matrix(w2_ref, q))
        dpre = (dact * (cdf + pre * density(pre))).astype(bf16)
        first = dot_tn(b_ref[...], dpre).astype(bf16)
        rows = width // groups
        for i in range(groups):
            piece = first[i * rows : (i + 1) * rows]
            if by_core:
                put_chunk(dw1, low, i, piece, q * rows)
            else:
                dw1_ref[i, q * rows : (q + 1) * rows, :] = piece
        part = dot_nt(dpre, quarter_in(w1_ref, q))
        back = part if back is None else back + part
    if by_core:
        for i in range(groups):
            leave_chunk(dw1, low, i, keep1_ref, send1_ref, out_sems.at[1, i])
    normed, inverse = norm_rows(stream_ref[...])
    addend, gain_grad = norm_back(back, normed, inverse, gain_ref[...])
    held_out[...] = grad_ref[...] + addend
    last = pltpu.make_async_copy(held_out, out_ref, last_sem)
    last.start()
    gain_out[...] = gain_grad
    wait_chunks(dw2, low, keep2_ref, out_sems.at[0])
    if by_core:
        wait_chunks(dw1, low, keep1_ref, out_sems.at[1])
    last.wait()


def pick_hots(picks, experts):
    lane = lax.broadcasted_iota(jnp.int32, (picks.shape[0], experts), 1)
    return [(picks[:, j : j + 1] == lane).astype(f32) for j in range(2)]


def softmax_rows(logits):
    raised = jnp.exp(logits - jnp.max(logits, axis=-1, keepdims=True))
    return raised / jnp.sum(raised, axis=-1, keepdims=True)


def router_matrix(flat, width, experts):
    block = width // experts
    row = lax.broadcasted_iota(jnp.int32, (block, width), 0)
    lane = lax.broadcasted_iota(jnp.int32, (block, width), 1)
    mine = (lane // experts == row).astype(f32)
    lane = lax.broadcasted_iota(jnp.int32, (width, experts), 0)
    column = lax.broadcasted_iota(jnp.int32, (width, experts), 1)
    pick = (lax.rem(lane, experts) == column).astype(f32).astype(bf16)
    parts = [dot((mine * flat[i : i + 1]).astype(bf16), pick) for i in range(experts)]
    return jnp.concatenate(parts).astype(bf16)


def dispatch(stream_ref, gain, wr_ref, picks_ref, rows_ref, c_ref, probs_ref, x_ref):
    width = stream_ref.shape[1]
    experts = wr_ref.shape[1]
    normed, _ = norm_rows(stream_ref[...])
    c_ref[...] = (normed * gain).astype(bf16)
    probs = softmax_rows(dot(c_ref[...], wr_ref[...]))
    probs_ref[...] = probs
    hots = pick_hots(picks_ref, experts)
    selects = slot_selects(rows_ref, x_ref.shape[0])
    gates = None
    for j in range(2):
        part = dot(selects[j], split_lanes(jnp.sum(probs * hots[j], axis=-1, keepdims=True)))
        gates = part if gates is None else gates + part
    x_ref[:, 0:width] = dot(selects[0] + selects[1], c_ref[...]).astype(bf16)
    x_ref[:, width:] = gates.astype(bf16)


def add_lanes(wide):
    wide = wide.astype(f32)
    return wide[:, 0:1] + wide[:, 1:2] + wide[:, 2:3]


def expert_kernel(dims, spans, me_ref, x_ref, g_ref, *refs):
    parts, quarter, blocks = dims
    weight_refs, refs = refs[: len(spans)], refs[len(spans) :]
    y_refs, refs = refs[: blocks // 2], refs[blocks // 2 :]
    dx_ref, dy_ref, act_ref, dpre_ref, weights, y_near, y_sum, dx_sum, sems = refs
    q = pl.program_id(0)
    width = g_ref.shape[1]
    half = parts // 2
    me = me_ref[0]

    @pl.when(q == 0)
    def _():
        copies = [
            pltpu.make_async_copy(ref, weights.at[place ^ me, first : first + ref.shape[0]], sems.at[i])
            for i, ((place, first), ref) in enumerate(zip(spans, weight_refs))
        ]
        for copy in copies:
            copy.start()
        dy_ref[...] = (add_lanes(x_ref[:, width:]) * g_ref[...].astype(f32)).astype(bf16)
        for copy in copies:
            copy.wait()

    first = weights[0:half, pl.ds(pl.multiple_of(q * quarter, 16), quarter), :].reshape(width, width)
    if 4 * quarter >= width:
        per = 4 * quarter // width
        at = pl.ds(pl.multiple_of(lax.rem(q, per) * width, 16), width)
        second = weights[half + q // per, at, :]
    else:
        per = width // (4 * quarter)
        second = weights[pl.ds(half + q * per, per)].reshape(width, width)
    pre = dot(x_ref[:, 0:width], first)
    cdf = normal_cdf(pre)
    act = (pre * cdf).astype(bf16)
    act_ref[...] = act
    dact = dot_nt(dy_ref[...], second)
    dpre = (dact * (cdf + pre * density(pre))).astype(bf16)
    dpre_ref[...] = dpre
    y_part = dot(act, second)
    dx_part = dot_nt(dpre, first)

    @pl.when(q == 0)
    def _():
        y_sum[...] = y_part
        dx_sum[...] = dx_part

    @pl.when(q > 0)
    def _():
        y_sum[...] += y_part
        dx_sum[...] += dx_part

    @pl.when(q == pl.num_programs(0) - 1)
    def _():
        y = y_sum[...].astype(bf16).astype(f32)
        stride = y.shape[0] // blocks
        for block in range(blocks):
            y_near[block ^ me_ref[1]] = y[block * stride : (block + 1) * stride].astype(bf16)
        for pair, ref in enumerate(y_refs):
            ref[...] = y_near[2 * pair : 2 * pair + 2]
        dx_ref[:, 0:width] = dx_sum[...].astype(bf16)
        gate_grad = jnp.sum(g_ref[...].astype(f32) * y, axis=-1, keepdims=True)
        dx_ref[:, width:] = split_lanes(gate_grad)


def expert_grad_kernel(dims, dp_ref, x_ref, dy_ref, act_ref, dpre_ref, *refs):
    parts, quarter = dims
    out_refs, scratch, sems = refs[: 2 * parts], refs[-2], refs[-1]
    q = pl.program_id(0)
    me = dp_ref[0]
    width = dy_ref.shape[1]
    half = parts // 2
    rows = scratch.shape[1]
    first = dot_tn(x_ref[:, 0:width], dpre_ref[...]).astype(bf16)
    count = width // half
    for i in range(half):
        at = pl.ds(pl.multiple_of(q * quarter, 16), quarter)
        scratch[i ^ me, at, :] = first[i * count : (i + 1) * count]
    second = dot_tn(act_ref[...], dy_ref[...]).astype(bf16)
    if rows >= width:
        per = rows // width
        at = pl.ds(pl.multiple_of(lax.rem(q, per) * width, 16), width)
        scratch[(half + q // per) ^ me, at, :] = second
    else:
        per = width // rows
        for i in range(per):
            scratch[(half + q * per + i) ^ me] = second[i * rows : (i + 1) * rows]

    @pl.when(q == pl.num_programs(0) - 1)
    def _():
        copies = []
        for side, bit in ((0, 1), (1, parts // 2)):
            lists = [r for r in range(parts) if r & bit], [r for r in range(parts) if not r & bit]
            for which, group in enumerate(lists):
                for i, r in enumerate(group):
                    copies.append(
                        pltpu.make_async_copy(
                            scratch.at[r, side * rows // 2 : (side + 1) * rows // 2],
                            out_refs[side * parts + which * half + i],
                            sems.at[side * parts + r],
                        )
                    )
        for copy in copies:
            copy.start()
        for copy in copies:
            copy.wait()


def combine_kernel(
    stream_ref, gain_ref, wr_ref, picks_ref, cols_ref, cot_ref, c_ref, probs_ref, dx_ref,
    grad_ref, gain_out, router_out,
):
    width = stream_ref.shape[1]
    experts = wr_ref.shape[1]
    probs = probs_ref[...]
    hots = pick_hots(picks_ref, experts)
    selects = token_selects(cols_ref, dx_ref.shape[0])
    prob_grad = None
    for j in range(2):
        part = add_lanes(dot(selects[j], dx_ref[:, width:])) * hots[j]
        prob_grad = part if prob_grad is None else prob_grad + part
    logit_grad = probs * (prob_grad - jnp.sum(prob_grad * probs, axis=-1, keepdims=True))
    logit_grad = logit_grad.astype(bf16)
    router_out[...] = dot_tn(logit_grad, c_ref[...])
    back = dot(selects[0] + selects[1], dx_ref[:, 0:width]) + dot_nt(logit_grad, wr_ref[...])
    normed, inverse = norm_rows(stream_ref[...])
    addend, gain_grad = norm_back(back, normed, inverse, gain_ref[...])
    grad_ref[...] = cot_ref[...].astype(f32) + addend
    gain_out[...] = gain_grad


def output_kernel(stream_ref, picks_ref, near_ref, probs_ref, *refs):
    y_refs, (other_ref, out_ref, wide) = refs[:-3], refs[-3:]
    stride = other_ref.shape[1]
    for pair, ref in enumerate(y_refs):
        wide[2 * pair * stride : (2 * pair + 1) * stride] = ref[0].astype(f32)
        wide[(2 * pair + 1) * stride : (2 * pair + 2) * stride] = other_ref[pair].astype(f32)
    y = wide[...].astype(bf16)
    seq = out_ref.shape[0]
    probs = probs_ref[...]
    hots = pick_hots(picks_ref, probs.shape[1])
    selects = token_selects(near_ref, y.shape[0])
    total = stream_ref[...]
    for j in range(2):
        gate = jnp.sum(probs * hots[j], axis=-1, keepdims=True)
        total = total + gate * dot(selects[j], y)
    out_ref[...] = total[0:seq]


def add_pair(left, right):
    return (left.astype(f32) + right.astype(f32)).astype(bf16)


def pack_sets_kernel(*refs):
    out_ref = refs[-1]
    for i, ref in enumerate(refs[:-1]):
        out_ref[i // 4, i % 4] = ref[...]


def fold_layers_kernel(cut, top_ref, *refs):
    layers, refs = [refs[2 * i : 2 * i + 2] for i in range(4)], refs[8:]
    uppers, (send_x, keep_x, send_y, keep_y, scratch) = refs[:4], refs[4:]
    middle = send_x.shape[2]
    place = pl.program_id(0)
    for layer, (keep, got) in enumerate(layers):
        value = add_pair(keep[0], got[0])
        for j, upper in enumerate(uppers):

            @pl.when(lax.rem(place, 4) == j)
            def _():
                upper[layer, place // 4] = value[:cut]

        scratch[layer ^ top_ref[0]] = value[cut:]
    for i in range(2):
        keep_x[i, 0] = scratch[2 * i, 0:middle]
        send_x[i, 0] = scratch[2 * i + 1, 0:middle]
        keep_y[i, 0] = scratch[i, middle:]
        send_y[i, 0] = scratch[i + 2, middle:]


def fold_plane_kernel(keep_x, got_x, keep_y, got_y, own_a, send_y, own_b, send_x):
    for keep, got, own, send in ((keep_x, got_x, own_a, send_y), (keep_y, got_y, own_b, send_x)):
        own[...] = add_pair(keep[0], got[0])
        send[...] = add_pair(keep[1], got[1])


def fold_rows_kernel(own_a, got_a, own_b, got_b, *outs):
    middle = own_a.shape[1]
    for place in range(own_a.shape[0]):
        out = outs[place % 4].at[place // 4]
        out[0:middle] = add_pair(own_a[place], got_a[place])
        out[middle:] = add_pair(own_b[place], got_b[place])


def fold_uppers_kernel(top_ref, *refs):
    refs, outs, scratch = refs[:-5], refs[-5:-1], refs[-1]
    for layer in range(4):
        scratch[layer ^ top_ref[0]] = sum(ref[layer].astype(f32) for ref in refs).astype(bf16)
    for place, out in enumerate(outs):
        out[...] = scratch[place]


def fold_expert_kernel(highs, *refs):
    count = len(refs) // 6
    ins, outs = refs[: 4 * count], refs[4 * count :]
    for side, high in enumerate(highs):
        half = count // 2
        for i in range(count):
            which, at = (i // half, i % half) if high else (i % 2, i // 2)
            keep, got = ins[2 * side * count + i], ins[(2 * side + 1) * count + i]
            outs[side * count + which * half + at][...] = add_pair(keep[...], got[...])


def swap(value, axes, mask):
    size = 1
    for axis in axes:
        size *= lax.axis_size(axis)
    return lax.ppermute(value, axes, [(i, i ^ mask) for i in range(size)])


def after(value, *others):
    return lax.optimization_barrier((value, others))[0]


class Order:
    def __init__(self):
        self.latest = ()

    def land(self, value):
        self.latest = after(value, self.latest)
        return self.latest


def bit_groups(bits):
    return [bits[i : i + 2] for i in range(0, len(bits), 2)]


def all_sum_step(value, axes, bits):
    if len(bits) == 1:
        return value + swap(value, axes, 1 << bits[0])
    low, high = 1 << bits[0], 1 << bits[1]
    near, far, both = swap(value, axes, low), swap(value, axes, high), swap(value, axes, low | high)
    return (value + near) + (far + both)


def reduce_bits(value, axes, bits):
    for bit in bits:
        pairs = value.reshape((value.shape[0] // 2, 2) + value.shape[1:])
        value = pairs[:, 0] + swap(pairs[:, 1], axes, 1 << bit)
    return value[0]


def shape(dims, dtype=f32):
    return jax.ShapeDtypeStruct(dims, dtype)


def on_device(
    tokens,
    cotangent,
    expert_picks,
    priority,
    dense_master,
    dense_momentum,
    dense_variance,
    expert_master,
    expert_momentum,
    expert_variance,
):
    both = ("dp", "expert")
    dp_ranks = lax.axis_size("dp")
    expert_ranks = lax.axis_size("expert")
    devices = dp_ranks * expert_ranks
    local_experts = expert_master.shape[0]
    experts = local_experts * expert_ranks
    images, seq, width = tokens.shape
    assert local_experts == 1 and images == 1
    assert devices & (devices - 1) == 0 and dp_ranks >= 4
    tiles = width // LANES
    dp_me = lax.axis_index("dp").astype(jnp.int32)
    me = dp_me * expert_ranks + lax.axis_index("expert").astype(jnp.int32)
    me_arr = me.reshape(1)
    dp_arr = dp_me.reshape(1)
    dp_bits = dp_ranks.bit_length() - 1
    all_bits = devices.bit_length() - 1

    own = dense_master.shape[0] // LANES
    expert_flat = expert_master.shape[1] // LANES
    hidden = expert_master.shape[1] * dp_ranks // (2 * width)
    matrix_rows = 8 * width + 2 * hidden
    rows = matrix_rows // devices
    step = own - rows * tiles
    tail = step * devices
    tail_rows = -(-tail // (16 * tiles)) * 16
    wide_ok = rows % 64 == 0
    expert_rows = expert_flat // tiles

    dense_flat = dense_master.reshape(own, LANES)
    forward_ring = [(i, (i + 1) % devices) for i in range(devices)]
    backward_ring = [((i + 1) % devices, i) for i in range(devices)]
    tail_from = lax.ppermute(dense_flat[own - tail :], both, forward_ring)
    buf_rows = -(-(own + max(tail, tail_rows * tiles)) // 8) * 8
    chunk = pl.pallas_call(
        functools.partial(
            pack_dense_kernel, (rows, tail_rows, tail, own, step, tiles, devices, wide_ok)
        ),
        in_specs=[SMEM, VMEM, VMEM],
        out_specs=VMEM,
        out_shape=shape((rows + tail_rows, width), bf16),
        scratch_shapes=[pltpu.VMEM((buf_rows, LANES), f32)],
        compiler_params=params(),
        cost_estimate=cost(0, 6 * dense_master.size),
        name="pack_dense",
    )(me_arr, tail_from, dense_flat)

    expert_wide = (dp_me < dp_ranks // 2).astype(jnp.int32).reshape(1)
    expert_chunk = pl.pallas_call(
        functools.partial(pack_expert_kernel, (expert_rows, tiles)),
        in_specs=[SMEM, VMEM],
        out_specs=VMEM,
        out_shape=shape((expert_rows, width), bf16),
        compiler_params=params(),
        cost_estimate=cost(0, 6 * expert_master.size),
        name="pack_expert",
    )(expert_wide, expert_master.reshape(expert_flat, LANES))
    dp_axis = ("dp",)
    dp_order = list(range(dp_bits))

    def gather_step(parts, bit):
        return {**parts, **{at | (1 << bit): swap(part, dp_axis, 1 << bit) for at, part in parts.items()}}

    capacity = 2 * seq // experts
    stride = -(-capacity // 8) * 8
    slots = experts * stride
    padded = -(-seq // 16) * 16
    fill = padded - seq
    ranks = jnp.pad(priority, ((0, 0), (0, fill)), constant_values=1 << 20)
    picks = jnp.pad(expert_picks, ((0, fill), (0, 0)), constant_values=-1)
    cot = jnp.pad(cotangent.reshape(seq, width), ((0, fill), (0, 0)))
    stream = jnp.pad(tokens.reshape(seq, width).astype(f32), ((0, fill), (0, 0)))
    e_me = lax.axis_index("expert").astype(jnp.int32).reshape(1)
    pair_shape = shape((2, stride, width), bf16)
    cols, near_cols, rows_slots, outgoing_cot = pl.pallas_call(
        functools.partial(route_kernel, experts, capacity, stride),
        in_specs=[SMEM] + [VMEM] * 5,
        out_specs=[VMEM] * 4,
        out_shape=[shape((padded, 2), jnp.int32)] * 2
        + [shape((2, padded), jnp.int32), shape((slots, width), bf16)],
        compiler_params=params(),
        cost_estimate=cost(),
        name="route",
    )(e_me, ranks, ranks.reshape(padded, 1), picks, picks.T, cot)

    def exchange(value):
        dims = value.shape
        value = value.reshape(expert_ranks, slots // expert_ranks, dims[1])
        value = lax.all_to_all(value, "expert", split_axis=0, concat_axis=0, tiled=True)
        return value.reshape(dims)

    per = devices // 4
    per_bits = per.bit_length() - 1
    top_bits = (per_bits, per_bits + 1)
    chunk_rows = rows + tail_rows
    half_rows = expert_rows // 2
    orders = (dp_order, dp_order[::-1])
    expert_parts, expert_spans = [], []
    if per_bits == 3 and dp_bits == 2:
        masks = [1 << bit for bit in top_bits]
        order = Order()

        def spread(value):
            return [swap(value, both, mask) for mask in masks]

        sets = [chunk, swap(chunk, both, 2), swap(chunk, both, 4), None]
        near, far = [spread(chunk)] + [None] * 3, [None] * 4
        sets[1] = order.land(sets[1])
        near[1] = spread(sets[1])
        near[0] = order.land((near[0], expert_chunk, outgoing_cot, stream))[0]
        far[0] = swap(near[0][1], both, masks[0])
        near[1] = order.land(near[1])
        far[1] = swap(near[1][0], both, masks[1])
        sets[2] = order.land(sets[2])
        sets[3] = swap(sets[2], both, 2)
        near[2] = spread(sets[2])
        far[0], far[1] = order.land((far[0], far[1]))
        sets[3] = order.land(sets[3])
        near[3] = spread(sets[3])
        arriving_cot = exchange(after(outgoing_cot, sets[3]))
        near[2] = order.land(near[2])
        far[2] = swap(near[2][1], both, masks[0])
        near[3] = order.land(near[3])
        far[3] = swap(near[3][0], both, masks[1])

        def pack_sets(which):
            ins = [part for s in which for part in (sets[s], *near[s], far[s])]
            return pl.pallas_call(
                pack_sets_kernel,
                in_specs=[VMEM] * len(ins),
                out_specs=VMEM,
                out_shape=shape((len(which), 4, chunk_rows, width), bf16),
                compiler_params=params(),
                cost_estimate=cost(),
                name="pack_sets",
            )(*ins)

        packed = [pack_sets([0, 1])]
        far[2:], packed, arriving_cot = lax.optimization_barrier((far[2:], packed, arriving_cot))
        far[2], far[3] = order.land((far[2], far[3]))
        packed.append(pack_sets([2, 3]))
        arrays = packed + [swap(value, both, 1) for value in packed]
        spots = [((j >> 2) + 2 * (j & 1), ((j >> 1) & 1,), ()) for j in range(per)]
        own_shard = after(expert_chunk, near[3])
        beside = [swap(own_shard, dp_axis, mask) for mask in (1, 2)]
        across = [swap(beside[0][:half_rows], dp_axis, 2), swap(beside[1][half_rows:], dp_axis, 1)]
        expert_parts = [expert_chunk, *beside, *across]
        expert_spans = [(0, 0), (1, 0), (2, 0), (3, 0), (3, half_rows)]
    else:
        gathered = chunk[None]
        for bit in range(all_bits):
            gathered = jnp.concatenate([gathered, swap(gathered, both, 1 << bit)])
        arrays = [gathered.reshape(4, per, chunk_rows, width)]
        spots = [(0, (), (j,)) for j in range(per)]
        for side, bits in enumerate(orders):
            parts, places = [expert_chunk[side * half_rows : (side + 1) * half_rows]], [0]
            for bit in bits:
                parts = parts + [swap(part, dp_axis, 1 << bit) for part in parts]
                places = places + [place | (1 << bit) for place in places]
            expert_parts += parts
            expert_spans += [(place, side * half_rows) for place in places]
        arriving_cot = exchange(outgoing_cot)

    low = me & (per - 1)
    low_arr = low.reshape(1)
    place_arr = jnp.stack([low, me >> per_bits])
    layer_w = pltpu.VMEM((per, rows, width), bf16)
    if not wide_ok:
        first_in = lax.dynamic_index_in_dim(arrays[0], 2 ^ (me >> per_bits), 0, keepdims=False)
        first_in = jnp.take(first_in, jnp.arange(per) ^ low, axis=0)[:, :rows].reshape(width, 4, width)
        first_in = first_in.transpose(1, 0, 2).reshape(1, 4 * width, width)

    act_shape = shape((padded, width), bf16)
    stream_shape = shape((padded, width), f32)
    gain_shape = shape((1, width), f32)
    tok_flops = 2 * padded * width * width
    weight_bytes = 2 * width * width
    ANY = pl.BlockSpec(memory_space=pl.ANY)

    def call(kernel, ins, in_specs, outs, name, flops, nbytes, out_specs=None, scratch=()):
        out_specs = out_specs or [None] * len(outs)

        def whole(a):
            return pl.BlockSpec(a.shape, lambda *_, n=len(a.shape): (0,) * n)

        return pl.pallas_call(
            kernel,
            grid=(1,),
            in_specs=[s or whole(a) for a, s in zip(ins, in_specs, strict=True)],
            out_specs=[s or whole(a) for a, s in zip(outs, out_specs, strict=True)],
            out_shape=outs,
            scratch_shapes=list(scratch),
            compiler_params=params(),
            cost_estimate=cost(flops, nbytes),
            name=name,
        )(*ins)

    places = per // 2
    core_shape = shape((places, rows, width), bf16)
    by_core = pltpu.VMEM((2, places, rows, width), bf16)
    stream_vmem, act_vmem = pltpu.VMEM((padded, width), f32), pltpu.VMEM((padded, width), bf16)

    def attn_bwd(grad, value, kept, layer, which):
        return call(
            functools.partial(attn_bwd_kernel, seq, spots, layer),
            (place_arr, gain[which], grad, value, *kept[1:4], *arrays),
            (SMEM, None) + (ANY,) * (5 + len(arrays)),
            [stream_shape, gain_shape] + [act_shape] * 3,
            "attn_bwd",
            0,
            0,
            out_specs=[ANY, None, ANY, ANY, ANY],
            scratch=[
                stream_vmem,
                stream_vmem,
                *[act_vmem] * 3,
                stream_vmem,
                *[act_vmem] * 4,
                layer_w,
                pltpu.SemaphoreType.DMA((per,)),
                pltpu.SemaphoreType.DMA((5,)),
                pltpu.SemaphoreType.DMA((4,)),
            ],
        )

    def attn_weights(grad, kept, found):
        return call(
            attn_weights_kernel,
            (low_arr, grad, kept[0], kept[4], *found),
            (SMEM,) + (ANY,) * 6,
            [core_shape, core_shape],
            "attn_weights",
            0,
            0,
            out_specs=[ANY] * 2,
            scratch=[
                stream_vmem,
                *[act_vmem] * 5,
                by_core,
                pltpu.SemaphoreType.DMA((6,)),
                pltpu.SemaphoreType.DMA((per,)),
            ],
        )

    outs = [stream_shape] + [act_shape] * 5 + [stream_shape, act_shape, shape((padded, hidden), f32)]
    outs += [stream_shape] + [act_shape] * 5
    *results, gains, router, moe_in, probs, outgoing = call(
        functools.partial(forward_kernel, seq, spots, (rows, experts, len(arrays)), wide_ok),
        (place_arr, stream, picks, rows_slots, *arrays, *([] if wide_ok else [first_in])),
        (SMEM, None, None, None) + (ANY,) * len(arrays) + (() if wide_ok else (None,)),
        outs
        + [
            shape((4, width)),
            shape((width, experts), bf16),
            act_shape,
            shape((padded, experts)),
            shape((slots, width + LANES), bf16),
        ],
        "forward",
        0,
        0,
        out_specs=[ANY] * 15 + [None] * 5,
        scratch=[pltpu.VMEM(o.shape, o.dtype) for o in outs]
        + [
            pltpu.VMEM((4, per, rows, width), bf16),
            pltpu.VMEM((per, tail_rows, width), bf16),
            pltpu.SemaphoreType.DMA((4, per)),
            pltpu.SemaphoreType.DMA((per,)),
            pltpu.SemaphoreType.DMA((15,)),
        ],
    )
    stream_one, kept_one = results[0], results[1:6]
    stream_two, mlp_in, mlp_pre = results[6:9]
    stream_three, kept_two = results[9], results[10:]
    gain = [gains[i : i + 1] for i in range(4)]
    arriving = exchange(outgoing)

    quarter = expert_rows // 4
    slot_spec = pl.BlockSpec((slots, width), lambda q: (0, 0))
    wide_spec = pl.BlockSpec((slots, width + LANES), lambda q: (0, 0))
    pair_spec = pl.BlockSpec((2, stride, width), lambda q: (0, 0, 0))
    hidden_spec = pl.BlockSpec((slots, width), lambda q: (0, q))
    pairs = experts // 2
    *expert_out, input_back, slot_grad, expert_act, pre_grad = pl.pallas_call(
        functools.partial(expert_kernel, (dp_ranks, quarter, experts), expert_spans),
        grid=(4,),
        in_specs=[SMEM, wide_spec, slot_spec] + [ANY] * len(expert_parts),
        out_specs=[pair_spec] * pairs + [wide_spec, slot_spec, hidden_spec, hidden_spec],
        out_shape=[pair_shape] * pairs
        + [shape((slots, width + LANES), bf16), shape((slots, width), bf16)]
        + [shape((slots, hidden), bf16)] * 2,
        scratch_shapes=[
            pltpu.VMEM((dp_ranks, expert_rows, width), bf16),
            pltpu.VMEM((experts, stride, width), bf16),
            pltpu.VMEM((slots, width), f32),
            pltpu.VMEM((slots, width), f32),
            pltpu.SemaphoreType.DMA((len(expert_parts),)),
        ],
        compiler_params=params(),
        cost_estimate=cost(),
        name="expert",
    )(jnp.concatenate([dp_arr, e_me]), arriving, arriving_cot, *expert_parts)
    returned_grad = exchange(input_back)
    part_shape = shape((expert_rows // 2, width), bf16)
    expert_first = pl.pallas_call(
        functools.partial(expert_grad_kernel, (dp_ranks, quarter)),
        grid=(4,),
        in_specs=[SMEM, wide_spec, slot_spec, hidden_spec, hidden_spec],
        out_specs=[ANY] * (2 * dp_ranks),
        out_shape=[part_shape] * (2 * dp_ranks),
        scratch_shapes=[
            pltpu.VMEM((dp_ranks, expert_rows, width), bf16),
            pltpu.SemaphoreType.DMA((2 * dp_ranks,)),
        ],
        compiler_params=params(),
        cost_estimate=cost(),
        name="expert_grad",
    )(dp_arr, arriving, slot_grad, expert_act, pre_grad)
    count = dp_ranks // 2
    expert_first = [expert_first[i * count : (i + 1) * count] for i in range(4)]
    returned_grad = after(returned_grad, expert_first)

    cut = max(16, rows // 96 * 16)
    middle = (rows - cut) // 2
    top = (me >> per_bits).reshape(1)
    z_bits = list(range(1, per_bits))
    z_masks = [2 * j for j in (1, 2, 3)]
    assert places % 4 == 0

    def over_z(values):
        return [values[0]] + [swap(value, both, mask) for value, mask in zip(values[1:], z_masks)]

    def rest_of_z(values):
        if len(z_bits) == 2:
            return values
        total = sum(value.astype(f32) for value in values).astype(bf16)
        lead = total.ndim - 3
        total = jnp.moveaxis(total, lead, 0)
        return [reduce_bits(total, both, z_bits[2:])]

    grad, gain_four, router_grad = call(
        combine_kernel,
        (stream_three, gain[3], router, picks, cols, cot, moe_in, probs, returned_grad),
        (None,) * 9,
        [stream_shape, gain_shape, shape((experts, width))],
        "combine",
        0,
        0,
    )
    def to_other_core(parts):
        return [parts[0], swap(parts[1], both, 1)]

    expert_got = [
        [swap(value[i], dp_axis, mask) for i in range(dp_ranks // 2)]
        for value, mask in ((expert_first[0], 1), (expert_first[2], dp_ranks // 2))
    ]
    upper = grad
    grad, gain_three, *found = attn_bwd(upper, stream_two, kept_two, 1, 2)
    second_dw = to_other_core(attn_weights(upper, kept_two, found))

    mlp_out = [core_shape, core_shape]
    mlp_out = mlp_out * 2 if wide_ok else mlp_out + [shape((1, 4 * width, width), bf16)]
    grad, gain_two, *mlp_dw = call(
        functools.partial(mlp_bwd_kernel, wide_ok, spots, len(arrays)),
        (place_arr, gain[1], grad, stream_one, mlp_in, mlp_pre, *arrays, *([] if wide_ok else [first_in])),
        (SMEM, None) + (ANY,) * (4 + len(arrays)) + (() if wide_ok else (None,)),
        [stream_shape, gain_shape] + mlp_out,
        "mlp_bwd",
        0,
        0,
        out_specs=[ANY, None] + ([ANY] * 4 if wide_ok else [ANY] * 2 + [None]),
        scratch=[by_core] * (2 if wide_ok else 1)
        + [layer_w] * (2 if wide_ok else 1)
        + [stream_vmem, stream_vmem, act_vmem, pltpu.VMEM((padded, hidden), f32), stream_vmem]
        + [
            pltpu.SemaphoreType.DMA((2, per)),
            pltpu.SemaphoreType.DMA((4,)),
            pltpu.SemaphoreType.DMA((2, per)),
            pltpu.SemaphoreType.DMA,
        ],
    )
    if not wide_ok:
        wide_grad = mlp_dw[2].reshape(4, width, width).transpose(1, 0, 2).reshape(per, rows, width)
        wide_grad = jnp.take(wide_grad, jnp.arange(per) ^ low, axis=0)
        wide_grad = wide_grad.reshape(places, 2, rows, width)
        mlp_dw = mlp_dw[:2] + [wide_grad[:, 0], wide_grad[:, 1]]
    mlp_dw = [to_other_core(mlp_dw[i : i + 2]) for i in (0, 2)]

    upper = grad
    grad, gain_one, *found = attn_bwd(upper, stream, kept_one, 0, 0)
    small = call(
        stack_rows_kernel,
        (router_grad, gain_one, gain_two, gain_three, gain_four),
        (None,) * 5,
        [shape((experts + 4, width))],
        "stack_rows",
        0,
        0,
    )[0]
    found, expert_got, small = lax.optimization_barrier((found, expert_got, small))
    first_dw = to_other_core(attn_weights(upper, kept_one, found))

    small = lax.all_gather(small, both, axis=0, tiled=False)

    plane_shape = shape((2, places, middle, width), bf16)
    plane_spec = pl.BlockSpec((2, 1, middle, width), lambda i: (0, i, 0, 0))
    line_shape = shape((places, middle, width), bf16)
    line_spec = pl.BlockSpec((1, middle, width), lambda i: (i, 0, 0))
    upper_shape = shape((4, places // 4, cut, width), bf16)
    part_spec = pl.BlockSpec((1, rows, width), lambda i: (i, 0, 0))
    layers = (first_dw, second_dw, mlp_dw[1], mlp_dw[0])
    *uppers, send_x, keep_x, send_y, keep_y = pl.pallas_call(
        functools.partial(fold_layers_kernel, cut),
        grid=(places,),
        in_specs=[SMEM] + [part_spec] * 8,
        out_specs=[pl.BlockSpec(upper_shape.shape, lambda i: (0, 0, 0, 0))] * 4 + [plane_spec] * 4,
        out_shape=[upper_shape] * 4 + [plane_shape] * 4,
        scratch_shapes=[pltpu.VMEM((4, rows - cut, width), bf16)],
        compiler_params=params(),
        cost_estimate=cost(),
        name="fold_layers",
    )(top, *[part for layer in layers for part in layer])
    masks = [1 << bit for bit in top_bits]
    got_x, got_y = swap(send_x, both, masks[0]), swap(send_y, both, masks[1])
    uppers = over_z(uppers)
    expert_ins = [part for i in (0, 1) for group in (expert_first[2 * i + 1], expert_got[i]) for part in group]
    expert_second = call(
        functools.partial(fold_expert_kernel, (dp_bits == 1, True)),
        expert_ins,
        (None,) * len(expert_ins),
        [part_shape] * (2 * count),
        "fold_expert",
        0,
        0,
    )

    uppers = [value.reshape(4, -1, cut, width) for value in uppers]
    uppers = [value.reshape(4, cut, width) for value in rest_of_z(uppers)]
    uppers, expert_second = lax.optimization_barrier((uppers, expert_second))
    upper_rows = call(
        fold_uppers_kernel,
        (top, *uppers),
        (SMEM,) + (None,) * len(uppers),
        [shape((cut, width), bf16)] * 4,
        "fold_uppers",
        0,
        0,
        scratch=[pltpu.VMEM((4, cut, width), bf16)],
    )
    got_x, got_y, upper_rows = lax.optimization_barrier((got_x, got_y, upper_rows))

    expert_out = after(expert_out, upper_rows)
    expert_out = [expert_out[0]] + [swap(v, ("expert",), 2 * j) for j, v in enumerate(expert_out) if j]
    own_a, send_y, own_b, send_x = pl.pallas_call(
        fold_plane_kernel,
        grid=(places,),
        in_specs=[plane_spec] * 4,
        out_specs=[line_spec] * 4,
        out_shape=[line_shape] * 4,
        compiler_params=params(),
        cost_estimate=cost(),
        name="fold_plane",
    )(keep_x, got_x, keep_y, got_y)
    got_y, got_x = swap(send_y, both, masks[1]), swap(send_x, both, masks[0])
    got_x, got_y, expert_out = lax.optimization_barrier((got_x, got_y, expert_out))
    other_out = swap(jnp.stack([value[1] for value in expert_out]), ("expert",), 1)
    lower_rows = call(
        fold_rows_kernel,
        (own_a, got_y, own_b, got_x),
        (None,) * 4,
        [shape((places // 4, rows - cut, width), bf16)] * 4,
        "fold_rows",
        0,
        0,
    )
    lower_rows, other_out, expert_second = lax.optimization_barrier((lower_rows, other_out, expert_second))
    lower_rows = over_z(lower_rows)
    half = count // 2
    expert_groups = []
    for side, bits in enumerate(orders):
        keep, send = (expert_second[(2 * side + i) * half : (2 * side + i + 1) * half] for i in range(2))
        got = [swap(part, dp_axis, 1 << bits[1]) for part in send]
        expert_groups.append([list(pair) for pair in zip(keep, got)])
    if dp_bits > 2:
        for side, bits in enumerate(orders):
            value = [sum(pair) for pair in expert_groups[side]]
            for bit in bits[2:]:
                half = len(value) // 2
                keep, send = (value[:half], value[half:]) if side else (value[0::2], value[1::2])
                value = [k + swap(v, dp_axis, 1 << bit) for k, v in zip(keep, send)]
            expert_groups[side] = [value]
    expert_groups = [side[0] for side in expert_groups]
    upper_rows, expert_groups = lax.optimization_barrier((upper_rows, expert_groups))

    output = call(
        output_kernel,
        (stream_three, picks, near_cols, probs, *expert_out, other_out),
        (None,) * (5 + pairs),
        [shape((seq, width))],
        "output",
        0,
        0,
        scratch=[pltpu.VMEM((slots, width), f32)],
    )[0]

    def unpack(wide, groups, count, name):
        pieces = [piece for group in groups for piece in group]
        return pl.pallas_call(
            functools.partial(unpack_kernel, (count, tiles), [len(group) for group in groups]),
            in_specs=[SMEM] + [VMEM] * len(pieces),
            out_specs=[VMEM, VMEM],
            out_shape=[shape((count * tiles, LANES)), shape((1, LANES))],
            scratch_shapes=[pltpu.VMEM((count, width), f32)],
            compiler_params=params(),
            cost_estimate=cost(0, 6 * count * width),
            name=name,
        )(wide, *pieces)

    expert_grad, expert_square = unpack(expert_wide, expert_groups, expert_rows, "unpack_expert")
    lower_rows, output, expert_grad, expert_square = lax.optimization_barrier(
        (lower_rows, output, expert_grad, expert_square)
    )
    lower_rows = rest_of_z(lower_rows)
    upper_rows = [upper_rows[0]] + [
        swap(value, both, masks[0] * j) for j, value in enumerate(upper_rows) if j
    ]
    dense_groups = [upper_rows, [value.reshape(rows - cut, width) for value in lower_rows]]

    dense_wide = (me >= devices // 2) & (me < 3 * devices // 4) & wide_ok
    dense_rows, dense_square = unpack(dense_wide.astype(jnp.int32).reshape(1), dense_groups, rows, "unpack_dense")
    small = jnp.sum(after(small, dense_square), axis=0)
    gain_grads = small[experts:]
    small_square = jnp.sum(small * small)
    small = jnp.concatenate([small[:experts].T.reshape(-1, LANES), gain_grads.reshape(-1, LANES)])
    small = jnp.pad(small, ((0, tail - small.shape[0]), (0, 0)))

    head = lax.ppermute(dense_rows[:tail], both, backward_ring)
    head = jnp.where(me == devices - 1, small, head)
    square = dense_square + expert_square
    for bits in bit_groups(list(range(all_bits))):
        square = all_sum_step(square, both, bits)
    square_sum = jnp.sum(square) + small_square
    param_count = (dense_master.size + expert_master.size) * devices
    clip_factor = jnp.minimum(1.0, jnp.sqrt(param_count / (square_sum + 1e-06))).reshape(1)

    dense_update, momentum_dense, variance_dense, dense_grad = pl.pallas_call(
        functools.partial(adam_shift_kernel, (step, own)),
        in_specs=[SMEM, SMEM] + [VMEM] * 4,
        out_specs=[VMEM] * 4,
        out_shape=[shape((own, LANES))] * 4,
        scratch_shapes=[pltpu.VMEM((-(-(rows * tiles + tail) // 8) * 8, LANES), f32)],
        compiler_params=params(),
        cost_estimate=cost(),
        name="adam_dense",
    )(
        clip_factor,
        me_arr,
        dense_rows,
        head,
        dense_momentum.reshape(own, LANES),
        dense_variance.reshape(own, LANES),
    )
    expert_update, momentum_expert, variance_expert = adam(
        clip_factor,
        expert_grad,
        expert_momentum.reshape(expert_flat, LANES),
        expert_variance.reshape(expert_flat, LANES),
        expert_flat // 8,
    )
    image = (1, seq, width)
    return (
        output.reshape(image),
        grad[:seq].reshape(image),
        dense_grad.reshape(dense_master.shape),
        expert_grad.reshape(expert_master.shape),
        dense_update.reshape(dense_master.shape),
        momentum_dense.reshape(dense_master.shape),
        variance_dense.reshape(dense_master.shape),
        expert_update.reshape(expert_master.shape),
        momentum_expert.reshape(expert_master.shape),
        variance_expert.reshape(expert_master.shape),
        gain_grads,
    )


def solution(mesh):
    tokens = P(("dp", "expert"), None, None)
    flat = P(("dp", "expert"))
    pairs = P(("dp", "expert"), None)
    expert = P("expert", "dp")
    return jax.shard_map(
        on_device,
        mesh=mesh,
        in_specs=(tokens, tokens, pairs, pairs, flat, flat, flat, expert, expert, expert),
        out_specs=(tokens, tokens, flat, expert, flat, flat, flat, expert, expert, expert, P()),
        check_vma=False,
    )
```

```python
import functools
import math

import jax
import jax.numpy as jnp
from jax import lax
from jax.experimental import pallas as pl
from jax.experimental.pallas import tpu as pltpu
from jax.sharding import PartitionSpec as P

HEADS = 12
HEAD_DIM = 64
LANES = 128

f32 = jnp.float32
bf16 = jnp.bfloat16

eps_norm = 1e-06
beta_first = 0.9
beta_second = 0.999
adam_eps = 1e-08
adam_step = 10.0

VMEM = pl.BlockSpec(memory_space=pltpu.VMEM)
SMEM = pl.BlockSpec(memory_space=pltpu.SMEM)


def params(mib=56):
    return pltpu.CompilerParams(vmem_limit_bytes=mib << 20)


def cost(rows=0):
    return pl.CostEstimate(flops=1 + int(rows * 16.45e6), bytes_accessed=1, transcendentals=0)


def dot(a, b):
    return lax.dot_general(a, b, (((1,), (0,)), ((), ())), preferred_element_type=f32)


def dot_nt(a, b):
    return lax.dot_general(a, b, (((1,), (1,)), ((), ())), preferred_element_type=f32)


def dot_tn(a, b):
    return lax.dot_general(a, b, (((0,), (0,)), ((), ())), preferred_element_type=f32)


def norm_rows(hidden):
    center = hidden - jnp.mean(hidden, axis=-1, keepdims=True)
    inverse = lax.rsqrt(jnp.mean(center * center, axis=-1, keepdims=True) + eps_norm)
    return center * inverse, inverse


def norm_back(upstream, normed, inverse, gain):
    scaled = upstream * gain
    gain_grad = jnp.sum(upstream * normed, axis=0, keepdims=True)
    centered = (
        scaled
        - jnp.mean(scaled, axis=-1, keepdims=True)
        - normed * jnp.mean(scaled * normed, axis=-1, keepdims=True)
    )
    return inverse * centered, gain_grad


def normal_cdf(v):
    return 0.5 * (1.0 + lax.erf(v * 0.7071067811865476))


def density(v):
    return jnp.exp(-0.5 * v * v) * 0.3989422804014327


def to_rows(read, write, first_q, rows, wide, tiles):
    blocks = 4 if rows % 64 == 0 else 1
    count = rows // blocks
    for b in range(blocks):
        for j in range(tiles):
            if wide:
                write(b * count, count, j, read(first_q + tiles * b + j, count, 4 * tiles))
            else:
                write(b * count, count, j, read(first_q + tiles * count * b + j, count, tiles))


def pack_dense_kernel(dims, k_ref, tail_ref, own_ref, out_ref, buf):
    rows, tail_rows, tail, own, step, tiles, chunks, wide_ok = dims
    buf[0:tail] = tail_ref[...]
    buf[tail : tail + own] = own_ref[...]
    buf[tail + own :] = jnp.zeros((buf.shape[0] - tail - own, LANES), f32)
    k = k_ref[0]
    start = tail - step * k

    def read(first, count, stride):
        return buf[pl.ds(first, count, stride=stride), :]

    def write(first, count, j, value):
        out_ref[first : first + count, LANES * j : LANES * (j + 1)] = value.astype(bf16)

    wide = (k >= chunks // 2) & (k < 3 * chunks // 4) & wide_ok

    if wide_ok:

        @pl.when(wide)
        def _():
            to_rows(read, write, start, rows, True, tiles)

    @pl.when(jnp.logical_not(wide))
    def _():
        to_rows(read, write, start, rows, False, tiles)

    for j in range(tiles):
        write(rows, tail_rows, j, read(own + j, tail_rows, tiles))


def pack_expert_kernel(dims, wide_ref, own_ref, out_ref):
    rows, tiles = dims

    def read(first, count, stride):
        return own_ref[pl.ds(first, count, stride=stride), :]

    def write(first, count, j, value):
        out_ref[first : first + count, LANES * j : LANES * (j + 1)] = value.astype(bf16)

    wide = wide_ref[0] > 0

    @pl.when(wide)
    def _():
        to_rows(read, write, 0, rows, True, tiles)

    @pl.when(jnp.logical_not(wide))
    def _():
        to_rows(read, write, 0, rows, False, tiles)


def add_up(refs):
    return sum(ref[...].astype(f32) for ref in refs)


def unpack_kernel(dims, groups, wide_ref, *refs):
    rows, tiles = dims
    refs, (out_ref, square_ref, rows_ref) = refs[:-3], refs[-3:]
    if len(refs) > sum(groups):
        refs, (small_ref, before_ref) = refs[:-2], refs[-2:]
    else:
        small_ref = None
    at = 0
    for count in groups:
        value = add_up(refs[:count])
        refs = refs[count:]
        rows_ref[at : at + value.shape[0]] = value
        at += value.shape[0]
    wide = wide_ref[0] > 0

    def store(is_wide):
        total = jnp.zeros((1, LANES), f32)
        quarter = rows // 4
        for q in range(4):
            for j in range(tiles):
                piece = rows_ref[q * quarter : (q + 1) * quarter, LANES * j : LANES * (j + 1)]
                if is_wide:
                    at = pl.ds(tiles * q + j, quarter, stride=4 * tiles)
                else:
                    at = pl.ds(tiles * quarter * q + j, quarter, stride=tiles)
                out_ref[at, :] = piece
                total = total + jnp.sum(piece * piece, axis=0, keepdims=True)
        if small_ref is None:
            square_ref[...] = total
        else:
            count = small_ref.shape[0]
            square_ref[0:count] = small_ref[...]
            square_ref[count:] = jnp.zeros((square_ref.shape[0] - count, LANES), f32)
            square_ref[count : count + 1] = total + before_ref[...]

    @pl.when(wide)
    def _():
        store(True)

    @pl.when(jnp.logical_not(wide))
    def _():
        store(False)


def adam_values(clip, grad, momentum, variance):
    clipped = grad * clip
    momentum_new = beta_first * momentum + (1.0 - beta_first) * clipped
    variance_new = beta_second * variance + (1.0 - beta_second) * clipped * clipped
    first_hat = momentum_new / (1.0 - beta_first**adam_step)
    second_hat = variance_new / (1.0 - beta_second**adam_step)
    return -first_hat / (jnp.sqrt(second_hat) + adam_eps), momentum_new, variance_new


def adam_kernel(dims, k_ref, total_ref, head_ref, *refs):
    step, chunks, devices, param_count, router_rows = dims
    sources, refs = refs[:6], refs[6:]
    outs, dense_outs, gains_ref, refs = refs[:3], refs[3:7], refs[7], refs[8:]
    held, slots, buf, dense_slots, in_sems, sems, dense_in, dense_sems = refs[:3], *refs[3:]
    flat_ref, dense_m, dense_v = dense_slots.at[0], dense_slots.at[1], dense_slots.at[2]
    rows = slots.shape[2]

    def arriving(c, i):
        at = slice(c * rows, (c + 1) * rows)
        return pltpu.make_async_copy(sources[i].at[at], held[i].at[at], in_sems.at[c, i])

    def leaving(c, i):
        target = outs[i].at[c * rows : (c + 1) * rows]
        return pltpu.make_async_copy(slots.at[c % 4, i], target, sems.at[c % 4, i])

    for c in range(chunks):
        for i in range(3):
            arriving(c, i).start()
    count, own = sources[3].shape[0], sources[4].shape[0]
    dense_copies = [pltpu.make_async_copy(sources[3], buf.at[0:count], dense_in.at[0])]
    for i in (1, 2):
        dense_copies.append(pltpu.make_async_copy(sources[3 + i], dense_slots.at[i], dense_in.at[i]))
    for copy in dense_copies:
        copy.start()

    summed = head_ref.shape[0]
    squares = total_ref[summed : summed + 1]
    for at in range(0, summed, 8):
        part = total_ref[at : at + 8]
        squares = squares + jnp.sum(part * part, axis=0, keepdims=True)
    square_sum = jnp.sum(squares, axis=1, keepdims=True)
    clip = jnp.minimum(1.0, jnp.sqrt(param_count / (square_sum + 1e-06)))
    tiles = gains_ref.shape[1] // LANES
    for which in range(gains_ref.shape[0]):
        for j in range(tiles):
            at = router_rows + which * tiles + j
            gains_ref[which : which + 1, LANES * j : LANES * (j + 1)] = total_ref[at : at + 1]

    for c in range(chunks):
        at = slice(c * rows, (c + 1) * rows)
        for i in range(3):
            arriving(c, i).wait()
            if c >= 4:
                leaving(c - 4, i).wait()
        values = adam_values(clip, held[0][at], held[1][at], held[2][at])
        for i, value in enumerate(values):
            slots[c % 4, i] = value
            leaving(c, i).start()
    for copy in dense_copies:
        copy.wait()
    last = k_ref[0] == devices - 1

    @pl.when(last)
    def _():
        buf[count : count + summed] = total_ref[0:summed]

    @pl.when(jnp.logical_not(last))
    def _():
        buf[count : count + summed] = head_ref[...]

    grad = buf[pl.ds(step * k_ref[0], own), :]
    values = adam_values(clip, grad, dense_m[...], dense_v[...])
    for i, value in enumerate((grad, *values)):
        dense_slots[i] = value
    targets = (dense_outs[3], *dense_outs[:3])
    copies = start_all([dense_slots.at[i] for i in range(4)], targets, dense_sems)
    for c in range(max(0, chunks - 4), chunks):
        for i in range(3):
            leaving(c, i).wait()
    wait_all(copies)


def route_kernel(
    experts, capacity, stride, me_ref, prio_row, prio_col, picks, picks_t, cot,
    cols_ref, near_ref, rows_ref, g_ref,
):
    count = picks.shape[0]
    me = me_ref[0]
    before = (prio_row[...] < prio_col[...]).astype(f32).astype(bf16)
    lane = lax.broadcasted_iota(jnp.int32, (count, experts), 1)
    sub = lax.broadcasted_iota(jnp.int32, (experts, count), 0)
    hot = [(picks[:, j : j + 1] == lane).astype(f32) for j in range(2)]
    hot_t = [(picks_t[j : j + 1, :] == sub).astype(f32) for j in range(2)]
    first = jnp.sum(hot[0], axis=0, keepdims=True)
    first_t = jnp.sum(hot_t[0], axis=1, keepdims=True)
    for j in range(2):
        earlier = dot(before, hot[j].astype(bf16)) + (first if j else 0.0)
        earlier_t = dot_nt(hot_t[j].astype(bf16), before) + (first_t if j else 0.0)
        place = jnp.sum(earlier * hot[j], axis=1, keepdims=True).astype(jnp.int32)
        place_t = jnp.sum(earlier_t * hot_t[j], axis=0, keepdims=True).astype(jnp.int32)
        pick, pick_t = picks[:, j : j + 1], picks_t[j : j + 1, :]
        kept = (place < capacity) & (pick >= 0)
        cols_ref[:, j : j + 1] = jnp.where(kept, pick * stride + place, -1)
        near_ref[:, j : j + 1] = jnp.where(kept, (pick ^ me) * stride + place, -1)
        kept = (place_t < capacity) & (pick_t >= 0)
        rows_ref[j : j + 1, :] = jnp.where(kept, pick_t * stride + place_t, -1)
    first, second = slot_selects(rows_ref, experts * stride)
    g_ref[...] = dot(first + second, cot[...]).astype(bf16)


def slot_selects(rows_ref, slots):
    sub = lax.broadcasted_iota(jnp.int32, (slots, rows_ref.shape[1]), 0)
    return [(rows_ref[j : j + 1, :] == sub).astype(f32).astype(bf16) for j in range(2)]


def token_selects(cols_ref, slots):
    lane = lax.broadcasted_iota(jnp.int32, (cols_ref.shape[0], slots), 1)
    return [(cols_ref[:, j : j + 1] == lane).astype(f32).astype(bf16) for j in range(2)]


def split_lanes(column):
    high = column.astype(bf16).astype(f32)
    rest = column - high
    middle = rest.astype(bf16).astype(f32)
    low = rest - middle
    lane = lax.broadcasted_iota(jnp.int32, (column.shape[0], LANES), 1)
    wide = jnp.where(lane == 0, high, jnp.where(lane == 1, middle, jnp.where(lane == 2, low, 0.0)))
    return wide.astype(bf16)


def head_masks():
    lane = lax.broadcasted_iota(jnp.int32, (1, 2 * HEAD_DIM), 1)
    first = (lane < HEAD_DIM).astype(f32)
    return first.astype(bf16), (1.0 - first).astype(bf16)


def soft_scores(queries, key_rows, key_ok):
    scores = dot_nt(queries, key_rows) * HEAD_DIM ** (-0.5)
    scores = jnp.where(key_ok, scores, -1e30)
    top = jnp.max(scores, axis=-1, keepdims=True)
    raised = jnp.exp(scores - top)
    return raised * (1.0 / jnp.sum(raised, axis=-1, keepdims=True))


def put_chunk(scratch, low, chunk, value, first=0):
    place = chunk ^ low
    scratch[place & 1, place >> 1, first : first + value.shape[0], :] = value


def matrix(w_ref, index):
    per = w_ref.shape[0] // 4
    width = w_ref.shape[2]
    rows = width // per
    return w_ref[index * per : (index + 1) * per, 0:rows, :].reshape(width, width)


def quarter_in(w_ref, q):
    width = w_ref.shape[2]
    rows = width // w_ref.shape[0]
    return w_ref[:, q * rows : (q + 1) * rows, :].reshape(width, width)


def start_all(sources, targets, sems):
    copies = [pltpu.make_async_copy(a, b, sems.at[i]) for i, (a, b) in enumerate(zip(sources, targets))]
    for copy in copies:
        copy.start()
    return copies


def wait_all(copies):
    for copy in copies:
        copy.wait()


def layer_copies(spots, arrays, place_ref, layer, target, sems):
    low, top = place_ref[0], place_ref[1]
    found = []
    for j, (array, before, behind) in enumerate(spots):
        source = arrays[array].at[before + (layer ^ top,) + behind + (pl.ds(0, target.shape[1]),)]
        found.append(pltpu.make_async_copy(source, target.at[j ^ low], sems.at[j ^ low]))
    return found


def attn_fwd(seq, stream_ref, gain, w_ref, out_ref, a_ref, q_ref, k_ref, v_ref, o_ref):
    normed, _ = norm_rows(stream_ref[...])
    a_ref[...] = (normed * gain).astype(bf16)
    for index, ref in enumerate((q_ref, k_ref, v_ref)):
        ref[...] = dot(a_ref[...], matrix(w_ref, index)).astype(bf16)
    count = stream_ref.shape[0]
    key_ok = lax.broadcasted_iota(jnp.int32, (count, count), 1) < seq
    masks = head_masks()
    for pair in range(HEADS // 2):
        lanes = slice(2 * HEAD_DIM * pair, 2 * HEAD_DIM * (pair + 1))
        mixed = None
        for mask in masks:
            soft = soft_scores(q_ref[:, lanes] * mask, k_ref[:, lanes], key_ok).astype(bf16)
            part = dot(soft, v_ref[:, lanes] * mask)
            mixed = part if mixed is None else mixed + part
        o_ref[:, lanes] = mixed.astype(bf16)
    out_ref[...] = stream_ref[...] + dot(o_ref[...], matrix(w_ref, 3))


def attn_bwd(seq, grad_ref, stream_ref, gain, w_ref, q_ref, k_ref, v_ref, out_ref, dq_ref, dk_ref, dv_ref, do_ref):
    do_ref[...] = dot_nt(grad_ref[...].astype(bf16), matrix(w_ref, 3)).astype(bf16)
    count = grad_ref.shape[0]
    key_ok = lax.broadcasted_iota(jnp.int32, (count, count), 1) < seq
    masks = head_masks()
    scale = HEAD_DIM ** (-0.5)
    for pair in range(HEADS // 2):
        lanes = slice(2 * HEAD_DIM * pair, 2 * HEAD_DIM * (pair + 1))
        dq = dk = dv = None
        for mask in masks:
            q_h = q_ref[:, lanes] * mask
            k_h = k_ref[:, lanes] * mask
            do_h = do_ref[:, lanes] * mask
            soft = soft_scores(q_h, k_ref[:, lanes], key_ok)
            dsoft = dot_nt(do_h, v_ref[:, lanes])
            dv_h = dot_tn(soft.astype(bf16), do_h)
            inner = jnp.sum(dsoft * soft, axis=-1, keepdims=True)
            dscore = (soft * (dsoft - inner)).astype(bf16)
            dq_h = dot(dscore, k_h)
            dk_h = dot_tn(dscore, q_h)
            dq = dq_h if dq is None else dq + dq_h
            dk = dk_h if dk is None else dk + dk_h
            dv = dv_h if dv is None else dv + dv_h
        dq_ref[:, lanes] = (dq * scale).astype(bf16)
        dk_ref[:, lanes] = (dk * scale).astype(bf16)
        dv_ref[:, lanes] = dv.astype(bf16)
    back = None
    for index, ref in enumerate((dq_ref, dk_ref, dv_ref)):
        part = dot_nt(ref[...], matrix(w_ref, index))
        back = part if back is None else back + part
    normed, inverse = norm_rows(stream_ref[...])
    addend, gain_grad = norm_back(back, normed, inverse, gain)
    out_ref[...] = grad_ref[...] + addend
    return gain_grad


def leave_chunk(scratch, low, chunk, keep_ref, send_refs, sem):
    place = chunk ^ low
    source = scratch.at[place & 1, place >> 1]

    @pl.when((place & 1) == 0)
    def _():
        pltpu.make_async_copy(source, keep_ref.at[place >> 1], sem).start()

    at = 0
    for ref, count in send_refs:

        @pl.when(((place & 1) == 1) & ((place >> 1) >= at) & ((place >> 1) < at + count))
        def _():
            pltpu.make_async_copy(source, ref.at[(place >> 1) - at], sem).start()

        at += count


def wait_chunks(scratch, low, keep_ref, sems):
    for chunk in range(2 * scratch.shape[1]):
        place = chunk ^ low
        pltpu.make_async_copy(scratch.at[place & 1, place >> 1], keep_ref.at[place >> 1], sems.at[chunk]).wait()


def attn_weights(low, grad_ref, a_ref, o_ref, dq_ref, dk_ref, dv_ref, dw, keep_ref, send_ref, sems):
    rows = dw.shape[2]
    per = grad_ref.shape[1] // rows
    branch = grad_ref[...].astype(bf16)
    for index in range(4):
        left = o_ref if index == 3 else a_ref
        right = branch if index == 3 else (dq_ref, dk_ref, dv_ref)[index][...]
        value = dot_tn(left[...], right)
        for i in range(per):
            put_chunk(dw, low, index * per + i, value[i * rows : (i + 1) * rows].astype(bf16))
            leave_chunk(dw, low, index * per + i, keep_ref, send_ref, sems.at[index * per + i])


def attn_weights_kernel(low_ref, *refs):
    ins, keep_ref, send_ref, refs = refs[:6], refs[6], refs[7], refs[8:]
    held, (dw, in_sems, sems) = refs[:6], refs[6:]
    wait_all(start_all(ins, held, in_sems))
    attn_weights(low_ref[0], *held, dw, keep_ref, [(send_ref, dw.shape[1])], sems)
    wait_chunks(dw, low_ref[0], keep_ref, sems)


def mlp_fwd(stream_ref, gain, w1_ref, w2_ref, out_ref, b_ref, u_ref):
    width = stream_ref.shape[1]
    normed, _ = norm_rows(stream_ref[...])
    b_ref[...] = (normed * gain).astype(bf16)
    total = None
    for q in range(4):
        pre = dot(b_ref[...], quarter_in(w1_ref, q))
        u_ref[:, q * width : (q + 1) * width] = pre
        part = dot((pre * normal_cdf(pre)).astype(bf16), matrix(w2_ref, q))
        total = part if total is None else total + part
    out_ref[...] = stream_ref[...] + total


def forward_kernel(seq, spots, dims, by_core, place_ref, stream_ref, picks_ref, rows_ref, *refs):
    rows, experts, count = dims
    arrays, refs = refs[:count], refs[count:]
    if not by_core:
        w1_ref, refs = refs[0], refs[1:]
    outs, refs = refs[:15], refs[15:]
    gains_ref, wr_ref, c_ref, probs_ref, x_ref = refs[:5]
    held, (weights, tails, w_sems, tail_sems, out_sems) = refs[5:20], refs[20:]
    low, top = place_ref[0], place_ref[1]
    per = weights.shape[1]
    copies = {
        layer: layer_copies(spots, arrays, place_ref, layer, weights.at[layer], w_sems.at[layer])
        for layer in (0, 2, 3, 1)
    }
    tail_copies = []
    for j, (array, before, behind) in enumerate(spots):
        source = arrays[array].at[before + (3 ^ top,) + behind + (pl.ds(rows, tails.shape[1]),)]
        tail_copies.append(pltpu.make_async_copy(source, tails.at[j ^ low], tail_sems.at[j]))
    for copy in copies[0] + tail_copies:
        copy.start()
    for copy in copies[0] + tail_copies:
        copy.wait()
    for copy in copies[2] + copies[3] + copies[1]:
        copy.start()
    tail = tails[per - 1].astype(f32)
    gains = [tail[experts + i : experts + i + 1] for i in range(4)]
    gains_ref[...] = tail[experts : experts + 4]
    leaving = []

    def leave(first, last):
        for i in range(first, last):
            leaving.append(pltpu.make_async_copy(held[i], outs[i], out_sems.at[i]))
            leaving[-1].start()

    attn_fwd(seq, stream_ref, gains[0], weights.at[0], *held[0:6])
    leave(0, 6)
    for copy in copies[2] + copies[3]:
        copy.wait()
    mlp_fwd(held[0], gains[1], weights.at[2] if by_core else w1_ref, weights.at[3], *held[6:9])
    leave(6, 9)
    for copy in copies[1]:
        copy.wait()
    attn_fwd(seq, held[6], gains[2], weights.at[1], *held[9:15])
    leave(9, 15)
    wr_ref[...] = router_matrix(tail, stream_ref.shape[1], experts)
    dispatch(held[9], gains[3], wr_ref, picks_ref, rows_ref, c_ref, probs_ref, x_ref)
    for copy in leaving:
        copy.wait()


def mlp_bwd(low, grad_ref, stream_ref, gain, w1_ref, w2_ref, b_ref, u_ref, out_ref, put_first, put_second):
    width = grad_ref.shape[1]
    upper = grad_ref[...].astype(bf16)
    back = None
    for q in range(4):
        pre = u_ref[:, q * width : (q + 1) * width]
        cdf = normal_cdf(pre)
        act = (pre * cdf).astype(bf16)
        put_second(q, dot_tn(act, upper).astype(bf16))
        dact = dot_nt(upper, matrix(w2_ref, q))
        dpre = (dact * (cdf + pre * density(pre))).astype(bf16)
        put_first(q, dot_tn(b_ref[...], dpre).astype(bf16))
        part = dot_nt(dpre, quarter_in(w1_ref, q))
        back = part if back is None else back + part
    normed, inverse = norm_rows(stream_ref[...])
    addend, gain_grad = norm_back(back, normed, inverse, gain)
    out_ref[...] = grad_ref[...] + addend
    return gain_grad


def pick_hots(picks, experts):
    lane = lax.broadcasted_iota(jnp.int32, (picks.shape[0], experts), 1)
    return [(picks[:, j : j + 1] == lane).astype(f32) for j in range(2)]


def softmax_rows(logits):
    raised = jnp.exp(logits - jnp.max(logits, axis=-1, keepdims=True))
    return raised / jnp.sum(raised, axis=-1, keepdims=True)


def router_matrix(flat, width, experts):
    block = width // experts
    row = lax.broadcasted_iota(jnp.int32, (block, width), 0)
    lane = lax.broadcasted_iota(jnp.int32, (block, width), 1)
    mine = (lane // experts == row).astype(f32)
    lane = lax.broadcasted_iota(jnp.int32, (width, experts), 0)
    column = lax.broadcasted_iota(jnp.int32, (width, experts), 1)
    pick = (lax.rem(lane, experts) == column).astype(f32).astype(bf16)
    parts = [dot((mine * flat[i : i + 1]).astype(bf16), pick) for i in range(experts)]
    return jnp.concatenate(parts).astype(bf16)


def dispatch(stream_ref, gain, wr_ref, picks_ref, rows_ref, c_ref, probs_ref, x_ref):
    width = stream_ref.shape[1]
    experts = wr_ref.shape[1]
    normed, _ = norm_rows(stream_ref[...])
    c_ref[...] = (normed * gain).astype(bf16)
    probs = softmax_rows(dot(c_ref[...], wr_ref[...]))
    probs_ref[...] = probs
    hots = pick_hots(picks_ref, experts)
    selects = slot_selects(rows_ref, x_ref.shape[0])
    gates = None
    for j in range(2):
        part = dot(selects[j], split_lanes(jnp.sum(probs * hots[j], axis=-1, keepdims=True)))
        gates = part if gates is None else gates + part
    x_ref[:, 0:width] = dot(selects[0] + selects[1], c_ref[...]).astype(bf16)
    x_ref[:, width:] = gates.astype(bf16)


def add_lanes(wide):
    wide = wide.astype(f32)
    return wide[:, 0:1] + wide[:, 1:2] + wide[:, 2:3]


def expert_kernel(dims, spans, me_ref, x_ref, g_ref, *refs):
    parts, quarter, blocks = dims
    weight_refs, refs = refs[: len(spans)], refs[len(spans) :]
    y_refs, refs = refs[: blocks // 2], refs[blocks // 2 :]
    dx_ref, dy_ref, act_ref, dpre_ref, weights, y_near, y_sum, dx_sum, sems = refs
    q = pl.program_id(0)
    width = g_ref.shape[1]
    half = parts // 2
    me = me_ref[0]

    rows = weights.shape[1] // 2

    def copies(side):
        found = []
        for i, ((place, first), ref) in enumerate(zip(spans, weight_refs)):
            low, high = max(first, side * rows), min(first + ref.shape[0], (side + 1) * rows)
            if low < high:
                target = weights.at[place ^ me, low:high]
                found.append(pltpu.make_async_copy(ref.at[low - first : high - first], target, sems.at[side, i]))
        return found

    staged = 2 * quarter >= width // half and rows >= width

    @pl.when(q == 0)
    def _():
        for copy in copies(0) + copies(1):
            copy.start()
        dy_ref[...] = (add_lanes(x_ref[:, width:]) * g_ref[...].astype(f32)).astype(bf16)
        for copy in copies(0) if staged else copies(0) + copies(1):
            copy.wait()

    if staged:

        @pl.when(q == 1)
        def _():
            for copy in copies(1):
                copy.wait()

    first = weights[0:half, pl.ds(pl.multiple_of(q * quarter, 16), quarter), :].reshape(width, width)
    if 4 * quarter >= width:
        per = 4 * quarter // width
        at = pl.ds(pl.multiple_of(lax.rem(q, per) * width, 16), width)
        second = weights[half + q // per, at, :]
    else:
        per = width // (4 * quarter)
        second = weights[pl.ds(half + q * per, per)].reshape(width, width)
    pre = dot(x_ref[:, 0:width], first)
    cdf = normal_cdf(pre)
    act = (pre * cdf).astype(bf16)
    act_ref[...] = act
    dact = dot_nt(dy_ref[...], second)
    dpre = (dact * (cdf + pre * density(pre))).astype(bf16)
    dpre_ref[...] = dpre
    y_part = dot(act, second)
    dx_part = dot_nt(dpre, first)

    @pl.when(q == 0)
    def _():
        y_sum[...] = y_part
        dx_sum[...] = dx_part

    @pl.when(q > 0)
    def _():
        y_sum[...] += y_part
        dx_sum[...] += dx_part

    @pl.when(q == pl.num_programs(0) - 1)
    def _():
        y = y_sum[...].astype(bf16).astype(f32)
        stride = y.shape[0] // blocks
        for block in range(blocks):
            y_near[block ^ me_ref[1]] = y[block * stride : (block + 1) * stride].astype(bf16)
        for pair, ref in enumerate(y_refs):
            ref[...] = y_near[2 * pair : 2 * pair + 2]
        dx_ref[:, 0:width] = dx_sum[...].astype(bf16)
        gate_grad = jnp.sum(g_ref[...].astype(f32) * y, axis=-1, keepdims=True)
        dx_ref[:, width:] = split_lanes(gate_grad)


def expert_grad_kernel(dims, dp_ref, x_ref, dy_ref, act_ref, dpre_ref, *refs):
    parts, quarter = dims
    out_refs, scratch, sems = refs[:4], refs[-2], refs[-1]
    q = pl.program_id(0)
    me = dp_ref[0]
    width = dy_ref.shape[1]
    half = parts // 2
    rows = scratch.shape[1]
    side_rows = rows // 2

    def leave(owner, first, count, sem):
        place = owner ^ me
        side = first // side_rows
        source = scratch.at[place, pl.ds(first, count)]
        at = pl.ds(pl.multiple_of(lax.rem(first, side_rows), 16), count)
        for which, (bit, index) in enumerate(((1, place >> 1), (half, place & (half - 1)))):
            for taken, ref in enumerate((out_refs[2 * which + 1], out_refs[2 * which])):

                @pl.when((side == which) & (((place & bit) > 0) == (taken == 1)))
                def _():
                    pltpu.make_async_copy(source, ref.at[index, at], sem).start()

    first = dot_tn(x_ref[:, 0:width], dpre_ref[...]).astype(bf16)
    count = width // half
    at = pl.multiple_of(q * quarter, 16)
    for i in range(half):
        scratch[i ^ me, pl.ds(at, quarter), :] = first[i * count : (i + 1) * count]
        leave(i, at, quarter, sems.at[i])
    second = dot_tn(act_ref[...], dy_ref[...]).astype(bf16)
    step = min(width, side_rows)
    for i in range(width // step):
        flat = q * width + i * step
        owner, at = half + flat // rows, pl.multiple_of(lax.rem(flat, rows), 16)
        scratch[owner ^ me, pl.ds(at, step), :] = second[i * step : (i + 1) * step]
        leave(owner, at, step, sems.at[half + i])

    @pl.when(q == pl.num_programs(0) - 1)
    def _():
        whole = out_refs[0].at[0]
        for _ in range(4):
            for i in range(half):
                pltpu.make_async_copy(scratch.at[0, 0:quarter], whole.at[0:quarter], sems.at[i]).wait()
            for i in range(width // step):
                pltpu.make_async_copy(scratch.at[0, 0:step], whole.at[0:step], sems.at[half + i]).wait()


def combine(stream_ref, gain, wr_ref, picks_ref, cols_ref, cot_ref, c_ref, probs_ref, dx_ref, grad_ref):
    width = stream_ref.shape[1]
    experts = wr_ref.shape[1]
    probs = probs_ref[...]
    hots = pick_hots(picks_ref, experts)
    selects = token_selects(cols_ref, dx_ref.shape[0])
    prob_grad = None
    for j in range(2):
        part = add_lanes(dot(selects[j], dx_ref[:, width:])) * hots[j]
        prob_grad = part if prob_grad is None else prob_grad + part
    logit_grad = probs * (prob_grad - jnp.sum(prob_grad * probs, axis=-1, keepdims=True))
    logit_grad = logit_grad.astype(bf16)
    router_grad = dot_tn(c_ref[...], logit_grad)
    back = dot(selects[0] + selects[1], dx_ref[:, 0:width]) + dot_nt(logit_grad, wr_ref[...])
    normed, inverse = norm_rows(stream_ref[...])
    addend, gain_grad = norm_back(back, normed, inverse, gain)
    grad_ref[...] = cot_ref[...].astype(f32) + addend
    return gain_grad, router_grad


def put_router(out_ref, value, scratch):
    width, experts = value.shape
    many = LANES // experts
    scratch[...] = jnp.zeros_like(scratch)
    scratch[:, 0:experts] = value
    total = None
    for m in range(many):
        rows = scratch[pl.ds(m, width // many, stride=many), :]
        rows = pltpu.roll(rows, m * experts, 1) if m else rows
        total = rows if total is None else total + rows
    out_ref[0 : width // many, :] = total


def backward_kernel(
    seq, spots, count, by_core, place_ref, gains_ref, wr_ref, picks_ref, cols_ref, cot_ref, probs_ref, dx_ref, *refs
):
    ins, refs = refs[:15], refs[15:]
    arrays, refs = refs[:count], refs[count:]
    if not by_core:
        w1_ref, refs = refs[0], refs[1:]
    small_ref, upper_out, dq_out, dk_out, dv_out, grad_out, *refs = refs
    keep_ref, send_ref, keeps_ref, send2_ref, send_rest, *refs = refs
    places = send_ref.shape[0]
    most, rest = send2_ref.shape[0], places - send2_ref.shape[0]
    keeps = (keep_ref, keeps_ref.at[0])
    sends = ([(send_ref, places)], [(send2_ref, most), (send_rest.at[0], rest)])
    if by_core:
        send1_ref, *refs = refs
        keep1_ref, send1 = keeps_ref.at[1], [(send1_ref, most), (send_rest.at[1], rest)]
    else:
        dw1_ref, *refs = refs
    held, refs = refs[:15], refs[15:]
    grads, refs = refs[:4], refs[4:]
    dq_ref, dk_ref, dv_ref, do_ref, dw, dw2, w2_ref, w_attn, *refs = refs
    if by_core:
        dw1, w1_ref, *refs = refs
    router_scratch, in_sems, w_sems, out_sems, last_sems = refs
    low = place_ref[0]
    experts = wr_ref.shape[1]

    def fetch(first, last):
        copies = [pltpu.make_async_copy(ins[i], held[i], in_sems.at[i]) for i in range(first, last)]
        for copy in copies:
            copy.start()
        return copies

    def fetch_layer(layer, target, at):
        copies = layer_copies(spots, arrays, place_ref, layer, target, w_sems.at[at])
        for copy in copies:
            copy.start()
        return copies

    part = fetch(0, 2)
    second = fetch_layer(1, w_attn.at[0], 0) + fetch(2, 8)
    wait_all(part)
    gain_four, router_grad = combine(
        held[0], gains_ref[3:4], wr_ref, picks_ref, cols_ref, cot_ref, held[1], probs_ref, dx_ref, grads[0]
    )
    tiles = router_grad.shape[0] // LANES
    router_rows = router_grad.shape[0] * experts // LANES
    small_ref[...] = jnp.zeros_like(small_ref)
    put_router(small_ref, router_grad, router_scratch)

    def put_gain(which, value):
        at = router_rows + which * tiles
        for j in range(tiles):
            small_ref[at + j : at + j + 1, :] = value[:, LANES * j : LANES * (j + 1)]

    put_gain(3, gain_four)
    middle = fetch(8, 11) + fetch_layer(3, w2_ref, 1)
    if by_core:
        middle += fetch_layer(2, w1_ref, 2)
    wait_all(second)
    stream, q, k, v, a, o = held[2:8]
    gain_three = attn_bwd(
        seq, grads[0], stream, gains_ref[2:3], w_attn.at[0], q, k, v, grads[1], dq_ref, dk_ref, dv_ref, do_ref
    )
    put_gain(2, gain_three)
    attn_weights(low, grads[0], a, o, dq_ref, dk_ref, dv_ref, dw, keeps[0], sends[0], out_sems.at[0])
    first = fetch(11, 15) + fetch_layer(0, w_attn.at[1], 3)
    wait_all(middle)
    stream, b, u = held[8:11]
    width = stream.shape[1]
    groups = w1_ref.shape[0]

    def put_first(q, value):
        rows = width // groups
        for i in range(groups):
            piece = value[i * rows : (i + 1) * rows]
            if by_core:
                put_chunk(dw1, low, i, piece, q * rows)
                if q == 3:
                    leave_chunk(dw1, low, i, keep1_ref, send1, out_sems.at[2, i])
            else:
                dw1_ref[i, q * rows : (q + 1) * rows, :] = piece

    def put_second(q, value):
        rows = dw2.shape[2]
        per = width // rows
        for i in range(per):
            put_chunk(dw2, low, q * per + i, value[i * rows : (i + 1) * rows])
            leave_chunk(dw2, low, q * per + i, keeps[1], sends[1], out_sems.at[1, q * per + i])

    gain_two = mlp_bwd(
        low, grads[1], stream, gains_ref[1:2], w1_ref, w2_ref, b, u, grads[2], put_first, put_second
    )
    put_gain(1, gain_two)
    leaving = start_all((grads[2],), (upper_out,), last_sems)
    wait_all(first)
    wait_chunks(dw, low, keeps[0], out_sems.at[0])
    stream, q, k, v = held[11:15]
    gain_one = attn_bwd(
        seq, grads[2], stream, gains_ref[0:1], w_attn.at[1], q, k, v, grads[3], dq_ref, dk_ref, dv_ref, do_ref
    )
    put_gain(0, gain_one)
    outs = ((dq_ref, dq_out), (dk_ref, dk_out), (dv_ref, dv_out), (grads[3], grad_out))
    for i, (source, target) in enumerate(outs):
        leaving.append(pltpu.make_async_copy(source, target, last_sems.at[1 + i]))
        leaving[-1].start()
    wait_chunks(dw2, low, keeps[1], out_sems.at[1])
    if by_core:
        wait_chunks(dw1, low, keep1_ref, out_sems.at[2])
    wait_all(leaving)


def output_kernel(stream_ref, picks_ref, near_ref, probs_ref, grad_ref, *refs):
    y_refs, (other_ref, out_ref, grad_out, wide) = refs[:-4], refs[-4:]
    stride = other_ref.shape[1]
    for pair, ref in enumerate(y_refs):
        wide[2 * pair * stride : (2 * pair + 1) * stride] = ref[0].astype(f32)
        wide[(2 * pair + 1) * stride : (2 * pair + 2) * stride] = other_ref[pair].astype(f32)
    y = wide[...].astype(bf16)
    tiles = stream_ref.shape[1] // LANES
    seq = out_ref.shape[0] // tiles
    probs = probs_ref[...]
    hots = pick_hots(picks_ref, probs.shape[1])
    selects = token_selects(near_ref, y.shape[0])
    total = stream_ref[...]
    for j in range(2):
        gate = jnp.sum(probs * hots[j], axis=-1, keepdims=True)
        total = total + gate * dot(selects[j], y)
    for value, ref in ((total, out_ref), (grad_ref, grad_out)):
        for j in range(tiles):
            ref[pl.ds(j, seq, stride=tiles), :] = value[0:seq, LANES * j : LANES * (j + 1)]


def add_pair(left, right):
    return (left.astype(f32) + right.astype(f32)).astype(bf16)


def pack_sets_kernel(*refs):
    out_ref = refs[-1]
    for i, ref in enumerate(refs[:-1]):
        out_ref[i // 4, i % 4] = ref[...]


def fold_layer_kernel(cut, layer, at, sources, top_ref, keep_ref, *refs):
    refs_in, uppers, (send_x, keep_x, send_y, keep_y), refs = refs, refs[-14:-10], refs[-10:-6], refs[-6:]
    kept, got, total, keep_sems, got_sems, out_sems = refs
    if at is not None:
        keep_ref = keep_ref.at[at]
    got_refs = []
    for ref, (index, many) in zip(refs_in, sources):
        ref = ref if index is None else ref.at[index]
        got_refs += [ref.at[i] for i in range(many)]
    count = kept.shape[0]
    middle = send_x.shape[2]
    place = layer ^ top_ref[0]
    for i in range(count):
        pltpu.make_async_copy(keep_ref.at[i], kept.at[i], keep_sems.at[i]).start()
        pltpu.make_async_copy(got_refs[i], got.at[i], got_sems.at[i]).start()
    for i in range(count):
        pltpu.make_async_copy(keep_ref.at[i], kept.at[i], keep_sems.at[i]).wait()
        pltpu.make_async_copy(got_refs[i], got.at[i], got_sems.at[i]).wait()
        total[i] = add_pair(kept[i], got[i])
        pltpu.make_async_copy(total.at[i, 0:cut], uppers[i % 4].at[layer, i // 4], out_sems.at[0, i]).start()
        for bit, send, keep, at, where, sem in (
            (place & 1, send_x, keep_x, place >> 1, slice(cut, cut + middle), out_sems.at[1, i]),
            (place >> 1, send_y, keep_y, place & 1, slice(cut + middle, cut + 2 * middle), out_sems.at[2, i]),
        ):
            for value, target in ((0, keep), (1, send)):

                @pl.when(bit == value)
                def _():
                    pltpu.make_async_copy(total.at[i, where], target.at[at, i], sem).start()

    for i in range(count):
        pltpu.make_async_copy(total.at[i, 0:cut], uppers[i % 4].at[layer, i // 4], out_sems.at[0, i]).wait()
        for sem in (out_sems.at[1, i], out_sems.at[2, i]):
            pltpu.make_async_copy(total.at[i, cut : cut + middle], keep_x.at[0, i], sem).wait()


def add_kernel(left, right, out_ref):
    out_ref[...] = add_pair(left[...], right[...])


def pause_kernel(ref, out_ref):
    for i in range(ref.shape[0]):
        out_ref[i] = ref[i]


def fold_plane_kernel(keep_x, got_x, keep_y, got_y, own_a, send_y, own_b, send_x):
    for keep, got, own, send in ((keep_x, got_x, own_a, send_y), (keep_y, got_y, own_b, send_x)):
        own[...] = add_pair(keep[0], got[0])
        send[...] = add_pair(keep[1], got[1])


def fold_rows_kernel(own_a, got_a, own_b, got_b, *outs):
    middle = own_a.shape[1]
    for place in range(own_a.shape[0]):
        out = outs[place % 4].at[place // 4]
        out[0:middle] = add_pair(own_a[place], got_a[place])
        out[middle:] = add_pair(own_b[place], got_b[place])


def fold_uppers_kernel(top_ref, *refs):
    refs, outs, scratch = refs[:-5], refs[-5:-1], refs[-1]
    for layer in range(4):
        scratch[layer ^ top_ref[0]] = sum(ref[layer].astype(f32) for ref in refs).astype(bf16)
    for place, out in enumerate(outs):
        out[...] = scratch[place]


def fold_expert_kernel(highs, *refs):
    ins, outs = refs[:4], refs[4:]
    count = ins[0].shape[0]
    for side, high in enumerate(highs):
        half = count // 2
        for i in range(count):
            which, at = (i // half, i % half) if high else (i % 2, i // 2)
            outs[side * count + which * half + at][...] = add_pair(ins[2 * side][i], ins[2 * side + 1][i])


def swap(value, axes, mask):
    size = 1
    for axis in axes:
        size *= lax.axis_size(axis)
    return lax.ppermute(value, axes, [(i, i ^ mask) for i in range(size)])


def after(value, *others):
    return lax.optimization_barrier((value, others))[0]


def pause(scalars, rows, others):
    scalars, others = lax.optimization_barrier((scalars, others))
    scalars = pl.pallas_call(
        pause_kernel,
        in_specs=[SMEM],
        out_specs=SMEM,
        out_shape=shape(scalars.shape, jnp.int32),
        compiler_params=params(),
        cost_estimate=cost(rows),
        name="pause",
    )(scalars)
    return scalars, others


class Order:
    def __init__(self):
        self.latest = ()

    def land(self, value):
        self.latest = after(value, self.latest)
        return self.latest


def bit_groups(bits):
    return [bits[i : i + 2] for i in range(0, len(bits), 2)]


def all_sum_step(value, axes, bits):
    if len(bits) == 1:
        return value + swap(value, axes, 1 << bits[0])
    low, high = 1 << bits[0], 1 << bits[1]
    near, far, both = swap(value, axes, low), swap(value, axes, high), swap(value, axes, low | high)
    return (value + near) + (far + both)


def reduce_bits(value, axes, bits):
    for bit in bits:
        pairs = value.reshape((value.shape[0] // 2, 2) + value.shape[1:])
        value = pairs[:, 0] + swap(pairs[:, 1], axes, 1 << bit)
    return value[0]


def shape(dims, dtype=f32):
    return jax.ShapeDtypeStruct(dims, dtype)


def on_device(
    tokens,
    cotangent,
    expert_picks,
    priority,
    dense_master,
    dense_momentum,
    dense_variance,
    expert_master,
    expert_momentum,
    expert_variance,
):
    both = ("dp", "expert")
    dp_ranks = lax.axis_size("dp")
    expert_ranks = lax.axis_size("expert")
    devices = dp_ranks * expert_ranks
    local_experts = expert_master.shape[0]
    experts = local_experts * expert_ranks
    images, seq, width = tokens.shape
    assert local_experts == 1 and images == 1
    assert devices & (devices - 1) == 0 and dp_ranks >= 4
    tiles = width // LANES
    dp_me = lax.axis_index("dp").astype(jnp.int32)
    me = dp_me * expert_ranks + lax.axis_index("expert").astype(jnp.int32)
    me_arr = me.reshape(1)
    dp_arr = dp_me.reshape(1)
    dp_bits = dp_ranks.bit_length() - 1
    all_bits = devices.bit_length() - 1

    own = dense_master.shape[0] // LANES
    expert_flat = expert_master.shape[1] // LANES
    hidden = expert_master.shape[1] * dp_ranks // (2 * width)
    matrix_rows = 8 * width + 2 * hidden
    rows = matrix_rows // devices
    step = own - rows * tiles
    tail = step * devices
    tail_rows = -(-tail // (16 * tiles)) * 16
    wide_ok = rows % 64 == 0
    expert_rows = expert_flat // tiles

    dense_flat = dense_master.reshape(own, LANES)
    forward_ring = [(i, (i + 1) % devices) for i in range(devices)]
    backward_ring = [((i + 1) % devices, i) for i in range(devices)]
    tail_from = lax.ppermute(dense_flat[own - tail :], both, forward_ring)
    buf_rows = -(-(own + max(tail, tail_rows * tiles)) // 8) * 8
    chunk = pl.pallas_call(
        functools.partial(
            pack_dense_kernel, (rows, tail_rows, tail, own, step, tiles, devices, wide_ok)
        ),
        in_specs=[SMEM, VMEM, VMEM],
        out_specs=VMEM,
        out_shape=shape((rows + tail_rows, width), bf16),
        scratch_shapes=[pltpu.VMEM((buf_rows, LANES), f32)],
        compiler_params=params(),
        cost_estimate=cost(),
        name="pack_dense",
    )(me_arr, tail_from, dense_flat)

    expert_wide = (dp_me < dp_ranks // 2).astype(jnp.int32).reshape(1)
    expert_chunk = pl.pallas_call(
        functools.partial(pack_expert_kernel, (expert_rows, tiles)),
        in_specs=[SMEM, VMEM],
        out_specs=VMEM,
        out_shape=shape((expert_rows, width), bf16),
        compiler_params=params(),
        cost_estimate=cost(),
        name="pack_expert",
    )(expert_wide, expert_master.reshape(expert_flat, LANES))
    dp_axis = ("dp",)
    dp_order = list(range(dp_bits))

    def gather_step(parts, bit):
        return {**parts, **{at | (1 << bit): swap(part, dp_axis, 1 << bit) for at, part in parts.items()}}

    capacity = 2 * seq // experts
    stride = -(-capacity // 8) * 8
    slots = experts * stride
    padded = -(-seq // 16) * 16
    fill = padded - seq
    ranks = jnp.pad(priority, ((0, 0), (0, fill)), constant_values=1 << 20)
    picks = jnp.pad(expert_picks, ((0, fill), (0, 0)), constant_values=-1)
    cot = jnp.pad(cotangent.reshape(seq, width), ((0, fill), (0, 0)))
    stream = jnp.pad(tokens.reshape(seq, width).astype(f32), ((0, fill), (0, 0)))
    e_me = lax.axis_index("expert").astype(jnp.int32).reshape(1)
    pair_shape = shape((2, stride, width), bf16)
    cols, near_cols, rows_slots, outgoing_cot = pl.pallas_call(
        functools.partial(route_kernel, experts, capacity, stride),
        in_specs=[SMEM] + [VMEM] * 5,
        out_specs=[VMEM] * 4,
        out_shape=[shape((padded, 2), jnp.int32)] * 2
        + [shape((2, padded), jnp.int32), shape((slots, width), bf16)],
        compiler_params=params(),
        cost_estimate=cost(),
        name="route",
    )(e_me, ranks, ranks.reshape(padded, 1), picks, picks.T, cot)

    def exchange(value):
        dims = value.shape
        value = value.reshape(expert_ranks, slots // expert_ranks, dims[1])
        value = lax.all_to_all(value, "expert", split_axis=0, concat_axis=0, tiled=True)
        return value.reshape(dims)

    per = devices // 4
    per_bits = per.bit_length() - 1
    top_bits = (per_bits, per_bits + 1)
    chunk_rows = rows + tail_rows
    low = me & (per - 1)
    low_arr = low.reshape(1)
    place_arr = jnp.stack([low, me >> per_bits])
    expert_me = jnp.concatenate([dp_arr, e_me])
    half_rows = expert_rows // 2
    orders = (dp_order, dp_order[::-1])
    expert_parts, expert_spans = [], []
    if per_bits == 3 and dp_bits == 2:
        masks = [1 << bit for bit in top_bits]
        split = chunk_rows // 32 * 16 + 16
        order = Order()

        def spread(value):
            return [swap(value, both, mask) for mask in masks]

        sets = [chunk, swap(chunk, both, 2), None, None]
        near, far = [spread(chunk)] + [None] * 3, [None] * 4
        near[0] = order.land(near[0])
        sets[1] = order.land(sets[1])
        near[1] = spread(sets[1])
        sets[2] = swap(after(chunk, sets[1]), both, 4)
        halves = [swap(near[0][1][:split], both, masks[0]), swap(near[0][0][split:], both, masks[1])]
        near[1] = order.land(near[1])
        halves, expert_chunk, outgoing_cot, stream = order.land((halves, expert_chunk, outgoing_cot, stream))
        sets[2] = order.land(sets[2])
        sets[3] = swap(sets[2], both, 2)
        near[2] = spread(sets[2])
        far[0] = jnp.concatenate(halves)
        far[1], far[2] = swap(far[0], both, 2), swap(far[0], both, 4)
        sets[3] = order.land(sets[3])
        near[3] = spread(sets[3])
        near[2] = order.land(near[2])
        near[3] = order.land(near[3])
        far[1] = order.land(far[1])
        far[2] = order.land(far[2])
        place_arr, far[2] = pause(place_arr, 800, far[2])
        far[3] = swap(far[2], both, 2)
        arriving_cot = exchange(after(outgoing_cot, far[2]))

        def pack_sets(which):
            ins = [part for s in which for part in (sets[s], *near[s], far[s])]
            return pl.pallas_call(
                pack_sets_kernel,
                in_specs=[VMEM] * len(ins),
                out_specs=VMEM,
                out_shape=shape((len(which), 4, chunk_rows, width), bf16),
                compiler_params=params(),
                cost_estimate=cost(),
                name="pack_sets",
            )(*ins)

        packed = [pack_sets([0, 1])]
        far[3], packed = lax.optimization_barrier((far[3], packed))
        far[3] = order.land(far[3])
        packed.append(pack_sets([2, 3]))
        arrays = packed + [swap(value, both, 1) for value in packed]
        spots = [((j >> 2) + 2 * (j & 1), ((j >> 1) & 1,), ()) for j in range(per)]
        own_shard = after(expert_chunk, near[3])
        beside = [swap(own_shard, dp_axis, mask) for mask in (1, 2)]
        place_arr, beside = pause(place_arr, 650, beside)
        place_arr, arriving_cot = pause(place_arr, 1900, arriving_cot)
        place_arr, arrays[2] = pause(place_arr, 300, arrays[2])
        across = [swap(beside[0][:half_rows], dp_axis, 2), swap(beside[1][half_rows:], dp_axis, 1)]
        expert_me, across = pause(expert_me, 400, across)
        expert_parts = [expert_chunk, *beside, *across]
        expert_spans = [(0, 0), (1, 0), (2, 0), (3, 0), (3, half_rows)]
    else:
        gathered = chunk[None]
        for bit in range(all_bits):
            gathered = jnp.concatenate([gathered, swap(gathered, both, 1 << bit)])
        arrays = [gathered.reshape(4, per, chunk_rows, width)]
        spots = [(0, (), (j,)) for j in range(per)]
        for side, bits in enumerate(orders):
            parts, places = [expert_chunk[side * half_rows : (side + 1) * half_rows]], [0]
            for bit in bits:
                parts = parts + [swap(part, dp_axis, 1 << bit) for part in parts]
                places = places + [place | (1 << bit) for place in places]
            expert_parts += parts
            expert_spans += [(place, side * half_rows) for place in places]
        arriving_cot = exchange(outgoing_cot)

    layer_w = pltpu.VMEM((per, rows, width), bf16)
    if not wide_ok:
        first_in = lax.dynamic_index_in_dim(arrays[0], 2 ^ (me >> per_bits), 0, keepdims=False)
        first_in = jnp.take(first_in, jnp.arange(per) ^ low, axis=0)[:, :rows].reshape(width, 4, width)
        first_in = first_in.transpose(1, 0, 2).reshape(1, 4 * width, width)

    act_shape = shape((padded, width), bf16)
    stream_shape = shape((padded, width), f32)
    gain_shape = shape((1, width), f32)
    tok_flops = 2 * padded * width * width
    weight_bytes = 2 * width * width
    ANY = pl.BlockSpec(memory_space=pl.ANY)

    def call(kernel, ins, in_specs, outs, name, rows=0, mib=56, out_specs=None, scratch=(), aliases=None):
        out_specs = out_specs or [None] * len(outs)

        def whole(a):
            return pl.BlockSpec(a.shape, lambda *_, n=len(a.shape): (0,) * n)

        return pl.pallas_call(
            kernel,
            grid=(1,),
            in_specs=[s or whole(a) for a, s in zip(ins, in_specs, strict=True)],
            out_specs=[s or whole(a) for a, s in zip(outs, out_specs, strict=True)],
            out_shape=outs,
            scratch_shapes=list(scratch),
            compiler_params=params(mib),
            cost_estimate=cost(rows),
            input_output_aliases=aliases or {},
            name=name,
        )(*ins)

    places = per // 2
    core_shape = shape((places, rows, width), bf16)
    by_core = pltpu.VMEM((2, places, rows, width), bf16)
    stream_vmem, act_vmem = pltpu.VMEM((padded, width), f32), pltpu.VMEM((padded, width), bf16)

    def attn_weights_call(grad, kept, found):
        return call(
            attn_weights_kernel,
            (low_arr, grad, kept[0], kept[4], *found),
            (SMEM,) + (ANY,) * 6,
            [core_shape, core_shape],
            "attn_weights",
            0,
            out_specs=[ANY] * 2,
            scratch=[
                stream_vmem,
                *[act_vmem] * 5,
                by_core,
                pltpu.SemaphoreType.DMA((6,)),
                pltpu.SemaphoreType.DMA((per,)),
            ],
        )

    outs = [stream_shape] + [act_shape] * 5 + [stream_shape, act_shape, shape((padded, hidden), f32)]
    outs += [stream_shape] + [act_shape] * 5
    *results, gains, router, moe_in, probs, outgoing = call(
        functools.partial(forward_kernel, seq, spots, (rows, experts, len(arrays)), wide_ok),
        (place_arr, stream, picks, rows_slots, *arrays, *([] if wide_ok else [first_in])),
        (SMEM, None, None, None) + (ANY,) * len(arrays) + (() if wide_ok else (None,)),
        outs
        + [
            shape((4, width)),
            shape((width, experts), bf16),
            act_shape,
            shape((padded, experts)),
            shape((slots, width + LANES), bf16),
        ],
        "forward",
        0,
        out_specs=[ANY] * 15 + [None] * 5,
        scratch=[pltpu.VMEM(o.shape, o.dtype) for o in outs]
        + [
            pltpu.VMEM((4, per, rows, width), bf16),
            pltpu.VMEM((per, tail_rows, width), bf16),
            pltpu.SemaphoreType.DMA((4, per)),
            pltpu.SemaphoreType.DMA((per,)),
            pltpu.SemaphoreType.DMA((15,)),
        ],
    )
    stream_one, kept_one = results[0], results[1:6]
    stream_two, mlp_in, mlp_pre = results[6:9]
    stream_three, kept_two = results[9], results[10:]
    arriving = exchange(outgoing)

    quarter = expert_rows // 4
    slot_spec = pl.BlockSpec((slots, width), lambda q: (0, 0))
    wide_spec = pl.BlockSpec((slots, width + LANES), lambda q: (0, 0))
    pair_spec = pl.BlockSpec((2, stride, width), lambda q: (0, 0, 0))
    hidden_spec = pl.BlockSpec((slots, width), lambda q: (0, q))
    pairs = experts // 2
    *expert_out, input_back, slot_grad, expert_act, pre_grad = pl.pallas_call(
        functools.partial(expert_kernel, (dp_ranks, quarter, experts), expert_spans),
        grid=(4,),
        in_specs=[SMEM, wide_spec, slot_spec] + [ANY] * len(expert_parts),
        out_specs=[pair_spec] * pairs + [wide_spec, slot_spec, hidden_spec, hidden_spec],
        out_shape=[pair_shape] * pairs
        + [shape((slots, width + LANES), bf16), shape((slots, width), bf16)]
        + [shape((slots, hidden), bf16)] * 2,
        scratch_shapes=[
            pltpu.VMEM((dp_ranks, expert_rows, width), bf16),
            pltpu.VMEM((experts, stride, width), bf16),
            pltpu.VMEM((slots, width), f32),
            pltpu.VMEM((slots, width), f32),
            pltpu.SemaphoreType.DMA((2, len(expert_parts))),
        ],
        compiler_params=params(),
        cost_estimate=cost(),
        name="expert",
    )(expert_me, arriving, arriving_cot, *expert_parts)
    returned_grad = exchange(input_back)
    part_shape = shape((expert_rows // 2, width), bf16)
    count = dp_ranks // 2
    expert_first = pl.pallas_call(
        functools.partial(expert_grad_kernel, (dp_ranks, quarter)),
        grid=(4,),
        in_specs=[SMEM, wide_spec, slot_spec, hidden_spec, hidden_spec],
        out_specs=[ANY] * 4,
        out_shape=[shape((count,) + part_shape.shape, bf16)] * 4,
        scratch_shapes=[
            pltpu.VMEM((dp_ranks, expert_rows, width), bf16),
            pltpu.SemaphoreType.DMA((2 * dp_ranks,)),
        ],
        compiler_params=params(),
        cost_estimate=cost(),
        name="expert_grad",
    )(dp_arr, arriving, slot_grad, expert_act, pre_grad)
    returned_grad = after(returned_grad, expert_first)

    cut = max(16, rows // 64 * 16)
    middle = (rows - cut) // 2
    top = (me >> per_bits).reshape(1)
    z_bits = list(range(1, per_bits))
    z_masks = [2 * j for j in (1, 2, 3)]
    assert places % 4 == 0

    def add_call(left, right):
        return call(add_kernel, (left, right), (None, None), [shape(left.shape, bf16)], "add", mib=12)[0]

    def over_z(values, meanwhile=None):
        farthest = swap(values[3], both, 2)
        near = swap(values[1], both, 2)
        if meanwhile is not None:
            farthest, *meanwhile[:] = lax.optimization_barrier((farthest, *meanwhile))
        return [values[0], near, swap(add_call(values[2], farthest), both, 4)]

    def rest_of_z(values):
        if len(z_bits) == 2:
            return values
        total = sum(value.astype(f32) for value in values).astype(bf16)
        lead = total.ndim - 3
        total = jnp.moveaxis(total, lead, 0)
        return [reduce_bits(total, both, z_bits[2:])]

    def to_other_core(parts):
        return [parts[0], swap(parts[1], both, 1)]

    expert_got = [swap(expert_first[0], dp_axis, 1), swap(expert_first[2], dp_axis, dp_ranks // 2)]
    backward_ins = (
        (stream_three, moe_in, stream_two, *kept_two[1:4], kept_two[0], kept_two[4])
        + (stream_one, mlp_in, mlp_pre, stream, *kept_one[1:4])
    )
    held_vmem = [stream_vmem, act_vmem, stream_vmem] + [act_vmem] * 5
    held_vmem += [stream_vmem, act_vmem, pltpu.VMEM((padded, hidden), f32), stream_vmem] + [act_vmem] * 3
    kinds = 2 if wide_ok else 1
    most, rest = places * 3 // 4, places // 4
    keeps_shape = shape((kinds,) + core_shape.shape, bf16)
    most_shape, rest_shape = shape((most, rows, width), bf16), shape((kinds, rest, rows, width), bf16)
    first_dw_out = [most_shape] if wide_ok else [shape((1, 4 * width, width), bf16)]
    small, upper, dq, dk, dv, grad, *dws = call(
        functools.partial(backward_kernel, seq, spots, len(arrays), wide_ok),
        (place_arr, gains, router, picks, cols, cot, probs, returned_grad, *backward_ins, *arrays)
        + (() if wide_ok else (first_in,)),
        (SMEM,) + (None,) * 7 + (ANY,) * (15 + len(arrays)) + (() if wide_ok else (None,)),
        [shape((tail, LANES)), stream_shape, act_shape, act_shape, act_shape, stream_shape]
        + [core_shape, core_shape, keeps_shape, most_shape, rest_shape]
        + first_dw_out,
        "backward",
        out_specs=[None] + [ANY] * 10 + ([ANY] if wide_ok else [None]),
        scratch=held_vmem
        + [stream_vmem] * 4
        + [act_vmem] * 4
        + [by_core, by_core, layer_w, pltpu.VMEM((2, per, rows, width), bf16)]
        + ([by_core, layer_w] if wide_ok else [])
        + [
            pltpu.VMEM((width, LANES), f32),
            pltpu.SemaphoreType.DMA((15,)),
            pltpu.SemaphoreType.DMA((4, per)),
            pltpu.SemaphoreType.DMA((3, per)),
            pltpu.SemaphoreType.DMA((5,)),
        ],
    )
    if not wide_ok:
        wide_grad = dws[5].reshape(4, width, width).transpose(1, 0, 2).reshape(per, rows, width)
        wide_grad = jnp.take(wide_grad, jnp.arange(per) ^ low, axis=0)
        wide_grad = wide_grad.reshape(places, 2, rows, width)
        dws[2] = jnp.concatenate([dws[2], wide_grad[None, :, 0]])
        dws[4] = jnp.concatenate([dws[4], wide_grad[None, most:, 1]])
        dws[5] = wide_grad[:most, 1]
    most_got = [swap(dws[3], both, 1), swap(dws[5], both, 1)]
    rest_got = swap(dws[4], both, 1)
    first_dw = attn_weights_call(upper, kept_one, (dq, dk, dv))
    layer_got = {0: [(swap(first_dw[1], both, 1), None, places)], 1: [(swap(dws[1], both, 1), None, places)]}
    for i, layer in enumerate((3, 2)):
        layer_got[layer] = [(most_got[i], None, most), (rest_got, i, rest)]
    layer_keep = {3: (dws[2], 0), 2: (dws[2], 1), 1: (dws[0], None), 0: (first_dw[0], None)}

    plane_shape = shape((2, places, middle, width), bf16)
    plane_spec = pl.BlockSpec((2, 1, middle, width), lambda i: (0, i, 0, 0))
    line_shape = shape((places, middle, width), bf16)
    line_spec = pl.BlockSpec((1, middle, width), lambda i: (i, 0, 0))
    upper_shape = shape((4, places // 4, cut, width), bf16)
    sums = ()
    for layer in (3, 2, 1, 0):
        keep, at = layer_keep[layer]
        parts = layer_got[layer]
        if layer == 3:
            keep = after(keep, first_dw)
        if layer == 1:
            expert_got, sums = lax.optimization_barrier((expert_got, sums))
            top, expert_got = pause(top, 1600, expert_got)
        sums = call(
            functools.partial(fold_layer_kernel, cut, layer, at, [part[1:] for part in parts]),
            (top, keep, *[part[0] for part in parts], *sums),
            (SMEM,) + (ANY,) * (1 + len(parts) + len(sums)),
            [upper_shape] * 4 + [plane_shape] * 4,
            "fold_layer",
            out_specs=[ANY] * 8,
            scratch=[pltpu.VMEM((places, rows, width), bf16)] * 3
            + [
                pltpu.SemaphoreType.DMA((places,)),
                pltpu.SemaphoreType.DMA((places,)),
                pltpu.SemaphoreType.DMA((3, places)),
            ],
            aliases={2 + len(parts) + i: i for i in range(len(sums))},
        )
    *uppers, send_x, keep_x, send_y, keep_y = sums
    masks = [1 << bit for bit in top_bits]
    got_x, got_y = swap(send_x, both, masks[0]), swap(send_y, both, masks[1])
    uppers = over_z(uppers)
    expert_ins = (expert_first[1], expert_got[0], expert_first[3], expert_got[1])
    expert_second = call(
        functools.partial(fold_expert_kernel, (dp_bits == 1, True)),
        expert_ins,
        (None,) * len(expert_ins),
        [part_shape] * (2 * count),
        "fold_expert",
        0,
    )

    uppers = [value.reshape(4, -1, cut, width) for value in uppers]
    uppers = [value.reshape(4, cut, width) for value in rest_of_z(uppers)]
    upper_rows = call(
        fold_uppers_kernel,
        (top, *uppers),
        (SMEM,) + (None,) * len(uppers),
        [shape((cut, width), bf16)] * 4,
        "fold_uppers",
        100,
        scratch=[pltpu.VMEM((4, cut, width), bf16)],
    )
    got_x, got_y, expert_second = lax.optimization_barrier((got_x, got_y, expert_second))
    expert_out = [expert_out[0]] + [swap(v, ("expert",), 2 * j) for j, v in enumerate(expert_out) if j]
    own_a, send_y, own_b, send_x = pl.pallas_call(
        fold_plane_kernel,
        grid=(places,),
        in_specs=[plane_spec] * 4,
        out_specs=[line_spec] * 4,
        out_shape=[line_shape] * 4,
        compiler_params=params(),
        cost_estimate=cost(),
        name="fold_plane",
    )(keep_x, got_x, keep_y, got_y)
    got_y, got_x = swap(send_y, both, masks[1]), swap(send_x, both, masks[0])
    expert_second, expert_out, upper_rows = lax.optimization_barrier((expert_second, expert_out, upper_rows))
    other_out = swap(jnp.stack([value[1] for value in expert_out]), ("expert",), 1)
    lower_rows = call(
        fold_rows_kernel,
        (own_a, got_y, own_b, got_x),
        (None,) * 4,
        [shape((places // 4, rows - cut, width), bf16)] * 4,
        "fold_rows",
        0,
    )
    lower_rows, other_out = lax.optimization_barrier((lower_rows, other_out))
    output, grad = call(
        output_kernel,
        (stream_three, picks, near_cols, probs, grad, *expert_out, other_out),
        (None,) * (6 + pairs),
        [shape((seq * tiles, LANES))] * 2,
        "output",
        mib=16,
        scratch=[pltpu.VMEM((slots, width), f32)],
    )
    image = (1, seq, width)
    meanwhile = [output.reshape(image), grad.reshape(image)]
    lower_rows = over_z(lower_rows, meanwhile)
    output, grad = meanwhile
    half = count // 2
    expert_groups = []
    for side, bits in enumerate(orders):
        keep, send = (expert_second[(2 * side + i) * half : (2 * side + i + 1) * half] for i in range(2))
        got = [swap(part, dp_axis, 1 << bits[1]) for part in send]
        expert_groups.append([list(pair) for pair in zip(keep, got)])
    if dp_bits > 2:
        for side, bits in enumerate(orders):
            value = [sum(pair) for pair in expert_groups[side]]
            for bit in bits[2:]:
                half = len(value) // 2
                keep, send = (value[:half], value[half:]) if side else (value[0::2], value[1::2])
                value = [k + swap(v, dp_axis, 1 << bit) for k, v in zip(keep, send)]
            expert_groups[side] = [value]
    expert_groups = [side[0] for side in expert_groups]
    upper_rows, expert_groups = lax.optimization_barrier((upper_rows, expert_groups))

    def unpack(wide, groups, count, name, extra=(), square_shape=(1, LANES)):
        pieces = [piece for group in groups for piece in group] + list(extra)
        return pl.pallas_call(
            functools.partial(unpack_kernel, (count, tiles), [len(group) for group in groups]),
            in_specs=[SMEM] + [VMEM] * len(pieces),
            out_specs=[VMEM, VMEM],
            out_shape=[shape((count * tiles, LANES)), shape(square_shape)],
            scratch_shapes=[pltpu.VMEM((count, width), f32)],
            compiler_params=params(),
            cost_estimate=cost(),
            name=name,
        )(wide, *pieces)

    expert_grad, expert_square = unpack(expert_wide, expert_groups, expert_rows, "unpack_expert")
    lower_rows, output, expert_grad, expert_square = lax.optimization_barrier(
        (lower_rows, output, expert_grad, expert_square)
    )
    lower_rows = rest_of_z(lower_rows)
    upper_rows = [upper_rows[0]] + [
        swap(value, both, masks[0] * j) for j, value in enumerate(upper_rows) if j
    ]
    dense_groups = [upper_rows, [value.reshape(rows - cut, width) for value in lower_rows]]

    dense_wide = (me >= devices // 2) & (me < 3 * devices // 4) & wide_ok
    dense_rows, total = unpack(
        dense_wide.astype(jnp.int32).reshape(1),
        dense_groups,
        rows,
        "unpack_dense",
        (small, expert_square),
        (tail + 8, LANES),
    )
    head = lax.ppermute(dense_rows[:tail], both, backward_ring)
    groups = bit_groups(list(range(all_bits)))
    for bits in groups[:-1]:
        total = all_sum_step(total, both, bits)
    total, head = lax.optimization_barrier((total, head))
    total = all_sum_step(total, both, groups[-1])
    param_count = (dense_master.size + expert_master.size) * devices

    chunks = 16
    results = pl.pallas_call(
        functools.partial(adam_kernel, (step, chunks, devices, param_count, width * experts // LANES)),
        in_specs=[SMEM, VMEM, VMEM] + [ANY] * 6,
        out_specs=[ANY] * 7 + [VMEM],
        out_shape=[shape((expert_flat, LANES))] * 3 + [shape((own, LANES))] * 4 + [shape((4, width))],
        scratch_shapes=[pltpu.VMEM((expert_flat, LANES), f32)] * 3
        + [
            pltpu.VMEM((4, 3, expert_flat // chunks, LANES), f32),
            pltpu.VMEM((-(-(rows * tiles + tail) // 8) * 8, LANES), f32),
            pltpu.VMEM((4, own, LANES), f32),
            pltpu.SemaphoreType.DMA((chunks, 3)),
            pltpu.SemaphoreType.DMA((4, 3)),
            pltpu.SemaphoreType.DMA((3,)),
            pltpu.SemaphoreType.DMA((4,)),
        ],
        compiler_params=params(),
        cost_estimate=cost(),
        name="adam",
    )(
        me_arr,
        total,
        head,
        expert_grad,
        expert_momentum.reshape(expert_flat, LANES),
        expert_variance.reshape(expert_flat, LANES),
        dense_rows,
        dense_momentum.reshape(own, LANES),
        dense_variance.reshape(own, LANES),
    )
    gain_grads = results[7]
    expert_update, momentum_expert, variance_expert = results[:3]
    dense_update, momentum_dense, variance_dense, dense_grad = results[3:7]
    return (
        output,
        grad,
        dense_grad.reshape(dense_master.shape),
        expert_grad.reshape(expert_master.shape),
        dense_update.reshape(dense_master.shape),
        momentum_dense.reshape(dense_master.shape),
        variance_dense.reshape(dense_master.shape),
        expert_update.reshape(expert_master.shape),
        momentum_expert.reshape(expert_master.shape),
        variance_expert.reshape(expert_master.shape),
        gain_grads,
    )


def solution(mesh):
    tokens = P(("dp", "expert"), None, None)
    flat = P(("dp", "expert"))
    pairs = P(("dp", "expert"), None)
    expert = P("expert", "dp")
    return jax.shard_map(
        on_device,
        mesh=mesh,
        in_specs=(tokens, tokens, pairs, pairs, flat, flat, flat, expert, expert, expert),
        out_specs=(tokens, tokens, flat, expert, flat, flat, flat, expert, expert, expert, P()),
        check_vma=False,
    )
```

```python
import functools
import math

import jax
import jax.numpy as jnp
from jax import lax
from jax.experimental import pallas as pl
from jax.experimental.pallas import tpu as pltpu
from jax.sharding import PartitionSpec as P

HEADS = 12
HEAD_DIM = 64
LANES = 128

f32 = jnp.float32
bf16 = jnp.bfloat16

eps_norm = 1e-06
beta_first = 0.9
beta_second = 0.999
adam_eps = 1e-08
adam_step = 10.0

VMEM = pl.BlockSpec(memory_space=pltpu.VMEM)
SMEM = pl.BlockSpec(memory_space=pltpu.SMEM)


def params(mib=56):
    return pltpu.CompilerParams(vmem_limit_bytes=mib << 20)


def cost(rows=0):
    return pl.CostEstimate(flops=1 + int(rows * 16.45e6), bytes_accessed=1, transcendentals=0)


def dot(a, b):
    return lax.dot_general(a, b, (((1,), (0,)), ((), ())), preferred_element_type=f32)


def dot_nt(a, b):
    return lax.dot_general(a, b, (((1,), (1,)), ((), ())), preferred_element_type=f32)


def dot_tn(a, b):
    return lax.dot_general(a, b, (((0,), (0,)), ((), ())), preferred_element_type=f32)


def norm_rows(hidden):
    center = hidden - jnp.mean(hidden, axis=-1, keepdims=True)
    inverse = lax.rsqrt(jnp.mean(center * center, axis=-1, keepdims=True) + eps_norm)
    return center * inverse, inverse


def norm_back(upstream, normed, inverse, gain):
    scaled = upstream * gain
    gain_grad = jnp.sum(upstream * normed, axis=0, keepdims=True)
    centered = (
        scaled
        - jnp.mean(scaled, axis=-1, keepdims=True)
        - normed * jnp.mean(scaled * normed, axis=-1, keepdims=True)
    )
    return inverse * centered, gain_grad


def normal_cdf(v):
    return 0.5 * (1.0 + lax.erf(v * 0.7071067811865476))


def density(v):
    return jnp.exp(-0.5 * v * v) * 0.3989422804014327


def to_rows(read, write, first_q, rows, wide, tiles):
    blocks = 4 if rows % 64 == 0 else 1
    count = rows // blocks
    for b in range(blocks):
        for j in range(tiles):
            if wide:
                write(b * count, count, j, read(first_q + tiles * b + j, count, 4 * tiles))
            else:
                write(b * count, count, j, read(first_q + tiles * count * b + j, count, tiles))


def pack_dense_kernel(dims, k_ref, tail_ref, own_ref, out_ref, buf):
    rows, tail_rows, tail, own, step, tiles, chunks, wide_ok = dims
    buf[0:tail] = tail_ref[...]
    buf[tail : tail + own] = own_ref[...]
    buf[tail + own :] = jnp.zeros((buf.shape[0] - tail - own, LANES), f32)
    k = k_ref[0]
    start = tail - step * k

    def read(first, count, stride):
        return buf[pl.ds(first, count, stride=stride), :]

    def write(first, count, j, value):
        out_ref[first : first + count, LANES * j : LANES * (j + 1)] = value.astype(bf16)

    wide = (k >= chunks // 2) & (k < 3 * chunks // 4) & wide_ok

    if wide_ok:

        @pl.when(wide)
        def _():
            to_rows(read, write, start, rows, True, tiles)

    @pl.when(jnp.logical_not(wide))
    def _():
        to_rows(read, write, start, rows, False, tiles)

    for j in range(tiles):
        write(rows, tail_rows, j, read(own + j, tail_rows, tiles))


def pack_expert_kernel(dims, cuts, wide_ref, own_ref, *out_refs):
    rows, tiles = dims

    def read(first, count, stride):
        return own_ref[pl.ds(first, count, stride=stride), :]

    def write(first, count, j, value):
        value = value.astype(bf16)
        for (low, high), ref in zip(cuts, out_refs):
            start, end = max(first, low), min(first + count, high)
            if start < end:
                ref[start - low : end - low, LANES * j : LANES * (j + 1)] = value[start - first : end - first]

    wide = wide_ref[0] > 0

    @pl.when(wide)
    def _():
        to_rows(read, write, 0, rows, True, tiles)

    @pl.when(jnp.logical_not(wide))
    def _():
        to_rows(read, write, 0, rows, False, tiles)


def add_up(refs):
    return sum(ref[...].astype(f32) for ref in refs)


def unpack_kernel(dims, groups, wide_ref, *refs):
    rows, tiles = dims
    (*refs, rows_ref), small_ref = refs, None
    if len(refs) > sum(groups) + 2:
        *refs, small_ref, before_ref, out_ref, square_ref, head_ref = refs
    else:
        *refs, out_ref, square_ref = refs
    at = 0
    for count in groups:
        value = add_up(refs[:count])
        refs = refs[count:]
        rows_ref[at : at + value.shape[0]] = value
        at += value.shape[0]
    wide = wide_ref[0] > 0

    def store(is_wide):
        total = jnp.zeros((1, LANES), f32)
        quarter = rows // 4
        for q in range(4):
            for j in range(tiles):
                piece = rows_ref[q * quarter : (q + 1) * quarter, LANES * j : LANES * (j + 1)]
                if is_wide:
                    at = pl.ds(tiles * q + j, quarter, stride=4 * tiles)
                else:
                    at = pl.ds(tiles * quarter * q + j, quarter, stride=tiles)
                out_ref[at, :] = piece
                total = total + jnp.sum(piece * piece, axis=0, keepdims=True)
        if small_ref is None:
            square_ref[...] = total
        else:
            count = small_ref.shape[0]
            square_ref[0:count] = small_ref[...]
            square_ref[count:] = jnp.zeros((square_ref.shape[0] - count, LANES), f32)
            square_ref[count : count + 1] = total + before_ref[...]
            head_ref[...] = out_ref[0:count]

    @pl.when(wide)
    def _():
        store(True)

    @pl.when(jnp.logical_not(wide))
    def _():
        store(False)


def adam_values(clip, grad, momentum, variance):
    clipped = grad * clip
    momentum_new = beta_first * momentum + (1.0 - beta_first) * clipped
    variance_new = beta_second * variance + (1.0 - beta_second) * clipped * clipped
    first_hat = momentum_new / (1.0 - beta_first**adam_step)
    second_hat = variance_new / (1.0 - beta_second**adam_step)
    return -first_hat / (jnp.sqrt(second_hat) + adam_eps), momentum_new, variance_new


def adam_kernel(dims, k_ref, total_ref, head_ref, *refs):
    step, chunks, devices, param_count, router_rows = dims
    sources, refs = refs[:6], refs[6:]
    outs, dense_outs, gains_ref, refs = refs[:3], refs[3:7], refs[7], refs[8:]
    held, slots, buf, dense_slots, in_sems, sems, dense_in, dense_sems = refs[:3], *refs[3:]
    flat_ref, dense_m, dense_v = dense_slots.at[0], dense_slots.at[1], dense_slots.at[2]
    rows = slots.shape[2]

    def arriving(c, i):
        at = slice(c * rows, (c + 1) * rows)
        return pltpu.make_async_copy(sources[i].at[at], held[i].at[at], in_sems.at[c, i])

    def leaving(c, i):
        target = outs[i].at[c * rows : (c + 1) * rows]
        return pltpu.make_async_copy(slots.at[c % 4, i], target, sems.at[c % 4, i])

    for c in range(chunks):
        for i in range(3):
            arriving(c, i).start()
    count, own = sources[3].shape[0], sources[4].shape[0]
    dense_copies = [pltpu.make_async_copy(sources[3], buf.at[0:count], dense_in.at[0])]
    for i in (1, 2):
        dense_copies.append(pltpu.make_async_copy(sources[3 + i], dense_slots.at[i], dense_in.at[i]))
    for copy in dense_copies:
        copy.start()

    summed = head_ref.shape[0]
    squares = total_ref[summed : summed + 1]
    for at in range(0, summed, 8):
        part = total_ref[at : at + 8]
        squares = squares + jnp.sum(part * part, axis=0, keepdims=True)
    square_sum = jnp.sum(squares, axis=1, keepdims=True)
    clip = jnp.minimum(1.0, jnp.sqrt(param_count / (square_sum + 1e-06)))
    tiles = gains_ref.shape[1] // LANES
    for which in range(gains_ref.shape[0]):
        for j in range(tiles):
            at = router_rows + which * tiles + j
            gains_ref[which : which + 1, LANES * j : LANES * (j + 1)] = total_ref[at : at + 1]

    for c in range(chunks):
        at = slice(c * rows, (c + 1) * rows)
        for i in range(3):
            arriving(c, i).wait()
            if c >= 4:
                leaving(c - 4, i).wait()
        values = adam_values(clip, held[0][at], held[1][at], held[2][at])
        for i, value in enumerate(values):
            slots[c % 4, i] = value
            leaving(c, i).start()
    for copy in dense_copies:
        copy.wait()
    last = k_ref[0] == devices - 1

    @pl.when(last)
    def _():
        buf[count : count + summed] = total_ref[0:summed]

    @pl.when(jnp.logical_not(last))
    def _():
        buf[count : count + summed] = head_ref[...]

    grad = buf[pl.ds(step * k_ref[0], own), :]
    values = adam_values(clip, grad, dense_m[...], dense_v[...])
    for i, value in enumerate((grad, *values)):
        dense_slots[i] = value
    targets = (dense_outs[3], *dense_outs[:3])
    copies = start_all([dense_slots.at[i] for i in range(4)], targets, dense_sems)
    for c in range(max(0, chunks - 4), chunks):
        for i in range(3):
            leaving(c, i).wait()
    wait_all(copies)


def route_kernel(
    experts, capacity, stride, me_ref, prio_row, prio_col, picks, picks_t, cot,
    cols_ref, near_ref, rows_ref, g_ref,
):
    count = picks.shape[0]
    me = me_ref[0]
    before = (prio_row[...] < prio_col[...]).astype(f32).astype(bf16)
    lane = lax.broadcasted_iota(jnp.int32, (count, experts), 1)
    sub = lax.broadcasted_iota(jnp.int32, (experts, count), 0)
    hot = [(picks[:, j : j + 1] == lane).astype(f32) for j in range(2)]
    hot_t = [(picks_t[j : j + 1, :] == sub).astype(f32) for j in range(2)]
    first = jnp.sum(hot[0], axis=0, keepdims=True)
    first_t = jnp.sum(hot_t[0], axis=1, keepdims=True)
    for j in range(2):
        earlier = dot(before, hot[j].astype(bf16)) + (first if j else 0.0)
        earlier_t = dot_nt(hot_t[j].astype(bf16), before) + (first_t if j else 0.0)
        place = jnp.sum(earlier * hot[j], axis=1, keepdims=True).astype(jnp.int32)
        place_t = jnp.sum(earlier_t * hot_t[j], axis=0, keepdims=True).astype(jnp.int32)
        pick, pick_t = picks[:, j : j + 1], picks_t[j : j + 1, :]
        kept = (place < capacity) & (pick >= 0)
        cols_ref[:, j : j + 1] = jnp.where(kept, pick * stride + place, -1)
        near_ref[:, j : j + 1] = jnp.where(kept, (pick ^ me) * stride + place, -1)
        kept = (place_t < capacity) & (pick_t >= 0)
        rows_ref[j : j + 1, :] = jnp.where(kept, pick_t * stride + place_t, -1)
    first, second = slot_selects(rows_ref, experts * stride)
    g_ref[...] = dot(first + second, cot[...]).astype(bf16)


def slot_selects(rows_ref, slots):
    sub = lax.broadcasted_iota(jnp.int32, (slots, rows_ref.shape[1]), 0)
    return [(rows_ref[j : j + 1, :] == sub).astype(f32).astype(bf16) for j in range(2)]


def token_selects(cols_ref, slots):
    lane = lax.broadcasted_iota(jnp.int32, (cols_ref.shape[0], slots), 1)
    return [(cols_ref[:, j : j + 1] == lane).astype(f32).astype(bf16) for j in range(2)]


def split_lanes(column):
    high = column.astype(bf16).astype(f32)
    rest = column - high
    middle = rest.astype(bf16).astype(f32)
    low = rest - middle
    lane = lax.broadcasted_iota(jnp.int32, (column.shape[0], LANES), 1)
    wide = jnp.where(lane == 0, high, jnp.where(lane == 1, middle, jnp.where(lane == 2, low, 0.0)))
    return wide.astype(bf16)


def head_masks():
    lane = lax.broadcasted_iota(jnp.int32, (1, 2 * HEAD_DIM), 1)
    first = (lane < HEAD_DIM).astype(f32)
    return first.astype(bf16), (1.0 - first).astype(bf16)


def soft_scores(queries, key_rows, key_ok):
    scores = dot_nt(queries, key_rows) * HEAD_DIM ** (-0.5)
    scores = jnp.where(key_ok, scores, -1e30)
    top = jnp.max(scores, axis=-1, keepdims=True)
    raised = jnp.exp(scores - top)
    return raised * (1.0 / jnp.sum(raised, axis=-1, keepdims=True))


def put_chunk(scratch, low, chunk, value, first=0):
    place = chunk ^ low
    scratch[place & 1, place >> 1, first : first + value.shape[0], :] = value


def matrix(w_ref, index):
    per = w_ref.shape[0] // 4
    width = w_ref.shape[2]
    rows = width // per
    return w_ref[index * per : (index + 1) * per, 0:rows, :].reshape(width, width)


def quarter_in(w_ref, q):
    width = w_ref.shape[2]
    rows = width // w_ref.shape[0]
    return w_ref[:, q * rows : (q + 1) * rows, :].reshape(width, width)


def start_all(sources, targets, sems):
    copies = [pltpu.make_async_copy(a, b, sems.at[i]) for i, (a, b) in enumerate(zip(sources, targets))]
    for copy in copies:
        copy.start()
    return copies


def wait_all(copies):
    for copy in copies:
        copy.wait()


def layer_copies(spots, arrays, place_ref, layer, target, sems):
    low, top = place_ref[0], place_ref[1]
    found = []
    for j, (array, before, behind) in enumerate(spots):
        source = arrays[array].at[before + (layer ^ top,) + behind + (pl.ds(0, target.shape[1]),)]
        found.append(pltpu.make_async_copy(source, target.at[j ^ low], sems.at[j ^ low]))
    return found


def attn_fwd(seq, stream_ref, gain, w_ref, out_ref, a_ref, q_ref, k_ref, v_ref, o_ref):
    normed, _ = norm_rows(stream_ref[...])
    a_ref[...] = (normed * gain).astype(bf16)
    for index, ref in enumerate((q_ref, k_ref, v_ref)):
        ref[...] = dot(a_ref[...], matrix(w_ref, index)).astype(bf16)
    count = stream_ref.shape[0]
    key_ok = lax.broadcasted_iota(jnp.int32, (count, count), 1) < seq
    masks = head_masks()
    for pair in range(HEADS // 2):
        lanes = slice(2 * HEAD_DIM * pair, 2 * HEAD_DIM * (pair + 1))
        mixed = None
        for mask in masks:
            soft = soft_scores(q_ref[:, lanes] * mask, k_ref[:, lanes], key_ok).astype(bf16)
            part = dot(soft, v_ref[:, lanes] * mask)
            mixed = part if mixed is None else mixed + part
        o_ref[:, lanes] = mixed.astype(bf16)
    out_ref[...] = stream_ref[...] + dot(o_ref[...], matrix(w_ref, 3))


def attn_bwd(seq, grad_ref, stream_ref, gain, w_ref, q_ref, k_ref, v_ref, out_ref, dq_ref, dk_ref, dv_ref, do_ref):
    do_ref[...] = dot_nt(grad_ref[...].astype(bf16), matrix(w_ref, 3)).astype(bf16)
    count = grad_ref.shape[0]
    key_ok = lax.broadcasted_iota(jnp.int32, (count, count), 1) < seq
    masks = head_masks()
    scale = HEAD_DIM ** (-0.5)
    for pair in range(HEADS // 2):
        lanes = slice(2 * HEAD_DIM * pair, 2 * HEAD_DIM * (pair + 1))
        dq = dk = dv = None
        for mask in masks:
            q_h = q_ref[:, lanes] * mask
            k_h = k_ref[:, lanes] * mask
            do_h = do_ref[:, lanes] * mask
            soft = soft_scores(q_h, k_ref[:, lanes], key_ok)
            dsoft = dot_nt(do_h, v_ref[:, lanes])
            dv_h = dot_tn(soft.astype(bf16), do_h)
            inner = jnp.sum(dsoft * soft, axis=-1, keepdims=True)
            dscore = (soft * (dsoft - inner)).astype(bf16)
            dq_h = dot(dscore, k_h)
            dk_h = dot_tn(dscore, q_h)
            dq = dq_h if dq is None else dq + dq_h
            dk = dk_h if dk is None else dk + dk_h
            dv = dv_h if dv is None else dv + dv_h
        dq_ref[:, lanes] = (dq * scale).astype(bf16)
        dk_ref[:, lanes] = (dk * scale).astype(bf16)
        dv_ref[:, lanes] = dv.astype(bf16)
    back = None
    for index, ref in enumerate((dq_ref, dk_ref, dv_ref)):
        part = dot_nt(ref[...], matrix(w_ref, index))
        back = part if back is None else back + part
    normed, inverse = norm_rows(stream_ref[...])
    addend, gain_grad = norm_back(back, normed, inverse, gain)
    out_ref[...] = grad_ref[...] + addend
    return gain_grad


def leave_chunk(scratch, low, chunk, keep_ref, send_refs, sem):
    place = chunk ^ low
    source = scratch.at[place & 1, place >> 1]

    @pl.when((place & 1) == 0)
    def _():
        pltpu.make_async_copy(source, keep_ref.at[place >> 1], sem).start()

    at = 0
    for ref, count in send_refs:

        @pl.when(((place & 1) == 1) & ((place >> 1) >= at) & ((place >> 1) < at + count))
        def _():
            pltpu.make_async_copy(source, ref.at[(place >> 1) - at], sem).start()

        at += count


def wait_chunks(scratch, low, keep_ref, sems):
    for chunk in range(2 * scratch.shape[1]):
        place = chunk ^ low
        pltpu.make_async_copy(scratch.at[place & 1, place >> 1], keep_ref.at[place >> 1], sems.at[chunk]).wait()


def attn_weights(low, grad_ref, a_ref, o_ref, dq_ref, dk_ref, dv_ref, dw, keep_ref, send_ref, sems):
    rows = dw.shape[2]
    per = grad_ref.shape[1] // rows
    branch = grad_ref[...].astype(bf16)
    for index in range(4):
        left = o_ref if index == 3 else a_ref
        right = branch if index == 3 else (dq_ref, dk_ref, dv_ref)[index][...]
        value = dot_tn(left[...], right)
        for i in range(per):
            put_chunk(dw, low, index * per + i, value[i * rows : (i + 1) * rows].astype(bf16))
            leave_chunk(dw, low, index * per + i, keep_ref, send_ref, sems.at[index * per + i])


def attn_weights_kernel(low_ref, *refs):
    ins, keep_ref, send_ref, refs = refs[:6], refs[6], refs[7], refs[8:]
    held, (dw, in_sems, sems) = refs[:6], refs[6:]
    wait_all(start_all(ins, held, in_sems))
    attn_weights(low_ref[0], *held, dw, keep_ref, [(send_ref, dw.shape[1])], sems)
    wait_chunks(dw, low_ref[0], keep_ref, sems)


def mlp_fwd(stream_ref, gain, w1_ref, w2_ref, out_ref, b_ref, u_ref):
    width = stream_ref.shape[1]
    normed, _ = norm_rows(stream_ref[...])
    b_ref[...] = (normed * gain).astype(bf16)
    total = None
    for q in range(4):
        pre = dot(b_ref[...], quarter_in(w1_ref, q))
        u_ref[:, q * width : (q + 1) * width] = pre
        part = dot((pre * normal_cdf(pre)).astype(bf16), matrix(w2_ref, q))
        total = part if total is None else total + part
    out_ref[...] = stream_ref[...] + total


def forward_kernel(seq, spots, dims, by_core, place_ref, stream_ref, picks_ref, rows_ref, *refs):
    rows, experts, count = dims
    arrays, refs = refs[:count], refs[count:]
    if not by_core:
        w1_ref, refs = refs[0], refs[1:]
    outs, refs = refs[:15], refs[15:]
    gains_ref, wr_ref, c_ref, probs_ref, x_ref = refs[:5]
    held, (weights, tails, w_sems, tail_sems, out_sems) = refs[5:20], refs[20:]
    low, top = place_ref[0], place_ref[1]
    per = weights.shape[1]
    copies = {
        layer: layer_copies(spots, arrays, place_ref, layer, weights.at[layer], w_sems.at[layer])
        for layer in (0, 2, 3, 1)
    }
    tail_copies = []
    for j, (array, before, behind) in enumerate(spots):
        source = arrays[array].at[before + (3 ^ top,) + behind + (pl.ds(rows, tails.shape[1]),)]
        tail_copies.append(pltpu.make_async_copy(source, tails.at[j ^ low], tail_sems.at[j]))
    for copy in copies[0] + tail_copies:
        copy.start()
    for copy in copies[0] + tail_copies:
        copy.wait()
    for copy in copies[2] + copies[3] + copies[1]:
        copy.start()
    tail = tails[per - 1].astype(f32)
    gains = [tail[experts + i : experts + i + 1] for i in range(4)]
    gains_ref[...] = tail[experts : experts + 4]
    leaving = []

    def leave(first, last):
        for i in range(first, last):
            leaving.append(pltpu.make_async_copy(held[i], outs[i], out_sems.at[i]))
            leaving[-1].start()

    attn_fwd(seq, stream_ref, gains[0], weights.at[0], *held[0:6])
    leave(0, 6)
    for copy in copies[2] + copies[3]:
        copy.wait()
    mlp_fwd(held[0], gains[1], weights.at[2] if by_core else w1_ref, weights.at[3], *held[6:9])
    leave(6, 9)
    for copy in copies[1]:
        copy.wait()
    attn_fwd(seq, held[6], gains[2], weights.at[1], *held[9:15])
    leave(9, 15)
    wr_ref[...] = router_matrix(tail, stream_ref.shape[1], experts)
    dispatch(held[9], gains[3], wr_ref, picks_ref, rows_ref, c_ref, probs_ref, x_ref)
    for copy in leaving:
        copy.wait()


def mlp_bwd(low, grad_ref, stream_ref, gain, w1_ref, w2_ref, b_ref, u_ref, out_ref, put_first, put_second):
    width = grad_ref.shape[1]
    upper = grad_ref[...].astype(bf16)
    back = None
    for q in range(4):
        pre = u_ref[:, q * width : (q + 1) * width]
        cdf = normal_cdf(pre)
        act = (pre * cdf).astype(bf16)
        put_second(q, dot_tn(act, upper).astype(bf16))
        dact = dot_nt(upper, matrix(w2_ref, q))
        dpre = (dact * (cdf + pre * density(pre))).astype(bf16)
        put_first(q, dot_tn(b_ref[...], dpre).astype(bf16))
        part = dot_nt(dpre, quarter_in(w1_ref, q))
        back = part if back is None else back + part
    normed, inverse = norm_rows(stream_ref[...])
    addend, gain_grad = norm_back(back, normed, inverse, gain)
    out_ref[...] = grad_ref[...] + addend
    return gain_grad


def pick_hots(picks, experts):
    lane = lax.broadcasted_iota(jnp.int32, (picks.shape[0], experts), 1)
    return [(picks[:, j : j + 1] == lane).astype(f32) for j in range(2)]


def softmax_rows(logits):
    raised = jnp.exp(logits - jnp.max(logits, axis=-1, keepdims=True))
    return raised / jnp.sum(raised, axis=-1, keepdims=True)


def router_matrix(flat, width, experts):
    block = width // experts
    row = lax.broadcasted_iota(jnp.int32, (block, width), 0)
    lane = lax.broadcasted_iota(jnp.int32, (block, width), 1)
    mine = (lane // experts == row).astype(f32)
    lane = lax.broadcasted_iota(jnp.int32, (width, experts), 0)
    column = lax.broadcasted_iota(jnp.int32, (width, experts), 1)
    pick = (lax.rem(lane, experts) == column).astype(f32).astype(bf16)
    parts = [dot((mine * flat[i : i + 1]).astype(bf16), pick) for i in range(experts)]
    return jnp.concatenate(parts).astype(bf16)


def dispatch(stream_ref, gain, wr_ref, picks_ref, rows_ref, c_ref, probs_ref, x_ref):
    width = stream_ref.shape[1]
    experts = wr_ref.shape[1]
    normed, _ = norm_rows(stream_ref[...])
    c_ref[...] = (normed * gain).astype(bf16)
    probs = softmax_rows(dot(c_ref[...], wr_ref[...]))
    probs_ref[...] = probs
    hots = pick_hots(picks_ref, experts)
    selects = slot_selects(rows_ref, x_ref.shape[0])
    gates = None
    for j in range(2):
        part = dot(selects[j], split_lanes(jnp.sum(probs * hots[j], axis=-1, keepdims=True)))
        gates = part if gates is None else gates + part
    x_ref[:, 0:width] = dot(selects[0] + selects[1], c_ref[...]).astype(bf16)
    x_ref[:, width:] = gates.astype(bf16)


def add_lanes(wide):
    wide = wide.astype(f32)
    return wide[:, 0:1] + wide[:, 1:2] + wide[:, 2:3]


def expert_kernel(dims, spans, me_ref, x_ref, g_ref, *refs):
    parts, quarter, blocks = dims
    weight_refs, refs = refs[: len(spans)], refs[len(spans) :]
    y_refs, refs = refs[: blocks // 2], refs[blocks // 2 :]
    dx_ref, dy_ref, act_ref, dpre_ref, weights, y_near, y_sum, dx_sum, sems = refs
    q = pl.program_id(0)
    width = g_ref.shape[1]
    half = parts // 2
    me = me_ref[0]

    rows = weights.shape[1] // 2

    def copies(side):
        found = []
        for i, ((place, first), ref) in enumerate(zip(spans, weight_refs)):
            low, high = max(first, side * rows), min(first + ref.shape[0], (side + 1) * rows)
            if low < high:
                target = weights.at[place ^ me, low:high]
                found.append(pltpu.make_async_copy(ref.at[low - first : high - first], target, sems.at[side, i]))
        return found

    staged = 2 * quarter >= width // half and rows >= width

    @pl.when(q == 0)
    def _():
        for copy in copies(0) + copies(1):
            copy.start()
        dy_ref[...] = (add_lanes(x_ref[:, width:]) * g_ref[...].astype(f32)).astype(bf16)
        for copy in copies(0) if staged else copies(0) + copies(1):
            copy.wait()

    if staged:

        @pl.when(q == 1)
        def _():
            for copy in copies(1):
                copy.wait()

    first = weights[0:half, pl.ds(pl.multiple_of(q * quarter, 16), quarter), :].reshape(width, width)
    if 4 * quarter >= width:
        per = 4 * quarter // width
        at = pl.ds(pl.multiple_of(lax.rem(q, per) * width, 16), width)
        second = weights[half + q // per, at, :]
    else:
        per = width // (4 * quarter)
        second = weights[pl.ds(half + q * per, per)].reshape(width, width)
    pre = dot(x_ref[:, 0:width], first)
    cdf = normal_cdf(pre)
    act = (pre * cdf).astype(bf16)
    act_ref[...] = act
    dact = dot_nt(dy_ref[...], second)
    dpre = (dact * (cdf + pre * density(pre))).astype(bf16)
    dpre_ref[...] = dpre
    y_part = dot(act, second)
    dx_part = dot_nt(dpre, first)

    @pl.when(q == 0)
    def _():
        y_sum[...] = y_part
        dx_sum[...] = dx_part

    @pl.when(q > 0)
    def _():
        y_sum[...] += y_part
        dx_sum[...] += dx_part

    @pl.when(q == pl.num_programs(0) - 1)
    def _():
        y = y_sum[...].astype(bf16).astype(f32)
        stride = y.shape[0] // blocks
        for block in range(blocks):
            y_near[block ^ me_ref[1]] = y[block * stride : (block + 1) * stride].astype(bf16)
        for pair, ref in enumerate(y_refs):
            ref[...] = y_near[2 * pair : 2 * pair + 2]
        dx_ref[:, 0:width] = dx_sum[...].astype(bf16)
        gate_grad = jnp.sum(g_ref[...].astype(f32) * y, axis=-1, keepdims=True)
        dx_ref[:, width:] = split_lanes(gate_grad)


def expert_grad_kernel(dims, dp_ref, x_ref, dy_ref, act_ref, dpre_ref, *refs):
    parts, quarter = dims
    out_refs, scratch, sems = refs[:4], refs[-2], refs[-1]
    q = pl.program_id(0)
    me = dp_ref[0]
    width = dy_ref.shape[1]
    half = parts // 2
    rows = scratch.shape[1]
    side_rows = rows // 2

    def leave(owner, first, count, sem):
        place = owner ^ me
        side = first // side_rows
        source = scratch.at[place, pl.ds(first, count)]
        at = pl.ds(pl.multiple_of(lax.rem(first, side_rows), 16), count)
        for which, (bit, index) in enumerate(((1, place >> 1), (half, place & (half - 1)))):
            for taken, ref in enumerate((out_refs[2 * which + 1], out_refs[2 * which])):

                @pl.when((side == which) & (((place & bit) > 0) == (taken == 1)))
                def _():
                    pltpu.make_async_copy(source, ref.at[index, at], sem).start()

    first = dot_tn(x_ref[:, 0:width], dpre_ref[...]).astype(bf16)
    count = width // half
    at = pl.multiple_of(q * quarter, 16)
    for i in range(half):
        scratch[i ^ me, pl.ds(at, quarter), :] = first[i * count : (i + 1) * count]
        leave(i, at, quarter, sems.at[i])
    second = dot_tn(act_ref[...], dy_ref[...]).astype(bf16)
    step = min(width, side_rows)
    for i in range(width // step):
        flat = q * width + i * step
        owner, at = half + flat // rows, pl.multiple_of(lax.rem(flat, rows), 16)
        scratch[owner ^ me, pl.ds(at, step), :] = second[i * step : (i + 1) * step]
        leave(owner, at, step, sems.at[half + i])

    @pl.when(q == pl.num_programs(0) - 1)
    def _():
        whole = out_refs[0].at[0]
        for _ in range(4):
            for i in range(half):
                pltpu.make_async_copy(scratch.at[0, 0:quarter], whole.at[0:quarter], sems.at[i]).wait()
            for i in range(width // step):
                pltpu.make_async_copy(scratch.at[0, 0:step], whole.at[0:step], sems.at[half + i]).wait()


def combine(stream_ref, gain, wr_ref, picks_ref, cols_ref, cot_ref, c_ref, probs_ref, dx_ref, grad_ref):
    width = stream_ref.shape[1]
    experts = wr_ref.shape[1]
    probs = probs_ref[...]
    hots = pick_hots(picks_ref, experts)
    selects = token_selects(cols_ref, dx_ref.shape[0])
    prob_grad = None
    for j in range(2):
        part = add_lanes(dot(selects[j], dx_ref[:, width:])) * hots[j]
        prob_grad = part if prob_grad is None else prob_grad + part
    logit_grad = probs * (prob_grad - jnp.sum(prob_grad * probs, axis=-1, keepdims=True))
    logit_grad = logit_grad.astype(bf16)
    router_grad = dot_tn(c_ref[...], logit_grad)
    back = dot(selects[0] + selects[1], dx_ref[:, 0:width]) + dot_nt(logit_grad, wr_ref[...])
    normed, inverse = norm_rows(stream_ref[...])
    addend, gain_grad = norm_back(back, normed, inverse, gain)
    grad_ref[...] = cot_ref[...].astype(f32) + addend
    return gain_grad, router_grad


def put_router(out_ref, value, scratch):
    width, experts = value.shape
    many = LANES // experts
    scratch[...] = jnp.zeros_like(scratch)
    scratch[:, 0:experts] = value
    total = None
    for m in range(many):
        rows = scratch[pl.ds(m, width // many, stride=many), :]
        rows = pltpu.roll(rows, m * experts, 1) if m else rows
        total = rows if total is None else total + rows
    out_ref[0 : width // many, :] = total


def backward_kernel(
    seq, spots, count, by_core, place_ref, gains_ref, wr_ref, picks_ref, cols_ref, cot_ref, probs_ref, dx_ref, *refs
):
    ins, refs = refs[:15], refs[15:]
    arrays, refs = refs[:count], refs[count:]
    if not by_core:
        w1_ref, refs = refs[0], refs[1:]
    small_ref, upper_out, dq_out, dk_out, dv_out, grad_out, *refs = refs
    keep_ref, send_ref, keeps_ref, send2_ref, send_rest, *refs = refs
    places = send_ref.shape[0]
    most, rest = send2_ref.shape[0], places - send2_ref.shape[0]
    keeps = (keep_ref, keeps_ref.at[0])
    sends = ([(send_ref, places)], [(send2_ref, most), (send_rest.at[0], rest)])
    if by_core:
        send1_ref, *refs = refs
        keep1_ref, send1 = keeps_ref.at[1], [(send1_ref, most), (send_rest.at[1], rest)]
    else:
        dw1_ref, *refs = refs
    held, refs = refs[:15], refs[15:]
    grads, refs = refs[:4], refs[4:]
    dq_ref, dk_ref, dv_ref, do_ref, dw, dw2, w2_ref, w_attn, *refs = refs
    if by_core:
        dw1, w1_ref, *refs = refs
    router_scratch, in_sems, w_sems, out_sems, last_sems = refs
    low = place_ref[0]
    experts = wr_ref.shape[1]

    def fetch(first, last):
        copies = [pltpu.make_async_copy(ins[i], held[i], in_sems.at[i]) for i in range(first, last)]
        for copy in copies:
            copy.start()
        return copies

    def fetch_layer(layer, target, at):
        copies = layer_copies(spots, arrays, place_ref, layer, target, w_sems.at[at])
        for copy in copies:
            copy.start()
        return copies

    part = fetch(0, 2)
    second = fetch_layer(1, w_attn.at[0], 0) + fetch(2, 8)
    wait_all(part)
    gain_four, router_grad = combine(
        held[0], gains_ref[3:4], wr_ref, picks_ref, cols_ref, cot_ref, held[1], probs_ref, dx_ref, grads[0]
    )
    tiles = router_grad.shape[0] // LANES
    router_rows = router_grad.shape[0] * experts // LANES
    small_ref[...] = jnp.zeros_like(small_ref)
    put_router(small_ref, router_grad, router_scratch)

    def put_gain(which, value):
        at = router_rows + which * tiles
        for j in range(tiles):
            small_ref[at + j : at + j + 1, :] = value[:, LANES * j : LANES * (j + 1)]

    put_gain(3, gain_four)
    middle = fetch(8, 11) + fetch_layer(3, w2_ref, 1)
    if by_core:
        middle += fetch_layer(2, w1_ref, 2)
    wait_all(second)
    stream, q, k, v, a, o = held[2:8]
    gain_three = attn_bwd(
        seq, grads[0], stream, gains_ref[2:3], w_attn.at[0], q, k, v, grads[1], dq_ref, dk_ref, dv_ref, do_ref
    )
    put_gain(2, gain_three)
    attn_weights(low, grads[0], a, o, dq_ref, dk_ref, dv_ref, dw, keeps[0], sends[0], out_sems.at[0])
    first = fetch(11, 15) + fetch_layer(0, w_attn.at[1], 3)
    wait_all(middle)
    stream, b, u = held[8:11]
    width = stream.shape[1]
    groups = w1_ref.shape[0]

    def put_first(q, value):
        rows = width // groups
        for i in range(groups):
            piece = value[i * rows : (i + 1) * rows]
            if by_core:
                put_chunk(dw1, low, i, piece, q * rows)
                if q == 3:
                    leave_chunk(dw1, low, i, keep1_ref, send1, out_sems.at[2, i])
            else:
                dw1_ref[i, q * rows : (q + 1) * rows, :] = piece

    def put_second(q, value):
        rows = dw2.shape[2]
        per = width // rows
        for i in range(per):
            put_chunk(dw2, low, q * per + i, value[i * rows : (i + 1) * rows])
            leave_chunk(dw2, low, q * per + i, keeps[1], sends[1], out_sems.at[1, q * per + i])

    gain_two = mlp_bwd(
        low, grads[1], stream, gains_ref[1:2], w1_ref, w2_ref, b, u, grads[2], put_first, put_second
    )
    put_gain(1, gain_two)
    leaving = start_all((grads[2],), (upper_out,), last_sems)
    wait_all(first)
    wait_chunks(dw, low, keeps[0], out_sems.at[0])
    stream, q, k, v = held[11:15]
    gain_one = attn_bwd(
        seq, grads[2], stream, gains_ref[0:1], w_attn.at[1], q, k, v, grads[3], dq_ref, dk_ref, dv_ref, do_ref
    )
    put_gain(0, gain_one)
    outs = ((dq_ref, dq_out), (dk_ref, dk_out), (dv_ref, dv_out), (grads[3], grad_out))
    for i, (source, target) in enumerate(outs):
        leaving.append(pltpu.make_async_copy(source, target, last_sems.at[1 + i]))
        leaving[-1].start()
    wait_chunks(dw2, low, keeps[1], out_sems.at[1])
    if by_core:
        wait_chunks(dw1, low, keep1_ref, out_sems.at[2])
    wait_all(leaving)


def output_kernel(stream_ref, picks_ref, near_ref, probs_ref, grad_ref, *refs):
    y_refs, (other_ref, out_ref, grad_out, wide) = refs[:-4], refs[-4:]
    stride = other_ref.shape[1]
    for pair, ref in enumerate(y_refs):
        wide[2 * pair * stride : (2 * pair + 1) * stride] = ref[0].astype(f32)
        wide[(2 * pair + 1) * stride : (2 * pair + 2) * stride] = other_ref[pair].astype(f32)
    y = wide[...].astype(bf16)
    tiles = stream_ref.shape[1] // LANES
    seq = out_ref.shape[0] // tiles
    probs = probs_ref[...]
    hots = pick_hots(picks_ref, probs.shape[1])
    selects = token_selects(near_ref, y.shape[0])
    total = stream_ref[...]
    for j in range(2):
        gate = jnp.sum(probs * hots[j], axis=-1, keepdims=True)
        total = total + gate * dot(selects[j], y)
    for value, ref in ((total, out_ref), (grad_ref, grad_out)):
        for j in range(tiles):
            ref[pl.ds(j, seq, stride=tiles), :] = value[0:seq, LANES * j : LANES * (j + 1)]


def add_pair(left, right):
    return (left.astype(f32) + right.astype(f32)).astype(bf16)


def pack_sets_kernel(*refs):
    out_ref = refs[-1]
    for i, ref in enumerate(refs[:-1]):
        out_ref[i // 4, i % 4] = ref[...]


def fold_layers_kernel(cut, plan, top_ref, *refs):
    uppers, (send_x, keep_x, send_y, keep_y), scratch = refs[-14:-10], refs[-10:-6], refs[-6:]
    kept, got, total, keep_sems, got_sems, out_sems = scratch
    count = kept.shape[1]
    middle = send_x.shape[2]
    ins = []
    for layer, at, sources in plan:
        keep_ref, refs = refs[0], refs[1:]
        keep_ref = keep_ref if at is None else keep_ref.at[at]
        got_refs = []
        for index, many in sources:
            ref, refs = refs[0], refs[1:]
            ref = ref if index is None else ref.at[index]
            got_refs += [ref.at[i] for i in range(many)]
        ins.append((layer, keep_ref, got_refs))

    def arriving(n, i):
        _, keep_ref, got_refs = ins[n]
        return (
            pltpu.make_async_copy(keep_ref.at[i], kept.at[n, i], keep_sems.at[n, i]),
            pltpu.make_async_copy(got_refs[i], got.at[n, i], got_sems.at[n, i]),
        )

    steps = [(n, i) for n in range(len(ins)) for i in range(count)]
    for n, i in steps:
        for copy in arriving(n, i):
            copy.start()
    for n, i in steps:
        layer = ins[n][0]
        place = layer ^ top_ref[0]
        for copy in arriving(n, i):
            copy.wait()
        total[n, i] = add_pair(kept[n, i], got[n, i])
        pltpu.make_async_copy(total.at[n, i, 0:cut], uppers[i % 4].at[layer, i // 4], out_sems.at[n, 0, i]).start()
        for bit, send, keep, at, where, sem in (
            (place & 1, send_x, keep_x, place >> 1, slice(cut, cut + middle), out_sems.at[n, 1, i]),
            (place >> 1, send_y, keep_y, place & 1, slice(cut + middle, cut + 2 * middle), out_sems.at[n, 2, i]),
        ):
            for value, target in ((0, keep), (1, send)):

                @pl.when(bit == value)
                def _():
                    pltpu.make_async_copy(total.at[n, i, where], target.at[at, i], sem).start()

    for n, i in steps:
        layer = ins[n][0]
        pltpu.make_async_copy(total.at[n, i, 0:cut], uppers[i % 4].at[layer, i // 4], out_sems.at[n, 0, i]).wait()
        for part in (1, 2):
            pltpu.make_async_copy(total.at[n, i, cut : cut + middle], keep_x.at[0, i], out_sems.at[n, part, i]).wait()


def add_kernel(left, right, out_ref):
    out_ref[...] = add_pair(left[...], right[...])


def pause_kernel(ref, out_ref):
    for i in range(ref.shape[0]):
        out_ref[i] = ref[i]


def fold_plane_kernel(keep_x, got_x, keep_y, got_y, own_a, send_y, own_b, send_x):
    for keep, got, own, send in ((keep_x, got_x, own_a, send_y), (keep_y, got_y, own_b, send_x)):
        own[...] = add_pair(keep[0], got[0])
        send[...] = add_pair(keep[1], got[1])


def fold_rows_kernel(own_a, got_a, own_b, got_b, *outs):
    middle = own_a.shape[1]
    for place in range(own_a.shape[0]):
        out = outs[place % 4].at[place // 4]
        out[0:middle] = add_pair(own_a[place], got_a[place])
        out[middle:] = add_pair(own_b[place], got_b[place])


def fold_uppers_kernel(top_ref, *refs):
    refs, outs, scratch = refs[:-5], refs[-5:-1], refs[-1]
    for layer in range(4):
        scratch[layer ^ top_ref[0]] = sum(ref[layer].astype(f32) for ref in refs).astype(bf16)
    for place, out in enumerate(outs):
        out[...] = scratch[place]


def fold_expert_kernel(highs, *refs):
    ins, outs = refs[:4], refs[4:]
    count = ins[0].shape[0]
    for side, high in enumerate(highs):
        half = count // 2
        for i in range(count):
            which, at = (i // half, i % half) if high else (i % 2, i // 2)
            outs[side * count + which * half + at][...] = add_pair(ins[2 * side][i], ins[2 * side + 1][i])


def swap(value, axes, mask):
    size = 1
    for axis in axes:
        size *= lax.axis_size(axis)
    return lax.ppermute(value, axes, [(i, i ^ mask) for i in range(size)])


def after(value, *others):
    return lax.optimization_barrier((value, others))[0]


def pause(scalars, rows, others):
    scalars, others = lax.optimization_barrier((scalars, others))
    scalars = pl.pallas_call(
        pause_kernel,
        in_specs=[SMEM],
        out_specs=SMEM,
        out_shape=shape(scalars.shape, jnp.int32),
        compiler_params=params(),
        cost_estimate=cost(rows),
        name="pause",
    )(scalars)
    return scalars, others


class Order:
    def __init__(self):
        self.latest = ()

    def land(self, value):
        self.latest = after(value, self.latest)
        return self.latest


def bit_groups(bits):
    return [bits[i : i + 2] for i in range(0, len(bits), 2)]


def all_sum_step(value, axes, bits):
    if len(bits) == 1:
        return value + swap(value, axes, 1 << bits[0])
    low, high = 1 << bits[0], 1 << bits[1]
    near, far, both = swap(value, axes, low), swap(value, axes, high), swap(value, axes, low | high)
    return (value + near) + (far + both)


def reduce_bits(value, axes, bits):
    for bit in bits:
        pairs = value.reshape((value.shape[0] // 2, 2) + value.shape[1:])
        value = pairs[:, 0] + swap(pairs[:, 1], axes, 1 << bit)
    return value[0]


def shape(dims, dtype=f32):
    return jax.ShapeDtypeStruct(dims, dtype)


def on_device(
    tokens,
    cotangent,
    expert_picks,
    priority,
    dense_master,
    dense_momentum,
    dense_variance,
    expert_master,
    expert_momentum,
    expert_variance,
):
    both = ("dp", "expert")
    dp_ranks = lax.axis_size("dp")
    expert_ranks = lax.axis_size("expert")
    devices = dp_ranks * expert_ranks
    local_experts = expert_master.shape[0]
    experts = local_experts * expert_ranks
    images, seq, width = tokens.shape
    assert local_experts == 1 and images == 1
    assert devices & (devices - 1) == 0 and dp_ranks >= 4
    tiles = width // LANES
    dp_me = lax.axis_index("dp").astype(jnp.int32)
    me = dp_me * expert_ranks + lax.axis_index("expert").astype(jnp.int32)
    me_arr = me.reshape(1)
    dp_arr = dp_me.reshape(1)
    dp_bits = dp_ranks.bit_length() - 1
    all_bits = devices.bit_length() - 1

    own = dense_master.shape[0] // LANES
    expert_flat = expert_master.shape[1] // LANES
    hidden = expert_master.shape[1] * dp_ranks // (2 * width)
    matrix_rows = 8 * width + 2 * hidden
    rows = matrix_rows // devices
    step = own - rows * tiles
    tail = step * devices
    tail_rows = -(-tail // (16 * tiles)) * 16
    wide_ok = rows % 64 == 0
    expert_rows = expert_flat // tiles

    dense_flat = dense_master.reshape(own, LANES)
    forward_ring = [(i, (i + 1) % devices) for i in range(devices)]
    backward_ring = [((i + 1) % devices, i) for i in range(devices)]
    tail_from = lax.ppermute(dense_flat[own - tail :], both, forward_ring)
    buf_rows = -(-(own + max(tail, tail_rows * tiles)) // 8) * 8
    chunk = pl.pallas_call(
        functools.partial(
            pack_dense_kernel, (rows, tail_rows, tail, own, step, tiles, devices, wide_ok)
        ),
        in_specs=[SMEM, VMEM, VMEM],
        out_specs=VMEM,
        out_shape=shape((rows + tail_rows, width), bf16),
        scratch_shapes=[pltpu.VMEM((buf_rows, LANES), f32)],
        compiler_params=params(),
        cost_estimate=cost(),
        name="pack_dense",
    )(me_arr, tail_from, dense_flat)

    expert_wide = (dp_me < dp_ranks // 2).astype(jnp.int32).reshape(1)
    quarter = expert_rows // 4
    cuts = [(0, 2), (2, 4), (0, 1), (1, 2), (2, 3), (3, 4)]
    cuts = [(low * quarter, high * quarter) for low, high in cuts]
    expert_chunks = pl.pallas_call(
        functools.partial(pack_expert_kernel, (expert_rows, tiles), cuts),
        in_specs=[SMEM, VMEM],
        out_specs=[VMEM] * 6,
        out_shape=[shape((high - low, width), bf16) for low, high in cuts],
        compiler_params=params(),
        cost_estimate=cost(),
        name="pack_expert",
    )(expert_wide, expert_master.reshape(expert_flat, LANES))
    dp_axis = ("dp",)
    dp_order = list(range(dp_bits))

    def gather_step(parts, bit):
        return {**parts, **{at | (1 << bit): swap(part, dp_axis, 1 << bit) for at, part in parts.items()}}

    capacity = 2 * seq // experts
    stride = -(-capacity // 8) * 8
    slots = experts * stride
    padded = -(-seq // 16) * 16
    fill = padded - seq
    ranks = jnp.pad(priority, ((0, 0), (0, fill)), constant_values=1 << 20)
    picks = jnp.pad(expert_picks, ((0, fill), (0, 0)), constant_values=-1)
    cot = jnp.pad(cotangent.reshape(seq, width), ((0, fill), (0, 0)))
    stream = jnp.pad(tokens.reshape(seq, width).astype(f32), ((0, fill), (0, 0)))
    e_me = lax.axis_index("expert").astype(jnp.int32).reshape(1)
    pair_shape = shape((2, stride, width), bf16)
    cols, near_cols, rows_slots, outgoing_cot = pl.pallas_call(
        functools.partial(route_kernel, experts, capacity, stride),
        in_specs=[SMEM] + [VMEM] * 5,
        out_specs=[VMEM] * 4,
        out_shape=[shape((padded, 2), jnp.int32)] * 2
        + [shape((2, padded), jnp.int32), shape((slots, width), bf16)],
        compiler_params=params(),
        cost_estimate=cost(),
        name="route",
    )(e_me, ranks, ranks.reshape(padded, 1), picks, picks.T, cot)

    def exchange(value):
        dims = value.shape
        value = value.reshape(expert_ranks, slots // expert_ranks, dims[1])
        value = lax.all_to_all(value, "expert", split_axis=0, concat_axis=0, tiled=True)
        return value.reshape(dims)

    per = devices // 4
    per_bits = per.bit_length() - 1
    top_bits = (per_bits, per_bits + 1)
    chunk_rows = rows + tail_rows
    low = me & (per - 1)
    low_arr = low.reshape(1)
    place_arr = jnp.stack([low, me >> per_bits])
    expert_me = jnp.concatenate([dp_arr, e_me])
    half_rows = expert_rows // 2
    orders = (dp_order, dp_order[::-1])
    expert_parts, expert_spans = [], []
    if per_bits == 3 and dp_bits == 2:
        masks = [1 << bit for bit in top_bits]
        split = chunk_rows // 32 * 16 + 16
        order = Order()

        def spread(value):
            return [swap(value, both, mask) for mask in masks]

        sets = [chunk, swap(chunk, both, 2), None, None]
        near, far = [spread(chunk)] + [None] * 3, [None] * 4
        near[0] = order.land(near[0])
        sets[1] = order.land(sets[1])
        near[1] = spread(sets[1])
        sets[2] = swap(after(chunk, sets[1]), both, 4)
        halves = [swap(near[0][1][:split], both, masks[0]), swap(near[0][0][split:], both, masks[1])]
        near[1] = order.land(near[1])
        halves = order.land(halves)
        x_half, y_half, *quarters = expert_chunks
        early = [swap(quarters[2], dp_axis, 1), swap(quarters[0], dp_axis, 2)]
        early, outgoing_cot, stream = order.land((early, outgoing_cot, stream))
        sets[2] = order.land(sets[2])
        sets[3] = swap(sets[2], both, 2)
        near[2] = spread(sets[2])
        far[0] = jnp.concatenate(halves)
        sets[3], far[0] = order.land((sets[3], far[0]))
        far[1], far[2] = swap(far[0], both, 2), swap(far[0], both, 4)
        near[3] = spread(sets[3])
        near[2] = order.land(near[2])
        near[3] = order.land(near[3])
        far[1] = order.land(far[1])
        far[2] = order.land(far[2])
        place_arr, far[2] = pause(place_arr, 200, far[2])
        far[3] = swap(far[2], both, 2)
        arriving_cot = exchange(after(outgoing_cot, far[2]))

        def pack_sets(which):
            ins = [part for s in which for part in (sets[s], *near[s], far[s])]
            return pl.pallas_call(
                pack_sets_kernel,
                in_specs=[VMEM] * len(ins),
                out_specs=VMEM,
                out_shape=shape((len(which), 4, chunk_rows, width), bf16),
                compiler_params=params(),
                cost_estimate=cost(),
                name="pack_sets",
            )(*ins)

        packed = [pack_sets([0, 1])]
        far[3], packed = lax.optimization_barrier((far[3], packed))
        far[3] = order.land(far[3])
        packed.append(pack_sets([2, 3]))
        arrays = packed + [swap(value, both, 1) for value in packed]
        spots = [((j >> 2) + 2 * (j & 1), ((j >> 1) & 1,), ()) for j in range(per)]
        x_out, y_out = after((x_half, y_half), near[3])
        beside = [swap(x_out, dp_axis, 1), swap(y_out, dp_axis, 2)]
        place_arr, beside = pause(place_arr, 3000, beside)
        across = [swap(beside[0], dp_axis, 2), swap(beside[1], dp_axis, 1)]
        late = after((quarters[3], quarters[1]), beside)
        late = [swap(late[0], dp_axis, 1), swap(late[1], dp_axis, 2)]
        place_arr, arrays[2] = pause(place_arr, 300, arrays[2])
        expert_me, (across, arriving_cot) = pause(expert_me, 400, (across, arriving_cot))
        expert_parts = [x_half, y_half, beside[0], early[0], late[0], beside[1], early[1], late[1], *across]
        expert_spans = [(0, 0), (0, 2), (1, 0), (1, 2), (1, 3), (2, 2), (2, 0), (2, 1), (3, 0), (3, 2)]
        expert_spans = [(place, first * quarter) for place, first in expert_spans]
    else:
        gathered = chunk[None]
        for bit in range(all_bits):
            gathered = jnp.concatenate([gathered, swap(gathered, both, 1 << bit)])
        arrays = [gathered.reshape(4, per, chunk_rows, width)]
        spots = [(0, (), (j,)) for j in range(per)]
        for side, bits in enumerate(orders):
            parts, places = [expert_chunks[side]], [0]
            for bit in bits:
                parts = parts + [swap(part, dp_axis, 1 << bit) for part in parts]
                places = places + [place | (1 << bit) for place in places]
            expert_parts += parts
            expert_spans += [(place, side * half_rows) for place in places]
        arriving_cot = exchange(outgoing_cot)

    layer_w = pltpu.VMEM((per, rows, width), bf16)
    if not wide_ok:
        first_in = lax.dynamic_index_in_dim(arrays[0], 2 ^ (me >> per_bits), 0, keepdims=False)
        first_in = jnp.take(first_in, jnp.arange(per) ^ low, axis=0)[:, :rows].reshape(width, 4, width)
        first_in = first_in.transpose(1, 0, 2).reshape(1, 4 * width, width)

    act_shape = shape((padded, width), bf16)
    stream_shape = shape((padded, width), f32)
    gain_shape = shape((1, width), f32)
    tok_flops = 2 * padded * width * width
    weight_bytes = 2 * width * width
    ANY = pl.BlockSpec(memory_space=pl.ANY)

    def call(kernel, ins, in_specs, outs, name, rows=0, mib=56, out_specs=None, scratch=(), aliases=None):
        out_specs = out_specs or [None] * len(outs)

        def whole(a):
            return pl.BlockSpec(a.shape, lambda *_, n=len(a.shape): (0,) * n)

        return pl.pallas_call(
            kernel,
            grid=(1,),
            in_specs=[s or whole(a) for a, s in zip(ins, in_specs, strict=True)],
            out_specs=[s or whole(a) for a, s in zip(outs, out_specs, strict=True)],
            out_shape=outs,
            scratch_shapes=list(scratch),
            compiler_params=params(mib),
            cost_estimate=cost(rows),
            input_output_aliases=aliases or {},
            name=name,
        )(*ins)

    places = per // 2
    core_shape = shape((places, rows, width), bf16)
    by_core = pltpu.VMEM((2, places, rows, width), bf16)
    stream_vmem, act_vmem = pltpu.VMEM((padded, width), f32), pltpu.VMEM((padded, width), bf16)

    def attn_weights_call(grad, kept, found):
        return call(
            attn_weights_kernel,
            (low_arr, grad, kept[0], kept[4], *found),
            (SMEM,) + (ANY,) * 6,
            [core_shape, core_shape],
            "attn_weights",
            0,
            out_specs=[ANY] * 2,
            scratch=[
                stream_vmem,
                *[act_vmem] * 5,
                by_core,
                pltpu.SemaphoreType.DMA((6,)),
                pltpu.SemaphoreType.DMA((per,)),
            ],
        )

    outs = [stream_shape] + [act_shape] * 5 + [stream_shape, act_shape, shape((padded, hidden), f32)]
    outs += [stream_shape] + [act_shape] * 5
    *results, gains, router, moe_in, probs, outgoing = call(
        functools.partial(forward_kernel, seq, spots, (rows, experts, len(arrays)), wide_ok),
        (place_arr, stream, picks, rows_slots, *arrays, *([] if wide_ok else [first_in])),
        (SMEM, None, None, None) + (ANY,) * len(arrays) + (() if wide_ok else (None,)),
        outs
        + [
            shape((4, width)),
            shape((width, experts), bf16),
            act_shape,
            shape((padded, experts)),
            shape((slots, width + LANES), bf16),
        ],
        "forward",
        0,
        out_specs=[ANY] * 15 + [None] * 5,
        scratch=[pltpu.VMEM(o.shape, o.dtype) for o in outs]
        + [
            pltpu.VMEM((4, per, rows, width), bf16),
            pltpu.VMEM((per, tail_rows, width), bf16),
            pltpu.SemaphoreType.DMA((4, per)),
            pltpu.SemaphoreType.DMA((per,)),
            pltpu.SemaphoreType.DMA((15,)),
        ],
    )
    stream_one, kept_one = results[0], results[1:6]
    stream_two, mlp_in, mlp_pre = results[6:9]
    stream_three, kept_two = results[9], results[10:]
    arriving = exchange(outgoing)

    slot_spec = pl.BlockSpec((slots, width), lambda q: (0, 0))
    wide_spec = pl.BlockSpec((slots, width + LANES), lambda q: (0, 0))
    pair_spec = pl.BlockSpec((2, stride, width), lambda q: (0, 0, 0))
    hidden_spec = pl.BlockSpec((slots, width), lambda q: (0, q))
    pairs = experts // 2
    *expert_out, input_back, slot_grad, expert_act, pre_grad = pl.pallas_call(
        functools.partial(expert_kernel, (dp_ranks, quarter, experts), expert_spans),
        grid=(4,),
        in_specs=[SMEM, wide_spec, slot_spec] + [ANY] * len(expert_parts),
        out_specs=[pair_spec] * pairs + [wide_spec, slot_spec, hidden_spec, hidden_spec],
        out_shape=[pair_shape] * pairs
        + [shape((slots, width + LANES), bf16), shape((slots, width), bf16)]
        + [shape((slots, hidden), bf16)] * 2,
        scratch_shapes=[
            pltpu.VMEM((dp_ranks, expert_rows, width), bf16),
            pltpu.VMEM((experts, stride, width), bf16),
            pltpu.VMEM((slots, width), f32),
            pltpu.VMEM((slots, width), f32),
            pltpu.SemaphoreType.DMA((2, len(expert_parts))),
        ],
        compiler_params=params(),
        cost_estimate=cost(),
        name="expert",
    )(expert_me, arriving, arriving_cot, *expert_parts)
    returned_grad = exchange(input_back)
    part_shape = shape((expert_rows // 2, width), bf16)
    count = dp_ranks // 2
    expert_first = pl.pallas_call(
        functools.partial(expert_grad_kernel, (dp_ranks, quarter)),
        grid=(4,),
        in_specs=[SMEM, wide_spec, slot_spec, hidden_spec, hidden_spec],
        out_specs=[ANY] * 4,
        out_shape=[shape((count,) + part_shape.shape, bf16)] * 4,
        scratch_shapes=[
            pltpu.VMEM((dp_ranks, expert_rows, width), bf16),
            pltpu.SemaphoreType.DMA((2 * dp_ranks,)),
        ],
        compiler_params=params(),
        cost_estimate=cost(),
        name="expert_grad",
    )(dp_arr, arriving, slot_grad, expert_act, pre_grad)
    returned_grad = after(returned_grad, expert_first)

    cut = max(16, rows // 48 * 16)
    middle = (rows - cut) // 2
    top = (me >> per_bits).reshape(1)
    z_bits = list(range(1, per_bits))
    z_masks = [2 * j for j in (1, 2, 3)]
    assert places % 4 == 0

    def add_call(left, right):
        return call(add_kernel, (left, right), (None, None), [shape(left.shape, bf16)], "add", mib=12)[0]

    def over_z(values, meanwhile=None):
        farthest = swap(values[3], both, 2)
        if meanwhile is not None:
            farthest, *meanwhile[:] = lax.optimization_barrier((farthest, *meanwhile))
        near = swap(after(values[1], farthest), both, 2)
        return [values[0], near, swap(add_call(values[2], farthest), both, 4)]

    def rest_of_z(values):
        if len(z_bits) == 2:
            return values
        total = sum(value.astype(f32) for value in values).astype(bf16)
        lead = total.ndim - 3
        total = jnp.moveaxis(total, lead, 0)
        return [reduce_bits(total, both, z_bits[2:])]

    def to_other_core(parts):
        return [parts[0], swap(parts[1], both, 1)]

    expert_got = [swap(expert_first[0], dp_axis, 1), swap(expert_first[2], dp_axis, dp_ranks // 2)]
    returned_grad, expert_out = lax.optimization_barrier((returned_grad, expert_out))
    expert_out = [expert_out[0]] + [swap(v, ("expert",), 2 * j) for j, v in enumerate(expert_out) if j]
    backward_ins = (
        (stream_three, moe_in, stream_two, *kept_two[1:4], kept_two[0], kept_two[4])
        + (stream_one, mlp_in, mlp_pre, stream, *kept_one[1:4])
    )
    held_vmem = [stream_vmem, act_vmem, stream_vmem] + [act_vmem] * 5
    held_vmem += [stream_vmem, act_vmem, pltpu.VMEM((padded, hidden), f32), stream_vmem] + [act_vmem] * 3
    kinds = 2 if wide_ok else 1
    most, rest = places * 3 // 4, places // 4
    keeps_shape = shape((kinds,) + core_shape.shape, bf16)
    most_shape, rest_shape = shape((most, rows, width), bf16), shape((kinds, rest, rows, width), bf16)
    first_dw_out = [most_shape] if wide_ok else [shape((1, 4 * width, width), bf16)]
    small, upper, dq, dk, dv, grad, *dws = call(
        functools.partial(backward_kernel, seq, spots, len(arrays), wide_ok),
        (place_arr, gains, router, picks, cols, cot, probs, returned_grad, *backward_ins, *arrays)
        + (() if wide_ok else (first_in,)),
        (SMEM,) + (None,) * 7 + (ANY,) * (15 + len(arrays)) + (() if wide_ok else (None,)),
        [shape((tail, LANES)), stream_shape, act_shape, act_shape, act_shape, stream_shape]
        + [core_shape, core_shape, keeps_shape, most_shape, rest_shape]
        + first_dw_out,
        "backward",
        out_specs=[None] + [ANY] * 10 + ([ANY] if wide_ok else [None]),
        scratch=held_vmem
        + [stream_vmem] * 4
        + [act_vmem] * 4
        + [by_core, by_core, layer_w, pltpu.VMEM((2, per, rows, width), bf16)]
        + ([by_core, layer_w] if wide_ok else [])
        + [
            pltpu.VMEM((width, LANES), f32),
            pltpu.SemaphoreType.DMA((15,)),
            pltpu.SemaphoreType.DMA((4, per)),
            pltpu.SemaphoreType.DMA((3, per)),
            pltpu.SemaphoreType.DMA((5,)),
        ],
    )
    if not wide_ok:
        wide_grad = dws[5].reshape(4, width, width).transpose(1, 0, 2).reshape(per, rows, width)
        wide_grad = jnp.take(wide_grad, jnp.arange(per) ^ low, axis=0)
        wide_grad = wide_grad.reshape(places, 2, rows, width)
        dws[2] = jnp.concatenate([dws[2], wide_grad[None, :, 0]])
        dws[4] = jnp.concatenate([dws[4], wide_grad[None, most:, 1]])
        dws[5] = wide_grad[:most, 1]
    dws, expert_out = lax.optimization_barrier((dws, expert_out))
    most_got = [swap(dws[3], both, 1), swap(dws[5], both, 1)]
    rest_got = swap(dws[4], both, 1)
    first_dw = attn_weights_call(upper, kept_one, (dq, dk, dv))
    layer_got = {0: [(swap(first_dw[1], both, 1), None, places)], 1: [(swap(dws[1], both, 1), None, places)]}
    for i, layer in enumerate((3, 2)):
        layer_got[layer] = [(most_got[i], None, most), (rest_got, i, rest)]
    layer_keep = {3: (dws[2], 0), 2: (dws[2], 1), 1: (dws[0], None), 0: (first_dw[0], None)}

    plane_shape = shape((2, places, middle, width), bf16)
    plane_spec = pl.BlockSpec((2, 1, middle, width), lambda i: (0, i, 0, 0))
    line_shape = shape((places, middle, width), bf16)
    line_spec = pl.BlockSpec((1, middle, width), lambda i: (i, 0, 0))
    upper_shape = shape((4, places // 4, cut, width), bf16)
    sums = ()
    for pair in ((3, 2), (1, 0)):
        if pair[0] == 1:
            expert_got, sums = lax.optimization_barrier((expert_got, sums))
            top, expert_got = pause(top, 1600, expert_got)
        plan, ins = [], []
        for layer in pair:
            keep, at = layer_keep[layer]
            parts = layer_got[layer]
            plan.append((layer, at, [part[1:] for part in parts]))
            ins += [after(keep, first_dw) if layer == 3 else keep] + [part[0] for part in parts]
        sums = call(
            functools.partial(fold_layers_kernel, cut, plan),
            (top, *ins, *sums),
            (SMEM,) + (ANY,) * (len(ins) + len(sums)),
            [upper_shape] * 4 + [plane_shape] * 4,
            "fold_layers",
            out_specs=[ANY] * 8,
            scratch=[pltpu.VMEM((2, places, rows, width), bf16)] * 3
            + [
                pltpu.SemaphoreType.DMA((2, places)),
                pltpu.SemaphoreType.DMA((2, places)),
                pltpu.SemaphoreType.DMA((2, 3, places)),
            ],
            aliases={1 + len(ins) + i: i for i in range(len(sums))},
        )
    *uppers, send_x, keep_x, send_y, keep_y = sums
    masks = [1 << bit for bit in top_bits]
    got_x, got_y = swap(send_x, both, masks[0]), swap(send_y, both, masks[1])
    uppers = over_z(uppers)
    expert_ins = (expert_first[1], expert_got[0], expert_first[3], expert_got[1])
    expert_second = call(
        functools.partial(fold_expert_kernel, (dp_bits == 1, True)),
        expert_ins,
        (None,) * len(expert_ins),
        [part_shape] * (2 * count),
        "fold_expert",
        0,
    )

    uppers = [value.reshape(4, -1, cut, width) for value in uppers]
    uppers = [value.reshape(4, cut, width) for value in rest_of_z(uppers)]
    upper_rows = call(
        fold_uppers_kernel,
        (top, *uppers),
        (SMEM,) + (None,) * len(uppers),
        [shape((cut, width), bf16)] * 4,
        "fold_uppers",
        100,
        scratch=[pltpu.VMEM((4, cut, width), bf16)],
    )
    got_x, got_y, expert_second = lax.optimization_barrier((got_x, got_y, expert_second))
    own_a, send_y, own_b, send_x = pl.pallas_call(
        fold_plane_kernel,
        grid=(places,),
        in_specs=[plane_spec] * 4,
        out_specs=[line_spec] * 4,
        out_shape=[line_shape] * 4,
        compiler_params=params(),
        cost_estimate=cost(),
        name="fold_plane",
    )(keep_x, got_x, keep_y, got_y)
    got_y, got_x = swap(send_y, both, masks[1]), swap(send_x, both, masks[0])
    expert_second, upper_rows = lax.optimization_barrier((expert_second, upper_rows))
    other_out = swap(jnp.stack([value[1] for value in expert_out]), ("expert",), 1)
    lower_rows = call(
        fold_rows_kernel,
        (own_a, got_y, own_b, got_x),
        (None,) * 4,
        [shape((places // 4, rows - cut, width), bf16)] * 4,
        "fold_rows",
        0,
    )
    lower_rows, other_out = lax.optimization_barrier((lower_rows, other_out))
    output, grad = call(
        output_kernel,
        (stream_three, picks, near_cols, probs, grad, *expert_out, other_out),
        (None,) * (6 + pairs),
        [shape((seq * tiles, LANES))] * 2,
        "output",
        mib=16,
        scratch=[pltpu.VMEM((slots, width), f32)],
    )
    image = (1, seq, width)
    meanwhile = [output.reshape(image), grad.reshape(image)]
    lower_rows = over_z(lower_rows, meanwhile)
    output, grad = meanwhile
    half = count // 2
    expert_groups = []
    for side, bits in enumerate(orders):
        keep, send = (expert_second[(2 * side + i) * half : (2 * side + i + 1) * half] for i in range(2))
        got = [swap(part, dp_axis, 1 << bits[1]) for part in send]
        expert_groups.append([list(pair) for pair in zip(keep, got)])
    if dp_bits > 2:
        for side, bits in enumerate(orders):
            value = [sum(pair) for pair in expert_groups[side]]
            for bit in bits[2:]:
                half = len(value) // 2
                keep, send = (value[:half], value[half:]) if side else (value[0::2], value[1::2])
                value = [k + swap(v, dp_axis, 1 << bit) for k, v in zip(keep, send)]
            expert_groups[side] = [value]
    expert_groups = [side[0] for side in expert_groups]
    upper_rows, expert_groups = lax.optimization_barrier((upper_rows, expert_groups))

    def unpack(wide, groups, count, name, extra=(), more_shapes=((1, LANES),)):
        pieces = [piece for group in groups for piece in group] + list(extra)
        return pl.pallas_call(
            functools.partial(unpack_kernel, (count, tiles), [len(group) for group in groups]),
            in_specs=[SMEM] + [VMEM] * len(pieces),
            out_specs=[VMEM] * (1 + len(more_shapes)),
            out_shape=[shape((count * tiles, LANES))] + [shape(dims) for dims in more_shapes],
            scratch_shapes=[pltpu.VMEM((count, width), f32)],
            compiler_params=params(),
            cost_estimate=cost(),
            name=name,
        )(wide, *pieces)

    expert_grad, expert_square = unpack(expert_wide, expert_groups, expert_rows, "unpack_expert")
    lower_rows, output, expert_grad, expert_square = lax.optimization_barrier(
        (lower_rows, output, expert_grad, expert_square)
    )
    lower_rows = rest_of_z(lower_rows)
    upper_rows = [upper_rows[0]] + [
        swap(value, both, masks[0] * j) for j, value in enumerate(upper_rows) if j
    ]
    dense_groups = [upper_rows, [value.reshape(rows - cut, width) for value in lower_rows]]

    dense_wide = (me >= devices // 2) & (me < 3 * devices // 4) & wide_ok
    dense_rows, total, head = unpack(
        dense_wide.astype(jnp.int32).reshape(1),
        dense_groups,
        rows,
        "unpack_dense",
        (small, expert_square),
        ((tail + 8, LANES), (tail, LANES)),
    )
    head = lax.ppermute(head, both, backward_ring)
    groups = bit_groups(list(range(all_bits)))
    for bits in groups[:-1]:
        total = all_sum_step(total, both, bits)
    total, head = lax.optimization_barrier((total, head))
    total = all_sum_step(total, both, groups[-1])
    param_count = (dense_master.size + expert_master.size) * devices

    chunks = 16
    results = pl.pallas_call(
        functools.partial(adam_kernel, (step, chunks, devices, param_count, width * experts // LANES)),
        in_specs=[SMEM, VMEM, VMEM] + [ANY] * 6,
        out_specs=[ANY] * 7 + [VMEM],
        out_shape=[shape((expert_flat, LANES))] * 3 + [shape((own, LANES))] * 4 + [shape((4, width))],
        scratch_shapes=[pltpu.VMEM((expert_flat, LANES), f32)] * 3
        + [
            pltpu.VMEM((4, 3, expert_flat // chunks, LANES), f32),
            pltpu.VMEM((-(-(rows * tiles + tail) // 8) * 8, LANES), f32),
            pltpu.VMEM((4, own, LANES), f32),
            pltpu.SemaphoreType.DMA((chunks, 3)),
            pltpu.SemaphoreType.DMA((4, 3)),
            pltpu.SemaphoreType.DMA((3,)),
            pltpu.SemaphoreType.DMA((4,)),
        ],
        compiler_params=params(),
        cost_estimate=cost(),
        name="adam",
    )(
        me_arr,
        total,
        head,
        expert_grad,
        expert_momentum.reshape(expert_flat, LANES),
        expert_variance.reshape(expert_flat, LANES),
        dense_rows,
        dense_momentum.reshape(own, LANES),
        dense_variance.reshape(own, LANES),
    )
    gain_grads = results[7]
    expert_update, momentum_expert, variance_expert = results[:3]
    dense_update, momentum_dense, variance_dense, dense_grad = results[3:7]
    return (
        output,
        grad,
        dense_grad.reshape(dense_master.shape),
        expert_grad.reshape(expert_master.shape),
        dense_update.reshape(dense_master.shape),
        momentum_dense.reshape(dense_master.shape),
        variance_dense.reshape(dense_master.shape),
        expert_update.reshape(expert_master.shape),
        momentum_expert.reshape(expert_master.shape),
        variance_expert.reshape(expert_master.shape),
        gain_grads,
    )


def solution(mesh):
    tokens = P(("dp", "expert"), None, None)
    flat = P(("dp", "expert"))
    pairs = P(("dp", "expert"), None)
    expert = P("expert", "dp")
    return jax.shard_map(
        on_device,
        mesh=mesh,
        in_specs=(tokens, tokens, pairs, pairs, flat, flat, flat, expert, expert, expert),
        out_specs=(tokens, tokens, flat, expert, flat, flat, flat, expert, expert, expert, P()),
        check_vma=False,
    )
```

```python
import functools
import math

import jax
import jax.numpy as jnp
from jax import lax
from jax.experimental import pallas as pl
from jax.experimental.pallas import tpu as pltpu
from jax.sharding import PartitionSpec as P

HEADS = 12
HEAD_DIM = 64
LANES = 128

f32 = jnp.float32
bf16 = jnp.bfloat16

eps_norm = 1e-06
beta_first = 0.9
beta_second = 0.999
adam_eps = 1e-08
adam_step = 10.0

VMEM = pl.BlockSpec(memory_space=pltpu.VMEM)
SMEM = pl.BlockSpec(memory_space=pltpu.SMEM)


def params(mib=56):
    return pltpu.CompilerParams(vmem_limit_bytes=mib << 20)


def cost(rows=0):
    return pl.CostEstimate(flops=1 + int(rows * 16.45e6), bytes_accessed=1, transcendentals=0)


def dot(a, b):
    return lax.dot_general(a, b, (((1,), (0,)), ((), ())), preferred_element_type=f32)


def dot_nt(a, b):
    return lax.dot_general(a, b, (((1,), (1,)), ((), ())), preferred_element_type=f32)


def dot_tn(a, b):
    return lax.dot_general(a, b, (((0,), (0,)), ((), ())), preferred_element_type=f32)


def norm_rows(hidden):
    center = hidden - jnp.mean(hidden, axis=-1, keepdims=True)
    inverse = lax.rsqrt(jnp.mean(center * center, axis=-1, keepdims=True) + eps_norm)
    return center * inverse, inverse


def norm_back(upstream, normed, inverse, gain):
    scaled = upstream * gain
    gain_grad = jnp.sum(upstream * normed, axis=0, keepdims=True)
    centered = (
        scaled
        - jnp.mean(scaled, axis=-1, keepdims=True)
        - normed * jnp.mean(scaled * normed, axis=-1, keepdims=True)
    )
    return inverse * centered, gain_grad


def normal_cdf(v):
    return 0.5 * (1.0 + lax.erf(v * 0.7071067811865476))


def density(v):
    return jnp.exp(-0.5 * v * v) * 0.3989422804014327


def to_rows(read, write, first_q, rows, wide, tiles):
    blocks = 4 if rows % 64 == 0 else 1
    count = rows // blocks
    for b in range(blocks):
        for j in range(tiles):
            if wide:
                write(b * count, count, j, read(first_q + tiles * b + j, count, 4 * tiles))
            else:
                write(b * count, count, j, read(first_q + tiles * count * b + j, count, tiles))


def pack_dense_kernel(dims, k_ref, tail_ref, own_ref, out_ref, buf):
    rows, tail_rows, tail, own, step, tiles, chunks, wide_ok = dims
    buf[0:tail] = tail_ref[...]
    buf[tail : tail + own] = own_ref[...]
    buf[tail + own :] = jnp.zeros((buf.shape[0] - tail - own, LANES), f32)
    k = k_ref[0]
    start = tail - step * k

    def read(first, count, stride):
        return buf[pl.ds(first, count, stride=stride), :]

    def write(first, count, j, value):
        out_ref[first : first + count, LANES * j : LANES * (j + 1)] = value.astype(bf16)

    wide = (k >= chunks // 2) & (k < 3 * chunks // 4) & wide_ok

    if wide_ok:

        @pl.when(wide)
        def _():
            to_rows(read, write, start, rows, True, tiles)

    @pl.when(jnp.logical_not(wide))
    def _():
        to_rows(read, write, start, rows, False, tiles)

    for j in range(tiles):
        write(rows, tail_rows, j, read(own + j, tail_rows, tiles))


def pack_expert_kernel(dims, cuts, wide_ref, own_ref, *out_refs):
    rows, tiles = dims

    def read(first, count, stride):
        return own_ref[pl.ds(first, count, stride=stride), :]

    def write(first, count, j, value):
        value = value.astype(bf16)
        for (low, high), ref in zip(cuts, out_refs):
            start, end = max(first, low), min(first + count, high)
            if start < end:
                ref[start - low : end - low, LANES * j : LANES * (j + 1)] = value[start - first : end - first]

    wide = wide_ref[0] > 0

    @pl.when(wide)
    def _():
        to_rows(read, write, 0, rows, True, tiles)

    @pl.when(jnp.logical_not(wide))
    def _():
        to_rows(read, write, 0, rows, False, tiles)


def add_up(refs):
    return sum(ref[...].astype(f32) for ref in refs)


def unpack_kernel(dims, groups, wide_ref, *refs):
    rows, tiles = dims
    (*refs, rows_ref), small_ref = refs, None
    if len(refs) > sum(groups) + 2:
        *refs, small_ref, before_ref, out_ref, square_ref, head_ref = refs
    else:
        *refs, out_ref, square_ref = refs
    at = 0
    for count in groups:
        value = add_up(refs[:count])
        refs = refs[count:]
        rows_ref[at : at + value.shape[0]] = value
        at += value.shape[0]
    wide = wide_ref[0] > 0

    def store(is_wide):
        total = jnp.zeros((1, LANES), f32)
        quarter = rows // 4
        for q in range(4):
            for j in range(tiles):
                piece = rows_ref[q * quarter : (q + 1) * quarter, LANES * j : LANES * (j + 1)]
                if is_wide:
                    at = pl.ds(tiles * q + j, quarter, stride=4 * tiles)
                else:
                    at = pl.ds(tiles * quarter * q + j, quarter, stride=tiles)
                out_ref[at, :] = piece
                total = total + jnp.sum(piece * piece, axis=0, keepdims=True)
        if small_ref is None:
            square_ref[...] = total
        else:
            count = small_ref.shape[0]
            square_ref[0:count] = small_ref[...]
            square_ref[count:] = jnp.zeros((square_ref.shape[0] - count, LANES), f32)
            square_ref[count : count + 1] = total + before_ref[...]
            head_ref[...] = out_ref[0:count]

    @pl.when(wide)
    def _():
        store(True)

    @pl.when(jnp.logical_not(wide))
    def _():
        store(False)


def adam_values(clip, grad, momentum, variance):
    clipped = grad * clip
    momentum_new = beta_first * momentum + (1.0 - beta_first) * clipped
    variance_new = beta_second * variance + (1.0 - beta_second) * clipped * clipped
    first_hat = momentum_new / (1.0 - beta_first**adam_step)
    second_hat = variance_new / (1.0 - beta_second**adam_step)
    return -first_hat / (jnp.sqrt(second_hat) + adam_eps), momentum_new, variance_new


def adam_kernel(dims, k_ref, total_ref, head_ref, *refs):
    step, chunks, devices, param_count, router_rows = dims
    sources, refs = refs[:6], refs[6:]
    outs, dense_outs, gains_ref, refs = refs[:3], refs[3:7], refs[7], refs[8:]
    held, slots, buf, dense_slots, in_sems, sems, dense_in, dense_sems = refs[:3], *refs[3:]
    flat_ref, dense_m, dense_v = dense_slots.at[0], dense_slots.at[1], dense_slots.at[2]
    rows = slots.shape[2]

    def arriving(c, i):
        at = slice(c * rows, (c + 1) * rows)
        return pltpu.make_async_copy(sources[i].at[at], held[i].at[at], in_sems.at[c, i])

    def leaving(c, i):
        target = outs[i].at[c * rows : (c + 1) * rows]
        return pltpu.make_async_copy(slots.at[c % 4, i], target, sems.at[c % 4, i])

    count, own = sources[3].shape[0], sources[4].shape[0]
    dense_copies = [pltpu.make_async_copy(sources[3], buf.at[0:count], dense_in.at[0])]
    for i in (1, 2):
        dense_copies.append(pltpu.make_async_copy(sources[3 + i], dense_slots.at[i], dense_in.at[i]))
    for copy in dense_copies:
        copy.start()
    for c in range(chunks):
        for i in range(3):
            arriving(c, i).start()

    summed = head_ref.shape[0]
    squares = total_ref[summed : summed + 1]
    for at in range(0, summed, 8):
        part = total_ref[at : at + 8]
        squares = squares + jnp.sum(part * part, axis=0, keepdims=True)
    square_sum = jnp.sum(squares, axis=1, keepdims=True)
    clip = jnp.minimum(1.0, jnp.sqrt(param_count / (square_sum + 1e-06)))
    tiles = gains_ref.shape[1] // LANES
    for which in range(gains_ref.shape[0]):
        for j in range(tiles):
            at = router_rows + which * tiles + j
            gains_ref[which : which + 1, LANES * j : LANES * (j + 1)] = total_ref[at : at + 1]

    for copy in dense_copies:
        copy.wait()
    last = k_ref[0] == devices - 1

    @pl.when(last)
    def _():
        buf[count : count + summed] = total_ref[0:summed]

    @pl.when(jnp.logical_not(last))
    def _():
        buf[count : count + summed] = head_ref[...]

    grad = buf[pl.ds(step * k_ref[0], own), :]
    values = adam_values(clip, grad, dense_m[...], dense_v[...])
    for i, value in enumerate((grad, *values)):
        dense_slots[i] = value
    targets = (dense_outs[3], *dense_outs[:3])
    copies = start_all([dense_slots.at[i] for i in range(4)], targets, dense_sems)
    for c in range(chunks):
        at = slice(c * rows, (c + 1) * rows)
        for i in range(3):
            arriving(c, i).wait()
            if c >= 4:
                leaving(c - 4, i).wait()
        values = adam_values(clip, held[0][at], held[1][at], held[2][at])
        for i, value in enumerate(values):
            slots[c % 4, i] = value
            leaving(c, i).start()
    for c in range(max(0, chunks - 4), chunks):
        for i in range(3):
            leaving(c, i).wait()
    wait_all(copies)


def route_kernel(
    experts, capacity, stride, me_ref, prio_row, prio_col, picks, picks_t, cot,
    cols_ref, near_ref, rows_ref, g_ref,
):
    count = picks.shape[0]
    me = me_ref[0]
    before = (prio_row[...] < prio_col[...]).astype(f32).astype(bf16)
    lane = lax.broadcasted_iota(jnp.int32, (count, experts), 1)
    sub = lax.broadcasted_iota(jnp.int32, (experts, count), 0)
    hot = [(picks[:, j : j + 1] == lane).astype(f32) for j in range(2)]
    hot_t = [(picks_t[j : j + 1, :] == sub).astype(f32) for j in range(2)]
    first = jnp.sum(hot[0], axis=0, keepdims=True)
    first_t = jnp.sum(hot_t[0], axis=1, keepdims=True)
    for j in range(2):
        earlier = dot(before, hot[j].astype(bf16)) + (first if j else 0.0)
        earlier_t = dot_nt(hot_t[j].astype(bf16), before) + (first_t if j else 0.0)
        place = jnp.sum(earlier * hot[j], axis=1, keepdims=True).astype(jnp.int32)
        place_t = jnp.sum(earlier_t * hot_t[j], axis=0, keepdims=True).astype(jnp.int32)
        pick, pick_t = picks[:, j : j + 1], picks_t[j : j + 1, :]
        kept = (place < capacity) & (pick >= 0)
        cols_ref[:, j : j + 1] = jnp.where(kept, pick * stride + place, -1)
        near_ref[:, j : j + 1] = jnp.where(kept, (pick ^ me) * stride + place, -1)
        kept = (place_t < capacity) & (pick_t >= 0)
        rows_ref[j : j + 1, :] = jnp.where(kept, pick_t * stride + place_t, -1)
    first, second = slot_selects(rows_ref, experts * stride)
    g_ref[...] = dot(first + second, cot[...]).astype(bf16)


def slot_selects(rows_ref, slots):
    sub = lax.broadcasted_iota(jnp.int32, (slots, rows_ref.shape[1]), 0)
    return [(rows_ref[j : j + 1, :] == sub).astype(f32).astype(bf16) for j in range(2)]


def token_selects(cols_ref, slots):
    lane = lax.broadcasted_iota(jnp.int32, (cols_ref.shape[0], slots), 1)
    return [(cols_ref[:, j : j + 1] == lane).astype(f32).astype(bf16) for j in range(2)]


def split_lanes(column):
    high = column.astype(bf16).astype(f32)
    rest = column - high
    middle = rest.astype(bf16).astype(f32)
    low = rest - middle
    lane = lax.broadcasted_iota(jnp.int32, (column.shape[0], LANES), 1)
    wide = jnp.where(lane == 0, high, jnp.where(lane == 1, middle, jnp.where(lane == 2, low, 0.0)))
    return wide.astype(bf16)


def head_masks():
    lane = lax.broadcasted_iota(jnp.int32, (1, 2 * HEAD_DIM), 1)
    first = (lane < HEAD_DIM).astype(f32)
    return first.astype(bf16), (1.0 - first).astype(bf16)


def soft_scores(queries, key_rows, key_ok):
    scores = dot_nt(queries, key_rows) * HEAD_DIM ** (-0.5)
    scores = jnp.where(key_ok, scores, -1e30)
    top = jnp.max(scores, axis=-1, keepdims=True)
    raised = jnp.exp(scores - top)
    return raised * (1.0 / jnp.sum(raised, axis=-1, keepdims=True))


def put_chunk(scratch, low, chunk, value, first=0):
    place = chunk ^ low
    scratch[place & 1, place >> 1, first : first + value.shape[0], :] = value


def matrix(w_ref, index):
    per = w_ref.shape[0] // 4
    width = w_ref.shape[2]
    rows = width // per
    return w_ref[index * per : (index + 1) * per, 0:rows, :].reshape(width, width)


def quarter_in(w_ref, q):
    width = w_ref.shape[2]
    rows = width // w_ref.shape[0]
    return w_ref[:, q * rows : (q + 1) * rows, :].reshape(width, width)


def start_all(sources, targets, sems):
    copies = [pltpu.make_async_copy(a, b, sems.at[i]) for i, (a, b) in enumerate(zip(sources, targets))]
    for copy in copies:
        copy.start()
    return copies


def wait_all(copies):
    for copy in copies:
        copy.wait()


def layer_copies(spots, arrays, place_ref, layer, target, sems):
    low, top = place_ref[0], place_ref[1]
    found = []
    for j, (array, before, behind) in enumerate(spots):
        source = arrays[array].at[before + (layer ^ top,) + behind + (pl.ds(0, target.shape[1]),)]
        found.append(pltpu.make_async_copy(source, target.at[j ^ low], sems.at[j ^ low]))
    return found


def attn_fwd(seq, stream_ref, gain, w_ref, out_ref, a_ref, q_ref, k_ref, v_ref, o_ref):
    normed, _ = norm_rows(stream_ref[...])
    a_ref[...] = (normed * gain).astype(bf16)
    for index, ref in enumerate((q_ref, k_ref, v_ref)):
        ref[...] = dot(a_ref[...], matrix(w_ref, index)).astype(bf16)
    count = stream_ref.shape[0]
    key_ok = lax.broadcasted_iota(jnp.int32, (count, count), 1) < seq
    masks = head_masks()
    for pair in range(HEADS // 2):
        lanes = slice(2 * HEAD_DIM * pair, 2 * HEAD_DIM * (pair + 1))
        mixed = None
        for mask in masks:
            soft = soft_scores(q_ref[:, lanes] * mask, k_ref[:, lanes], key_ok).astype(bf16)
            part = dot(soft, v_ref[:, lanes] * mask)
            mixed = part if mixed is None else mixed + part
        o_ref[:, lanes] = mixed.astype(bf16)
    out_ref[...] = stream_ref[...] + dot(o_ref[...], matrix(w_ref, 3))


def attn_bwd(seq, grad_ref, stream_ref, gain, w_ref, q_ref, k_ref, v_ref, out_ref, dq_ref, dk_ref, dv_ref, do_ref):
    do_ref[...] = dot_nt(grad_ref[...].astype(bf16), matrix(w_ref, 3)).astype(bf16)
    count = grad_ref.shape[0]
    key_ok = lax.broadcasted_iota(jnp.int32, (count, count), 1) < seq
    masks = head_masks()
    scale = HEAD_DIM ** (-0.5)
    for pair in range(HEADS // 2):
        lanes = slice(2 * HEAD_DIM * pair, 2 * HEAD_DIM * (pair + 1))
        dq = dk = dv = None
        for mask in masks:
            q_h = q_ref[:, lanes] * mask
            k_h = k_ref[:, lanes] * mask
            do_h = do_ref[:, lanes] * mask
            soft = soft_scores(q_h, k_ref[:, lanes], key_ok)
            dsoft = dot_nt(do_h, v_ref[:, lanes])
            dv_h = dot_tn(soft.astype(bf16), do_h)
            inner = jnp.sum(dsoft * soft, axis=-1, keepdims=True)
            dscore = (soft * (dsoft - inner)).astype(bf16)
            dq_h = dot(dscore, k_h)
            dk_h = dot_tn(dscore, q_h)
            dq = dq_h if dq is None else dq + dq_h
            dk = dk_h if dk is None else dk + dk_h
            dv = dv_h if dv is None else dv + dv_h
        dq_ref[:, lanes] = (dq * scale).astype(bf16)
        dk_ref[:, lanes] = (dk * scale).astype(bf16)
        dv_ref[:, lanes] = dv.astype(bf16)
    back = None
    for index, ref in enumerate((dq_ref, dk_ref, dv_ref)):
        part = dot_nt(ref[...], matrix(w_ref, index))
        back = part if back is None else back + part
    normed, inverse = norm_rows(stream_ref[...])
    addend, gain_grad = norm_back(back, normed, inverse, gain)
    out_ref[...] = grad_ref[...] + addend
    return gain_grad


def leave_chunk(scratch, low, chunk, keep_ref, send_refs, sem):
    place = chunk ^ low
    source = scratch.at[place & 1, place >> 1]

    @pl.when((place & 1) == 0)
    def _():
        pltpu.make_async_copy(source, keep_ref.at[place >> 1], sem).start()

    at = 0
    for ref, count in send_refs:

        @pl.when(((place & 1) == 1) & ((place >> 1) >= at) & ((place >> 1) < at + count))
        def _():
            pltpu.make_async_copy(source, ref.at[(place >> 1) - at], sem).start()

        at += count


def wait_chunks(scratch, low, keep_ref, sems):
    for chunk in range(2 * scratch.shape[1]):
        place = chunk ^ low
        pltpu.make_async_copy(scratch.at[place & 1, place >> 1], keep_ref.at[place >> 1], sems.at[chunk]).wait()


def attn_weights(low, grad_ref, a_ref, o_ref, dq_ref, dk_ref, dv_ref, dw, keep_ref, send_ref, sems):
    rows = dw.shape[2]
    per = grad_ref.shape[1] // rows
    branch = grad_ref[...].astype(bf16)
    for index in range(4):
        left = o_ref if index == 3 else a_ref
        right = branch if index == 3 else (dq_ref, dk_ref, dv_ref)[index][...]
        value = dot_tn(left[...], right)
        for i in range(per):
            put_chunk(dw, low, index * per + i, value[i * rows : (i + 1) * rows].astype(bf16))
            leave_chunk(dw, low, index * per + i, keep_ref, send_ref, sems.at[index * per + i])


def attn_weights_kernel(low_ref, *refs):
    ins, keep_ref, send_ref, refs = refs[:6], refs[6], refs[7], refs[8:]
    held, (dw, in_sems, sems) = refs[:6], refs[6:]
    wait_all(start_all(ins, held, in_sems))
    attn_weights(low_ref[0], *held, dw, keep_ref, [(send_ref, dw.shape[1])], sems)
    wait_chunks(dw, low_ref[0], keep_ref, sems)


def mlp_fwd(stream_ref, gain, w1_ref, w2_ref, out_ref, b_ref, u_ref, cdf_ref):
    width = stream_ref.shape[1]
    normed, _ = norm_rows(stream_ref[...])
    b_ref[...] = (normed * gain).astype(bf16)
    total = None
    for q in range(4):
        pre = dot(b_ref[...], quarter_in(w1_ref, q))
        cdf = normal_cdf(pre)
        u_ref[:, q * width : (q + 1) * width] = pre
        cdf_ref[:, q * width : (q + 1) * width] = cdf
        part = dot((pre * cdf).astype(bf16), matrix(w2_ref, q))
        total = part if total is None else total + part
    out_ref[...] = stream_ref[...] + total


def forward_kernel(seq, spots, dims, by_core, place_ref, stream_ref, picks_ref, rows_ref, *refs):
    rows, experts, count = dims
    arrays, refs = refs[:count], refs[count:]
    if not by_core:
        w1_ref, refs = refs[0], refs[1:]
    outs, refs = refs[:16], refs[16:]
    gains_ref, wr_ref, c_ref, probs_ref, x_ref = refs[:5]
    held, (weights, tails, w_sems, tail_sems, out_sems) = refs[5:21], refs[21:]
    low, top = place_ref[0], place_ref[1]
    per = weights.shape[1]
    copies = {
        layer: layer_copies(spots, arrays, place_ref, layer, weights.at[layer], w_sems.at[layer])
        for layer in (0, 2, 3, 1)
    }
    tail_copies = []
    for j, (array, before, behind) in enumerate(spots):
        source = arrays[array].at[before + (3 ^ top,) + behind + (pl.ds(rows, tails.shape[1]),)]
        tail_copies.append(pltpu.make_async_copy(source, tails.at[j ^ low], tail_sems.at[j]))
    for copy in copies[0] + tail_copies:
        copy.start()
    for copy in copies[0] + tail_copies:
        copy.wait()
    for copy in copies[2] + copies[3] + copies[1]:
        copy.start()
    tail = tails[per - 1].astype(f32)
    gains = [tail[experts + i : experts + i + 1] for i in range(4)]
    gains_ref[...] = tail[experts : experts + 4]
    leaving = []

    def leave(first, last):
        for i in range(first, last):
            leaving.append(pltpu.make_async_copy(held[i], outs[i], out_sems.at[i]))
            leaving[-1].start()

    attn_fwd(seq, stream_ref, gains[0], weights.at[0], *held[0:6])
    leave(0, 6)
    for copy in copies[2] + copies[3]:
        copy.wait()
    mlp_fwd(held[0], gains[1], weights.at[2] if by_core else w1_ref, weights.at[3], *held[6:10])
    leave(6, 10)
    for copy in copies[1]:
        copy.wait()
    attn_fwd(seq, held[6], gains[2], weights.at[1], *held[10:16])
    leave(10, 16)
    wr_ref[...] = router_matrix(tail, stream_ref.shape[1], experts)
    dispatch(held[10], gains[3], wr_ref, picks_ref, rows_ref, c_ref, probs_ref, x_ref)
    for copy in leaving:
        copy.wait()


def mlp_bwd(grad_ref, stream_ref, gain, w1_ref, w2_ref, b_ref, u_ref, cdf_ref, out_ref, put_first, put_second):
    width = grad_ref.shape[1]
    upper = grad_ref[...].astype(bf16)
    back = None
    for q in range(4):
        pre = u_ref[:, q * width : (q + 1) * width]
        cdf = cdf_ref[:, q * width : (q + 1) * width]
        act = (pre * cdf).astype(bf16)
        put_second(q, dot_tn(act, upper).astype(bf16))
        dact = dot_nt(upper, matrix(w2_ref, q))
        dpre = (dact * (cdf + pre * density(pre))).astype(bf16)
        put_first(q, dot_tn(b_ref[...], dpre).astype(bf16))
        part = dot_nt(dpre, quarter_in(w1_ref, q))
        back = part if back is None else back + part
    normed, inverse = norm_rows(stream_ref[...])
    addend, gain_grad = norm_back(back, normed, inverse, gain)
    out_ref[...] = grad_ref[...] + addend
    return gain_grad


def pick_hots(picks, experts):
    lane = lax.broadcasted_iota(jnp.int32, (picks.shape[0], experts), 1)
    return [(picks[:, j : j + 1] == lane).astype(f32) for j in range(2)]


def softmax_rows(logits):
    raised = jnp.exp(logits - jnp.max(logits, axis=-1, keepdims=True))
    return raised / jnp.sum(raised, axis=-1, keepdims=True)


def router_matrix(flat, width, experts):
    block = width // experts
    row = lax.broadcasted_iota(jnp.int32, (block, width), 0)
    lane = lax.broadcasted_iota(jnp.int32, (block, width), 1)
    mine = (lane // experts == row).astype(f32)
    lane = lax.broadcasted_iota(jnp.int32, (width, experts), 0)
    column = lax.broadcasted_iota(jnp.int32, (width, experts), 1)
    pick = (lax.rem(lane, experts) == column).astype(f32).astype(bf16)
    parts = [dot((mine * flat[i : i + 1]).astype(bf16), pick) for i in range(experts)]
    return jnp.concatenate(parts).astype(bf16)


def dispatch(stream_ref, gain, wr_ref, picks_ref, rows_ref, c_ref, probs_ref, x_ref):
    width = stream_ref.shape[1]
    experts = wr_ref.shape[1]
    normed, _ = norm_rows(stream_ref[...])
    c_ref[...] = (normed * gain).astype(bf16)
    probs = softmax_rows(dot(c_ref[...], wr_ref[...]))
    probs_ref[...] = probs
    hots = pick_hots(picks_ref, experts)
    selects = slot_selects(rows_ref, x_ref.shape[0])
    gates = None
    for j in range(2):
        part = dot(selects[j], split_lanes(jnp.sum(probs * hots[j], axis=-1, keepdims=True)))
        gates = part if gates is None else gates + part
    x_ref[:, 0:width] = dot(selects[0] + selects[1], c_ref[...]).astype(bf16)
    x_ref[:, width:] = gates.astype(bf16)


def add_lanes(wide):
    wide = wide.astype(f32)
    return wide[:, 0:1] + wide[:, 1:2] + wide[:, 2:3]


def expert_kernel(dims, spans, me_ref, x_ref, g_ref, *refs):
    parts, quarter, blocks = dims
    weight_refs, refs = refs[: len(spans)], refs[len(spans) :]
    y_refs, refs = refs[: blocks // 2], refs[blocks // 2 :]
    dx_ref, dy_ref, act_ref, dpre_ref, weights, y_near, y_sum, dx_sum, sems = refs
    q = pl.program_id(0)
    width = g_ref.shape[1]
    half = parts // 2
    me = me_ref[0]

    rows = weights.shape[1] // 2

    def copies(side):
        found = []
        for i, ((place, first), ref) in enumerate(zip(spans, weight_refs)):
            low, high = max(first, side * rows), min(first + ref.shape[0], (side + 1) * rows)
            if low < high:
                target = weights.at[place ^ me, low:high]
                found.append(pltpu.make_async_copy(ref.at[low - first : high - first], target, sems.at[side, i]))
        return found

    staged = 2 * quarter >= width // half and rows >= width

    @pl.when(q == 0)
    def _():
        for copy in copies(0) + copies(1):
            copy.start()
        dy_ref[...] = (add_lanes(x_ref[:, width:]) * g_ref[...].astype(f32)).astype(bf16)
        for copy in copies(0) if staged else copies(0) + copies(1):
            copy.wait()

    if staged:

        @pl.when(q == 1)
        def _():
            for copy in copies(1):
                copy.wait()

    first = weights[0:half, pl.ds(pl.multiple_of(q * quarter, 16), quarter), :].reshape(width, width)
    if 4 * quarter >= width:
        per = 4 * quarter // width
        at = pl.ds(pl.multiple_of(lax.rem(q, per) * width, 16), width)
        second = weights[half + q // per, at, :]
    else:
        per = width // (4 * quarter)
        second = weights[pl.ds(half + q * per, per)].reshape(width, width)
    pre = dot(x_ref[:, 0:width], first)
    cdf = normal_cdf(pre)
    act = (pre * cdf).astype(bf16)
    act_ref[...] = act
    dact = dot_nt(dy_ref[...], second)
    dpre = (dact * (cdf + pre * density(pre))).astype(bf16)
    dpre_ref[...] = dpre
    y_part = dot(act, second)
    dx_part = dot_nt(dpre, first)

    @pl.when(q == 0)
    def _():
        y_sum[...] = y_part
        dx_sum[...] = dx_part

    @pl.when(q > 0)
    def _():
        y_sum[...] += y_part
        dx_sum[...] += dx_part

    @pl.when(q == pl.num_programs(0) - 1)
    def _():
        y = y_sum[...].astype(bf16).astype(f32)
        stride = y.shape[0] // blocks
        for block in range(blocks):
            y_near[block ^ me_ref[1]] = y[block * stride : (block + 1) * stride].astype(bf16)
        for pair, ref in enumerate(y_refs):
            ref[...] = y_near[2 * pair : 2 * pair + 2]
        dx_ref[:, 0:width] = dx_sum[...].astype(bf16)
        gate_grad = jnp.sum(g_ref[...].astype(f32) * y, axis=-1, keepdims=True)
        dx_ref[:, width:] = split_lanes(gate_grad)


def expert_grad_kernel(dims, dp_ref, x_ref, dy_ref, act_ref, dpre_ref, *refs):
    parts, quarter = dims
    out_refs, scratch, sems = refs[:4], refs[-2], refs[-1]
    q = pl.program_id(0)
    me = dp_ref[0]
    width = dy_ref.shape[1]
    half = parts // 2
    rows = scratch.shape[1]
    side_rows = rows // 2

    def leave(owner, first, count, sem):
        place = owner ^ me
        side = first // side_rows
        source = scratch.at[place, pl.ds(first, count)]
        at = pl.ds(pl.multiple_of(lax.rem(first, side_rows), 16), count)
        for which, (bit, index) in enumerate(((1, place >> 1), (half, place & (half - 1)))):
            for taken, ref in enumerate((out_refs[2 * which + 1], out_refs[2 * which])):

                @pl.when((side == which) & (((place & bit) > 0) == (taken == 1)))
                def _():
                    pltpu.make_async_copy(source, ref.at[index, at], sem).start()

    first = dot_tn(x_ref[:, 0:width], dpre_ref[...]).astype(bf16)
    count = width // half
    at = pl.multiple_of(q * quarter, 16)
    for i in range(half):
        scratch[i ^ me, pl.ds(at, quarter), :] = first[i * count : (i + 1) * count]
        leave(i, at, quarter, sems.at[i])
    second = dot_tn(act_ref[...], dy_ref[...]).astype(bf16)
    step = min(width, side_rows)
    for i in range(width // step):
        flat = q * width + i * step
        owner, at = half + flat // rows, pl.multiple_of(lax.rem(flat, rows), 16)
        scratch[owner ^ me, pl.ds(at, step), :] = second[i * step : (i + 1) * step]
        leave(owner, at, step, sems.at[half + i])

    @pl.when(q == pl.num_programs(0) - 1)
    def _():
        whole = out_refs[0].at[0]
        for _ in range(4):
            for i in range(half):
                pltpu.make_async_copy(scratch.at[0, 0:quarter], whole.at[0:quarter], sems.at[i]).wait()
            for i in range(width // step):
                pltpu.make_async_copy(scratch.at[0, 0:step], whole.at[0:step], sems.at[half + i]).wait()


def combine(stream_ref, gain, wr_ref, picks_ref, cols_ref, cot_ref, c_ref, probs_ref, dx_ref, grad_ref):
    width = stream_ref.shape[1]
    experts = wr_ref.shape[1]
    probs = probs_ref[...]
    hots = pick_hots(picks_ref, experts)
    selects = token_selects(cols_ref, dx_ref.shape[0])
    prob_grad = None
    for j in range(2):
        part = add_lanes(dot(selects[j], dx_ref[:, width:])) * hots[j]
        prob_grad = part if prob_grad is None else prob_grad + part
    logit_grad = probs * (prob_grad - jnp.sum(prob_grad * probs, axis=-1, keepdims=True))
    logit_grad = logit_grad.astype(bf16)
    router_grad = dot_tn(c_ref[...], logit_grad)
    back = dot(selects[0] + selects[1], dx_ref[:, 0:width]) + dot_nt(logit_grad, wr_ref[...])
    normed, inverse = norm_rows(stream_ref[...])
    addend, gain_grad = norm_back(back, normed, inverse, gain)
    grad_ref[...] = cot_ref[...].astype(f32) + addend
    return gain_grad, router_grad


def put_router(out_ref, value, scratch):
    width, experts = value.shape
    many = LANES // experts
    scratch[...] = jnp.zeros_like(scratch)
    scratch[:, 0:experts] = value
    total = None
    for m in range(many):
        rows = scratch[pl.ds(m, width // many, stride=many), :]
        rows = pltpu.roll(rows, m * experts, 1) if m else rows
        total = rows if total is None else total + rows
    out_ref[0 : width // many, :] = total


def backward_kernel(
    seq, spots, count, by_core, place_ref, gains_ref, wr_ref, picks_ref, cols_ref, cot_ref, probs_ref, dx_ref, *refs
):
    ins, refs = refs[:16], refs[16:]
    arrays, refs = refs[:count], refs[count:]
    if not by_core:
        w1_ref, refs = refs[0], refs[1:]
    small_ref, upper_out, dq_out, dk_out, dv_out, grad_out, *refs = refs
    keep_ref, send_ref, keeps_ref, send2_ref, send_rest, *refs = refs
    places = send_ref.shape[0]
    most, rest = send2_ref.shape[0], places - send2_ref.shape[0]
    keeps = (keep_ref, keeps_ref.at[0])
    sends = ([(send_ref, places)], [(send2_ref, most), (send_rest.at[0], rest)])
    if by_core:
        send1_ref, *refs = refs
        keep1_ref, send1 = keeps_ref.at[1], [(send1_ref, most), (send_rest.at[1], rest)]
    else:
        dw1_ref, *refs = refs
    held, refs = refs[:16], refs[16:]
    grads, refs = refs[:4], refs[4:]
    dq_ref, dk_ref, dv_ref, do_ref, dw, dw2, w2_ref, w_attn, *refs = refs
    if by_core:
        dw1, w1_ref, *refs = refs
    router_scratch, in_sems, w_sems, out_sems, last_sems = refs
    low = place_ref[0]
    experts = wr_ref.shape[1]

    def fetch(first, last):
        copies = [pltpu.make_async_copy(ins[i], held[i], in_sems.at[i]) for i in range(first, last)]
        for copy in copies:
            copy.start()
        return copies

    def fetch_layer(layer, target, at):
        copies = layer_copies(spots, arrays, place_ref, layer, target, w_sems.at[at])
        for copy in copies:
            copy.start()
        return copies

    part = fetch(0, 2)
    second = fetch_layer(1, w_attn.at[0], 0) + fetch(2, 8)
    wait_all(part)
    gain_four, router_grad = combine(
        held[0], gains_ref[3:4], wr_ref, picks_ref, cols_ref, cot_ref, held[1], probs_ref, dx_ref, grads[0]
    )
    tiles = router_grad.shape[0] // LANES
    router_rows = router_grad.shape[0] * experts // LANES
    small_ref[...] = jnp.zeros_like(small_ref)
    put_router(small_ref, router_grad, router_scratch)

    def put_gain(which, value):
        at = router_rows + which * tiles
        for j in range(tiles):
            small_ref[at + j : at + j + 1, :] = value[:, LANES * j : LANES * (j + 1)]

    put_gain(3, gain_four)
    middle = fetch(8, 12) + fetch_layer(3, w2_ref, 1)
    if by_core:
        middle += fetch_layer(2, w1_ref, 2)
    wait_all(second)
    stream, q, k, v, a, o = held[2:8]
    gain_three = attn_bwd(
        seq, grads[0], stream, gains_ref[2:3], w_attn.at[0], q, k, v, grads[1], dq_ref, dk_ref, dv_ref, do_ref
    )
    put_gain(2, gain_three)
    attn_weights(low, grads[0], a, o, dq_ref, dk_ref, dv_ref, dw, keeps[0], sends[0], out_sems.at[0])
    first = fetch(12, 16) + fetch_layer(0, w_attn.at[1], 3)
    wait_all(middle)
    stream, b, u, cdf = held[8:12]
    width = stream.shape[1]
    groups = w1_ref.shape[0]

    def put_first(q, value):
        rows = width // groups
        for i in range(groups):
            piece = value[i * rows : (i + 1) * rows]
            if by_core:
                put_chunk(dw1, low, i, piece, q * rows)
                if q == 3:
                    leave_chunk(dw1, low, i, keep1_ref, send1, out_sems.at[2, i])
            else:
                dw1_ref[i, q * rows : (q + 1) * rows, :] = piece

    def put_second(q, value):
        rows = dw2.shape[2]
        per = width // rows
        for i in range(per):
            put_chunk(dw2, low, q * per + i, value[i * rows : (i + 1) * rows])
            leave_chunk(dw2, low, q * per + i, keeps[1], sends[1], out_sems.at[1, q * per + i])

    gain_two = mlp_bwd(
        grads[1], stream, gains_ref[1:2], w1_ref, w2_ref, b, u, cdf, grads[2], put_first, put_second
    )
    put_gain(1, gain_two)
    leaving = start_all((grads[2],), (upper_out,), last_sems)
    wait_all(first)
    wait_chunks(dw, low, keeps[0], out_sems.at[0])
    stream, q, k, v = held[12:16]
    gain_one = attn_bwd(
        seq, grads[2], stream, gains_ref[0:1], w_attn.at[1], q, k, v, grads[3], dq_ref, dk_ref, dv_ref, do_ref
    )
    put_gain(0, gain_one)
    outs = ((dq_ref, dq_out), (dk_ref, dk_out), (dv_ref, dv_out), (grads[3], grad_out))
    for i, (source, target) in enumerate(outs):
        leaving.append(pltpu.make_async_copy(source, target, last_sems.at[1 + i]))
        leaving[-1].start()
    wait_chunks(dw2, low, keeps[1], out_sems.at[1])
    if by_core:
        wait_chunks(dw1, low, keep1_ref, out_sems.at[2])
    wait_all(leaving)


def output_kernel(stream_ref, picks_ref, near_ref, probs_ref, grad_ref, *refs):
    y_refs, (other_ref, out_ref, grad_out, wide) = refs[:-4], refs[-4:]
    stride = other_ref.shape[1]
    for pair, ref in enumerate(y_refs):
        wide[2 * pair * stride : (2 * pair + 1) * stride] = ref[0].astype(f32)
        wide[(2 * pair + 1) * stride : (2 * pair + 2) * stride] = other_ref[pair].astype(f32)
    y = wide[...].astype(bf16)
    tiles = stream_ref.shape[1] // LANES
    seq = out_ref.shape[0] // tiles
    probs = probs_ref[...]
    hots = pick_hots(picks_ref, probs.shape[1])
    selects = token_selects(near_ref, y.shape[0])
    total = stream_ref[...]
    for j in range(2):
        gate = jnp.sum(probs * hots[j], axis=-1, keepdims=True)
        total = total + gate * dot(selects[j], y)
    for value, ref in ((total, out_ref), (grad_ref, grad_out)):
        for j in range(tiles):
            ref[pl.ds(j, seq, stride=tiles), :] = value[0:seq, LANES * j : LANES * (j + 1)]


def add_pair(left, right):
    return (left.astype(f32) + right.astype(f32)).astype(bf16)


def pack_sets_kernel(*refs):
    *parts, out_ref, sems = refs
    wait_all(start_all(parts, [out_ref.at[i // 4, i % 4] for i in range(len(parts))], sems))


def fold_layers_kernel(cut, plan, top_ref, *refs):
    uppers, (send_x, keep_x, send_y, keep_y), scratch = refs[-14:-10], refs[-10:-6], refs[-6:]
    kept, got, total, keep_sems, got_sems, out_sems = scratch
    count = kept.shape[1]
    middle = send_x.shape[2]
    ins = []
    for layer, at, sources in plan:
        keep_ref, refs = refs[0], refs[1:]
        keep_ref = keep_ref if at is None else keep_ref.at[at]
        got_refs = []
        for index, many in sources:
            ref, refs = refs[0], refs[1:]
            ref = ref if index is None else ref.at[index]
            got_refs += [ref.at[i] for i in range(many)]
        ins.append((layer, keep_ref, got_refs))

    def arriving(n, i):
        _, keep_ref, got_refs = ins[n]
        return (
            pltpu.make_async_copy(keep_ref.at[i], kept.at[n, i], keep_sems.at[n, i]),
            pltpu.make_async_copy(got_refs[i], got.at[n, i], got_sems.at[n, i]),
        )

    steps = [(n, i) for n in range(len(ins)) for i in range(count)]
    for n, i in steps:
        for copy in arriving(n, i):
            copy.start()
    for n, i in steps:
        layer = ins[n][0]
        place = layer ^ top_ref[0]
        for copy in arriving(n, i):
            copy.wait()
        total[n, i] = add_pair(kept[n, i], got[n, i])
        pltpu.make_async_copy(total.at[n, i, 0:cut], uppers[i % 4].at[layer, i // 4], out_sems.at[n, 0, i]).start()
        for bit, send, keep, at, where, sem in (
            (place & 1, send_x, keep_x, place >> 1, slice(cut, cut + middle), out_sems.at[n, 1, i]),
            (place >> 1, send_y, keep_y, place & 1, slice(cut + middle, cut + 2 * middle), out_sems.at[n, 2, i]),
        ):
            for value, target in ((0, keep), (1, send)):

                @pl.when(bit == value)
                def _():
                    pltpu.make_async_copy(total.at[n, i, where], target.at[at, i], sem).start()

    for n, i in steps:
        layer = ins[n][0]
        pltpu.make_async_copy(total.at[n, i, 0:cut], uppers[i % 4].at[layer, i // 4], out_sems.at[n, 0, i]).wait()
        for part in (1, 2):
            pltpu.make_async_copy(total.at[n, i, cut : cut + middle], keep_x.at[0, i], out_sems.at[n, part, i]).wait()


def add_kernel(left, right, out_ref):
    out_ref[...] = add_pair(left[...], right[...])


def pause_kernel(ref, out_ref):
    for i in range(ref.shape[0]):
        out_ref[i] = ref[i]


def fold_plane_kernel(keep_x, got_x, keep_y, got_y, own_a, send_y, own_b, send_x):
    for keep, got, own, send in ((keep_x, got_x, own_a, send_y), (keep_y, got_y, own_b, send_x)):
        own[...] = add_pair(keep[0], got[0])
        send[...] = add_pair(keep[1], got[1])


def fold_rows_kernel(own_a, got_a, own_b, got_b, *outs):
    middle = own_a.shape[1]
    for place in range(own_a.shape[0]):
        out = outs[place % 4].at[place // 4]
        out[0:middle] = add_pair(own_a[place], got_a[place])
        out[middle:] = add_pair(own_b[place], got_b[place])


def fold_uppers_kernel(top_ref, *refs):
    refs, outs, scratch = refs[:-5], refs[-5:-1], refs[-1]
    for layer in range(4):
        scratch[layer ^ top_ref[0]] = sum(ref[layer].astype(f32) for ref in refs).astype(bf16)
    for place, out in enumerate(outs):
        out[...] = scratch[place]


def fold_expert_kernel(highs, *refs):
    ins, outs = refs[:4], refs[4:]
    count = ins[0].shape[0]
    for side, high in enumerate(highs):
        half = count // 2
        for i in range(count):
            which, at = (i // half, i % half) if high else (i % 2, i // 2)
            outs[side * count + which * half + at][...] = add_pair(ins[2 * side][i], ins[2 * side + 1][i])


def swap(value, axes, mask):
    size = 1
    for axis in axes:
        size *= lax.axis_size(axis)
    return lax.ppermute(value, axes, [(i, i ^ mask) for i in range(size)])


def after(value, *others):
    return lax.optimization_barrier((value, others))[0]


def pause(scalars, rows, others):
    scalars, others = lax.optimization_barrier((scalars, others))
    scalars = pl.pallas_call(
        pause_kernel,
        in_specs=[SMEM],
        out_specs=SMEM,
        out_shape=shape(scalars.shape, jnp.int32),
        compiler_params=params(),
        cost_estimate=cost(rows),
        name="pause",
    )(scalars)
    return scalars, others


class Order:
    def __init__(self):
        self.latest = ()

    def land(self, value):
        self.latest = after(value, self.latest)
        return self.latest


def bit_groups(bits):
    return [bits[i : i + 2] for i in range(0, len(bits), 2)]


def all_sum_step(value, axes, bits):
    if len(bits) == 1:
        return value + swap(value, axes, 1 << bits[0])
    low, high = 1 << bits[0], 1 << bits[1]
    near, far, both = swap(value, axes, low), swap(value, axes, high), swap(value, axes, low | high)
    return (value + near) + (far + both)


def reduce_bits(value, axes, bits):
    for bit in bits:
        pairs = value.reshape((value.shape[0] // 2, 2) + value.shape[1:])
        value = pairs[:, 0] + swap(pairs[:, 1], axes, 1 << bit)
    return value[0]


def shape(dims, dtype=f32):
    return jax.ShapeDtypeStruct(dims, dtype)


def on_device(
    tokens,
    cotangent,
    expert_picks,
    priority,
    dense_master,
    dense_momentum,
    dense_variance,
    expert_master,
    expert_momentum,
    expert_variance,
):
    both = ("dp", "expert")
    dp_ranks = lax.axis_size("dp")
    expert_ranks = lax.axis_size("expert")
    devices = dp_ranks * expert_ranks
    local_experts = expert_master.shape[0]
    experts = local_experts * expert_ranks
    images, seq, width = tokens.shape
    assert local_experts == 1 and images == 1
    assert devices & (devices - 1) == 0 and dp_ranks >= 4
    tiles = width // LANES
    dp_me = lax.axis_index("dp").astype(jnp.int32)
    me = dp_me * expert_ranks + lax.axis_index("expert").astype(jnp.int32)
    me_arr = me.reshape(1)
    dp_arr = dp_me.reshape(1)
    dp_bits = dp_ranks.bit_length() - 1
    all_bits = devices.bit_length() - 1

    own = dense_master.shape[0] // LANES
    expert_flat = expert_master.shape[1] // LANES
    hidden = expert_master.shape[1] * dp_ranks // (2 * width)
    matrix_rows = 8 * width + 2 * hidden
    rows = matrix_rows // devices
    step = own - rows * tiles
    tail = step * devices
    tail_rows = -(-tail // (16 * tiles)) * 16
    wide_ok = rows % 64 == 0
    expert_rows = expert_flat // tiles

    dense_flat = dense_master.reshape(own, LANES)
    forward_ring = [(i, (i + 1) % devices) for i in range(devices)]
    backward_ring = [((i + 1) % devices, i) for i in range(devices)]
    tail_from = lax.ppermute(dense_flat[own - tail :], both, forward_ring)
    buf_rows = -(-(own + max(tail, tail_rows * tiles)) // 8) * 8
    chunk = pl.pallas_call(
        functools.partial(
            pack_dense_kernel, (rows, tail_rows, tail, own, step, tiles, devices, wide_ok)
        ),
        in_specs=[SMEM, VMEM, VMEM],
        out_specs=VMEM,
        out_shape=shape((rows + tail_rows, width), bf16),
        scratch_shapes=[pltpu.VMEM((buf_rows, LANES), f32)],
        compiler_params=params(),
        cost_estimate=cost(),
        name="pack_dense",
    )(me_arr, tail_from, dense_flat)

    expert_wide = (dp_me < dp_ranks // 2).astype(jnp.int32).reshape(1)
    quarter = expert_rows // 4
    cuts = [(0, 2), (2, 4), (0, 1), (1, 2), (2, 3), (3, 4)]
    cuts = [(low * quarter, high * quarter) for low, high in cuts]
    expert_chunks = pl.pallas_call(
        functools.partial(pack_expert_kernel, (expert_rows, tiles), cuts),
        in_specs=[SMEM, VMEM],
        out_specs=[VMEM] * 6,
        out_shape=[shape((high - low, width), bf16) for low, high in cuts],
        compiler_params=params(),
        cost_estimate=cost(),
        name="pack_expert",
    )(expert_wide, expert_master.reshape(expert_flat, LANES))
    dp_axis = ("dp",)
    dp_order = list(range(dp_bits))

    def gather_step(parts, bit):
        return {**parts, **{at | (1 << bit): swap(part, dp_axis, 1 << bit) for at, part in parts.items()}}

    capacity = 2 * seq // experts
    stride = -(-capacity // 8) * 8
    slots = experts * stride
    padded = -(-seq // 16) * 16
    fill = padded - seq
    ranks = jnp.pad(priority, ((0, 0), (0, fill)), constant_values=1 << 20)
    picks = jnp.pad(expert_picks, ((0, fill), (0, 0)), constant_values=-1)
    cot = jnp.pad(cotangent.reshape(seq, width), ((0, fill), (0, 0)))
    stream = jnp.pad(tokens.reshape(seq, width).astype(f32), ((0, fill), (0, 0)))
    e_me = lax.axis_index("expert").astype(jnp.int32).reshape(1)
    pair_shape = shape((2, stride, width), bf16)
    cols, near_cols, rows_slots, outgoing_cot = pl.pallas_call(
        functools.partial(route_kernel, experts, capacity, stride),
        in_specs=[SMEM] + [VMEM] * 5,
        out_specs=[VMEM] * 4,
        out_shape=[shape((padded, 2), jnp.int32)] * 2
        + [shape((2, padded), jnp.int32), shape((slots, width), bf16)],
        compiler_params=params(),
        cost_estimate=cost(),
        name="route",
    )(e_me, ranks, ranks.reshape(padded, 1), picks, picks.T, cot)

    def exchange(value):
        dims = value.shape
        value = value.reshape(expert_ranks, slots // expert_ranks, dims[1])
        value = lax.all_to_all(value, "expert", split_axis=0, concat_axis=0, tiled=True)
        return value.reshape(dims)

    per = devices // 4
    per_bits = per.bit_length() - 1
    top_bits = (per_bits, per_bits + 1)
    chunk_rows = rows + tail_rows
    low = me & (per - 1)
    low_arr = low.reshape(1)
    place_arr = jnp.stack([low, me >> per_bits])
    expert_me = jnp.concatenate([dp_arr, e_me])
    half_rows = expert_rows // 2
    orders = (dp_order, dp_order[::-1])
    expert_parts, expert_spans = [], []
    if per_bits == 3 and dp_bits == 2:
        masks = [1 << bit for bit in top_bits]
        split = chunk_rows // 32 * 16 + 16
        order = Order()

        def spread(value):
            return [swap(value, both, mask) for mask in masks]

        sets = [chunk, swap(chunk, both, 2), None, None]
        near, far = [spread(chunk)] + [None] * 3, [None] * 4
        near[0] = order.land(near[0])
        sets[1] = order.land(sets[1])
        near[1] = spread(sets[1])
        sets[2] = swap(after(chunk, sets[1]), both, 4)
        halves = [swap(near[0][1][:split], both, masks[0]), swap(near[0][0][split:], both, masks[1])]
        near[1] = order.land(near[1])
        halves = order.land(halves)
        far[0] = jnp.concatenate(halves)
        x_half, y_half, *quarters = expert_chunks
        first, second = after((quarters[2], quarters[0]), halves)
        early = [swap(first, dp_axis, 1), swap(second, dp_axis, 2)]
        sets[2], outgoing_cot, stream = order.land((sets[2], outgoing_cot, stream))
        sets[3] = swap(sets[2], both, 2)
        near[2] = spread(sets[2])
        early = order.land(early)
        place_arr, early = pause(place_arr, 100, early)
        sets[3], far[0], place_arr = order.land((sets[3], far[0], place_arr))
        far[1], far[2] = swap(far[0], both, 2), swap(far[0], both, 4)
        near[3] = spread(sets[3])
        near[2] = order.land(near[2])
        near[3] = order.land(near[3])
        far[1] = order.land(far[1])
        far[2] = order.land(far[2])
        far[3] = swap(far[2], both, 2)
        arriving_cot = exchange(after(outgoing_cot, far[2]))

        def pack_sets(which):
            ins = [part for s in which for part in (sets[s], *near[s], far[s])]
            return pl.pallas_call(
                pack_sets_kernel,
                in_specs=[pl.BlockSpec(memory_space=pl.ANY)] * len(ins),
                out_specs=VMEM,
                out_shape=shape((len(which), 4, chunk_rows, width), bf16),
                scratch_shapes=[pltpu.SemaphoreType.DMA((len(ins),))],
                compiler_params=params(),
                cost_estimate=cost(),
                name="pack_sets",
            )(*ins)

        x_out, y_out = after((x_half, y_half), near[3])
        beside = [swap(x_out, dp_axis, 1), swap(y_out, dp_axis, 2)]
        packed = [pack_sets([0, 1, 2])]
        first_swap = swap(packed[0], both, 1)
        far[3], beside = order.land(after((far[3], beside), packed))
        packed.append(pack_sets([3]))
        arrays = [*packed, first_swap, swap(packed[1], both, 1)]
        at = ((0, 0), (0, 1), (0, 2), (1, 0))
        spots = [(at[j >> 1][0] + 2 * (j & 1), (at[j >> 1][1],), ()) for j in range(per)]
        place_arr, beside = pause(place_arr, 4400, beside)
        across = [swap(beside[0], dp_axis, 2), swap(beside[1], dp_axis, 1)]
        late = after((quarters[3], quarters[1]), beside)
        late = [swap(late[0], dp_axis, 1), swap(late[1], dp_axis, 2)]
        place_arr, arrays[2] = pause(place_arr, 300, arrays[2])
        expert_me, (across, arriving_cot) = pause(expert_me, 400, (across, arriving_cot))
        expert_parts = [x_half, y_half, beside[0], early[0], late[0], beside[1], early[1], late[1], *across]
        expert_spans = [(0, 0), (0, 2), (1, 0), (1, 2), (1, 3), (2, 2), (2, 0), (2, 1), (3, 0), (3, 2)]
        expert_spans = [(place, first * quarter) for place, first in expert_spans]
    else:
        gathered = chunk[None]
        for bit in range(all_bits):
            gathered = jnp.concatenate([gathered, swap(gathered, both, 1 << bit)])
        arrays = [gathered.reshape(4, per, chunk_rows, width)]
        spots = [(0, (), (j,)) for j in range(per)]
        for side, bits in enumerate(orders):
            parts, places = [expert_chunks[side]], [0]
            for bit in bits:
                parts = parts + [swap(part, dp_axis, 1 << bit) for part in parts]
                places = places + [place | (1 << bit) for place in places]
            expert_parts += parts
            expert_spans += [(place, side * half_rows) for place in places]
        arriving_cot = exchange(outgoing_cot)

    layer_w = pltpu.VMEM((per, rows, width), bf16)
    if not wide_ok:
        first_in = lax.dynamic_index_in_dim(arrays[0], 2 ^ (me >> per_bits), 0, keepdims=False)
        first_in = jnp.take(first_in, jnp.arange(per) ^ low, axis=0)[:, :rows].reshape(width, 4, width)
        first_in = first_in.transpose(1, 0, 2).reshape(1, 4 * width, width)

    act_shape = shape((padded, width), bf16)
    stream_shape = shape((padded, width), f32)
    gain_shape = shape((1, width), f32)
    tok_flops = 2 * padded * width * width
    weight_bytes = 2 * width * width
    ANY = pl.BlockSpec(memory_space=pl.ANY)

    def call(kernel, ins, in_specs, outs, name, rows=0, mib=56, out_specs=None, scratch=(), aliases=None):
        out_specs = out_specs or [None] * len(outs)

        def whole(a):
            return pl.BlockSpec(a.shape, lambda *_, n=len(a.shape): (0,) * n)

        return pl.pallas_call(
            kernel,
            grid=(1,),
            in_specs=[s or whole(a) for a, s in zip(ins, in_specs, strict=True)],
            out_specs=[s or whole(a) for a, s in zip(outs, out_specs, strict=True)],
            out_shape=outs,
            scratch_shapes=list(scratch),
            compiler_params=params(mib),
            cost_estimate=cost(rows),
            input_output_aliases=aliases or {},
            name=name,
        )(*ins)

    places = per // 2
    core_shape = shape((places, rows, width), bf16)
    by_core = pltpu.VMEM((2, places, rows, width), bf16)
    stream_vmem, act_vmem = pltpu.VMEM((padded, width), f32), pltpu.VMEM((padded, width), bf16)

    def attn_weights_call(grad, kept, found):
        return call(
            attn_weights_kernel,
            (low_arr, grad, kept[0], kept[4], *found),
            (SMEM,) + (ANY,) * 6,
            [core_shape, core_shape],
            "attn_weights",
            0,
            out_specs=[ANY] * 2,
            scratch=[
                stream_vmem,
                *[act_vmem] * 5,
                by_core,
                pltpu.SemaphoreType.DMA((6,)),
                pltpu.SemaphoreType.DMA((per,)),
            ],
        )

    outs = [stream_shape] + [act_shape] * 5 + [stream_shape, act_shape] + [shape((padded, hidden))] * 2
    outs += [stream_shape] + [act_shape] * 5
    *results, gains, router, moe_in, probs, outgoing = call(
        functools.partial(forward_kernel, seq, spots, (rows, experts, len(arrays)), wide_ok),
        (place_arr, stream, picks, rows_slots, *arrays, *([] if wide_ok else [first_in])),
        (SMEM, None, None, None) + (ANY,) * len(arrays) + (() if wide_ok else (None,)),
        outs
        + [
            shape((4, width)),
            shape((width, experts), bf16),
            act_shape,
            shape((padded, experts)),
            shape((slots, width + LANES), bf16),
        ],
        "forward",
        0,
        out_specs=[ANY] * 16 + [None] * 5,
        scratch=[pltpu.VMEM(o.shape, o.dtype) for o in outs]
        + [
            pltpu.VMEM((4, per, rows, width), bf16),
            pltpu.VMEM((per, tail_rows, width), bf16),
            pltpu.SemaphoreType.DMA((4, per)),
            pltpu.SemaphoreType.DMA((per,)),
            pltpu.SemaphoreType.DMA((16,)),
        ],
    )
    stream_one, kept_one = results[0], results[1:6]
    stream_two, mlp_in, mlp_pre, mlp_cdf = results[6:10]
    stream_three, kept_two = results[10], results[11:]
    arriving = exchange(outgoing)

    slot_spec = pl.BlockSpec((slots, width), lambda q: (0, 0))
    wide_spec = pl.BlockSpec((slots, width + LANES), lambda q: (0, 0))
    pair_spec = pl.BlockSpec((2, stride, width), lambda q: (0, 0, 0))
    hidden_spec = pl.BlockSpec((slots, width), lambda q: (0, q))
    pairs = experts // 2
    *expert_out, input_back, slot_grad, expert_act, pre_grad = pl.pallas_call(
        functools.partial(expert_kernel, (dp_ranks, quarter, experts), expert_spans),
        grid=(4,),
        in_specs=[SMEM, wide_spec, slot_spec] + [ANY] * len(expert_parts),
        out_specs=[pair_spec] * pairs + [wide_spec, slot_spec, hidden_spec, hidden_spec],
        out_shape=[pair_shape] * pairs
        + [shape((slots, width + LANES), bf16), shape((slots, width), bf16)]
        + [shape((slots, hidden), bf16)] * 2,
        scratch_shapes=[
            pltpu.VMEM((dp_ranks, expert_rows, width), bf16),
            pltpu.VMEM((experts, stride, width), bf16),
            pltpu.VMEM((slots, width), f32),
            pltpu.VMEM((slots, width), f32),
            pltpu.SemaphoreType.DMA((2, len(expert_parts))),
        ],
        compiler_params=params(),
        cost_estimate=cost(),
        name="expert",
    )(expert_me, arriving, arriving_cot, *expert_parts)
    returned_grad = exchange(input_back)
    part_shape = shape((expert_rows // 2, width), bf16)
    count = dp_ranks // 2
    expert_first = pl.pallas_call(
        functools.partial(expert_grad_kernel, (dp_ranks, quarter)),
        grid=(4,),
        in_specs=[SMEM, wide_spec, slot_spec, hidden_spec, hidden_spec],
        out_specs=[ANY] * 4,
        out_shape=[shape((count,) + part_shape.shape, bf16)] * 4,
        scratch_shapes=[
            pltpu.VMEM((dp_ranks, expert_rows, width), bf16),
            pltpu.SemaphoreType.DMA((2 * dp_ranks,)),
        ],
        compiler_params=params(),
        cost_estimate=cost(),
        name="expert_grad",
    )(dp_arr, arriving, slot_grad, expert_act, pre_grad)
    returned_grad = after(returned_grad, expert_first)

    cut = max(16, rows // 48 * 16)
    middle = (rows - cut) // 2
    top = (me >> per_bits).reshape(1)
    z_bits = list(range(1, per_bits))
    z_masks = [2 * j for j in (1, 2, 3)]
    assert places % 4 == 0

    def add_call(left, right):
        return call(add_kernel, (left, right), (None, None), [shape(left.shape, bf16)], "add", mib=12)[0]

    def over_z(values, meanwhile=None):
        farthest = swap(values[3], both, 2)
        if meanwhile is not None:
            farthest, *meanwhile[:] = lax.optimization_barrier((farthest, *meanwhile))
        near = swap(after(values[1], farthest), both, 2)
        return [values[0], near, swap(add_call(values[2], farthest), both, 4)]

    def rest_of_z(values):
        if len(z_bits) == 2:
            return values
        total = sum(value.astype(f32) for value in values).astype(bf16)
        lead = total.ndim - 3
        total = jnp.moveaxis(total, lead, 0)
        return [reduce_bits(total, both, z_bits[2:])]

    def to_other_core(parts):
        return [parts[0], swap(parts[1], both, 1)]

    expert_got = [swap(expert_first[0], dp_axis, 1), swap(expert_first[2], dp_axis, dp_ranks // 2)]
    returned_grad, expert_out = lax.optimization_barrier((returned_grad, expert_out))
    expert_out = [expert_out[0]] + [swap(v, ("expert",), 2 * j) for j, v in enumerate(expert_out) if j]
    backward_ins = (
        (stream_three, moe_in, stream_two, *kept_two[1:4], kept_two[0], kept_two[4])
        + (stream_one, mlp_in, mlp_pre, mlp_cdf, stream, *kept_one[1:4])
    )
    held_vmem = [stream_vmem, act_vmem, stream_vmem] + [act_vmem] * 5
    held_vmem += [stream_vmem, act_vmem] + [pltpu.VMEM((padded, hidden), f32)] * 2 + [stream_vmem] + [act_vmem] * 3
    kinds = 2 if wide_ok else 1
    most, rest = places * 3 // 4, places // 4
    keeps_shape = shape((kinds,) + core_shape.shape, bf16)
    most_shape, rest_shape = shape((most, rows, width), bf16), shape((kinds, rest, rows, width), bf16)
    first_dw_out = [most_shape] if wide_ok else [shape((1, 4 * width, width), bf16)]
    small, upper, dq, dk, dv, grad, *dws = call(
        functools.partial(backward_kernel, seq, spots, len(arrays), wide_ok),
        (place_arr, gains, router, picks, cols, cot, probs, returned_grad, *backward_ins, *arrays)
        + (() if wide_ok else (first_in,)),
        (SMEM,) + (None,) * 7 + (ANY,) * (16 + len(arrays)) + (() if wide_ok else (None,)),
        [shape((tail, LANES)), stream_shape, act_shape, act_shape, act_shape, stream_shape]
        + [core_shape, core_shape, keeps_shape, most_shape, rest_shape]
        + first_dw_out,
        "backward",
        out_specs=[None] + [ANY] * 10 + ([ANY] if wide_ok else [None]),
        scratch=held_vmem
        + [stream_vmem] * 4
        + [act_vmem] * 4
        + [by_core, by_core, layer_w, pltpu.VMEM((2, per, rows, width), bf16)]
        + ([by_core, layer_w] if wide_ok else [])
        + [
            pltpu.VMEM((width, LANES), f32),
            pltpu.SemaphoreType.DMA((16,)),
            pltpu.SemaphoreType.DMA((4, per)),
            pltpu.SemaphoreType.DMA((3, per)),
            pltpu.SemaphoreType.DMA((5,)),
        ],
    )
    if not wide_ok:
        wide_grad = dws[5].reshape(4, width, width).transpose(1, 0, 2).reshape(per, rows, width)
        wide_grad = jnp.take(wide_grad, jnp.arange(per) ^ low, axis=0)
        wide_grad = wide_grad.reshape(places, 2, rows, width)
        dws[2] = jnp.concatenate([dws[2], wide_grad[None, :, 0]])
        dws[4] = jnp.concatenate([dws[4], wide_grad[None, most:, 1]])
        dws[5] = wide_grad[:most, 1]
    dws, expert_out = lax.optimization_barrier((dws, expert_out))
    most_got = [swap(dws[3], both, 1), swap(dws[5], both, 1)]
    rest_got = swap(dws[4], both, 1)
    first_dw = attn_weights_call(upper, kept_one, (dq, dk, dv))
    layer_got = {0: [(swap(first_dw[1], both, 1), None, places)], 1: [(swap(dws[1], both, 1), None, places)]}
    for i, layer in enumerate((3, 2)):
        layer_got[layer] = [(most_got[i], None, most), (rest_got, i, rest)]
    layer_keep = {3: (dws[2], 0), 2: (dws[2], 1), 1: (dws[0], None), 0: (first_dw[0], None)}

    plane_shape = shape((2, places, middle, width), bf16)
    plane_spec = pl.BlockSpec((2, 1, middle, width), lambda i: (0, i, 0, 0))
    line_shape = shape((places, middle, width), bf16)
    line_spec = pl.BlockSpec((1, middle, width), lambda i: (i, 0, 0))
    upper_shape = shape((4, places // 4, cut, width), bf16)
    sums = ()
    for pair in ((3, 2), (1, 0)):
        if pair[0] == 1:
            expert_got, sums = lax.optimization_barrier((expert_got, sums))
            top, expert_got = pause(top, 1600, expert_got)
        plan, ins = [], []
        for layer in pair:
            keep, at = layer_keep[layer]
            parts = layer_got[layer]
            plan.append((layer, at, [part[1:] for part in parts]))
            ins += [after(keep, first_dw) if layer == 3 else keep] + [part[0] for part in parts]
        sums = call(
            functools.partial(fold_layers_kernel, cut, plan),
            (top, *ins, *sums),
            (SMEM,) + (ANY,) * (len(ins) + len(sums)),
            [upper_shape] * 4 + [plane_shape] * 4,
            "fold_layers",
            out_specs=[ANY] * 8,
            scratch=[pltpu.VMEM((2, places, rows, width), bf16)] * 3
            + [
                pltpu.SemaphoreType.DMA((2, places)),
                pltpu.SemaphoreType.DMA((2, places)),
                pltpu.SemaphoreType.DMA((2, 3, places)),
            ],
            aliases={1 + len(ins) + i: i for i in range(len(sums))},
        )
    *uppers, send_x, keep_x, send_y, keep_y = sums
    masks = [1 << bit for bit in top_bits]
    got_x, got_y = swap(send_x, both, masks[0]), swap(send_y, both, masks[1])
    uppers = over_z(uppers)
    expert_ins = (expert_first[1], expert_got[0], expert_first[3], expert_got[1])
    expert_second = call(
        functools.partial(fold_expert_kernel, (dp_bits == 1, True)),
        expert_ins,
        (None,) * len(expert_ins),
        [part_shape] * (2 * count),
        "fold_expert",
        0,
    )

    uppers = [value.reshape(4, -1, cut, width) for value in uppers]
    uppers = [value.reshape(4, cut, width) for value in rest_of_z(uppers)]
    upper_rows = call(
        fold_uppers_kernel,
        (top, *uppers),
        (SMEM,) + (None,) * len(uppers),
        [shape((cut, width), bf16)] * 4,
        "fold_uppers",
        100,
        scratch=[pltpu.VMEM((4, cut, width), bf16)],
    )
    got_x, got_y, expert_second = lax.optimization_barrier((got_x, got_y, expert_second))
    own_a, send_y, own_b, send_x = pl.pallas_call(
        fold_plane_kernel,
        grid=(places,),
        in_specs=[plane_spec] * 4,
        out_specs=[line_spec] * 4,
        out_shape=[line_shape] * 4,
        compiler_params=params(),
        cost_estimate=cost(),
        name="fold_plane",
    )(keep_x, got_x, keep_y, got_y)
    got_y, got_x = swap(send_y, both, masks[1]), swap(send_x, both, masks[0])
    expert_second, upper_rows = lax.optimization_barrier((expert_second, upper_rows))
    other_out = swap(jnp.stack([value[1] for value in expert_out]), ("expert",), 1)
    lower_rows = call(
        fold_rows_kernel,
        (own_a, got_y, own_b, got_x),
        (None,) * 4,
        [shape((places // 4, rows - cut, width), bf16)] * 4,
        "fold_rows",
        0,
    )
    lower_rows, other_out = lax.optimization_barrier((lower_rows, other_out))
    output, grad = call(
        output_kernel,
        (stream_three, picks, near_cols, probs, grad, *expert_out, other_out),
        (None,) * (6 + pairs),
        [shape((seq * tiles, LANES))] * 2,
        "output",
        mib=16,
        scratch=[pltpu.VMEM((slots, width), f32)],
    )
    image = (1, seq, width)
    meanwhile = [output.reshape(image), grad.reshape(image)]
    lower_rows = over_z(lower_rows, meanwhile)
    output, grad = meanwhile
    half = count // 2
    expert_groups = []
    for side, bits in enumerate(orders):
        keep, send = (expert_second[(2 * side + i) * half : (2 * side + i + 1) * half] for i in range(2))
        got = [swap(part, dp_axis, 1 << bits[1]) for part in send]
        expert_groups.append([list(pair) for pair in zip(keep, got)])
    if dp_bits > 2:
        for side, bits in enumerate(orders):
            value = [sum(pair) for pair in expert_groups[side]]
            for bit in bits[2:]:
                half = len(value) // 2
                keep, send = (value[:half], value[half:]) if side else (value[0::2], value[1::2])
                value = [k + swap(v, dp_axis, 1 << bit) for k, v in zip(keep, send)]
            expert_groups[side] = [value]
    expert_groups = [side[0] for side in expert_groups]
    upper_rows, expert_groups = lax.optimization_barrier((upper_rows, expert_groups))

    def unpack(wide, groups, count, name, extra=(), more_shapes=((1, LANES),)):
        pieces = [piece for group in groups for piece in group] + list(extra)
        return pl.pallas_call(
            functools.partial(unpack_kernel, (count, tiles), [len(group) for group in groups]),
            in_specs=[SMEM] + [VMEM] * len(pieces),
            out_specs=[VMEM] * (1 + len(more_shapes)),
            out_shape=[shape((count * tiles, LANES))] + [shape(dims) for dims in more_shapes],
            scratch_shapes=[pltpu.VMEM((count, width), f32)],
            compiler_params=params(),
            cost_estimate=cost(),
            name=name,
        )(wide, *pieces)

    expert_grad, expert_square = unpack(expert_wide, expert_groups, expert_rows, "unpack_expert")
    lower_rows, output, expert_grad, expert_square = lax.optimization_barrier(
        (lower_rows, output, expert_grad, expert_square)
    )
    lower_rows = rest_of_z(lower_rows)
    upper_rows = [upper_rows[0]] + [
        swap(value, both, masks[0] * j) for j, value in enumerate(upper_rows) if j
    ]
    dense_groups = [upper_rows, [value.reshape(rows - cut, width) for value in lower_rows]]

    dense_wide = (me >= devices // 2) & (me < 3 * devices // 4) & wide_ok
    dense_rows, total, head = unpack(
        dense_wide.astype(jnp.int32).reshape(1),
        dense_groups,
        rows,
        "unpack_dense",
        (small, expert_square),
        ((tail + 8, LANES), (tail, LANES)),
    )
    head = lax.ppermute(head, both, backward_ring)
    groups = bit_groups(list(range(all_bits)))
    for bits in groups[:-1]:
        total = all_sum_step(total, both, bits)
    total, head = lax.optimization_barrier((total, head))
    total = all_sum_step(total, both, groups[-1])
    param_count = (dense_master.size + expert_master.size) * devices

    chunks = 16
    results = pl.pallas_call(
        functools.partial(adam_kernel, (step, chunks, devices, param_count, width * experts // LANES)),
        in_specs=[SMEM, VMEM, VMEM] + [ANY] * 6,
        out_specs=[ANY] * 7 + [VMEM],
        out_shape=[shape((expert_flat, LANES))] * 3 + [shape((own, LANES))] * 4 + [shape((4, width))],
        scratch_shapes=[pltpu.VMEM((expert_flat, LANES), f32)] * 3
        + [
            pltpu.VMEM((4, 3, expert_flat // chunks, LANES), f32),
            pltpu.VMEM((-(-(rows * tiles + tail) // 8) * 8, LANES), f32),
            pltpu.VMEM((4, own, LANES), f32),
            pltpu.SemaphoreType.DMA((chunks, 3)),
            pltpu.SemaphoreType.DMA((4, 3)),
            pltpu.SemaphoreType.DMA((3,)),
            pltpu.SemaphoreType.DMA((4,)),
        ],
        compiler_params=params(),
        cost_estimate=cost(),
        name="adam",
    )(
        me_arr,
        total,
        head,
        expert_grad,
        expert_momentum.reshape(expert_flat, LANES),
        expert_variance.reshape(expert_flat, LANES),
        dense_rows,
        dense_momentum.reshape(own, LANES),
        dense_variance.reshape(own, LANES),
    )
    gain_grads = results[7]
    expert_update, momentum_expert, variance_expert = results[:3]
    dense_update, momentum_dense, variance_dense, dense_grad = results[3:7]
    return (
        output,
        grad,
        dense_grad.reshape(dense_master.shape),
        expert_grad.reshape(expert_master.shape),
        dense_update.reshape(dense_master.shape),
        momentum_dense.reshape(dense_master.shape),
        variance_dense.reshape(dense_master.shape),
        expert_update.reshape(expert_master.shape),
        momentum_expert.reshape(expert_master.shape),
        variance_expert.reshape(expert_master.shape),
        gain_grads,
    )


def solution(mesh):
    tokens = P(("dp", "expert"), None, None)
    flat = P(("dp", "expert"))
    pairs = P(("dp", "expert"), None)
    expert = P("expert", "dp")
    return jax.shard_map(
        on_device,
        mesh=mesh,
        in_specs=(tokens, tokens, pairs, pairs, flat, flat, flat, expert, expert, expert),
        out_specs=(tokens, tokens, flat, expert, flat, flat, flat, expert, expert, expert, P()),
        check_vma=False,
    )
```

```python
import functools
import math

import jax
import jax.numpy as jnp
from jax import lax
from jax.experimental import pallas as pl
from jax.experimental.pallas import tpu as pltpu
from jax.sharding import PartitionSpec as P

HEADS = 12
HEAD_DIM = 64
LANES = 128

f32 = jnp.float32
bf16 = jnp.bfloat16

eps_norm = 1e-06
beta_first = 0.9
beta_second = 0.999
adam_eps = 1e-08
adam_step = 10.0

VMEM = pl.BlockSpec(memory_space=pltpu.VMEM)
SMEM = pl.BlockSpec(memory_space=pltpu.SMEM)


def params(mib=56):
    return pltpu.CompilerParams(vmem_limit_bytes=mib << 20)


def cost(rows=0):
    return pl.CostEstimate(flops=1 + int(rows * 16.45e6), bytes_accessed=1, transcendentals=0)


def dot(a, b):
    return lax.dot_general(a, b, (((1,), (0,)), ((), ())), preferred_element_type=f32)


def dot_nt(a, b):
    return lax.dot_general(a, b, (((1,), (1,)), ((), ())), preferred_element_type=f32)


def dot_tn(a, b):
    return lax.dot_general(a, b, (((0,), (0,)), ((), ())), preferred_element_type=f32)


def norm_rows(hidden):
    center = hidden - jnp.mean(hidden, axis=-1, keepdims=True)
    inverse = lax.rsqrt(jnp.mean(center * center, axis=-1, keepdims=True) + eps_norm)
    return center * inverse, inverse


def norm_back(upstream, normed, inverse, gain):
    scaled = upstream * gain
    gain_grad = jnp.sum(upstream * normed, axis=0, keepdims=True)
    centered = (
        scaled
        - jnp.mean(scaled, axis=-1, keepdims=True)
        - normed * jnp.mean(scaled * normed, axis=-1, keepdims=True)
    )
    return inverse * centered, gain_grad


def normal_cdf(v):
    return 0.5 * (1.0 + lax.erf(v * 0.7071067811865476))


def density(v):
    return jnp.exp(-0.5 * v * v) * 0.3989422804014327


def to_rows(read, write, first_q, rows, wide, tiles):
    blocks = 4 if rows % 64 == 0 else 1
    count = rows // blocks
    for b in range(blocks):
        for j in range(tiles):
            if wide:
                write(b * count, count, j, read(first_q + tiles * b + j, count, 4 * tiles))
            else:
                write(b * count, count, j, read(first_q + tiles * count * b + j, count, tiles))


def pack_dense_kernel(dims, k_ref, tail_ref, own_ref, out_ref, buf):
    rows, tail_rows, tail, own, step, tiles, chunks, wide_ok = dims
    buf[0:tail] = tail_ref[...]
    buf[tail : tail + own] = own_ref[...]
    buf[tail + own :] = jnp.zeros((buf.shape[0] - tail - own, LANES), f32)
    k = k_ref[0]
    start = tail - step * k

    def read(first, count, stride):
        return buf[pl.ds(first, count, stride=stride), :]

    def write(first, count, j, value):
        out_ref[first : first + count, LANES * j : LANES * (j + 1)] = value.astype(bf16)

    wide = (k >= chunks // 2) & (k < 3 * chunks // 4) & wide_ok

    if wide_ok:

        @pl.when(wide)
        def _():
            to_rows(read, write, start, rows, True, tiles)

    @pl.when(jnp.logical_not(wide))
    def _():
        to_rows(read, write, start, rows, False, tiles)

    for j in range(tiles):
        write(rows, tail_rows, j, read(own + j, tail_rows, tiles))


def pack_expert_kernel(dims, cuts, wide_ref, own_ref, *out_refs):
    rows, tiles = dims

    def read(first, count, stride):
        return own_ref[pl.ds(first, count, stride=stride), :]

    def write(first, count, j, value):
        value = value.astype(bf16)
        for (low, high), ref in zip(cuts, out_refs):
            start, end = max(first, low), min(first + count, high)
            if start < end:
                ref[start - low : end - low, LANES * j : LANES * (j + 1)] = value[start - first : end - first]

    wide = wide_ref[0] > 0

    @pl.when(wide)
    def _():
        to_rows(read, write, 0, rows, True, tiles)

    @pl.when(jnp.logical_not(wide))
    def _():
        to_rows(read, write, 0, rows, False, tiles)


def add_up(refs):
    return sum(ref[...].astype(f32) for ref in refs)


def unpack_kernel(dims, groups, wide_ref, *refs):
    rows, tiles = dims
    (*refs, rows_ref), small_ref = refs, None
    if len(refs) > sum(groups) + 2:
        *refs, small_ref, before_ref, out_ref, square_ref, head_ref = refs
    else:
        *refs, out_ref, square_ref = refs
    at = 0
    for count in groups:
        value = add_up(refs[:count])
        refs = refs[count:]
        rows_ref[at : at + value.shape[0]] = value
        at += value.shape[0]
    wide = wide_ref[0] > 0

    def store(is_wide):
        total = jnp.zeros((1, LANES), f32)
        quarter = rows // 4
        for q in range(4):
            for j in range(tiles):
                piece = rows_ref[q * quarter : (q + 1) * quarter, LANES * j : LANES * (j + 1)]
                if is_wide:
                    at = pl.ds(tiles * q + j, quarter, stride=4 * tiles)
                else:
                    at = pl.ds(tiles * quarter * q + j, quarter, stride=tiles)
                out_ref[at, :] = piece
                total = total + jnp.sum(piece * piece, axis=0, keepdims=True)
        if small_ref is None:
            square_ref[...] = total
        else:
            count = small_ref.shape[0]
            square_ref[0:count] = small_ref[...]
            square_ref[count:] = jnp.zeros((square_ref.shape[0] - count, LANES), f32)
            square_ref[count : count + 1] = total + before_ref[...]
            head_ref[...] = out_ref[0:count]

    @pl.when(wide)
    def _():
        store(True)

    @pl.when(jnp.logical_not(wide))
    def _():
        store(False)


def adam_values(clip, grad, momentum, variance):
    clipped = grad * clip
    momentum_new = beta_first * momentum + (1.0 - beta_first) * clipped
    variance_new = beta_second * variance + (1.0 - beta_second) * clipped * clipped
    first_hat = momentum_new / (1.0 - beta_first**adam_step)
    second_hat = variance_new / (1.0 - beta_second**adam_step)
    return -first_hat / (jnp.sqrt(second_hat) + adam_eps), momentum_new, variance_new


def adam_kernel(dims, k_ref, total_ref, head_ref, *refs):
    step, chunks, devices, param_count, router_rows = dims
    sources, refs = refs[:6], refs[6:]
    outs, dense_outs, gains_ref, refs = refs[:3], refs[3:7], refs[7], refs[8:]
    held, slots, buf, dense_slots, in_sems, sems, dense_in, dense_sems = refs[:3], *refs[3:]
    flat_ref, dense_m, dense_v = dense_slots.at[0], dense_slots.at[1], dense_slots.at[2]
    rows = slots.shape[2]

    def arriving(c, i):
        at = slice(c * rows, (c + 1) * rows)
        return pltpu.make_async_copy(sources[i].at[at], held[i].at[at], in_sems.at[c, i])

    def leaving(c, i):
        target = outs[i].at[c * rows : (c + 1) * rows]
        return pltpu.make_async_copy(slots.at[c % 4, i], target, sems.at[c % 4, i])

    count, own = sources[3].shape[0], sources[4].shape[0]
    dense_copies = [pltpu.make_async_copy(sources[3], buf.at[0:count], dense_in.at[0])]
    for i in (1, 2):
        dense_copies.append(pltpu.make_async_copy(sources[3 + i], dense_slots.at[i], dense_in.at[i]))
    for copy in dense_copies:
        copy.start()
    for c in range(chunks):
        for i in range(3):
            arriving(c, i).start()

    summed = head_ref.shape[0]
    squares = total_ref[summed : summed + 1]
    for at in range(0, summed, 8):
        part = total_ref[at : at + 8]
        squares = squares + jnp.sum(part * part, axis=0, keepdims=True)
    square_sum = jnp.sum(squares, axis=1, keepdims=True)
    clip = jnp.minimum(1.0, jnp.sqrt(param_count / (square_sum + 1e-06)))
    tiles = gains_ref.shape[1] // LANES
    for which in range(gains_ref.shape[0]):
        for j in range(tiles):
            at = router_rows + which * tiles + j
            gains_ref[which : which + 1, LANES * j : LANES * (j + 1)] = total_ref[at : at + 1]

    for copy in dense_copies:
        copy.wait()
    last = k_ref[0] == devices - 1

    @pl.when(last)
    def _():
        buf[count : count + summed] = total_ref[0:summed]

    @pl.when(jnp.logical_not(last))
    def _():
        buf[count : count + summed] = head_ref[...]

    grad = buf[pl.ds(step * k_ref[0], own), :]
    values = adam_values(clip, grad, dense_m[...], dense_v[...])
    for i, value in enumerate((grad, *values)):
        dense_slots[i] = value
    targets = (dense_outs[3], *dense_outs[:3])
    copies = start_all([dense_slots.at[i] for i in range(4)], targets, dense_sems)
    for c in range(chunks):
        at = slice(c * rows, (c + 1) * rows)
        for i in range(3):
            arriving(c, i).wait()
            if c >= 4:
                leaving(c - 4, i).wait()
        values = adam_values(clip, held[0][at], held[1][at], held[2][at])
        for i, value in enumerate(values):
            slots[c % 4, i] = value
            leaving(c, i).start()
    for c in range(max(0, chunks - 4), chunks):
        for i in range(3):
            leaving(c, i).wait()
    wait_all(copies)


def route_kernel(
    experts, capacity, stride, me_ref, prio_row, prio_col, picks, picks_t, cot,
    cols_ref, near_ref, rows_ref, g_ref,
):
    count = picks.shape[0]
    me = me_ref[0]
    before = (prio_row[...] < prio_col[...]).astype(f32).astype(bf16)
    lane = lax.broadcasted_iota(jnp.int32, (count, experts), 1)
    sub = lax.broadcasted_iota(jnp.int32, (experts, count), 0)
    hot = [(picks[:, j : j + 1] == lane).astype(f32) for j in range(2)]
    hot_t = [(picks_t[j : j + 1, :] == sub).astype(f32) for j in range(2)]
    first = jnp.sum(hot[0], axis=0, keepdims=True)
    first_t = jnp.sum(hot_t[0], axis=1, keepdims=True)
    for j in range(2):
        earlier = dot(before, hot[j].astype(bf16)) + (first if j else 0.0)
        earlier_t = dot_nt(hot_t[j].astype(bf16), before) + (first_t if j else 0.0)
        place = jnp.sum(earlier * hot[j], axis=1, keepdims=True).astype(jnp.int32)
        place_t = jnp.sum(earlier_t * hot_t[j], axis=0, keepdims=True).astype(jnp.int32)
        pick, pick_t = picks[:, j : j + 1], picks_t[j : j + 1, :]
        kept = (place < capacity) & (pick >= 0)
        cols_ref[:, j : j + 1] = jnp.where(kept, pick * stride + place, -1)
        near_ref[:, j : j + 1] = jnp.where(kept, (pick ^ me) * stride + place, -1)
        kept = (place_t < capacity) & (pick_t >= 0)
        rows_ref[j : j + 1, :] = jnp.where(kept, pick_t * stride + place_t, -1)
    first, second = slot_selects(rows_ref, experts * stride)
    g_ref[...] = dot(first + second, cot[...]).astype(bf16)


def slot_selects(rows_ref, slots):
    sub = lax.broadcasted_iota(jnp.int32, (slots, rows_ref.shape[1]), 0)
    return [(rows_ref[j : j + 1, :] == sub).astype(f32).astype(bf16) for j in range(2)]


def token_selects(cols_ref, slots):
    lane = lax.broadcasted_iota(jnp.int32, (cols_ref.shape[0], slots), 1)
    return [(cols_ref[:, j : j + 1] == lane).astype(f32).astype(bf16) for j in range(2)]


def split_lanes(column):
    high = column.astype(bf16).astype(f32)
    rest = column - high
    middle = rest.astype(bf16).astype(f32)
    low = rest - middle
    lane = lax.broadcasted_iota(jnp.int32, (column.shape[0], LANES), 1)
    wide = jnp.where(lane == 0, high, jnp.where(lane == 1, middle, jnp.where(lane == 2, low, 0.0)))
    return wide.astype(bf16)


def head_masks():
    lane = lax.broadcasted_iota(jnp.int32, (1, 2 * HEAD_DIM), 1)
    first = (lane < HEAD_DIM).astype(f32)
    return first.astype(bf16), (1.0 - first).astype(bf16)


def soft_scores(queries, key_rows, key_ok):
    scores = dot_nt(queries, key_rows) * HEAD_DIM ** (-0.5)
    scores = jnp.where(key_ok, scores, -1e30)
    top = jnp.max(scores, axis=-1, keepdims=True)
    raised = jnp.exp(scores - top)
    return raised * (1.0 / jnp.sum(raised, axis=-1, keepdims=True))


def put_chunk(scratch, low, chunk, value, first=0):
    place = chunk ^ low
    scratch[place & 1, place >> 1, first : first + value.shape[0], :] = value


def matrix(w_ref, index):
    per = w_ref.shape[0] // 4
    width = w_ref.shape[2]
    rows = width // per
    return w_ref[index * per : (index + 1) * per, 0:rows, :].reshape(width, width)


def quarter_in(w_ref, q):
    width = w_ref.shape[2]
    rows = width // w_ref.shape[0]
    return w_ref[:, q * rows : (q + 1) * rows, :].reshape(width, width)


def start_all(sources, targets, sems):
    copies = [pltpu.make_async_copy(a, b, sems.at[i]) for i, (a, b) in enumerate(zip(sources, targets))]
    for copy in copies:
        copy.start()
    return copies


def wait_all(copies):
    for copy in copies:
        copy.wait()


def layer_copies(spots, arrays, place_ref, layer, target, sems):
    low, top = place_ref[0], place_ref[1]
    found = []
    for j, (array, before, behind) in enumerate(spots):
        source = arrays[array].at[before + (layer ^ top,) + behind + (pl.ds(0, target.shape[1]),)]
        found.append(pltpu.make_async_copy(source, target.at[j ^ low], sems.at[j ^ low]))
    return found


def attn_fwd(seq, stream_ref, gain, w_ref, out_ref, a_ref, q_ref, k_ref, v_ref, o_ref):
    normed, _ = norm_rows(stream_ref[...])
    a_ref[...] = (normed * gain).astype(bf16)
    for index, ref in enumerate((q_ref, k_ref, v_ref)):
        ref[...] = dot(a_ref[...], matrix(w_ref, index)).astype(bf16)
    count = stream_ref.shape[0]
    key_ok = lax.broadcasted_iota(jnp.int32, (count, count), 1) < seq
    masks = head_masks()
    for pair in range(HEADS // 2):
        lanes = slice(2 * HEAD_DIM * pair, 2 * HEAD_DIM * (pair + 1))
        mixed = None
        for mask in masks:
            soft = soft_scores(q_ref[:, lanes] * mask, k_ref[:, lanes], key_ok).astype(bf16)
            part = dot(soft, v_ref[:, lanes] * mask)
            mixed = part if mixed is None else mixed + part
        o_ref[:, lanes] = mixed.astype(bf16)
    out_ref[...] = stream_ref[...] + dot(o_ref[...], matrix(w_ref, 3))


def attn_bwd(seq, grad_ref, stream_ref, gain, w_ref, q_ref, k_ref, v_ref, out_ref, dq_ref, dk_ref, dv_ref, do_ref):
    do_ref[...] = dot_nt(grad_ref[...].astype(bf16), matrix(w_ref, 3)).astype(bf16)
    count = grad_ref.shape[0]
    key_ok = lax.broadcasted_iota(jnp.int32, (count, count), 1) < seq
    masks = head_masks()
    scale = HEAD_DIM ** (-0.5)
    for pair in range(HEADS // 2):
        lanes = slice(2 * HEAD_DIM * pair, 2 * HEAD_DIM * (pair + 1))
        dq = dk = dv = None
        for mask in masks:
            q_h = q_ref[:, lanes] * mask
            k_h = k_ref[:, lanes] * mask
            do_h = do_ref[:, lanes] * mask
            soft = soft_scores(q_h, k_ref[:, lanes], key_ok)
            dsoft = dot_nt(do_h, v_ref[:, lanes])
            dv_h = dot_tn(soft.astype(bf16), do_h)
            inner = jnp.sum(dsoft * soft, axis=-1, keepdims=True)
            dscore = (soft * (dsoft - inner)).astype(bf16)
            dq_h = dot(dscore, k_h)
            dk_h = dot_tn(dscore, q_h)
            dq = dq_h if dq is None else dq + dq_h
            dk = dk_h if dk is None else dk + dk_h
            dv = dv_h if dv is None else dv + dv_h
        dq_ref[:, lanes] = (dq * scale).astype(bf16)
        dk_ref[:, lanes] = (dk * scale).astype(bf16)
        dv_ref[:, lanes] = dv.astype(bf16)
    back = None
    for index, ref in enumerate((dq_ref, dk_ref, dv_ref)):
        part = dot_nt(ref[...], matrix(w_ref, index))
        back = part if back is None else back + part
    normed, inverse = norm_rows(stream_ref[...])
    addend, gain_grad = norm_back(back, normed, inverse, gain)
    out_ref[...] = grad_ref[...] + addend
    return gain_grad


def leave_chunk(scratch, low, chunk, keep_ref, send_refs, sem):
    place = chunk ^ low
    source = scratch.at[place & 1, place >> 1]

    @pl.when((place & 1) == 0)
    def _():
        pltpu.make_async_copy(source, keep_ref.at[place >> 1], sem).start()

    at = 0
    for ref, count in send_refs:

        @pl.when(((place & 1) == 1) & ((place >> 1) >= at) & ((place >> 1) < at + count))
        def _():
            pltpu.make_async_copy(source, ref.at[(place >> 1) - at], sem).start()

        at += count


def wait_chunks(scratch, low, keep_ref, sems):
    for chunk in range(2 * scratch.shape[1]):
        place = chunk ^ low
        pltpu.make_async_copy(scratch.at[place & 1, place >> 1], keep_ref.at[place >> 1], sems.at[chunk]).wait()


def attn_weights(low, grad_ref, a_ref, o_ref, dq_ref, dk_ref, dv_ref, dw, keep_ref, send_ref, sems):
    rows = dw.shape[2]
    per = grad_ref.shape[1] // rows
    branch = grad_ref[...].astype(bf16)
    for index in range(4):
        left = o_ref if index == 3 else a_ref
        right = branch if index == 3 else (dq_ref, dk_ref, dv_ref)[index][...]
        value = dot_tn(left[...], right)
        for i in range(per):
            put_chunk(dw, low, index * per + i, value[i * rows : (i + 1) * rows].astype(bf16))
            leave_chunk(dw, low, index * per + i, keep_ref, send_ref, sems.at[index * per + i])


def attn_weights_kernel(low_ref, *refs):
    ins, keep_ref, send_ref, refs = refs[:6], refs[6], refs[7], refs[8:]
    held, (dw, in_sems, sems) = refs[:6], refs[6:]
    wait_all(start_all(ins, held, in_sems))
    attn_weights(low_ref[0], *held, dw, keep_ref, [(send_ref, dw.shape[1])], sems)
    wait_chunks(dw, low_ref[0], keep_ref, sems)


def mlp_fwd(stream_ref, gain, w1_ref, w2_ref, out_ref, b_ref, u_ref, cdf_ref):
    width = stream_ref.shape[1]
    normed, _ = norm_rows(stream_ref[...])
    b_ref[...] = (normed * gain).astype(bf16)
    total = None
    for q in range(4):
        pre = dot(b_ref[...], quarter_in(w1_ref, q))
        cdf = normal_cdf(pre)
        u_ref[:, q * width : (q + 1) * width] = pre
        cdf_ref[:, q * width : (q + 1) * width] = cdf
        part = dot((pre * cdf).astype(bf16), matrix(w2_ref, q))
        total = part if total is None else total + part
    out_ref[...] = stream_ref[...] + total


def forward_kernel(seq, spots, dims, by_core, place_ref, stream_ref, picks_ref, rows_ref, *refs):
    rows, experts, count = dims
    arrays, refs = refs[:count], refs[count:]
    if not by_core:
        w1_ref, refs = refs[0], refs[1:]
    outs, refs = refs[:16], refs[16:]
    gains_ref, wr_ref, c_ref, probs_ref, x_ref = refs[:5]
    held, (weights, tails, w_sems, tail_sems, out_sems) = refs[5:21], refs[21:]
    low, top = place_ref[0], place_ref[1]
    per = weights.shape[1]
    copies = {
        layer: layer_copies(spots, arrays, place_ref, layer, weights.at[layer], w_sems.at[layer])
        for layer in (0, 2, 3, 1)
    }
    tail_copies = []
    for j, (array, before, behind) in enumerate(spots):
        source = arrays[array].at[before + (3 ^ top,) + behind + (pl.ds(rows, tails.shape[1]),)]
        tail_copies.append(pltpu.make_async_copy(source, tails.at[j ^ low], tail_sems.at[j]))
    for copy in copies[0] + tail_copies:
        copy.start()
    for copy in copies[0] + tail_copies:
        copy.wait()
    for copy in copies[2] + copies[3] + copies[1]:
        copy.start()
    tail = tails[per - 1].astype(f32)
    gains = [tail[experts + i : experts + i + 1] for i in range(4)]
    gains_ref[...] = tail[experts : experts + 4]
    leaving = []

    def leave(first, last):
        for i in range(first, last):
            leaving.append(pltpu.make_async_copy(held[i], outs[i], out_sems.at[i]))
            leaving[-1].start()

    attn_fwd(seq, stream_ref, gains[0], weights.at[0], *held[0:6])
    leave(0, 6)
    for copy in copies[2] + copies[3]:
        copy.wait()
    mlp_fwd(held[0], gains[1], weights.at[2] if by_core else w1_ref, weights.at[3], *held[6:10])
    leave(6, 10)
    for copy in copies[1]:
        copy.wait()
    attn_fwd(seq, held[6], gains[2], weights.at[1], *held[10:16])
    leave(10, 16)
    wr_ref[...] = router_matrix(tail, stream_ref.shape[1], experts)
    dispatch(held[10], gains[3], wr_ref, picks_ref, rows_ref, c_ref, probs_ref, x_ref)
    for copy in leaving:
        copy.wait()


def mlp_bwd(grad_ref, stream_ref, gain, w1_ref, w2_ref, b_ref, u_ref, cdf_ref, out_ref, put_first, put_second):
    width = grad_ref.shape[1]
    upper = grad_ref[...].astype(bf16)
    back = None
    for q in range(4):
        pre = u_ref[:, q * width : (q + 1) * width]
        cdf = cdf_ref[:, q * width : (q + 1) * width]
        act = (pre * cdf).astype(bf16)
        put_second(q, dot_tn(act, upper).astype(bf16))
        dact = dot_nt(upper, matrix(w2_ref, q))
        dpre = (dact * (cdf + pre * density(pre))).astype(bf16)
        put_first(q, dot_tn(b_ref[...], dpre).astype(bf16))
        part = dot_nt(dpre, quarter_in(w1_ref, q))
        back = part if back is None else back + part
    normed, inverse = norm_rows(stream_ref[...])
    addend, gain_grad = norm_back(back, normed, inverse, gain)
    out_ref[...] = grad_ref[...] + addend
    return gain_grad


def pick_hots(picks, experts):
    lane = lax.broadcasted_iota(jnp.int32, (picks.shape[0], experts), 1)
    return [(picks[:, j : j + 1] == lane).astype(f32) for j in range(2)]


def softmax_rows(logits):
    raised = jnp.exp(logits - jnp.max(logits, axis=-1, keepdims=True))
    return raised / jnp.sum(raised, axis=-1, keepdims=True)


def router_matrix(flat, width, experts):
    block = width // experts
    row = lax.broadcasted_iota(jnp.int32, (block, width), 0)
    lane = lax.broadcasted_iota(jnp.int32, (block, width), 1)
    mine = (lane // experts == row).astype(f32)
    lane = lax.broadcasted_iota(jnp.int32, (width, experts), 0)
    column = lax.broadcasted_iota(jnp.int32, (width, experts), 1)
    pick = (lax.rem(lane, experts) == column).astype(f32).astype(bf16)
    parts = [dot((mine * flat[i : i + 1]).astype(bf16), pick) for i in range(experts)]
    return jnp.concatenate(parts).astype(bf16)


def dispatch(stream_ref, gain, wr_ref, picks_ref, rows_ref, c_ref, probs_ref, x_ref):
    width = stream_ref.shape[1]
    experts = wr_ref.shape[1]
    normed, _ = norm_rows(stream_ref[...])
    c_ref[...] = (normed * gain).astype(bf16)
    probs = softmax_rows(dot(c_ref[...], wr_ref[...]))
    probs_ref[...] = probs
    hots = pick_hots(picks_ref, experts)
    selects = slot_selects(rows_ref, x_ref.shape[0])
    gates = None
    for j in range(2):
        part = dot(selects[j], split_lanes(jnp.sum(probs * hots[j], axis=-1, keepdims=True)))
        gates = part if gates is None else gates + part
    x_ref[:, 0:width] = dot(selects[0] + selects[1], c_ref[...]).astype(bf16)
    x_ref[:, width:] = gates.astype(bf16)


def add_lanes(wide):
    wide = wide.astype(f32)
    return wide[:, 0:1] + wide[:, 1:2] + wide[:, 2:3]


def expert_kernel(dims, spans, me_ref, x_ref, g_ref, *refs):
    parts, quarter, blocks = dims
    weight_refs, refs = refs[: len(spans)], refs[len(spans) :]
    y_refs, refs = refs[: blocks // 2], refs[blocks // 2 :]
    dx_ref, dy_ref, act_ref, dpre_ref, weights, y_near, y_sum, dx_sum, sems = refs
    q = pl.program_id(0)
    width = g_ref.shape[1]
    half = parts // 2
    me = me_ref[0]

    rows = weights.shape[1] // 2

    def copies(side):
        found = []
        for i, ((place, first), ref) in enumerate(zip(spans, weight_refs)):
            low, high = max(first, side * rows), min(first + ref.shape[0], (side + 1) * rows)
            if low < high:
                target = weights.at[place ^ me, low:high]
                found.append(pltpu.make_async_copy(ref.at[low - first : high - first], target, sems.at[side, i]))
        return found

    staged = 2 * quarter >= width // half and rows >= width

    @pl.when(q == 0)
    def _():
        for copy in copies(0) + copies(1):
            copy.start()
        dy_ref[...] = (add_lanes(x_ref[:, width:]) * g_ref[...].astype(f32)).astype(bf16)
        for copy in copies(0) if staged else copies(0) + copies(1):
            copy.wait()

    if staged:

        @pl.when(q == 1)
        def _():
            for copy in copies(1):
                copy.wait()

    first = weights[0:half, pl.ds(pl.multiple_of(q * quarter, 16), quarter), :].reshape(width, width)
    if 4 * quarter >= width:
        per = 4 * quarter // width
        at = pl.ds(pl.multiple_of(lax.rem(q, per) * width, 16), width)
        second = weights[half + q // per, at, :]
    else:
        per = width // (4 * quarter)
        second = weights[pl.ds(half + q * per, per)].reshape(width, width)
    pre = dot(x_ref[:, 0:width], first)
    cdf = normal_cdf(pre)
    act = (pre * cdf).astype(bf16)
    act_ref[...] = act
    dact = dot_nt(dy_ref[...], second)
    dpre = (dact * (cdf + pre * density(pre))).astype(bf16)
    dpre_ref[...] = dpre
    y_part = dot(act, second)
    dx_part = dot_nt(dpre, first)

    @pl.when(q == 0)
    def _():
        y_sum[...] = y_part
        dx_sum[...] = dx_part

    @pl.when(q > 0)
    def _():
        y_sum[...] += y_part
        dx_sum[...] += dx_part

    @pl.when(q == pl.num_programs(0) - 1)
    def _():
        y = y_sum[...].astype(bf16).astype(f32)
        stride = y.shape[0] // blocks
        for block in range(blocks):
            y_near[block ^ me_ref[1]] = y[block * stride : (block + 1) * stride].astype(bf16)
        for pair, ref in enumerate(y_refs):
            ref[...] = y_near[2 * pair : 2 * pair + 2]
        dx_ref[:, 0:width] = dx_sum[...].astype(bf16)
        gate_grad = jnp.sum(g_ref[...].astype(f32) * y, axis=-1, keepdims=True)
        dx_ref[:, width:] = split_lanes(gate_grad)


def expert_grad_kernel(dims, dp_ref, x_ref, dy_ref, act_ref, dpre_ref, *refs):
    parts, quarter = dims
    out_refs, scratch, sems = refs[:4], refs[-2], refs[-1]
    q = pl.program_id(0)
    me = dp_ref[0]
    width = dy_ref.shape[1]
    half = parts // 2
    rows = scratch.shape[1]
    side_rows = rows // 2

    def leave(owner, first, count, sem):
        place = owner ^ me
        side = first // side_rows
        source = scratch.at[place, pl.ds(first, count)]
        at = pl.ds(pl.multiple_of(lax.rem(first, side_rows), 16), count)
        for which, (bit, index) in enumerate(((1, place >> 1), (half, place & (half - 1)))):
            for taken, ref in enumerate((out_refs[2 * which + 1], out_refs[2 * which])):

                @pl.when((side == which) & (((place & bit) > 0) == (taken == 1)))
                def _():
                    pltpu.make_async_copy(source, ref.at[index, at], sem).start()

    first = dot_tn(x_ref[:, 0:width], dpre_ref[...]).astype(bf16)
    count = width // half
    at = pl.multiple_of(q * quarter, 16)
    for i in range(half):
        scratch[i ^ me, pl.ds(at, quarter), :] = first[i * count : (i + 1) * count]
        leave(i, at, quarter, sems.at[i])
    second = dot_tn(act_ref[...], dy_ref[...]).astype(bf16)
    step = min(width, side_rows)
    for i in range(width // step):
        flat = q * width + i * step
        owner, at = half + flat // rows, pl.multiple_of(lax.rem(flat, rows), 16)
        scratch[owner ^ me, pl.ds(at, step), :] = second[i * step : (i + 1) * step]
        leave(owner, at, step, sems.at[half + i])

    @pl.when(q == pl.num_programs(0) - 1)
    def _():
        whole = out_refs[0].at[0]
        for _ in range(4):
            for i in range(half):
                pltpu.make_async_copy(scratch.at[0, 0:quarter], whole.at[0:quarter], sems.at[i]).wait()
            for i in range(width // step):
                pltpu.make_async_copy(scratch.at[0, 0:step], whole.at[0:step], sems.at[half + i]).wait()


def combine(stream_ref, gain, wr_ref, picks_ref, cols_ref, cot_ref, c_ref, probs_ref, dx_ref, grad_ref):
    width = stream_ref.shape[1]
    experts = wr_ref.shape[1]
    probs = probs_ref[...]
    hots = pick_hots(picks_ref, experts)
    selects = token_selects(cols_ref, dx_ref.shape[0])
    prob_grad = None
    for j in range(2):
        part = add_lanes(dot(selects[j], dx_ref[:, width:])) * hots[j]
        prob_grad = part if prob_grad is None else prob_grad + part
    logit_grad = probs * (prob_grad - jnp.sum(prob_grad * probs, axis=-1, keepdims=True))
    logit_grad = logit_grad.astype(bf16)
    router_grad = dot_tn(c_ref[...], logit_grad)
    back = dot(selects[0] + selects[1], dx_ref[:, 0:width]) + dot_nt(logit_grad, wr_ref[...])
    normed, inverse = norm_rows(stream_ref[...])
    addend, gain_grad = norm_back(back, normed, inverse, gain)
    grad_ref[...] = cot_ref[...].astype(f32) + addend
    return gain_grad, router_grad


def put_router(out_ref, value, scratch):
    width, experts = value.shape
    many = LANES // experts
    scratch[...] = jnp.zeros_like(scratch)
    scratch[:, 0:experts] = value
    total = None
    for m in range(many):
        rows = scratch[pl.ds(m, width // many, stride=many), :]
        rows = pltpu.roll(rows, m * experts, 1) if m else rows
        total = rows if total is None else total + rows
    out_ref[0 : width // many, :] = total


def backward_kernel(
    seq, spots, count, by_core, place_ref, gains_ref, wr_ref, picks_ref, cols_ref, cot_ref, probs_ref, dx_ref, *refs
):
    ins, refs = refs[:16], refs[16:]
    arrays, refs = refs[:count], refs[count:]
    if not by_core:
        w1_ref, refs = refs[0], refs[1:]
    small_ref, upper_out, dq_out, dk_out, dv_out, grad_out, *refs = refs
    keep_ref, send_ref, keeps_ref, send2_ref, send_rest, *refs = refs
    places = send_ref.shape[0]
    most, rest = send2_ref.shape[0], places - send2_ref.shape[0]
    keeps = (keep_ref, keeps_ref.at[0])
    sends = ([(send_ref, places)], [(send2_ref, most), (send_rest.at[0], rest)])
    if by_core:
        send1_ref, *refs = refs
        keep1_ref, send1 = keeps_ref.at[1], [(send1_ref, most), (send_rest.at[1], rest)]
    else:
        dw1_ref, *refs = refs
    held, refs = refs[:16], refs[16:]
    grads, refs = refs[:4], refs[4:]
    dq_ref, dk_ref, dv_ref, do_ref, dw, dw2, w2_ref, w_attn, *refs = refs
    if by_core:
        dw1, w1_ref, *refs = refs
    router_scratch, in_sems, w_sems, out_sems, last_sems = refs
    low = place_ref[0]
    experts = wr_ref.shape[1]

    def fetch(first, last):
        copies = [pltpu.make_async_copy(ins[i], held[i], in_sems.at[i]) for i in range(first, last)]
        for copy in copies:
            copy.start()
        return copies

    def fetch_layer(layer, target, at):
        copies = layer_copies(spots, arrays, place_ref, layer, target, w_sems.at[at])
        for copy in copies:
            copy.start()
        return copies

    part = fetch(0, 2)
    second = fetch_layer(1, w_attn.at[0], 0) + fetch(2, 8)
    wait_all(part)
    gain_four, router_grad = combine(
        held[0], gains_ref[3:4], wr_ref, picks_ref, cols_ref, cot_ref, held[1], probs_ref, dx_ref, grads[0]
    )
    tiles = router_grad.shape[0] // LANES
    router_rows = router_grad.shape[0] * experts // LANES
    small_ref[...] = jnp.zeros_like(small_ref)
    put_router(small_ref, router_grad, router_scratch)

    def put_gain(which, value):
        at = router_rows + which * tiles
        for j in range(tiles):
            small_ref[at + j : at + j + 1, :] = value[:, LANES * j : LANES * (j + 1)]

    put_gain(3, gain_four)
    middle = fetch(8, 12) + fetch_layer(3, w2_ref, 1)
    if by_core:
        middle += fetch_layer(2, w1_ref, 2)
    wait_all(second)
    stream, q, k, v, a, o = held[2:8]
    gain_three = attn_bwd(
        seq, grads[0], stream, gains_ref[2:3], w_attn.at[0], q, k, v, grads[1], dq_ref, dk_ref, dv_ref, do_ref
    )
    put_gain(2, gain_three)
    attn_weights(low, grads[0], a, o, dq_ref, dk_ref, dv_ref, dw, keeps[0], sends[0], out_sems.at[0])
    first = fetch(12, 16) + fetch_layer(0, w_attn.at[1], 3)
    wait_all(middle)
    stream, b, u, cdf = held[8:12]
    width = stream.shape[1]
    groups = w1_ref.shape[0]

    def put_first(q, value):
        rows = width // groups
        for i in range(groups):
            piece = value[i * rows : (i + 1) * rows]
            if by_core:
                put_chunk(dw1, low, i, piece, q * rows)
                if q == 3:
                    leave_chunk(dw1, low, i, keep1_ref, send1, out_sems.at[2, i])
            else:
                dw1_ref[i, q * rows : (q + 1) * rows, :] = piece

    def put_second(q, value):
        rows = dw2.shape[2]
        per = width // rows
        for i in range(per):
            put_chunk(dw2, low, q * per + i, value[i * rows : (i + 1) * rows])
            leave_chunk(dw2, low, q * per + i, keeps[1], sends[1], out_sems.at[1, q * per + i])

    gain_two = mlp_bwd(
        grads[1], stream, gains_ref[1:2], w1_ref, w2_ref, b, u, cdf, grads[2], put_first, put_second
    )
    put_gain(1, gain_two)
    leaving = start_all((grads[2],), (upper_out,), last_sems)
    wait_all(first)
    wait_chunks(dw, low, keeps[0], out_sems.at[0])
    stream, q, k, v = held[12:16]
    gain_one = attn_bwd(
        seq, grads[2], stream, gains_ref[0:1], w_attn.at[1], q, k, v, grads[3], dq_ref, dk_ref, dv_ref, do_ref
    )
    put_gain(0, gain_one)
    outs = ((dq_ref, dq_out), (dk_ref, dk_out), (dv_ref, dv_out), (grads[3], grad_out))
    for i, (source, target) in enumerate(outs):
        leaving.append(pltpu.make_async_copy(source, target, last_sems.at[1 + i]))
        leaving[-1].start()
    wait_chunks(dw2, low, keeps[1], out_sems.at[1])
    if by_core:
        wait_chunks(dw1, low, keep1_ref, out_sems.at[2])
    wait_all(leaving)


def output_kernel(stream_ref, picks_ref, near_ref, probs_ref, grad_ref, *refs):
    y_refs, (other_ref, out_ref, grad_out, wide) = refs[:-4], refs[-4:]
    stride = other_ref.shape[1]
    for pair, ref in enumerate(y_refs):
        wide[2 * pair * stride : (2 * pair + 1) * stride] = ref[0].astype(f32)
        wide[(2 * pair + 1) * stride : (2 * pair + 2) * stride] = other_ref[pair].astype(f32)
    y = wide[...].astype(bf16)
    tiles = stream_ref.shape[1] // LANES
    seq = out_ref.shape[0] // tiles
    probs = probs_ref[...]
    hots = pick_hots(picks_ref, probs.shape[1])
    selects = token_selects(near_ref, y.shape[0])
    total = stream_ref[...]
    for j in range(2):
        gate = jnp.sum(probs * hots[j], axis=-1, keepdims=True)
        total = total + gate * dot(selects[j], y)
    for value, ref in ((total, out_ref), (grad_ref, grad_out)):
        for j in range(tiles):
            ref[pl.ds(j, seq, stride=tiles), :] = value[0:seq, LANES * j : LANES * (j + 1)]


def add_pair(left, right):
    return (left.astype(f32) + right.astype(f32)).astype(bf16)


def pack_sets_kernel(*refs):
    *parts, out_ref, sems = refs
    wait_all(start_all(parts, [out_ref.at[i // 4, i % 4] for i in range(len(parts))], sems))


def fold_layers_kernel(cut, plan, top_ref, *refs):
    uppers, (keep_x, send_y, keep_y, send_x), scratch = refs[-14:-10], refs[-10:-6], refs[-6:]
    kept, got, total, keep_sems, got_sems, out_sems = scratch
    count = kept.shape[1]
    x_part = slice(cut, cut + send_x.shape[1])
    y_part = slice(x_part.stop, x_part.stop + send_y.shape[2])
    ins = []
    for layer, at, sources in plan:
        keep_ref, refs = refs[0], refs[1:]
        keep_ref = keep_ref if at is None else keep_ref.at[at]
        got_refs = []
        for index, many in sources:
            ref, refs = refs[0], refs[1:]
            ref = ref if index is None else ref.at[index]
            got_refs += [ref.at[i] for i in range(many)]
        ins.append((layer, keep_ref, got_refs))

    def arriving(n, i):
        _, keep_ref, got_refs = ins[n]
        return (
            pltpu.make_async_copy(keep_ref.at[i], kept.at[n, i], keep_sems.at[n, i]),
            pltpu.make_async_copy(got_refs[i], got.at[n, i], got_sems.at[n, i]),
        )

    steps = [(n, i) for n in range(len(ins)) for i in range(count)]
    for n, i in steps:
        for copy in arriving(n, i):
            copy.start()
    for n, i in steps:
        layer = ins[n][0]
        place = layer ^ top_ref[0]
        for copy in arriving(n, i):
            copy.wait()
        total[n, i] = add_pair(kept[n, i], got[n, i])
        pltpu.make_async_copy(total.at[n, i, 0:cut], uppers[i % 4].at[layer, i // 4], out_sems.at[n, 0, i]).start()
        for bit, send, keep, where, sem in (
            (place & 1, send_x.at[i], keep_x.at[place >> 1, i], x_part, out_sems.at[n, 1, i]),
            (place >> 1, send_y.at[place & 1, i], keep_y.at[place & 1, i], y_part, out_sems.at[n, 2, i]),
        ):
            for value, target in ((0, keep), (1, send)):

                @pl.when(bit == value)
                def _():
                    pltpu.make_async_copy(total.at[n, i, where], target, sem).start()

    for n, i in steps:
        layer = ins[n][0]
        pltpu.make_async_copy(total.at[n, i, 0:cut], uppers[i % 4].at[layer, i // 4], out_sems.at[n, 0, i]).wait()
        pltpu.make_async_copy(total.at[n, i, x_part], keep_x.at[0, i], out_sems.at[n, 1, i]).wait()
        pltpu.make_async_copy(total.at[n, i, y_part], keep_y.at[0, i], out_sems.at[n, 2, i]).wait()


def add_kernel(left, right, out_ref):
    out_ref[...] = add_pair(left[...], right[...])


def pause_kernel(ref, out_ref):
    for i in range(ref.shape[0]):
        out_ref[i] = ref[i]


def fold_plane_kernel(top_ref, keep_x, got_one, got_two, keep_y, got_y, own_a, send_y, own_b, send_x):
    for place in range(2):

        @pl.when(top_ref[0] >> 1 == place)
        def _():
            near, far = (got_two, got_one) if place == 0 else (got_one, got_two)
            own_a[...] = add_pair(keep_x[0], near[...])
            send_y[...] = add_pair(keep_x[1], far[...])

    own_b[...] = add_pair(keep_y[0], got_y[0])
    send_x[...] = add_pair(keep_y[1], got_y[1])


def fold_rows_kernel(own_a, got_a, own_b, got_b, *outs):
    middle = own_a.shape[1]
    for place in range(own_a.shape[0]):
        out = outs[place % 4].at[place // 4]
        out[0:middle] = add_pair(own_a[place], got_a[place])
        out[middle:] = add_pair(own_b[place], got_b[place])


def fold_uppers_kernel(top_ref, *refs):
    refs, outs, scratch = refs[:-5], refs[-5:-1], refs[-1]
    for layer in range(4):
        scratch[layer ^ top_ref[0]] = sum(ref[layer].astype(f32) for ref in refs).astype(bf16)
    for place, out in enumerate(outs):
        out[...] = scratch[place]


def fold_expert_kernel(highs, *refs):
    ins, outs = refs[:4], refs[4:]
    count = ins[0].shape[0]
    for side, high in enumerate(highs):
        half = count // 2
        for i in range(count):
            which, at = (i // half, i % half) if high else (i % 2, i // 2)
            outs[side * count + which * half + at][...] = add_pair(ins[2 * side][i], ins[2 * side + 1][i])


def swap(value, axes, mask):
    size = 1
    for axis in axes:
        size *= lax.axis_size(axis)
    return lax.ppermute(value, axes, [(i, i ^ mask) for i in range(size)])


def after(value, *others):
    return lax.optimization_barrier((value, others))[0]


def pause(scalars, rows, others):
    scalars, others = lax.optimization_barrier((scalars, others))
    scalars = pl.pallas_call(
        pause_kernel,
        in_specs=[SMEM],
        out_specs=SMEM,
        out_shape=shape(scalars.shape, jnp.int32),
        compiler_params=params(),
        cost_estimate=cost(rows),
        name="pause",
    )(scalars)
    return scalars, others


class Order:
    def __init__(self):
        self.latest = ()

    def land(self, value):
        self.latest = after(value, self.latest)
        return self.latest


def bit_groups(bits):
    odd = len(bits) % 2
    return [bits[:odd]] * odd + [bits[i : i + 2] for i in range(odd, len(bits), 2)]


def all_sum_step(value, axes, bits):
    if len(bits) == 1:
        return value + swap(value, axes, 1 << bits[0])
    low, high = 1 << bits[0], 1 << bits[1]
    near, far, both = swap(value, axes, low), swap(value, axes, high), swap(value, axes, low | high)
    return (value + near) + (far + both)


def reduce_bits(value, axes, bits):
    for bit in bits:
        pairs = value.reshape((value.shape[0] // 2, 2) + value.shape[1:])
        value = pairs[:, 0] + swap(pairs[:, 1], axes, 1 << bit)
    return value[0]


def shape(dims, dtype=f32):
    return jax.ShapeDtypeStruct(dims, dtype)


def on_device(
    tokens,
    cotangent,
    expert_picks,
    priority,
    dense_master,
    dense_momentum,
    dense_variance,
    expert_master,
    expert_momentum,
    expert_variance,
):
    both = ("dp", "expert")
    dp_ranks = lax.axis_size("dp")
    expert_ranks = lax.axis_size("expert")
    devices = dp_ranks * expert_ranks
    local_experts = expert_master.shape[0]
    experts = local_experts * expert_ranks
    images, seq, width = tokens.shape
    assert local_experts == 1 and images == 1
    assert devices & (devices - 1) == 0 and dp_ranks >= 4
    tiles = width // LANES
    dp_me = lax.axis_index("dp").astype(jnp.int32)
    me = dp_me * expert_ranks + lax.axis_index("expert").astype(jnp.int32)
    me_arr = me.reshape(1)
    dp_arr = dp_me.reshape(1)
    dp_bits = dp_ranks.bit_length() - 1
    all_bits = devices.bit_length() - 1

    own = dense_master.shape[0] // LANES
    expert_flat = expert_master.shape[1] // LANES
    hidden = expert_master.shape[1] * dp_ranks // (2 * width)
    matrix_rows = 8 * width + 2 * hidden
    rows = matrix_rows // devices
    step = own - rows * tiles
    tail = step * devices
    tail_rows = -(-tail // (16 * tiles)) * 16
    wide_ok = rows % 64 == 0
    expert_rows = expert_flat // tiles

    dense_flat = dense_master.reshape(own, LANES)
    forward_ring = [(i, (i + 1) % devices) for i in range(devices)]
    backward_ring = [((i + 1) % devices, i) for i in range(devices)]
    tail_from = lax.ppermute(dense_flat[own - tail :], both, forward_ring)
    buf_rows = -(-(own + max(tail, tail_rows * tiles)) // 8) * 8
    chunk = pl.pallas_call(
        functools.partial(
            pack_dense_kernel, (rows, tail_rows, tail, own, step, tiles, devices, wide_ok)
        ),
        in_specs=[SMEM, VMEM, VMEM],
        out_specs=VMEM,
        out_shape=shape((rows + tail_rows, width), bf16),
        scratch_shapes=[pltpu.VMEM((buf_rows, LANES), f32)],
        compiler_params=params(),
        cost_estimate=cost(),
        name="pack_dense",
    )(me_arr, tail_from, dense_flat)

    expert_wide = (dp_me < dp_ranks // 2).astype(jnp.int32).reshape(1)
    quarter = expert_rows // 4
    cuts = [(0, 2), (2, 4), (0, 1), (1, 2), (2, 3), (3, 4)]
    cuts = [(low * quarter, high * quarter) for low, high in cuts]
    expert_chunks = pl.pallas_call(
        functools.partial(pack_expert_kernel, (expert_rows, tiles), cuts),
        in_specs=[SMEM, VMEM],
        out_specs=[VMEM] * 6,
        out_shape=[shape((high - low, width), bf16) for low, high in cuts],
        compiler_params=params(),
        cost_estimate=cost(),
        name="pack_expert",
    )(expert_wide, expert_master.reshape(expert_flat, LANES))
    dp_axis = ("dp",)
    dp_order = list(range(dp_bits))

    def gather_step(parts, bit):
        return {**parts, **{at | (1 << bit): swap(part, dp_axis, 1 << bit) for at, part in parts.items()}}

    capacity = 2 * seq // experts
    stride = -(-capacity // 8) * 8
    slots = experts * stride
    padded = -(-seq // 16) * 16
    fill = padded - seq
    ranks = jnp.pad(priority, ((0, 0), (0, fill)), constant_values=1 << 20)
    picks = jnp.pad(expert_picks, ((0, fill), (0, 0)), constant_values=-1)
    cot = jnp.pad(cotangent.reshape(seq, width), ((0, fill), (0, 0)))
    stream = jnp.pad(tokens.reshape(seq, width).astype(f32), ((0, fill), (0, 0)))
    e_me = lax.axis_index("expert").astype(jnp.int32).reshape(1)
    pair_shape = shape((2, stride, width), bf16)
    cols, near_cols, rows_slots, outgoing_cot = pl.pallas_call(
        functools.partial(route_kernel, experts, capacity, stride),
        in_specs=[SMEM] + [VMEM] * 5,
        out_specs=[VMEM] * 4,
        out_shape=[shape((padded, 2), jnp.int32)] * 2
        + [shape((2, padded), jnp.int32), shape((slots, width), bf16)],
        compiler_params=params(),
        cost_estimate=cost(),
        name="route",
    )(e_me, ranks, ranks.reshape(padded, 1), picks, picks.T, cot)

    def exchange(value):
        dims = value.shape
        value = value.reshape(expert_ranks, slots // expert_ranks, dims[1])
        value = lax.all_to_all(value, "expert", split_axis=0, concat_axis=0, tiled=True)
        return value.reshape(dims)

    per = devices // 4
    per_bits = per.bit_length() - 1
    top_bits = (per_bits, per_bits + 1)
    chunk_rows = rows + tail_rows
    low = me & (per - 1)
    low_arr = low.reshape(1)
    place_arr = jnp.stack([low, me >> per_bits])
    expert_me = jnp.concatenate([dp_arr, e_me])
    half_rows = expert_rows // 2
    orders = (dp_order, dp_order[::-1])
    expert_parts, expert_spans = [], []
    if per_bits == 3 and dp_bits == 2:
        masks = [1 << bit for bit in top_bits]
        split = chunk_rows // 32 * 16 + 16
        order = Order()

        def spread(value):
            return [swap(value, both, mask) for mask in masks]

        sets = [chunk, swap(chunk, both, 2), None, None]
        near, far = [spread(chunk)] + [None] * 3, [None] * 4
        near[0] = order.land(near[0])
        sets[1] = order.land(sets[1])
        near[1] = spread(sets[1])
        sets[2] = swap(after(chunk, sets[1]), both, 4)
        halves = [swap(near[0][1][:split], both, masks[0]), swap(near[0][0][split:], both, masks[1])]
        near[1] = order.land(near[1])
        halves = order.land(halves)
        far[0] = jnp.concatenate(halves)
        x_half, y_half, *quarters = expert_chunks
        first, second = after((quarters[2], quarters[0]), halves)
        early = [swap(first, dp_axis, 1), swap(second, dp_axis, 2)]
        sets[2], outgoing_cot, stream = order.land((sets[2], outgoing_cot, stream))
        sets[3] = swap(sets[2], both, 2)
        near[2] = spread(sets[2])
        early = order.land(early)
        place_arr, early = pause(place_arr, 100, early)
        sets[3], far[0], place_arr = order.land((sets[3], far[0], place_arr))
        far[1], far[2] = swap(far[0], both, 2), swap(far[0], both, 4)
        near[3] = spread(sets[3])
        near[2] = order.land(near[2])
        near[3] = order.land(near[3])
        far[1] = order.land(far[1])
        far[2] = order.land(far[2])
        far[3] = swap(far[2], both, 2)
        arriving_cot = exchange(after(outgoing_cot, far[2]))

        def pack_sets(which):
            ins = [part for s in which for part in (sets[s], *near[s], far[s])]
            return pl.pallas_call(
                pack_sets_kernel,
                in_specs=[pl.BlockSpec(memory_space=pl.ANY)] * len(ins),
                out_specs=VMEM,
                out_shape=shape((len(which), 4, chunk_rows, width), bf16),
                scratch_shapes=[pltpu.SemaphoreType.DMA((len(ins),))],
                compiler_params=params(),
                cost_estimate=cost(),
                name="pack_sets",
            )(*ins)

        x_out, y_out = after((x_half, y_half), near[3])
        beside = [swap(x_out, dp_axis, 1), swap(y_out, dp_axis, 2)]
        packed = [pack_sets([0, 1, 2])]
        first_swap = swap(packed[0], both, 1)
        far[3], beside = order.land(after((far[3], beside), packed))
        packed.append(pack_sets([3]))
        arrays = [*packed, first_swap, swap(packed[1], both, 1)]
        at = ((0, 0), (0, 1), (0, 2), (1, 0))
        spots = [(at[j >> 1][0] + 2 * (j & 1), (at[j >> 1][1],), ()) for j in range(per)]
        place_arr, beside = pause(place_arr, 4400, beside)
        across = [swap(beside[0], dp_axis, 2), swap(beside[1], dp_axis, 1)]
        late = after((quarters[3], quarters[1]), beside)
        late = [swap(late[0], dp_axis, 1), swap(late[1], dp_axis, 2)]
        place_arr, arrays[2] = pause(place_arr, 300, arrays[2])
        expert_me, (across, arriving_cot) = pause(expert_me, 400, (across, arriving_cot))
        expert_parts = [x_half, y_half, beside[0], early[0], late[0], beside[1], early[1], late[1], *across]
        expert_spans = [(0, 0), (0, 2), (1, 0), (1, 2), (1, 3), (2, 2), (2, 0), (2, 1), (3, 0), (3, 2)]
        expert_spans = [(place, first * quarter) for place, first in expert_spans]
    else:
        gathered = chunk[None]
        for bit in range(all_bits):
            gathered = jnp.concatenate([gathered, swap(gathered, both, 1 << bit)])
        arrays = [gathered.reshape(4, per, chunk_rows, width)]
        spots = [(0, (), (j,)) for j in range(per)]
        for side, bits in enumerate(orders):
            parts, places = [expert_chunks[side]], [0]
            for bit in bits:
                parts = parts + [swap(part, dp_axis, 1 << bit) for part in parts]
                places = places + [place | (1 << bit) for place in places]
            expert_parts += parts
            expert_spans += [(place, side * half_rows) for place in places]
        arriving_cot = exchange(outgoing_cot)

    layer_w = pltpu.VMEM((per, rows, width), bf16)
    if not wide_ok:
        first_in = lax.dynamic_index_in_dim(arrays[0], 2 ^ (me >> per_bits), 0, keepdims=False)
        first_in = jnp.take(first_in, jnp.arange(per) ^ low, axis=0)[:, :rows].reshape(width, 4, width)
        first_in = first_in.transpose(1, 0, 2).reshape(1, 4 * width, width)

    act_shape = shape((padded, width), bf16)
    stream_shape = shape((padded, width), f32)
    gain_shape = shape((1, width), f32)
    tok_flops = 2 * padded * width * width
    weight_bytes = 2 * width * width
    ANY = pl.BlockSpec(memory_space=pl.ANY)

    def call(kernel, ins, in_specs, outs, name, rows=0, mib=56, out_specs=None, scratch=(), aliases=None):
        out_specs = out_specs or [None] * len(outs)

        def whole(a):
            return pl.BlockSpec(a.shape, lambda *_, n=len(a.shape): (0,) * n)

        return pl.pallas_call(
            kernel,
            grid=(1,),
            in_specs=[s or whole(a) for a, s in zip(ins, in_specs, strict=True)],
            out_specs=[s or whole(a) for a, s in zip(outs, out_specs, strict=True)],
            out_shape=outs,
            scratch_shapes=list(scratch),
            compiler_params=params(mib),
            cost_estimate=cost(rows),
            input_output_aliases=aliases or {},
            name=name,
        )(*ins)

    places = per // 2
    core_shape = shape((places, rows, width), bf16)
    by_core = pltpu.VMEM((2, places, rows, width), bf16)
    stream_vmem, act_vmem = pltpu.VMEM((padded, width), f32), pltpu.VMEM((padded, width), bf16)

    def attn_weights_call(grad, kept, found):
        return call(
            attn_weights_kernel,
            (low_arr, grad, kept[0], kept[4], *found),
            (SMEM,) + (ANY,) * 6,
            [core_shape, core_shape],
            "attn_weights",
            0,
            out_specs=[ANY] * 2,
            scratch=[
                stream_vmem,
                *[act_vmem] * 5,
                by_core,
                pltpu.SemaphoreType.DMA((6,)),
                pltpu.SemaphoreType.DMA((per,)),
            ],
        )

    outs = [stream_shape] + [act_shape] * 5 + [stream_shape, act_shape] + [shape((padded, hidden))] * 2
    outs += [stream_shape] + [act_shape] * 5
    *results, gains, router, moe_in, probs, outgoing = call(
        functools.partial(forward_kernel, seq, spots, (rows, experts, len(arrays)), wide_ok),
        (place_arr, stream, picks, rows_slots, *arrays, *([] if wide_ok else [first_in])),
        (SMEM, None, None, None) + (ANY,) * len(arrays) + (() if wide_ok else (None,)),
        outs
        + [
            shape((4, width)),
            shape((width, experts), bf16),
            act_shape,
            shape((padded, experts)),
            shape((slots, width + LANES), bf16),
        ],
        "forward",
        0,
        out_specs=[ANY] * 16 + [None] * 5,
        scratch=[pltpu.VMEM(o.shape, o.dtype) for o in outs]
        + [
            pltpu.VMEM((4, per, rows, width), bf16),
            pltpu.VMEM((per, tail_rows, width), bf16),
            pltpu.SemaphoreType.DMA((4, per)),
            pltpu.SemaphoreType.DMA((per,)),
            pltpu.SemaphoreType.DMA((16,)),
        ],
    )
    stream_one, kept_one = results[0], results[1:6]
    stream_two, mlp_in, mlp_pre, mlp_cdf = results[6:10]
    stream_three, kept_two = results[10], results[11:]
    arriving = exchange(outgoing)

    slot_spec = pl.BlockSpec((slots, width), lambda q: (0, 0))
    wide_spec = pl.BlockSpec((slots, width + LANES), lambda q: (0, 0))
    pair_spec = pl.BlockSpec((2, stride, width), lambda q: (0, 0, 0))
    hidden_spec = pl.BlockSpec((slots, width), lambda q: (0, q))
    pairs = experts // 2
    *expert_out, input_back, slot_grad, expert_act, pre_grad = pl.pallas_call(
        functools.partial(expert_kernel, (dp_ranks, quarter, experts), expert_spans),
        grid=(4,),
        in_specs=[SMEM, wide_spec, slot_spec] + [ANY] * len(expert_parts),
        out_specs=[pair_spec] * pairs + [wide_spec, slot_spec, hidden_spec, hidden_spec],
        out_shape=[pair_shape] * pairs
        + [shape((slots, width + LANES), bf16), shape((slots, width), bf16)]
        + [shape((slots, hidden), bf16)] * 2,
        scratch_shapes=[
            pltpu.VMEM((dp_ranks, expert_rows, width), bf16),
            pltpu.VMEM((experts, stride, width), bf16),
            pltpu.VMEM((slots, width), f32),
            pltpu.VMEM((slots, width), f32),
            pltpu.SemaphoreType.DMA((2, len(expert_parts))),
        ],
        compiler_params=params(),
        cost_estimate=cost(),
        name="expert",
    )(expert_me, arriving, arriving_cot, *expert_parts)
    returned_grad = exchange(input_back)
    part_shape = shape((expert_rows // 2, width), bf16)
    count = dp_ranks // 2
    expert_first = pl.pallas_call(
        functools.partial(expert_grad_kernel, (dp_ranks, quarter)),
        grid=(4,),
        in_specs=[SMEM, wide_spec, slot_spec, hidden_spec, hidden_spec],
        out_specs=[ANY] * 4,
        out_shape=[shape((count,) + part_shape.shape, bf16)] * 4,
        scratch_shapes=[
            pltpu.VMEM((dp_ranks, expert_rows, width), bf16),
            pltpu.SemaphoreType.DMA((2 * dp_ranks,)),
        ],
        compiler_params=params(),
        cost_estimate=cost(),
        name="expert_grad",
    )(dp_arr, arriving, slot_grad, expert_act, pre_grad)
    returned_grad = after(returned_grad, expert_first)

    cut = max(16, rows // 48 * 16)
    x_rows = max(16, (rows - cut) * 9 // 256 * 16)
    y_rows = rows - cut - x_rows
    top = (me >> per_bits).reshape(1)
    z_bits = list(range(1, per_bits))
    z_masks = [2 * j for j in (1, 2, 3)]
    assert places % 4 == 0

    def add_call(left, right, weight):
        return call(add_kernel, (left, right), (None, None), [shape(left.shape, bf16)], "add", weight, mib=12)[0]

    def over_z(values, meanwhile, weight=0):
        farthest = swap(values[3], both, 2)
        farthest, *meanwhile[:] = lax.optimization_barrier((farthest, *meanwhile))
        near = swap(after(values[1], farthest), both, 2)
        return [values[0], near, swap(add_call(values[2], farthest, weight), both, 4)]

    def rest_of_z(values):
        if len(z_bits) == 2:
            return values
        total = sum(value.astype(f32) for value in values).astype(bf16)
        lead = total.ndim - 3
        total = jnp.moveaxis(total, lead, 0)
        return [reduce_bits(total, both, z_bits[2:])]

    def to_other_core(parts):
        return [parts[0], swap(parts[1], both, 1)]

    expert_got = [swap(expert_first[0], dp_axis, 1), swap(expert_first[2], dp_axis, dp_ranks // 2)]
    returned_grad, expert_out = lax.optimization_barrier((returned_grad, expert_out))
    expert_out = [expert_out[0]] + [swap(v, ("expert",), 2 * j) for j, v in enumerate(expert_out) if j]
    backward_ins = (
        (stream_three, moe_in, stream_two, *kept_two[1:4], kept_two[0], kept_two[4])
        + (stream_one, mlp_in, mlp_pre, mlp_cdf, stream, *kept_one[1:4])
    )
    held_vmem = [stream_vmem, act_vmem, stream_vmem] + [act_vmem] * 5
    held_vmem += [stream_vmem, act_vmem] + [pltpu.VMEM((padded, hidden), f32)] * 2 + [stream_vmem] + [act_vmem] * 3
    kinds = 2 if wide_ok else 1
    most, rest = places * 3 // 4, places // 4
    keeps_shape = shape((kinds,) + core_shape.shape, bf16)
    most_shape, rest_shape = shape((most, rows, width), bf16), shape((kinds, rest, rows, width), bf16)
    first_dw_out = [most_shape] if wide_ok else [shape((1, 4 * width, width), bf16)]
    small, upper, dq, dk, dv, grad, *dws = call(
        functools.partial(backward_kernel, seq, spots, len(arrays), wide_ok),
        (place_arr, gains, router, picks, cols, cot, probs, returned_grad, *backward_ins, *arrays)
        + (() if wide_ok else (first_in,)),
        (SMEM,) + (None,) * 7 + (ANY,) * (16 + len(arrays)) + (() if wide_ok else (None,)),
        [shape((tail, LANES)), stream_shape, act_shape, act_shape, act_shape, stream_shape]
        + [core_shape, core_shape, keeps_shape, most_shape, rest_shape]
        + first_dw_out,
        "backward",
        out_specs=[None] + [ANY] * 10 + ([ANY] if wide_ok else [None]),
        scratch=held_vmem
        + [stream_vmem] * 4
        + [act_vmem] * 4
        + [by_core, by_core, layer_w, pltpu.VMEM((2, per, rows, width), bf16)]
        + ([by_core, layer_w] if wide_ok else [])
        + [
            pltpu.VMEM((width, LANES), f32),
            pltpu.SemaphoreType.DMA((16,)),
            pltpu.SemaphoreType.DMA((4, per)),
            pltpu.SemaphoreType.DMA((3, per)),
            pltpu.SemaphoreType.DMA((5,)),
        ],
    )
    if not wide_ok:
        wide_grad = dws[5].reshape(4, width, width).transpose(1, 0, 2).reshape(per, rows, width)
        wide_grad = jnp.take(wide_grad, jnp.arange(per) ^ low, axis=0)
        wide_grad = wide_grad.reshape(places, 2, rows, width)
        dws[2] = jnp.concatenate([dws[2], wide_grad[None, :, 0]])
        dws[4] = jnp.concatenate([dws[4], wide_grad[None, most:, 1]])
        dws[5] = wide_grad[:most, 1]
    dws, expert_out = lax.optimization_barrier((dws, expert_out))
    most_got = [swap(dws[3], both, 1), swap(dws[5], both, 1)]
    rest_got = swap(dws[4], both, 1)
    first_dw = attn_weights_call(upper, kept_one, (dq, dk, dv))
    layer_got = {0: [(swap(first_dw[1], both, 1), None, places)], 1: [(swap(dws[1], both, 1), None, places)]}
    for i, layer in enumerate((3, 2)):
        layer_got[layer] = [(most_got[i], None, most), (rest_got, i, rest)]
    layer_keep = {3: (dws[2], 0), 2: (dws[2], 1), 1: (dws[0], None), 0: (first_dw[0], None)}

    x_plane, y_plane = (shape((2, places, part, width), bf16) for part in (x_rows, y_rows))
    x_line, y_line = (shape((places, part, width), bf16) for part in (x_rows, y_rows))
    plane_specs = [pl.BlockSpec((2, 1, part, width), lambda i: (0, i, 0, 0)) for part in (x_rows, y_rows)]
    line_specs = [pl.BlockSpec((1, part, width), lambda i: (i, 0, 0)) for part in (x_rows, y_rows)]
    upper_shape = shape((4, places // 4, cut, width), bf16)
    sums, got_x = (), []
    masks = [1 << bit for bit in top_bits]
    for pair in ((3, 2), (1, 0)):
        if pair[0] == 1:
            expert_got, sums = lax.optimization_barrier((expert_got, sums))
            top, expert_got = pause(top, 1600, expert_got)
        plan, ins = [], []
        for layer in pair:
            keep, at = layer_keep[layer]
            parts = layer_got[layer]
            plan.append((layer, at, [part[1:] for part in parts]))
            ins += [after(keep, first_dw) if layer == 3 else keep] + [part[0] for part in parts]
        *sums, out = call(
            functools.partial(fold_layers_kernel, cut, plan),
            (top, *ins, *sums),
            (SMEM,) + (ANY,) * (len(ins) + len(sums)),
            [upper_shape] * 4 + [x_plane, y_plane, y_plane, x_line],
            "fold_layers",
            out_specs=[ANY] * 8,
            scratch=[pltpu.VMEM((2, places, rows, width), bf16)] * 3
            + [
                pltpu.SemaphoreType.DMA((2, places)),
                pltpu.SemaphoreType.DMA((2, places)),
                pltpu.SemaphoreType.DMA((2, 3, places)),
            ],
            aliases={1 + len(ins) + i: i for i in range(len(sums))},
        )
        got_x.append(swap(out, both, masks[0]))
    *uppers, keep_x, send_y, keep_y = sums
    got_y = swap(send_y, both, masks[1])
    me_top, landed = top, [got_x[0]]
    uppers = over_z(uppers, landed, 300)
    got_x[:1] = landed
    expert_ins = (expert_first[1], expert_got[0], expert_first[3], expert_got[1])
    expert_second = call(
        functools.partial(fold_expert_kernel, (dp_bits == 1, True)),
        expert_ins,
        (None,) * len(expert_ins),
        [part_shape] * (2 * count),
        "fold_expert",
        0,
    )

    top, uppers = pause(top, 250, uppers)
    uppers = [value.reshape(4, -1, cut, width) for value in uppers]
    uppers = [value.reshape(4, cut, width) for value in rest_of_z(uppers)]
    upper_rows = call(
        fold_uppers_kernel,
        (top, *uppers),
        (SMEM,) + (None,) * len(uppers),
        [shape((cut, width), bf16)] * 4,
        "fold_uppers",
        100,
        scratch=[pltpu.VMEM((4, cut, width), bf16)],
    )
    got_x, got_y, expert_second = lax.optimization_barrier((got_x, got_y, expert_second))
    own_a, send_y, own_b, send_x = pl.pallas_call(
        fold_plane_kernel,
        grid=(places,),
        in_specs=[SMEM, plane_specs[0], line_specs[0], line_specs[0], plane_specs[1], plane_specs[1]],
        out_specs=[line_specs[0]] * 2 + [line_specs[1]] * 2,
        out_shape=[x_line] * 2 + [y_line] * 2,
        compiler_params=params(),
        cost_estimate=cost(),
        name="fold_plane",
    )(me_top, keep_x, *got_x, keep_y, got_y)
    got_y, got_x = swap(send_y, both, masks[1]), swap(send_x, both, masks[0])
    got_y, got_x = after((got_y, got_x), top)
    expert_second = after(expert_second, got_y, got_x)
    other_out = swap(jnp.stack([value[1] for value in expert_out]), ("expert",), 1)
    lower_rows = call(
        fold_rows_kernel,
        (own_a, got_y, own_b, got_x),
        (None,) * 4,
        [shape((places // 4, rows - cut, width), bf16)] * 4,
        "fold_rows",
        0,
    )
    lower_rows, other_out = lax.optimization_barrier((lower_rows, other_out))
    output, grad = call(
        output_kernel,
        (stream_three, picks, near_cols, probs, grad, *expert_out, other_out),
        (None,) * (6 + pairs),
        [shape((seq * tiles, LANES))] * 2,
        "output",
        mib=16,
        scratch=[pltpu.VMEM((slots, width), f32)],
    )
    image = (1, seq, width)
    meanwhile = [output.reshape(image), grad.reshape(image), upper_rows]
    lower_rows = over_z(lower_rows, meanwhile, 250)
    output, grad, upper_rows = meanwhile
    half = count // 2
    expert_groups = []
    for side, bits in enumerate(orders):
        keep, send = (expert_second[(2 * side + i) * half : (2 * side + i + 1) * half] for i in range(2))
        got = [swap(part, dp_axis, 1 << bits[1]) for part in send]
        expert_groups.append([list(pair) for pair in zip(keep, got)])
    if dp_bits > 2:
        for side, bits in enumerate(orders):
            value = [sum(pair) for pair in expert_groups[side]]
            for bit in bits[2:]:
                half = len(value) // 2
                keep, send = (value[:half], value[half:]) if side else (value[0::2], value[1::2])
                value = [k + swap(v, dp_axis, 1 << bit) for k, v in zip(keep, send)]
            expert_groups[side] = [value]
    expert_groups = [side[0] for side in expert_groups]
    upper_rows, expert_groups = lax.optimization_barrier((upper_rows, expert_groups))

    def unpack(wide, groups, count, name, extra=(), more_shapes=((1, LANES),)):
        pieces = [piece for group in groups for piece in group] + list(extra)
        return pl.pallas_call(
            functools.partial(unpack_kernel, (count, tiles), [len(group) for group in groups]),
            in_specs=[SMEM] + [VMEM] * len(pieces),
            out_specs=[VMEM] * (1 + len(more_shapes)),
            out_shape=[shape((count * tiles, LANES))] + [shape(dims) for dims in more_shapes],
            scratch_shapes=[pltpu.VMEM((count, width), f32)],
            compiler_params=params(),
            cost_estimate=cost(),
            name=name,
        )(wide, *pieces)

    expert_grad, expert_square = unpack(expert_wide, expert_groups, expert_rows, "unpack_expert")
    lower_rows, output, expert_grad, expert_square = lax.optimization_barrier(
        (lower_rows, output, expert_grad, expert_square)
    )
    lower_rows = rest_of_z(lower_rows)
    upper_rows = [upper_rows[0]] + [
        swap(value, both, masks[0] * j) for j, value in enumerate(upper_rows) if j
    ]
    dense_groups = [upper_rows, [value.reshape(rows - cut, width) for value in lower_rows]]

    dense_wide = (me >= devices // 2) & (me < 3 * devices // 4) & wide_ok
    dense_rows, total, head = unpack(
        dense_wide.astype(jnp.int32).reshape(1),
        dense_groups,
        rows,
        "unpack_dense",
        (small, expert_square),
        ((tail + 8, LANES), (tail, LANES)),
    )
    head = lax.ppermute(head, both, backward_ring)
    groups = bit_groups(list(range(all_bits)))
    for bits in groups[:-1]:
        total = all_sum_step(total, both, bits)
    total, head = lax.optimization_barrier((total, head))
    total = all_sum_step(total, both, groups[-1])
    param_count = (dense_master.size + expert_master.size) * devices

    chunks = 16
    results = pl.pallas_call(
        functools.partial(adam_kernel, (step, chunks, devices, param_count, width * experts // LANES)),
        in_specs=[SMEM, VMEM, VMEM] + [ANY] * 6,
        out_specs=[ANY] * 7 + [VMEM],
        out_shape=[shape((expert_flat, LANES))] * 3 + [shape((own, LANES))] * 4 + [shape((4, width))],
        scratch_shapes=[pltpu.VMEM((expert_flat, LANES), f32)] * 3
        + [
            pltpu.VMEM((4, 3, expert_flat // chunks, LANES), f32),
            pltpu.VMEM((-(-(rows * tiles + tail) // 8) * 8, LANES), f32),
            pltpu.VMEM((4, own, LANES), f32),
            pltpu.SemaphoreType.DMA((chunks, 3)),
            pltpu.SemaphoreType.DMA((4, 3)),
            pltpu.SemaphoreType.DMA((3,)),
            pltpu.SemaphoreType.DMA((4,)),
        ],
        compiler_params=params(),
        cost_estimate=cost(),
        name="adam",
    )(
        me_arr,
        total,
        head,
        expert_grad,
        expert_momentum.reshape(expert_flat, LANES),
        expert_variance.reshape(expert_flat, LANES),
        dense_rows,
        dense_momentum.reshape(own, LANES),
        dense_variance.reshape(own, LANES),
    )
    gain_grads = results[7]
    expert_update, momentum_expert, variance_expert = results[:3]
    dense_update, momentum_dense, variance_dense, dense_grad = results[3:7]
    return (
        output,
        grad,
        dense_grad.reshape(dense_master.shape),
        expert_grad.reshape(expert_master.shape),
        dense_update.reshape(dense_master.shape),
        momentum_dense.reshape(dense_master.shape),
        variance_dense.reshape(dense_master.shape),
        expert_update.reshape(expert_master.shape),
        momentum_expert.reshape(expert_master.shape),
        variance_expert.reshape(expert_master.shape),
        gain_grads,
    )


def solution(mesh):
    tokens = P(("dp", "expert"), None, None)
    flat = P(("dp", "expert"))
    pairs = P(("dp", "expert"), None)
    expert = P("expert", "dp")
    return jax.shard_map(
        on_device,
        mesh=mesh,
        in_specs=(tokens, tokens, pairs, pairs, flat, flat, flat, expert, expert, expert),
        out_specs=(tokens, tokens, flat, expert, flat, flat, flat, expert, expert, expert, P()),
        check_vma=False,
    )
```

```python
import functools
import math

import jax
import jax.numpy as jnp
from jax import lax
from jax.experimental import pallas as pl
from jax.experimental.pallas import tpu as pltpu
from jax.sharding import PartitionSpec as P

HEADS = 12
HEAD_DIM = 64
LANES = 128

f32 = jnp.float32
bf16 = jnp.bfloat16

eps_norm = 1e-06
beta_first = 0.9
beta_second = 0.999
adam_eps = 1e-08
adam_step = 10.0

VMEM = pl.BlockSpec(memory_space=pltpu.VMEM)
SMEM = pl.BlockSpec(memory_space=pltpu.SMEM)


def params(mib=56):
    return pltpu.CompilerParams(vmem_limit_bytes=mib << 20)


def cost(rows=0):
    return pl.CostEstimate(flops=1 + int(rows * 16.45e6), bytes_accessed=1, transcendentals=0)


def dot(a, b):
    return lax.dot_general(a, b, (((1,), (0,)), ((), ())), preferred_element_type=f32)


def dot_nt(a, b):
    return lax.dot_general(a, b, (((1,), (1,)), ((), ())), preferred_element_type=f32)


def dot_tn(a, b):
    return lax.dot_general(a, b, (((0,), (0,)), ((), ())), preferred_element_type=f32)


def norm_rows(hidden):
    center = hidden - jnp.mean(hidden, axis=-1, keepdims=True)
    inverse = lax.rsqrt(jnp.mean(center * center, axis=-1, keepdims=True) + eps_norm)
    return center * inverse, inverse


def norm_back(upstream, normed, inverse, gain):
    scaled = upstream * gain
    gain_grad = jnp.sum(upstream * normed, axis=0, keepdims=True)
    centered = (
        scaled
        - jnp.mean(scaled, axis=-1, keepdims=True)
        - normed * jnp.mean(scaled * normed, axis=-1, keepdims=True)
    )
    return inverse * centered, gain_grad


def normal_cdf(v):
    return 0.5 * (1.0 + lax.erf(v * 0.7071067811865476))


def density(v):
    return jnp.exp(-0.5 * v * v) * 0.3989422804014327


def to_rows(read, write, first_q, rows, wide, tiles):
    blocks = 4 if rows % 64 == 0 else 1
    count = rows // blocks
    for b in range(blocks):
        for j in range(tiles):
            if wide:
                write(b * count, count, j, read(first_q + tiles * b + j, count, 4 * tiles))
            else:
                write(b * count, count, j, read(first_q + tiles * count * b + j, count, tiles))


def pack_dense_kernel(dims, k_ref, tail_ref, own_ref, out_ref, buf):
    rows, tail_rows, tail, own, step, tiles, chunks, wide_ok = dims
    buf[0:tail] = tail_ref[...]
    buf[tail : tail + own] = own_ref[...]
    buf[tail + own :] = jnp.zeros((buf.shape[0] - tail - own, LANES), f32)
    k = k_ref[0]
    start = tail - step * k

    def read(first, count, stride):
        return buf[pl.ds(first, count, stride=stride), :]

    def write(first, count, j, value):
        out_ref[first : first + count, LANES * j : LANES * (j + 1)] = value.astype(bf16)

    wide = (k >= chunks // 2) & (k < 3 * chunks // 4) & wide_ok

    if wide_ok:

        @pl.when(wide)
        def _():
            to_rows(read, write, start, rows, True, tiles)

    @pl.when(jnp.logical_not(wide))
    def _():
        to_rows(read, write, start, rows, False, tiles)

    for j in range(tiles):
        write(rows, tail_rows, j, read(own + j, tail_rows, tiles))


def pack_expert_kernel(dims, cuts, wide_ref, own_ref, *out_refs):
    rows, tiles = dims

    def read(first, count, stride):
        return own_ref[pl.ds(first, count, stride=stride), :]

    def write(first, count, j, value):
        value = value.astype(bf16)
        for (low, high), ref in zip(cuts, out_refs):
            start, end = max(first, low), min(first + count, high)
            if start < end:
                ref[start - low : end - low, LANES * j : LANES * (j + 1)] = value[start - first : end - first]

    wide = wide_ref[0] > 0

    @pl.when(wide)
    def _():
        to_rows(read, write, 0, rows, True, tiles)

    @pl.when(jnp.logical_not(wide))
    def _():
        to_rows(read, write, 0, rows, False, tiles)


def add_up(refs):
    return sum(ref[...].astype(f32) for ref in refs)


def unpack_kernel(dims, groups, wide_ref, *refs):
    rows, tiles = dims
    (*refs, rows_ref), small_ref = refs, None
    if len(refs) > sum(groups) + 2:
        *refs, small_ref, before_ref, out_ref, square_ref, head_ref = refs
    else:
        *refs, out_ref, square_ref = refs
    at = 0
    for count in groups:
        value = add_up(refs[:count])
        refs = refs[count:]
        rows_ref[at : at + value.shape[0]] = value
        at += value.shape[0]
    wide = wide_ref[0] > 0

    def store(is_wide):
        total = jnp.zeros((1, LANES), f32)
        quarter = rows // 4
        for q in range(4):
            for j in range(tiles):
                piece = rows_ref[q * quarter : (q + 1) * quarter, LANES * j : LANES * (j + 1)]
                if is_wide:
                    at = pl.ds(tiles * q + j, quarter, stride=4 * tiles)
                else:
                    at = pl.ds(tiles * quarter * q + j, quarter, stride=tiles)
                out_ref[at, :] = piece
                total = total + jnp.sum(piece * piece, axis=0, keepdims=True)
        if small_ref is None:
            square_ref[...] = total
        else:
            count = small_ref.shape[0]
            square_ref[0:count] = small_ref[...]
            square_ref[count:] = jnp.zeros((square_ref.shape[0] - count, LANES), f32)
            square_ref[count : count + 1] = total + before_ref[...]
            head_ref[...] = out_ref[0:count]

    @pl.when(wide)
    def _():
        store(True)

    @pl.when(jnp.logical_not(wide))
    def _():
        store(False)


def adam_values(clip, grad, momentum, variance):
    clipped = grad * clip
    momentum_new = beta_first * momentum + (1.0 - beta_first) * clipped
    variance_new = beta_second * variance + (1.0 - beta_second) * clipped * clipped
    first_hat = momentum_new / (1.0 - beta_first**adam_step)
    second_hat = variance_new / (1.0 - beta_second**adam_step)
    return -first_hat / (jnp.sqrt(second_hat) + adam_eps), momentum_new, variance_new


def adam_kernel(dims, k_ref, total_ref, head_ref, *refs):
    step, chunks, devices, param_count, router_rows = dims
    sources, refs = refs[:6], refs[6:]
    outs, dense_outs, gains_ref, refs = refs[:3], refs[3:7], refs[7], refs[8:]
    held, slots, buf, dense_slots, in_sems, sems, dense_in, dense_sems = refs[:3], *refs[3:]
    flat_ref, dense_m, dense_v = dense_slots.at[0], dense_slots.at[1], dense_slots.at[2]
    rows = slots.shape[2]

    def arriving(c, i):
        at = slice(c * rows, (c + 1) * rows)
        return pltpu.make_async_copy(sources[i].at[at], held[i].at[at], in_sems.at[c, i])

    def leaving(c, i):
        target = outs[i].at[c * rows : (c + 1) * rows]
        return pltpu.make_async_copy(slots.at[c % 4, i], target, sems.at[c % 4, i])

    count, own = sources[3].shape[0], sources[4].shape[0]
    dense_copies = [pltpu.make_async_copy(sources[3], buf.at[0:count], dense_in.at[0])]
    for i in (1, 2):
        dense_copies.append(pltpu.make_async_copy(sources[3 + i], dense_slots.at[i], dense_in.at[i]))
    for copy in dense_copies:
        copy.start()
    for c in range(chunks):
        for i in range(3):
            arriving(c, i).start()

    summed = head_ref.shape[0]
    squares = total_ref[summed : summed + 1]
    for at in range(0, summed, 8):
        part = total_ref[at : at + 8]
        squares = squares + jnp.sum(part * part, axis=0, keepdims=True)
    square_sum = jnp.sum(squares, axis=1, keepdims=True)
    clip = jnp.minimum(1.0, jnp.sqrt(param_count / (square_sum + 1e-06)))
    tiles = gains_ref.shape[1] // LANES
    for which in range(gains_ref.shape[0]):
        for j in range(tiles):
            at = router_rows + which * tiles + j
            gains_ref[which : which + 1, LANES * j : LANES * (j + 1)] = total_ref[at : at + 1]

    for copy in dense_copies:
        copy.wait()
    last = k_ref[0] == devices - 1

    @pl.when(last)
    def _():
        buf[count : count + summed] = total_ref[0:summed]

    @pl.when(jnp.logical_not(last))
    def _():
        buf[count : count + summed] = head_ref[...]

    grad = buf[pl.ds(step * k_ref[0], own), :]
    values = adam_values(clip, grad, dense_m[...], dense_v[...])
    for i, value in enumerate((grad, *values)):
        dense_slots[i] = value
    targets = (dense_outs[3], *dense_outs[:3])
    copies = start_all([dense_slots.at[i] for i in range(4)], targets, dense_sems)
    for c in range(chunks):
        at = slice(c * rows, (c + 1) * rows)
        for i in range(3):
            arriving(c, i).wait()
            if c >= 4:
                leaving(c - 4, i).wait()
        values = adam_values(clip, held[0][at], held[1][at], held[2][at])
        for i, value in enumerate(values):
            slots[c % 4, i] = value
            leaving(c, i).start()
    for c in range(max(0, chunks - 4), chunks):
        for i in range(3):
            leaving(c, i).wait()
    wait_all(copies)


def route_kernel(
    experts, capacity, stride, me_ref, prio_row, prio_col, picks, picks_t, cot,
    cols_ref, near_ref, rows_ref, g_ref,
):
    count = picks.shape[0]
    me = me_ref[0]
    before = (prio_row[...] < prio_col[...]).astype(f32).astype(bf16)
    lane = lax.broadcasted_iota(jnp.int32, (count, experts), 1)
    sub = lax.broadcasted_iota(jnp.int32, (experts, count), 0)
    hot = [(picks[:, j : j + 1] == lane).astype(f32) for j in range(2)]
    hot_t = [(picks_t[j : j + 1, :] == sub).astype(f32) for j in range(2)]
    first = jnp.sum(hot[0], axis=0, keepdims=True)
    first_t = jnp.sum(hot_t[0], axis=1, keepdims=True)
    for j in range(2):
        earlier = dot(before, hot[j].astype(bf16)) + (first if j else 0.0)
        earlier_t = dot_nt(hot_t[j].astype(bf16), before) + (first_t if j else 0.0)
        place = jnp.sum(earlier * hot[j], axis=1, keepdims=True).astype(jnp.int32)
        place_t = jnp.sum(earlier_t * hot_t[j], axis=0, keepdims=True).astype(jnp.int32)
        pick, pick_t = picks[:, j : j + 1], picks_t[j : j + 1, :]
        kept = (place < capacity) & (pick >= 0)
        cols_ref[:, j : j + 1] = jnp.where(kept, pick * stride + place, -1)
        near_ref[:, j : j + 1] = jnp.where(kept, (pick ^ me) * stride + place, -1)
        kept = (place_t < capacity) & (pick_t >= 0)
        rows_ref[j : j + 1, :] = jnp.where(kept, pick_t * stride + place_t, -1)
    first, second = slot_selects(rows_ref, experts * stride)
    g_ref[...] = dot(first + second, cot[...]).astype(bf16)


def slot_selects(rows_ref, slots):
    sub = lax.broadcasted_iota(jnp.int32, (slots, rows_ref.shape[1]), 0)
    return [(rows_ref[j : j + 1, :] == sub).astype(f32).astype(bf16) for j in range(2)]


def token_selects(cols_ref, slots):
    lane = lax.broadcasted_iota(jnp.int32, (cols_ref.shape[0], slots), 1)
    return [(cols_ref[:, j : j + 1] == lane).astype(f32).astype(bf16) for j in range(2)]


def split_lanes(column):
    high = column.astype(bf16).astype(f32)
    rest = column - high
    middle = rest.astype(bf16).astype(f32)
    low = rest - middle
    lane = lax.broadcasted_iota(jnp.int32, (column.shape[0], LANES), 1)
    wide = jnp.where(lane == 0, high, jnp.where(lane == 1, middle, jnp.where(lane == 2, low, 0.0)))
    return wide.astype(bf16)


def head_masks():
    lane = lax.broadcasted_iota(jnp.int32, (1, 2 * HEAD_DIM), 1)
    first = (lane < HEAD_DIM).astype(f32)
    return first.astype(bf16), (1.0 - first).astype(bf16)


def soft_scores(queries, key_rows, key_ok):
    scores = dot_nt(queries, key_rows) * HEAD_DIM ** (-0.5)
    scores = jnp.where(key_ok, scores, -1e30)
    top = jnp.max(scores, axis=-1, keepdims=True)
    raised = jnp.exp(scores - top)
    return raised * (1.0 / jnp.sum(raised, axis=-1, keepdims=True))


def put_chunk(scratch, low, chunk, value, first=0):
    place = chunk ^ low
    scratch[place & 1, place >> 1, first : first + value.shape[0], :] = value


def matrix(w_ref, index):
    per = w_ref.shape[0] // 4
    width = w_ref.shape[2]
    rows = width // per
    return w_ref[index * per : (index + 1) * per, 0:rows, :].reshape(width, width)


def quarter_in(w_ref, q):
    width = w_ref.shape[2]
    rows = width // w_ref.shape[0]
    return w_ref[:, q * rows : (q + 1) * rows, :].reshape(width, width)


def start_all(sources, targets, sems):
    copies = [pltpu.make_async_copy(a, b, sems.at[i]) for i, (a, b) in enumerate(zip(sources, targets))]
    for copy in copies:
        copy.start()
    return copies


def wait_all(copies):
    for copy in copies:
        copy.wait()


def layer_copies(spots, arrays, place_ref, layer, target, sems):
    low, top = place_ref[0], place_ref[1]
    found = []
    for j, (array, before, behind) in enumerate(spots):
        source = arrays[array].at[before + (layer ^ top,) + behind + (pl.ds(0, target.shape[1]),)]
        found.append(pltpu.make_async_copy(source, target.at[j ^ low], sems.at[j ^ low]))
    return found


def attn_fwd(seq, stream_ref, gain, w_ref, out_ref, a_ref, q_ref, k_ref, v_ref, o_ref):
    normed, _ = norm_rows(stream_ref[...])
    a_ref[...] = (normed * gain).astype(bf16)
    for index, ref in enumerate((q_ref, k_ref, v_ref)):
        ref[...] = dot(a_ref[...], matrix(w_ref, index)).astype(bf16)
    count = stream_ref.shape[0]
    key_ok = lax.broadcasted_iota(jnp.int32, (count, count), 1) < seq
    masks = head_masks()
    for pair in range(HEADS // 2):
        lanes = slice(2 * HEAD_DIM * pair, 2 * HEAD_DIM * (pair + 1))
        mixed = None
        for mask in masks:
            soft = soft_scores(q_ref[:, lanes] * mask, k_ref[:, lanes], key_ok).astype(bf16)
            part = dot(soft, v_ref[:, lanes] * mask)
            mixed = part if mixed is None else mixed + part
        o_ref[:, lanes] = mixed.astype(bf16)
    out_ref[...] = stream_ref[...] + dot(o_ref[...], matrix(w_ref, 3))


def attn_bwd(seq, grad_ref, stream_ref, gain, w_ref, q_ref, k_ref, v_ref, out_ref, dq_ref, dk_ref, dv_ref, do_ref):
    do_ref[...] = dot_nt(grad_ref[...].astype(bf16), matrix(w_ref, 3)).astype(bf16)
    count = grad_ref.shape[0]
    key_ok = lax.broadcasted_iota(jnp.int32, (count, count), 1) < seq
    masks = head_masks()
    scale = HEAD_DIM ** (-0.5)
    for pair in range(HEADS // 2):
        lanes = slice(2 * HEAD_DIM * pair, 2 * HEAD_DIM * (pair + 1))
        dq = dk = dv = None
        for mask in masks:
            q_h = q_ref[:, lanes] * mask
            k_h = k_ref[:, lanes] * mask
            do_h = do_ref[:, lanes] * mask
            soft = soft_scores(q_h, k_ref[:, lanes], key_ok)
            dsoft = dot_nt(do_h, v_ref[:, lanes])
            dv_h = dot_tn(soft.astype(bf16), do_h)
            inner = jnp.sum(dsoft * soft, axis=-1, keepdims=True)
            dscore = (soft * (dsoft - inner)).astype(bf16)
            dq_h = dot(dscore, k_h)
            dk_h = dot_tn(dscore, q_h)
            dq = dq_h if dq is None else dq + dq_h
            dk = dk_h if dk is None else dk + dk_h
            dv = dv_h if dv is None else dv + dv_h
        dq_ref[:, lanes] = (dq * scale).astype(bf16)
        dk_ref[:, lanes] = (dk * scale).astype(bf16)
        dv_ref[:, lanes] = dv.astype(bf16)
    back = None
    for index, ref in enumerate((dq_ref, dk_ref, dv_ref)):
        part = dot_nt(ref[...], matrix(w_ref, index))
        back = part if back is None else back + part
    normed, inverse = norm_rows(stream_ref[...])
    addend, gain_grad = norm_back(back, normed, inverse, gain)
    out_ref[...] = grad_ref[...] + addend
    return gain_grad


def leave_chunk(scratch, low, chunk, keep_ref, send_refs, sem):
    place = chunk ^ low
    source = scratch.at[place & 1, place >> 1]

    @pl.when((place & 1) == 0)
    def _():
        pltpu.make_async_copy(source, keep_ref.at[place >> 1], sem).start()

    at = 0
    for ref, count in send_refs:

        @pl.when(((place & 1) == 1) & ((place >> 1) >= at) & ((place >> 1) < at + count))
        def _():
            pltpu.make_async_copy(source, ref.at[(place >> 1) - at], sem).start()

        at += count


def wait_chunks(scratch, low, keep_ref, sems):
    for chunk in range(2 * scratch.shape[1]):
        place = chunk ^ low
        pltpu.make_async_copy(scratch.at[place & 1, place >> 1], keep_ref.at[place >> 1], sems.at[chunk]).wait()


def attn_weights(low, grad_ref, a_ref, o_ref, dq_ref, dk_ref, dv_ref, dw, keep_ref, send_ref, sems):
    rows = dw.shape[2]
    per = grad_ref.shape[1] // rows
    branch = grad_ref[...].astype(bf16)
    for index in range(4):
        left = o_ref if index == 3 else a_ref
        right = branch if index == 3 else (dq_ref, dk_ref, dv_ref)[index][...]
        value = dot_tn(left[...], right)
        for i in range(per):
            put_chunk(dw, low, index * per + i, value[i * rows : (i + 1) * rows].astype(bf16))
            leave_chunk(dw, low, index * per + i, keep_ref, send_ref, sems.at[index * per + i])


def attn_weights_kernel(low_ref, *refs):
    ins, keep_ref, send_ref, refs = refs[:6], refs[6], refs[7], refs[8:]
    held, (dw, in_sems, sems) = refs[:6], refs[6:]
    wait_all(start_all(ins, held, in_sems))
    attn_weights(low_ref[0], *held, dw, keep_ref, [(send_ref, dw.shape[1])], sems)
    wait_chunks(dw, low_ref[0], keep_ref, sems)


def mlp_fwd(stream_ref, gain, w1_ref, w2_ref, out_ref, b_ref, u_ref, cdf_ref):
    width = stream_ref.shape[1]
    normed, _ = norm_rows(stream_ref[...])
    b_ref[...] = (normed * gain).astype(bf16)
    total = None
    for q in range(4):
        pre = dot(b_ref[...], quarter_in(w1_ref, q))
        cdf = normal_cdf(pre)
        u_ref[:, q * width : (q + 1) * width] = pre
        cdf_ref[:, q * width : (q + 1) * width] = cdf
        part = dot((pre * cdf).astype(bf16), matrix(w2_ref, q))
        total = part if total is None else total + part
    out_ref[...] = stream_ref[...] + total


def forward_kernel(seq, spots, dims, by_core, place_ref, stream_ref, picks_ref, rows_ref, *refs):
    rows, experts, count = dims
    arrays, refs = refs[:count], refs[count:]
    if not by_core:
        w1_ref, refs = refs[0], refs[1:]
    outs, refs = refs[:16], refs[16:]
    gains_ref, wr_ref, c_ref, probs_ref, x_ref = refs[:5]
    held, (weights, tails, w_sems, tail_sems, out_sems) = refs[5:21], refs[21:]
    low, top = place_ref[0], place_ref[1]
    per = weights.shape[1]
    copies = {
        layer: layer_copies(spots, arrays, place_ref, layer, weights.at[layer], w_sems.at[layer])
        for layer in (0, 2, 3, 1)
    }
    tail_copies = []
    for j, (array, before, behind) in enumerate(spots):
        source = arrays[array].at[before + (3 ^ top,) + behind + (pl.ds(rows, tails.shape[1]),)]
        tail_copies.append(pltpu.make_async_copy(source, tails.at[j ^ low], tail_sems.at[j]))
    for copy in copies[0] + tail_copies:
        copy.start()
    for copy in copies[0] + tail_copies:
        copy.wait()
    for copy in copies[2] + copies[3] + copies[1]:
        copy.start()
    tail = tails[per - 1].astype(f32)
    gains = [tail[experts + i : experts + i + 1] for i in range(4)]
    gains_ref[...] = tail[experts : experts + 4]
    leaving = []

    def leave(first, last):
        for i in range(first, last):
            leaving.append(pltpu.make_async_copy(held[i], outs[i], out_sems.at[i]))
            leaving[-1].start()

    attn_fwd(seq, stream_ref, gains[0], weights.at[0], *held[0:6])
    leave(0, 6)
    for copy in copies[2] + copies[3]:
        copy.wait()
    mlp_fwd(held[0], gains[1], weights.at[2] if by_core else w1_ref, weights.at[3], *held[6:10])
    leave(6, 10)
    for copy in copies[1]:
        copy.wait()
    attn_fwd(seq, held[6], gains[2], weights.at[1], *held[10:16])
    leave(10, 16)
    wr_ref[...] = router_matrix(tail, stream_ref.shape[1], experts)
    dispatch(held[10], gains[3], wr_ref, picks_ref, rows_ref, c_ref, probs_ref, x_ref)
    for copy in leaving:
        copy.wait()


def mlp_bwd(grad_ref, stream_ref, gain, w1_ref, w2_ref, b_ref, u_ref, cdf_ref, out_ref, put_first, put_second):
    width = grad_ref.shape[1]
    upper = grad_ref[...].astype(bf16)
    back = None
    for q in range(4):
        pre = u_ref[:, q * width : (q + 1) * width]
        cdf = cdf_ref[:, q * width : (q + 1) * width]
        act = (pre * cdf).astype(bf16)
        put_second(q, dot_tn(act, upper).astype(bf16))
        dact = dot_nt(upper, matrix(w2_ref, q))
        dpre = (dact * (cdf + pre * density(pre))).astype(bf16)
        put_first(q, dot_tn(b_ref[...], dpre).astype(bf16))
        part = dot_nt(dpre, quarter_in(w1_ref, q))
        back = part if back is None else back + part
    normed, inverse = norm_rows(stream_ref[...])
    addend, gain_grad = norm_back(back, normed, inverse, gain)
    out_ref[...] = grad_ref[...] + addend
    return gain_grad


def pick_hots(picks, experts):
    lane = lax.broadcasted_iota(jnp.int32, (picks.shape[0], experts), 1)
    return [(picks[:, j : j + 1] == lane).astype(f32) for j in range(2)]


def softmax_rows(logits):
    raised = jnp.exp(logits - jnp.max(logits, axis=-1, keepdims=True))
    return raised / jnp.sum(raised, axis=-1, keepdims=True)


def router_matrix(flat, width, experts):
    block = width // experts
    row = lax.broadcasted_iota(jnp.int32, (block, width), 0)
    lane = lax.broadcasted_iota(jnp.int32, (block, width), 1)
    mine = (lane // experts == row).astype(f32)
    lane = lax.broadcasted_iota(jnp.int32, (width, experts), 0)
    column = lax.broadcasted_iota(jnp.int32, (width, experts), 1)
    pick = (lax.rem(lane, experts) == column).astype(f32).astype(bf16)
    parts = [dot((mine * flat[i : i + 1]).astype(bf16), pick) for i in range(experts)]
    return jnp.concatenate(parts).astype(bf16)


def dispatch(stream_ref, gain, wr_ref, picks_ref, rows_ref, c_ref, probs_ref, x_ref):
    width = stream_ref.shape[1]
    experts = wr_ref.shape[1]
    normed, _ = norm_rows(stream_ref[...])
    c_ref[...] = (normed * gain).astype(bf16)
    probs = softmax_rows(dot(c_ref[...], wr_ref[...]))
    probs_ref[...] = probs
    hots = pick_hots(picks_ref, experts)
    selects = slot_selects(rows_ref, x_ref.shape[0])
    gates = None
    for j in range(2):
        part = dot(selects[j], split_lanes(jnp.sum(probs * hots[j], axis=-1, keepdims=True)))
        gates = part if gates is None else gates + part
    x_ref[:, 0:width] = dot(selects[0] + selects[1], c_ref[...]).astype(bf16)
    x_ref[:, width:] = gates.astype(bf16)


def add_lanes(wide):
    wide = wide.astype(f32)
    return wide[:, 0:1] + wide[:, 1:2] + wide[:, 2:3]


def expert_kernel(dims, spans, me_ref, x_ref, g_ref, *refs):
    parts, quarter, blocks = dims
    weight_refs, refs = refs[: len(spans)], refs[len(spans) :]
    y_refs, refs = refs[: blocks // 2], refs[blocks // 2 :]
    dx_ref, dy_ref, act_ref, dpre_ref, weights, y_near, y_sum, dx_sum, sems = refs
    q = pl.program_id(0)
    width = g_ref.shape[1]
    half = parts // 2
    me = me_ref[0]

    rows = weights.shape[1] // 2

    def copies(side):
        found = []
        for i, ((place, first), ref) in enumerate(zip(spans, weight_refs)):
            low, high = max(first, side * rows), min(first + ref.shape[0], (side + 1) * rows)
            if low < high:
                target = weights.at[place ^ me, low:high]
                found.append(pltpu.make_async_copy(ref.at[low - first : high - first], target, sems.at[side, i]))
        return found

    staged = 2 * quarter >= width // half and rows >= width

    @pl.when(q == 0)
    def _():
        for copy in copies(0) + copies(1):
            copy.start()
        dy_ref[...] = (add_lanes(x_ref[:, width:]) * g_ref[...].astype(f32)).astype(bf16)
        for copy in copies(0) if staged else copies(0) + copies(1):
            copy.wait()

    if staged:

        @pl.when(q == 1)
        def _():
            for copy in copies(1):
                copy.wait()

    first = weights[0:half, pl.ds(pl.multiple_of(q * quarter, 16), quarter), :].reshape(width, width)
    if 4 * quarter >= width:
        per = 4 * quarter // width
        at = pl.ds(pl.multiple_of(lax.rem(q, per) * width, 16), width)
        second = weights[half + q // per, at, :]
    else:
        per = width // (4 * quarter)
        second = weights[pl.ds(half + q * per, per)].reshape(width, width)
    pre = dot(x_ref[:, 0:width], first)
    cdf = normal_cdf(pre)
    act = (pre * cdf).astype(bf16)
    act_ref[...] = act
    dact = dot_nt(dy_ref[...], second)
    dpre = (dact * (cdf + pre * density(pre))).astype(bf16)
    dpre_ref[...] = dpre
    y_part = dot(act, second)
    dx_part = dot_nt(dpre, first)

    @pl.when(q == 0)
    def _():
        y_sum[...] = y_part
        dx_sum[...] = dx_part

    @pl.when(q > 0)
    def _():
        y_sum[...] += y_part
        dx_sum[...] += dx_part

    @pl.when(q == pl.num_programs(0) - 1)
    def _():
        y = y_sum[...].astype(bf16).astype(f32)
        stride = y.shape[0] // blocks
        for block in range(blocks):
            y_near[block ^ me_ref[1]] = y[block * stride : (block + 1) * stride].astype(bf16)
        for pair, ref in enumerate(y_refs):
            ref[...] = y_near[2 * pair : 2 * pair + 2]
        dx_ref[:, 0:width] = dx_sum[...].astype(bf16)
        gate_grad = jnp.sum(g_ref[...].astype(f32) * y, axis=-1, keepdims=True)
        dx_ref[:, width:] = split_lanes(gate_grad)


def expert_grad_kernel(dims, dp_ref, x_ref, dy_ref, act_ref, dpre_ref, *refs):
    parts, quarter = dims
    out_refs, scratch, sems = refs[:4], refs[-2], refs[-1]
    q = pl.program_id(0)
    me = dp_ref[0]
    width = dy_ref.shape[1]
    half = parts // 2
    rows = scratch.shape[1]
    side_rows = rows // 2

    def leave(owner, first, count, sem):
        place = owner ^ me
        side = first // side_rows
        source = scratch.at[place, pl.ds(first, count)]
        at = pl.ds(pl.multiple_of(lax.rem(first, side_rows), 16), count)
        for which, (bit, index) in enumerate(((1, place >> 1), (half, place & (half - 1)))):
            for taken, ref in enumerate((out_refs[2 * which + 1], out_refs[2 * which])):

                @pl.when((side == which) & (((place & bit) > 0) == (taken == 1)))
                def _():
                    pltpu.make_async_copy(source, ref.at[index, at], sem).start()

    first = dot_tn(x_ref[:, 0:width], dpre_ref[...]).astype(bf16)
    count = width // half
    at = pl.multiple_of(q * quarter, 16)
    for i in range(half):
        scratch[i ^ me, pl.ds(at, quarter), :] = first[i * count : (i + 1) * count]
        leave(i, at, quarter, sems.at[i])
    second = dot_tn(act_ref[...], dy_ref[...]).astype(bf16)
    step = min(width, side_rows)
    for i in range(width // step):
        flat = q * width + i * step
        owner, at = half + flat // rows, pl.multiple_of(lax.rem(flat, rows), 16)
        scratch[owner ^ me, pl.ds(at, step), :] = second[i * step : (i + 1) * step]
        leave(owner, at, step, sems.at[half + i])

    @pl.when(q == pl.num_programs(0) - 1)
    def _():
        whole = out_refs[0].at[0]
        for _ in range(4):
            for i in range(half):
                pltpu.make_async_copy(scratch.at[0, 0:quarter], whole.at[0:quarter], sems.at[i]).wait()
            for i in range(width // step):
                pltpu.make_async_copy(scratch.at[0, 0:step], whole.at[0:step], sems.at[half + i]).wait()


def combine(stream_ref, gain, wr_ref, picks_ref, cols_ref, cot_ref, c_ref, probs_ref, dx_ref, grad_ref):
    width = stream_ref.shape[1]
    experts = wr_ref.shape[1]
    probs = probs_ref[...]
    hots = pick_hots(picks_ref, experts)
    selects = token_selects(cols_ref, dx_ref.shape[0])
    prob_grad = None
    for j in range(2):
        part = add_lanes(dot(selects[j], dx_ref[:, width:])) * hots[j]
        prob_grad = part if prob_grad is None else prob_grad + part
    logit_grad = probs * (prob_grad - jnp.sum(prob_grad * probs, axis=-1, keepdims=True))
    logit_grad = logit_grad.astype(bf16)
    router_grad = dot_tn(c_ref[...], logit_grad)
    back = dot(selects[0] + selects[1], dx_ref[:, 0:width]) + dot_nt(logit_grad, wr_ref[...])
    normed, inverse = norm_rows(stream_ref[...])
    addend, gain_grad = norm_back(back, normed, inverse, gain)
    grad_ref[...] = cot_ref[...].astype(f32) + addend
    return gain_grad, router_grad


def put_router(out_ref, value, scratch):
    width, experts = value.shape
    many = LANES // experts
    scratch[...] = jnp.zeros_like(scratch)
    scratch[:, 0:experts] = value
    total = None
    for m in range(many):
        rows = scratch[pl.ds(m, width // many, stride=many), :]
        rows = pltpu.roll(rows, m * experts, 1) if m else rows
        total = rows if total is None else total + rows
    out_ref[0 : width // many, :] = total


def backward_kernel(
    seq, spots, count, by_core, place_ref, gains_ref, wr_ref, picks_ref, cols_ref, cot_ref, probs_ref, dx_ref, *refs
):
    ins, refs = refs[:16], refs[16:]
    arrays, refs = refs[:count], refs[count:]
    if not by_core:
        w1_ref, refs = refs[0], refs[1:]
    small_ref, upper_out, dq_out, dk_out, dv_out, grad_out, *refs = refs
    keep_ref, send_ref, keeps_ref, send2_ref, send_rest, *refs = refs
    places = send_ref.shape[0]
    most, rest = send2_ref.shape[0], places - send2_ref.shape[0]
    keeps = (keep_ref, keeps_ref.at[0])
    sends = ([(send_ref, places)], [(send2_ref, most), (send_rest.at[0], rest)])
    if by_core:
        send1_ref, *refs = refs
        keep1_ref, send1 = keeps_ref.at[1], [(send1_ref, most), (send_rest.at[1], rest)]
    else:
        dw1_ref, *refs = refs
    held, refs = refs[:16], refs[16:]
    grads, refs = refs[:4], refs[4:]
    dq_ref, dk_ref, dv_ref, do_ref, dw, dw2, w2_ref, w_attn, *refs = refs
    if by_core:
        dw1, w1_ref, *refs = refs
    router_scratch, in_sems, w_sems, out_sems, last_sems = refs
    low = place_ref[0]
    experts = wr_ref.shape[1]

    def fetch(first, last):
        copies = [pltpu.make_async_copy(ins[i], held[i], in_sems.at[i]) for i in range(first, last)]
        for copy in copies:
            copy.start()
        return copies

    def fetch_layer(layer, target, at):
        copies = layer_copies(spots, arrays, place_ref, layer, target, w_sems.at[at])
        for copy in copies:
            copy.start()
        return copies

    part = fetch(0, 2)
    second = fetch_layer(1, w_attn.at[0], 0) + fetch(2, 8)
    wait_all(part)
    gain_four, router_grad = combine(
        held[0], gains_ref[3:4], wr_ref, picks_ref, cols_ref, cot_ref, held[1], probs_ref, dx_ref, grads[0]
    )
    tiles = router_grad.shape[0] // LANES
    router_rows = router_grad.shape[0] * experts // LANES
    small_ref[...] = jnp.zeros_like(small_ref)
    put_router(small_ref, router_grad, router_scratch)

    def put_gain(which, value):
        at = router_rows + which * tiles
        for j in range(tiles):
            small_ref[at + j : at + j + 1, :] = value[:, LANES * j : LANES * (j + 1)]

    put_gain(3, gain_four)
    middle = fetch(8, 12) + fetch_layer(3, w2_ref, 1)
    if by_core:
        middle += fetch_layer(2, w1_ref, 2)
    wait_all(second)
    stream, q, k, v, a, o = held[2:8]
    gain_three = attn_bwd(
        seq, grads[0], stream, gains_ref[2:3], w_attn.at[0], q, k, v, grads[1], dq_ref, dk_ref, dv_ref, do_ref
    )
    put_gain(2, gain_three)
    attn_weights(low, grads[0], a, o, dq_ref, dk_ref, dv_ref, dw, keeps[0], sends[0], out_sems.at[0])
    first = fetch(12, 16) + fetch_layer(0, w_attn.at[1], 3)
    wait_all(middle)
    stream, b, u, cdf = held[8:12]
    width = stream.shape[1]
    groups = w1_ref.shape[0]

    def put_first(q, value):
        rows = width // groups
        for i in range(groups):
            piece = value[i * rows : (i + 1) * rows]
            if by_core:
                put_chunk(dw1, low, i, piece, q * rows)
                if q == 3:
                    leave_chunk(dw1, low, i, keep1_ref, send1, out_sems.at[2, i])
            else:
                dw1_ref[i, q * rows : (q + 1) * rows, :] = piece

    def put_second(q, value):
        rows = dw2.shape[2]
        per = width // rows
        for i in range(per):
            put_chunk(dw2, low, q * per + i, value[i * rows : (i + 1) * rows])
            leave_chunk(dw2, low, q * per + i, keeps[1], sends[1], out_sems.at[1, q * per + i])

    gain_two = mlp_bwd(
        grads[1], stream, gains_ref[1:2], w1_ref, w2_ref, b, u, cdf, grads[2], put_first, put_second
    )
    put_gain(1, gain_two)
    leaving = start_all((grads[2],), (upper_out,), last_sems)
    wait_all(first)
    wait_chunks(dw, low, keeps[0], out_sems.at[0])
    stream, q, k, v = held[12:16]
    gain_one = attn_bwd(
        seq, grads[2], stream, gains_ref[0:1], w_attn.at[1], q, k, v, grads[3], dq_ref, dk_ref, dv_ref, do_ref
    )
    put_gain(0, gain_one)
    outs = ((dq_ref, dq_out), (dk_ref, dk_out), (dv_ref, dv_out), (grads[3], grad_out))
    for i, (source, target) in enumerate(outs):
        leaving.append(pltpu.make_async_copy(source, target, last_sems.at[1 + i]))
        leaving[-1].start()
    wait_chunks(dw2, low, keeps[1], out_sems.at[1])
    if by_core:
        wait_chunks(dw1, low, keep1_ref, out_sems.at[2])
    wait_all(leaving)


def output_kernel(stream_ref, picks_ref, near_ref, probs_ref, grad_ref, *refs):
    y_refs, (other_ref, out_ref, grad_out, wide) = refs[:-4], refs[-4:]
    stride = other_ref.shape[1]
    for pair, ref in enumerate(y_refs):
        wide[2 * pair * stride : (2 * pair + 1) * stride] = ref[0].astype(f32)
        wide[(2 * pair + 1) * stride : (2 * pair + 2) * stride] = other_ref[pair].astype(f32)
    y = wide[...].astype(bf16)
    tiles = stream_ref.shape[1] // LANES
    seq = out_ref.shape[0] // tiles
    probs = probs_ref[...]
    hots = pick_hots(picks_ref, probs.shape[1])
    selects = token_selects(near_ref, y.shape[0])
    total = stream_ref[...]
    for j in range(2):
        gate = jnp.sum(probs * hots[j], axis=-1, keepdims=True)
        total = total + gate * dot(selects[j], y)
    for value, ref in ((total, out_ref), (grad_ref, grad_out)):
        for j in range(tiles):
            ref[pl.ds(j, seq, stride=tiles), :] = value[0:seq, LANES * j : LANES * (j + 1)]


def add_pair(left, right):
    return (left.astype(f32) + right.astype(f32)).astype(bf16)


def pack_sets_kernel(*refs):
    *parts, out_ref, sems = refs
    wait_all(start_all(parts, [out_ref.at[i // 4, i % 4] for i in range(len(parts))], sems))


def fold_layers_kernel(cut, plan, top_ref, *refs):
    uppers, (keep_x, send_y, keep_y, send_x), scratch = refs[-14:-10], refs[-10:-6], refs[-6:]
    kept, got, total, keep_sems, got_sems, out_sems = scratch
    count = kept.shape[1]
    x_part = slice(cut, cut + send_x.shape[1])
    y_part = slice(x_part.stop, x_part.stop + send_y.shape[2])
    ins = []
    for layer, at, sources in plan:
        keep_ref, refs = refs[0], refs[1:]
        keep_ref = keep_ref if at is None else keep_ref.at[at]
        got_refs = []
        for index, many in sources:
            ref, refs = refs[0], refs[1:]
            ref = ref if index is None else ref.at[index]
            got_refs += [ref.at[i] for i in range(many)]
        ins.append((layer, keep_ref, got_refs))

    def arriving(n, i):
        _, keep_ref, got_refs = ins[n]
        return (
            pltpu.make_async_copy(keep_ref.at[i], kept.at[n, i], keep_sems.at[n, i]),
            pltpu.make_async_copy(got_refs[i], got.at[n, i], got_sems.at[n, i]),
        )

    steps = [(n, i) for n in range(len(ins)) for i in range(count)]
    for n, i in steps:
        for copy in arriving(n, i):
            copy.start()
    for n, i in steps:
        layer = ins[n][0]
        place = layer ^ top_ref[0]
        for copy in arriving(n, i):
            copy.wait()
        total[n, i] = add_pair(kept[n, i], got[n, i])
        pltpu.make_async_copy(total.at[n, i, 0:cut], uppers[i % 4].at[layer, i // 4], out_sems.at[n, 0, i]).start()
        for bit, send, keep, where, sem in (
            (place & 1, send_x.at[i], keep_x.at[place >> 1, i], x_part, out_sems.at[n, 1, i]),
            (place >> 1, send_y.at[place & 1, i], keep_y.at[place & 1, i], y_part, out_sems.at[n, 2, i]),
        ):
            for value, target in ((0, keep), (1, send)):

                @pl.when(bit == value)
                def _():
                    pltpu.make_async_copy(total.at[n, i, where], target, sem).start()

    for n, i in steps:
        layer = ins[n][0]
        pltpu.make_async_copy(total.at[n, i, 0:cut], uppers[i % 4].at[layer, i // 4], out_sems.at[n, 0, i]).wait()
        pltpu.make_async_copy(total.at[n, i, x_part], keep_x.at[0, i], out_sems.at[n, 1, i]).wait()
        pltpu.make_async_copy(total.at[n, i, y_part], keep_y.at[0, i], out_sems.at[n, 2, i]).wait()


def add_kernel(left, right, out_ref):
    out_ref[...] = add_pair(left[...], right[...])


def pause_kernel(ref, out_ref):
    for i in range(ref.shape[0]):
        out_ref[i] = ref[i]


def fold_plane_kernel(top_ref, keep_x, got_one, got_two, keep_y, got_y, own_a, send_y, own_b, send_x):
    for place in range(2):

        @pl.when(top_ref[0] >> 1 == place)
        def _():
            near, far = (got_two, got_one) if place == 0 else (got_one, got_two)
            own_a[...] = add_pair(keep_x[0], near[...])
            send_y[...] = add_pair(keep_x[1], far[...])

    own_b[...] = add_pair(keep_y[0], got_y[0])
    send_x[...] = add_pair(keep_y[1], got_y[1])


def fold_rows_kernel(own_a, got_a, own_b, got_b, *outs):
    middle = own_a.shape[1]
    for place in range(own_a.shape[0]):
        out = outs[place % 4].at[place // 4]
        out[0:middle] = add_pair(own_a[place], got_a[place])
        out[middle:] = add_pair(own_b[place], got_b[place])


def fold_uppers_kernel(top_ref, *refs):
    refs, outs, scratch = refs[:-5], refs[-5:-1], refs[-1]
    for layer in range(4):
        scratch[layer ^ top_ref[0]] = sum(ref[layer].astype(f32) for ref in refs).astype(bf16)
    for place, out in enumerate(outs):
        out[...] = scratch[place]


def fold_expert_kernel(highs, *refs):
    ins, outs = refs[:4], refs[4:]
    count = ins[0].shape[0]
    for side, high in enumerate(highs):
        half = count // 2
        for i in range(count):
            which, at = (i // half, i % half) if high else (i % 2, i // 2)
            outs[side * count + which * half + at][...] = add_pair(ins[2 * side][i], ins[2 * side + 1][i])


def swap(value, axes, mask):
    size = 1
    for axis in axes:
        size *= lax.axis_size(axis)
    return lax.ppermute(value, axes, [(i, i ^ mask) for i in range(size)])


def after(value, *others):
    return lax.optimization_barrier((value, others))[0]


def pause(scalars, rows, others):
    scalars, others = lax.optimization_barrier((scalars, others))
    scalars = pl.pallas_call(
        pause_kernel,
        in_specs=[SMEM],
        out_specs=SMEM,
        out_shape=shape(scalars.shape, jnp.int32),
        compiler_params=params(),
        cost_estimate=cost(rows),
        name="pause",
    )(scalars)
    return scalars, others


class Order:
    def __init__(self):
        self.latest = ()

    def land(self, value):
        self.latest = after(value, self.latest)
        return self.latest


def bit_groups(bits):
    odd = len(bits) % 2
    return [bits[:odd]] * odd + [bits[i : i + 2] for i in range(odd, len(bits), 2)]


def all_sum_step(value, axes, bits):
    if len(bits) == 1:
        return value + swap(value, axes, 1 << bits[0])
    low, high = 1 << bits[0], 1 << bits[1]
    near, far, both = swap(value, axes, low), swap(value, axes, high), swap(value, axes, low | high)
    return (value + near) + (far + both)


def reduce_bits(value, axes, bits):
    for bit in bits:
        pairs = value.reshape((value.shape[0] // 2, 2) + value.shape[1:])
        value = pairs[:, 0] + swap(pairs[:, 1], axes, 1 << bit)
    return value[0]


def shape(dims, dtype=f32):
    return jax.ShapeDtypeStruct(dims, dtype)


def on_device(
    tokens,
    cotangent,
    expert_picks,
    priority,
    dense_master,
    dense_momentum,
    dense_variance,
    expert_master,
    expert_momentum,
    expert_variance,
):
    both = ("dp", "expert")
    dp_ranks = lax.axis_size("dp")
    expert_ranks = lax.axis_size("expert")
    devices = dp_ranks * expert_ranks
    local_experts = expert_master.shape[0]
    experts = local_experts * expert_ranks
    images, seq, width = tokens.shape
    assert local_experts == 1 and images == 1
    assert devices & (devices - 1) == 0 and dp_ranks >= 4
    tiles = width // LANES
    dp_me = lax.axis_index("dp").astype(jnp.int32)
    me = dp_me * expert_ranks + lax.axis_index("expert").astype(jnp.int32)
    me_arr = me.reshape(1)
    dp_arr = dp_me.reshape(1)
    dp_bits = dp_ranks.bit_length() - 1
    all_bits = devices.bit_length() - 1

    own = dense_master.shape[0] // LANES
    expert_flat = expert_master.shape[1] // LANES
    hidden = expert_master.shape[1] * dp_ranks // (2 * width)
    matrix_rows = 8 * width + 2 * hidden
    rows = matrix_rows // devices
    step = own - rows * tiles
    tail = step * devices
    tail_rows = -(-tail // (16 * tiles)) * 16
    wide_ok = rows % 64 == 0
    expert_rows = expert_flat // tiles

    dense_flat = dense_master.reshape(own, LANES)
    forward_ring = [(i, (i + 1) % devices) for i in range(devices)]
    backward_ring = [((i + 1) % devices, i) for i in range(devices)]
    tail_from = lax.ppermute(dense_flat[own - tail :], both, forward_ring)
    buf_rows = -(-(own + max(tail, tail_rows * tiles)) // 8) * 8
    chunk = pl.pallas_call(
        functools.partial(
            pack_dense_kernel, (rows, tail_rows, tail, own, step, tiles, devices, wide_ok)
        ),
        in_specs=[SMEM, VMEM, VMEM],
        out_specs=VMEM,
        out_shape=shape((rows + tail_rows, width), bf16),
        scratch_shapes=[pltpu.VMEM((buf_rows, LANES), f32)],
        compiler_params=params(),
        cost_estimate=cost(),
        name="pack_dense",
    )(me_arr, tail_from, dense_flat)

    expert_wide = (dp_me < dp_ranks // 2).astype(jnp.int32).reshape(1)
    quarter = expert_rows // 4
    cuts = [(0, 2), (2, 4), (0, 1), (1, 2), (2, 3), (3, 4)]
    cuts = [(low * quarter, high * quarter) for low, high in cuts]
    expert_chunks = pl.pallas_call(
        functools.partial(pack_expert_kernel, (expert_rows, tiles), cuts),
        in_specs=[SMEM, VMEM],
        out_specs=[VMEM] * 6,
        out_shape=[shape((high - low, width), bf16) for low, high in cuts],
        compiler_params=params(),
        cost_estimate=cost(),
        name="pack_expert",
    )(expert_wide, expert_master.reshape(expert_flat, LANES))
    dp_axis = ("dp",)
    dp_order = list(range(dp_bits))

    def gather_step(parts, bit):
        return {**parts, **{at | (1 << bit): swap(part, dp_axis, 1 << bit) for at, part in parts.items()}}

    capacity = 2 * seq // experts
    stride = -(-capacity // 8) * 8
    slots = experts * stride
    padded = -(-seq // 16) * 16
    fill = padded - seq
    ranks = jnp.pad(priority, ((0, 0), (0, fill)), constant_values=1 << 20)
    picks = jnp.pad(expert_picks, ((0, fill), (0, 0)), constant_values=-1)
    cot = jnp.pad(cotangent.reshape(seq, width), ((0, fill), (0, 0)))
    stream = jnp.pad(tokens.reshape(seq, width).astype(f32), ((0, fill), (0, 0)))
    e_me = lax.axis_index("expert").astype(jnp.int32).reshape(1)
    pair_shape = shape((2, stride, width), bf16)
    cols, near_cols, rows_slots, outgoing_cot = pl.pallas_call(
        functools.partial(route_kernel, experts, capacity, stride),
        in_specs=[SMEM] + [VMEM] * 5,
        out_specs=[VMEM] * 4,
        out_shape=[shape((padded, 2), jnp.int32)] * 2
        + [shape((2, padded), jnp.int32), shape((slots, width), bf16)],
        compiler_params=params(),
        cost_estimate=cost(),
        name="route",
    )(e_me, ranks, ranks.reshape(padded, 1), picks, picks.T, cot)

    def exchange(value):
        dims = value.shape
        value = value.reshape(expert_ranks, slots // expert_ranks, dims[1])
        value = lax.all_to_all(value, "expert", split_axis=0, concat_axis=0, tiled=True)
        return value.reshape(dims)

    per = devices // 4
    per_bits = per.bit_length() - 1
    top_bits = (per_bits, per_bits + 1)
    chunk_rows = rows + tail_rows
    low = me & (per - 1)
    low_arr = low.reshape(1)
    place_arr = jnp.stack([low, me >> per_bits])
    expert_me = jnp.concatenate([dp_arr, e_me])
    half_rows = expert_rows // 2
    orders = (dp_order, dp_order[::-1])
    expert_parts, expert_spans = [], []
    if per_bits == 3 and dp_bits == 2:
        masks = [1 << bit for bit in top_bits]
        split = chunk_rows // 32 * 16 + 16
        order = Order()

        def spread(value):
            return [swap(value, both, mask) for mask in masks]

        sets = [chunk, swap(chunk, both, 2), None, None]
        near, far = [spread(chunk)] + [None] * 3, [None] * 4
        near[0] = order.land(near[0])
        sets[1] = order.land(sets[1])
        near[1] = spread(sets[1])
        sets[2] = swap(after(chunk, sets[1]), both, 4)
        halves = [swap(near[0][1][:split], both, masks[0]), swap(near[0][0][split:], both, masks[1])]
        near[1] = order.land(near[1])
        halves = order.land(halves)
        far[0] = jnp.concatenate(halves)
        x_half, y_half, *quarters = expert_chunks
        first, second = after((quarters[2], quarters[0]), halves)
        early = [swap(first, dp_axis, 1), swap(second, dp_axis, 2)]
        sets[2], outgoing_cot, stream = order.land((sets[2], outgoing_cot, stream))
        sets[3] = swap(sets[2], both, 2)
        near[2] = spread(sets[2])
        early = order.land(early)
        place_arr, early = pause(place_arr, 100, early)
        sets[3], far[0], place_arr = order.land((sets[3], far[0], place_arr))
        far[1], far[2] = swap(far[0], both, 2), swap(far[0], both, 4)
        near[3] = spread(sets[3])
        near[2] = order.land(near[2])
        near[3] = order.land(near[3])
        far[1] = order.land(far[1])
        far[2] = order.land(far[2])
        far[3] = swap(far[2], both, 2)
        arriving_cot = exchange(after(outgoing_cot, far[2]))

        def pack_sets(which):
            ins = [part for s in which for part in (sets[s], *near[s], far[s])]
            return pl.pallas_call(
                pack_sets_kernel,
                in_specs=[pl.BlockSpec(memory_space=pl.ANY)] * len(ins),
                out_specs=VMEM,
                out_shape=shape((len(which), 4, chunk_rows, width), bf16),
                scratch_shapes=[pltpu.SemaphoreType.DMA((len(ins),))],
                compiler_params=params(),
                cost_estimate=cost(),
                name="pack_sets",
            )(*ins)

        x_out, y_out = after((x_half, y_half), near[3])
        beside = [swap(x_out, dp_axis, 1), swap(y_out, dp_axis, 2)]
        packed = [pack_sets([0, 1, 2])]
        first_swap = swap(packed[0], both, 1)
        far[3], beside = order.land(after((far[3], beside), packed))
        packed.append(pack_sets([3]))
        arrays = [*packed, first_swap, swap(packed[1], both, 1)]
        at = ((0, 0), (0, 1), (0, 2), (1, 0))
        spots = [(at[j >> 1][0] + 2 * (j & 1), (at[j >> 1][1],), ()) for j in range(per)]
        place_arr, beside = pause(place_arr, 4400, beside)
        across = [swap(beside[0], dp_axis, 2), swap(beside[1], dp_axis, 1)]
        late = after((quarters[3], quarters[1]), beside)
        late = [swap(late[0], dp_axis, 1), swap(late[1], dp_axis, 2)]
        place_arr, arrays[2] = pause(place_arr, 300, arrays[2])
        expert_me, (across, arriving_cot) = pause(expert_me, 400, (across, arriving_cot))
        expert_parts = [x_half, y_half, beside[0], early[0], late[0], beside[1], early[1], late[1], *across]
        expert_spans = [(0, 0), (0, 2), (1, 0), (1, 2), (1, 3), (2, 2), (2, 0), (2, 1), (3, 0), (3, 2)]
        expert_spans = [(place, first * quarter) for place, first in expert_spans]
    else:
        gathered = chunk[None]
        for bit in range(all_bits):
            gathered = jnp.concatenate([gathered, swap(gathered, both, 1 << bit)])
        arrays = [gathered.reshape(4, per, chunk_rows, width)]
        spots = [(0, (), (j,)) for j in range(per)]
        for side, bits in enumerate(orders):
            parts, places = [expert_chunks[side]], [0]
            for bit in bits:
                parts = parts + [swap(part, dp_axis, 1 << bit) for part in parts]
                places = places + [place | (1 << bit) for place in places]
            expert_parts += parts
            expert_spans += [(place, side * half_rows) for place in places]
        arriving_cot = exchange(outgoing_cot)

    layer_w = pltpu.VMEM((per, rows, width), bf16)
    if not wide_ok:
        first_in = lax.dynamic_index_in_dim(arrays[0], 2 ^ (me >> per_bits), 0, keepdims=False)
        first_in = jnp.take(first_in, jnp.arange(per) ^ low, axis=0)[:, :rows].reshape(width, 4, width)
        first_in = first_in.transpose(1, 0, 2).reshape(1, 4 * width, width)

    act_shape = shape((padded, width), bf16)
    stream_shape = shape((padded, width), f32)
    gain_shape = shape((1, width), f32)
    tok_flops = 2 * padded * width * width
    weight_bytes = 2 * width * width
    ANY = pl.BlockSpec(memory_space=pl.ANY)

    def call(kernel, ins, in_specs, outs, name, rows=0, mib=56, out_specs=None, scratch=(), aliases=None):
        out_specs = out_specs or [None] * len(outs)

        def whole(a):
            return pl.BlockSpec(a.shape, lambda *_, n=len(a.shape): (0,) * n)

        return pl.pallas_call(
            kernel,
            grid=(1,),
            in_specs=[s or whole(a) for a, s in zip(ins, in_specs, strict=True)],
            out_specs=[s or whole(a) for a, s in zip(outs, out_specs, strict=True)],
            out_shape=outs,
            scratch_shapes=list(scratch),
            compiler_params=params(mib),
            cost_estimate=cost(rows),
            input_output_aliases=aliases or {},
            name=name,
        )(*ins)

    places = per // 2
    core_shape = shape((places, rows, width), bf16)
    by_core = pltpu.VMEM((2, places, rows, width), bf16)
    stream_vmem, act_vmem = pltpu.VMEM((padded, width), f32), pltpu.VMEM((padded, width), bf16)

    def attn_weights_call(grad, kept, found):
        return call(
            attn_weights_kernel,
            (low_arr, grad, kept[0], kept[4], *found),
            (SMEM,) + (ANY,) * 6,
            [core_shape, core_shape],
            "attn_weights",
            0,
            out_specs=[ANY] * 2,
            scratch=[
                stream_vmem,
                *[act_vmem] * 5,
                by_core,
                pltpu.SemaphoreType.DMA((6,)),
                pltpu.SemaphoreType.DMA((per,)),
            ],
        )

    outs = [stream_shape] + [act_shape] * 5 + [stream_shape, act_shape] + [shape((padded, hidden))] * 2
    outs += [stream_shape] + [act_shape] * 5
    *results, gains, router, moe_in, probs, outgoing = call(
        functools.partial(forward_kernel, seq, spots, (rows, experts, len(arrays)), wide_ok),
        (place_arr, stream, picks, rows_slots, *arrays, *([] if wide_ok else [first_in])),
        (SMEM, None, None, None) + (ANY,) * len(arrays) + (() if wide_ok else (None,)),
        outs
        + [
            shape((4, width)),
            shape((width, experts), bf16),
            act_shape,
            shape((padded, experts)),
            shape((slots, width + LANES), bf16),
        ],
        "forward",
        0,
        out_specs=[ANY] * 16 + [None] * 5,
        scratch=[pltpu.VMEM(o.shape, o.dtype) for o in outs]
        + [
            pltpu.VMEM((4, per, rows, width), bf16),
            pltpu.VMEM((per, tail_rows, width), bf16),
            pltpu.SemaphoreType.DMA((4, per)),
            pltpu.SemaphoreType.DMA((per,)),
            pltpu.SemaphoreType.DMA((16,)),
        ],
    )
    stream_one, kept_one = results[0], results[1:6]
    stream_two, mlp_in, mlp_pre, mlp_cdf = results[6:10]
    stream_three, kept_two = results[10], results[11:]
    arriving = exchange(outgoing)

    slot_spec = pl.BlockSpec((slots, width), lambda q: (0, 0))
    wide_spec = pl.BlockSpec((slots, width + LANES), lambda q: (0, 0))
    pair_spec = pl.BlockSpec((2, stride, width), lambda q: (0, 0, 0))
    hidden_spec = pl.BlockSpec((slots, width), lambda q: (0, q))
    pairs = experts // 2
    *expert_out, input_back, slot_grad, expert_act, pre_grad = pl.pallas_call(
        functools.partial(expert_kernel, (dp_ranks, quarter, experts), expert_spans),
        grid=(4,),
        in_specs=[SMEM, wide_spec, slot_spec] + [ANY] * len(expert_parts),
        out_specs=[pair_spec] * pairs + [wide_spec, slot_spec, hidden_spec, hidden_spec],
        out_shape=[pair_shape] * pairs
        + [shape((slots, width + LANES), bf16), shape((slots, width), bf16)]
        + [shape((slots, hidden), bf16)] * 2,
        scratch_shapes=[
            pltpu.VMEM((dp_ranks, expert_rows, width), bf16),
            pltpu.VMEM((experts, stride, width), bf16),
            pltpu.VMEM((slots, width), f32),
            pltpu.VMEM((slots, width), f32),
            pltpu.SemaphoreType.DMA((2, len(expert_parts))),
        ],
        compiler_params=params(),
        cost_estimate=cost(),
        name="expert",
    )(expert_me, arriving, arriving_cot, *expert_parts)
    returned_grad = exchange(input_back)
    part_shape = shape((expert_rows // 2, width), bf16)
    count = dp_ranks // 2
    expert_first = pl.pallas_call(
        functools.partial(expert_grad_kernel, (dp_ranks, quarter)),
        grid=(4,),
        in_specs=[SMEM, wide_spec, slot_spec, hidden_spec, hidden_spec],
        out_specs=[ANY] * 4,
        out_shape=[shape((count,) + part_shape.shape, bf16)] * 4,
        scratch_shapes=[
            pltpu.VMEM((dp_ranks, expert_rows, width), bf16),
            pltpu.SemaphoreType.DMA((2 * dp_ranks,)),
        ],
        compiler_params=params(),
        cost_estimate=cost(),
        name="expert_grad",
    )(dp_arr, arriving, slot_grad, expert_act, pre_grad)
    returned_grad = after(returned_grad, expert_first)

    cut = max(16, rows // 48 * 16)
    x_rows = max(16, (rows - cut) * 9 // 256 * 16)
    y_rows = rows - cut - x_rows
    top = (me >> per_bits).reshape(1)
    z_bits = list(range(1, per_bits))
    z_masks = [2 * j for j in (1, 2, 3)]
    assert places % 4 == 0

    def add_call(left, right, weight):
        return call(add_kernel, (left, right), (None, None), [shape(left.shape, bf16)], "add", weight, mib=12)[0]

    def over_z(values, meanwhile, weight=0):
        farthest = swap(values[3], both, 2)
        farthest, *meanwhile[:] = lax.optimization_barrier((farthest, *meanwhile))
        near = swap(after(values[1], farthest), both, 2)
        return [values[0], near, swap(add_call(values[2], farthest, weight), both, 4)]

    def rest_of_z(values):
        if len(z_bits) == 2:
            return values
        total = sum(value.astype(f32) for value in values).astype(bf16)
        lead = total.ndim - 3
        total = jnp.moveaxis(total, lead, 0)
        return [reduce_bits(total, both, z_bits[2:])]

    def to_other_core(parts):
        return [parts[0], swap(parts[1], both, 1)]

    expert_got = [swap(expert_first[0], dp_axis, 1), swap(expert_first[2], dp_axis, dp_ranks // 2)]
    returned_grad, expert_out = lax.optimization_barrier((returned_grad, expert_out))
    expert_out = [expert_out[0]] + [swap(v, ("expert",), 2 * j) for j, v in enumerate(expert_out) if j]
    backward_ins = (
        (stream_three, moe_in, stream_two, *kept_two[1:4], kept_two[0], kept_two[4])
        + (stream_one, mlp_in, mlp_pre, mlp_cdf, stream, *kept_one[1:4])
    )
    held_vmem = [stream_vmem, act_vmem, stream_vmem] + [act_vmem] * 5
    held_vmem += [stream_vmem, act_vmem] + [pltpu.VMEM((padded, hidden), f32)] * 2 + [stream_vmem] + [act_vmem] * 3
    kinds = 2 if wide_ok else 1
    most, rest = places * 3 // 4, places // 4
    keeps_shape = shape((kinds,) + core_shape.shape, bf16)
    most_shape, rest_shape = shape((most, rows, width), bf16), shape((kinds, rest, rows, width), bf16)
    first_dw_out = [most_shape] if wide_ok else [shape((1, 4 * width, width), bf16)]
    small, upper, dq, dk, dv, grad, *dws = call(
        functools.partial(backward_kernel, seq, spots, len(arrays), wide_ok),
        (place_arr, gains, router, picks, cols, cot, probs, returned_grad, *backward_ins, *arrays)
        + (() if wide_ok else (first_in,)),
        (SMEM,) + (None,) * 7 + (ANY,) * (16 + len(arrays)) + (() if wide_ok else (None,)),
        [shape((tail, LANES)), stream_shape, act_shape, act_shape, act_shape, stream_shape]
        + [core_shape, core_shape, keeps_shape, most_shape, rest_shape]
        + first_dw_out,
        "backward",
        out_specs=[None] + [ANY] * 10 + ([ANY] if wide_ok else [None]),
        scratch=held_vmem
        + [stream_vmem] * 4
        + [act_vmem] * 4
        + [by_core, by_core, layer_w, pltpu.VMEM((2, per, rows, width), bf16)]
        + ([by_core, layer_w] if wide_ok else [])
        + [
            pltpu.VMEM((width, LANES), f32),
            pltpu.SemaphoreType.DMA((16,)),
            pltpu.SemaphoreType.DMA((4, per)),
            pltpu.SemaphoreType.DMA((3, per)),
            pltpu.SemaphoreType.DMA((5,)),
        ],
    )
    if not wide_ok:
        wide_grad = dws[5].reshape(4, width, width).transpose(1, 0, 2).reshape(per, rows, width)
        wide_grad = jnp.take(wide_grad, jnp.arange(per) ^ low, axis=0)
        wide_grad = wide_grad.reshape(places, 2, rows, width)
        dws[2] = jnp.concatenate([dws[2], wide_grad[None, :, 0]])
        dws[4] = jnp.concatenate([dws[4], wide_grad[None, most:, 1]])
        dws[5] = wide_grad[:most, 1]
    dws, expert_out = lax.optimization_barrier((dws, expert_out))
    most_got = [swap(dws[3], both, 1), swap(dws[5], both, 1)]
    rest_got = swap(dws[4], both, 1)
    first_dw = attn_weights_call(upper, kept_one, (dq, dk, dv))
    layer_got = {0: [(swap(first_dw[1], both, 1), None, places)], 1: [(swap(dws[1], both, 1), None, places)]}
    for i, layer in enumerate((3, 2)):
        layer_got[layer] = [(most_got[i], None, most), (rest_got, i, rest)]
    layer_keep = {3: (dws[2], 0), 2: (dws[2], 1), 1: (dws[0], None), 0: (first_dw[0], None)}

    x_plane, y_plane = (shape((2, places, part, width), bf16) for part in (x_rows, y_rows))
    x_line, y_line = (shape((places, part, width), bf16) for part in (x_rows, y_rows))
    plane_specs = [pl.BlockSpec((2, 1, part, width), lambda i: (0, i, 0, 0)) for part in (x_rows, y_rows)]
    line_specs = [pl.BlockSpec((1, part, width), lambda i: (i, 0, 0)) for part in (x_rows, y_rows)]
    upper_shape = shape((4, places // 4, cut, width), bf16)
    sums, got_x = (), []
    masks = [1 << bit for bit in top_bits]
    for pair in ((3, 2), (1, 0)):
        if pair[0] == 1:
            expert_got, sums = lax.optimization_barrier((expert_got, sums))
            top, expert_got = pause(top, 1600, expert_got)
        plan, ins = [], []
        for layer in pair:
            keep, at = layer_keep[layer]
            parts = layer_got[layer]
            plan.append((layer, at, [part[1:] for part in parts]))
            ins += [after(keep, first_dw) if layer == 3 else keep] + [part[0] for part in parts]
        *sums, out = call(
            functools.partial(fold_layers_kernel, cut, plan),
            (top, *ins, *sums),
            (SMEM,) + (ANY,) * (len(ins) + len(sums)),
            [upper_shape] * 4 + [x_plane, y_plane, y_plane, x_line],
            "fold_layers",
            out_specs=[ANY] * 8,
            scratch=[pltpu.VMEM((2, places, rows, width), bf16)] * 3
            + [
                pltpu.SemaphoreType.DMA((2, places)),
                pltpu.SemaphoreType.DMA((2, places)),
                pltpu.SemaphoreType.DMA((2, 3, places)),
            ],
            aliases={1 + len(ins) + i: i for i in range(len(sums))},
        )
        got_x.append(swap(out, both, masks[0]))
    *uppers, keep_x, send_y, keep_y = sums
    got_y = swap(send_y, both, masks[1])
    me_top, landed = top, [got_x[0]]
    uppers = over_z(uppers, landed, 300)
    got_x[:1] = landed
    expert_ins = (expert_first[1], expert_got[0], expert_first[3], expert_got[1])
    expert_second = call(
        functools.partial(fold_expert_kernel, (dp_bits == 1, True)),
        expert_ins,
        (None,) * len(expert_ins),
        [part_shape] * (2 * count),
        "fold_expert",
        0,
    )

    top, uppers = pause(top, 250, uppers)
    uppers = [value.reshape(4, -1, cut, width) for value in uppers]
    uppers = [value.reshape(4, cut, width) for value in rest_of_z(uppers)]
    upper_rows = call(
        fold_uppers_kernel,
        (top, *uppers),
        (SMEM,) + (None,) * len(uppers),
        [shape((cut, width), bf16)] * 4,
        "fold_uppers",
        100,
        scratch=[pltpu.VMEM((4, cut, width), bf16)],
    )
    got_x, got_y, expert_second = lax.optimization_barrier((got_x, got_y, expert_second))
    own_a, send_y, own_b, send_x = pl.pallas_call(
        fold_plane_kernel,
        grid=(places,),
        in_specs=[SMEM, plane_specs[0], line_specs[0], line_specs[0], plane_specs[1], plane_specs[1]],
        out_specs=[line_specs[0]] * 2 + [line_specs[1]] * 2,
        out_shape=[x_line] * 2 + [y_line] * 2,
        compiler_params=params(),
        cost_estimate=cost(),
        name="fold_plane",
    )(me_top, keep_x, *got_x, keep_y, got_y)
    got_y, got_x = swap(send_y, both, masks[1]), swap(send_x, both, masks[0])
    got_y, got_x = after((got_y, got_x), top)
    expert_second = after(expert_second, got_y, got_x)
    other_out = swap(jnp.stack([value[1] for value in expert_out]), ("expert",), 1)
    lower_rows = call(
        fold_rows_kernel,
        (own_a, got_y, own_b, got_x),
        (None,) * 4,
        [shape((places // 4, rows - cut, width), bf16)] * 4,
        "fold_rows",
        0,
    )
    lower_rows, other_out = lax.optimization_barrier((lower_rows, other_out))
    output, grad = call(
        output_kernel,
        (stream_three, picks, near_cols, probs, grad, *expert_out, other_out),
        (None,) * (6 + pairs),
        [shape((seq * tiles, LANES))] * 2,
        "output",
        mib=16,
        scratch=[pltpu.VMEM((slots, width), f32)],
    )
    image = (1, seq, width)
    meanwhile = [output.reshape(image), grad.reshape(image), upper_rows]
    lower_rows = over_z(lower_rows, meanwhile, 250)
    output, grad, upper_rows = meanwhile
    half = count // 2
    expert_groups = []
    for side, bits in enumerate(orders):
        keep, send = (expert_second[(2 * side + i) * half : (2 * side + i + 1) * half] for i in range(2))
        got = [swap(part, dp_axis, 1 << bits[1]) for part in send]
        expert_groups.append([list(pair) for pair in zip(keep, got)])
    if dp_bits > 2:
        for side, bits in enumerate(orders):
            value = [sum(pair) for pair in expert_groups[side]]
            for bit in bits[2:]:
                half = len(value) // 2
                keep, send = (value[:half], value[half:]) if side else (value[0::2], value[1::2])
                value = [k + swap(v, dp_axis, 1 << bit) for k, v in zip(keep, send)]
            expert_groups[side] = [value]
    expert_groups = [side[0] for side in expert_groups]
    upper_rows, expert_groups = lax.optimization_barrier((upper_rows, expert_groups))

    def unpack(wide, groups, count, name, extra=(), more_shapes=((1, LANES),)):
        pieces = [piece for group in groups for piece in group] + list(extra)
        return pl.pallas_call(
            functools.partial(unpack_kernel, (count, tiles), [len(group) for group in groups]),
            in_specs=[SMEM] + [VMEM] * len(pieces),
            out_specs=[VMEM] * (1 + len(more_shapes)),
            out_shape=[shape((count * tiles, LANES))] + [shape(dims) for dims in more_shapes],
            scratch_shapes=[pltpu.VMEM((count, width), f32)],
            compiler_params=params(),
            cost_estimate=cost(),
            name=name,
        )(wide, *pieces)

    expert_grad, expert_square = unpack(expert_wide, expert_groups, expert_rows, "unpack_expert")
    lower_rows, output, expert_grad, expert_square = lax.optimization_barrier(
        (lower_rows, output, expert_grad, expert_square)
    )
    lower_rows = rest_of_z(lower_rows)
    upper_rows = [upper_rows[0]] + [
        swap(value, both, masks[0] * j) for j, value in enumerate(upper_rows) if j
    ]
    dense_groups = [upper_rows, [value.reshape(rows - cut, width) for value in lower_rows]]

    dense_wide = (me >= devices // 2) & (me < 3 * devices // 4) & wide_ok
    dense_rows, total, head = unpack(
        dense_wide.astype(jnp.int32).reshape(1),
        dense_groups,
        rows,
        "unpack_dense",
        (small, expert_square),
        ((tail + 8, LANES), (tail, LANES)),
    )
    head = lax.ppermute(head, both, backward_ring)
    groups = bit_groups(list(range(all_bits)))
    for bits in groups[:-1]:
        total = all_sum_step(total, both, bits)
    total, head = lax.optimization_barrier((total, head))
    total = all_sum_step(total, both, groups[-1])
    param_count = (dense_master.size + expert_master.size) * devices

    chunks = 8
    results = pl.pallas_call(
        functools.partial(adam_kernel, (step, chunks, devices, param_count, width * experts // LANES)),
        in_specs=[SMEM, VMEM, VMEM] + [ANY] * 6,
        out_specs=[ANY] * 7 + [VMEM],
        out_shape=[shape((expert_flat, LANES))] * 3 + [shape((own, LANES))] * 4 + [shape((4, width))],
        scratch_shapes=[pltpu.VMEM((expert_flat, LANES), f32)] * 3
        + [
            pltpu.VMEM((4, 3, expert_flat // chunks, LANES), f32),
            pltpu.VMEM((-(-(rows * tiles + tail) // 8) * 8, LANES), f32),
            pltpu.VMEM((4, own, LANES), f32),
            pltpu.SemaphoreType.DMA((chunks, 3)),
            pltpu.SemaphoreType.DMA((4, 3)),
            pltpu.SemaphoreType.DMA((3,)),
            pltpu.SemaphoreType.DMA((4,)),
        ],
        compiler_params=params(),
        cost_estimate=cost(),
        name="adam",
    )(
        me_arr,
        total,
        head,
        expert_grad,
        expert_momentum.reshape(expert_flat, LANES),
        expert_variance.reshape(expert_flat, LANES),
        dense_rows,
        dense_momentum.reshape(own, LANES),
        dense_variance.reshape(own, LANES),
    )
    gain_grads = results[7]
    expert_update, momentum_expert, variance_expert = results[:3]
    dense_update, momentum_dense, variance_dense, dense_grad = results[3:7]
    return (
        output,
        grad,
        dense_grad.reshape(dense_master.shape),
        expert_grad.reshape(expert_master.shape),
        dense_update.reshape(dense_master.shape),
        momentum_dense.reshape(dense_master.shape),
        variance_dense.reshape(dense_master.shape),
        expert_update.reshape(expert_master.shape),
        momentum_expert.reshape(expert_master.shape),
        variance_expert.reshape(expert_master.shape),
        gain_grads,
    )


def solution(mesh):
    tokens = P(("dp", "expert"), None, None)
    flat = P(("dp", "expert"))
    pairs = P(("dp", "expert"), None)
    expert = P("expert", "dp")
    return jax.shard_map(
        on_device,
        mesh=mesh,
        in_specs=(tokens, tokens, pairs, pairs, flat, flat, flat, expert, expert, expert),
        out_specs=(tokens, tokens, flat, expert, flat, flat, flat, expert, expert, expert, P()),
        check_vma=False,
    )
```
